32 devices in a mesh: dp: 8 (over z, x), mp: 4 (over y, core).
Axes of the slice: x: 2, y: 2, z: 4, core: 2. Of those that a mesh axis runs over, the one named last changes fastest.
Arguments:
- tokens: bfloat16 [8, 2048, 768], P('dp'), may hold values from -6 to 6
- segment_ids: int32 [8, 2048], P('dp'), may hold values from 0 to 7, never falling along the last dimension, each value on 1 to 1024 neighbouring positions
- gain_one: float32 [768], replicated, may hold values from 0.5 to 1.5
- bias_one: float32 [768], replicated, may hold values from -1.75 to 1.75
- query_weight: bfloat16 [768, 768], P(None, 'mp'), may hold values from -0.3125 to 0.3125
- query_bias: float32 [768], P('mp'), may hold values from -3 to 3
- key_weight: bfloat16 [768, 768], P(None, 'mp'), may hold values from -0.21875 to 0.21875
- value_weight: bfloat16 [768, 768], P(None, 'mp'), may hold values from -0.21875 to 0.21875
- value_bias: float32 [768], P('mp'), may hold values from -3 to 3
- output_weight: bfloat16 [768, 768], P('mp'), may hold values from -0.875 to 0.875
- output_bias: float32 [768], replicated, may hold values from -3 to 3
- gain_two: float32 [768], replicated, may hold values from 0.5 to 1.5
- bias_two: float32 [768], replicated, may hold values from -1.75 to 1.75
- inner_weight: bfloat16 [768, 3072], P(None, 'mp'), may hold values from -0.21875 to 0.21875
- inner_bias: float32 [3072], P('mp'), may hold values from -3 to 3
- outer_weight: bfloat16 [3072, 768], P('mp'), may hold values from -0.109375 to 0.109375
- outer_bias: float32 [768], replicated, may hold values from -3 to 3
- cotangent: bfloat16 [8, 2048, 768], P('dp'), may hold values from -6 to 6
Outputs:
- layer_out: bfloat16 [8, 2048, 768], P('dp')
- input_grad: float32 [8, 2048, 768], P('dp')
- grad_gain_one: float32 [768], replicated
- grad_bias_one: float32 [768], replicated
- grad_query_weight: float32 [768, 768], P(None, 'mp')
- grad_query_bias: float32 [768], P('mp')
- grad_key_weight: float32 [768, 768], P(None, 'mp')
- grad_value_weight: float32 [768, 768], P(None, 'mp')
- grad_value_bias: float32 [768], P('mp')
- grad_output_weight: float32 [768, 768], P('mp')
- grad_output_bias: float32 [768], replicated
- grad_gain_two: float32 [768], replicated
- grad_bias_two: float32 [768], replicated
- grad_inner_weight: float32 [768, 3072], P(None, 'mp')
- grad_inner_bias: float32 [3072], P('mp')
- grad_outer_weight: float32 [3072, 768], P('mp')
- grad_outer_bias: float32 [768], replicated
The draws below stay inside these ranges and needn't reach their ends.
Inputs may be any that keep to these rules, and one draw needn't show every extreme that they name: `segment_ids`: ids never fall along a row; a document holds at most 1024 characters and some document holds exactly that many.
All inputs are finite; a program needn't handle non-finite values.
Results may differ from the reference program's by a relative error of at most 0.013.
Values may be sent and summed in bfloat16 or wider, within the bound.
No kernel may reach another device: no remote copies, remote signals or barrier semaphores. Data moves between devices by JAX's collectives and lax.ppermute only.
A program may use at most 192 MiB of HBM per device.

```python
import math
import jax
import jax.numpy as jnp
import numpy as np
from jax import lax

D = 768
HEADS = 12
FF = 3072
HEAD = 64
LEN = 2048
ROWS = 8


def levels(own_key, shape, split, low, largest):
    def one(axis_at, blocks):
        steps = jax.random.uniform(jax.random.fold_in(jax.random.fold_in(own_key, 6), axis_at), (blocks,), jnp.float32, low / len(split), largest / len(split))
        return jnp.repeat(jnp.exp(steps), shape[axis_at] // blocks).reshape((-1,) + (1,) * (len(shape) - axis_at - 1))

    factor_of = one(*split[0])
    for cut in split[1:]:
        factor_of = factor_of * one(*cut)
    return factor_of


def split_up(number_of, total, most, slope):
    loads = [(1 << 20) // math.isqrt(grade ** slope) + 1 for grade in range(2, number_of + 1)]
    surplus, given = total - most - (number_of - 1), [1] * (number_of - 1)
    while surplus > 0:
        candidates = [i for i in range(number_of - 1) if given[i] < most]
        pool, remaining = sum([loads[i] for i in candidates]), surplus
        for i in candidates:
            addition = min(most - given[i], max(1, remaining * loads[i] // pool), surplus)
            given[i] = given[i] + addition
            surplus = surplus - addition
    return np.array([most] + given)


def uneven_parts(stream_key, count, total, bound, slope):
    if count == 2:
        one = jax.random.randint(stream_key, (), max(1, total - bound), min(bound, total - 1) + 1)
        return jnp.stack([one, total - one])
    sizes = jnp.asarray(split_up(count, total, bound, slope), jnp.int32)
    couples = (count - 1) // 2
    donor, sink = sizes[1:1 + 2 * couples:2], sizes[2:2 + 2 * couples:2]
    slack = jnp.minimum(donor - 1, bound - sink)
    shifted = jax.random.randint(jax.random.fold_in(stream_key, 1), (couples,), 0, 1 << 20) % (slack + 1)
    sizes = sizes.at[1:1 + 2 * couples:2].set(donor - shifted).at[2:2 + 2 * couples:2].set(sink + shifted)
    return sizes[jax.random.permutation(jax.random.fold_in(stream_key, 2), count)]


def centred(rng, dims, width, bound, split=(), dtype=jnp.bfloat16):
    drawn = width * jax.random.normal(rng, dims, jnp.float32)
    if split:
        drawn = drawn * levels(rng, dims, split, -0.22, 0.18)
    return jnp.clip(drawn, -bound, bound).astype(dtype)


def setup_inputs(seed: int = 0) -> dict:
    streams_of = jax.random.split(jax.random.key(seed), 19)
    return {
        "tokens": centred(streams_of[0], (ROWS, LEN, D), 1.0, 6.0, ((0, 8),)),
        "segment_ids": jax.vmap(lambda own: jnp.searchsorted(jnp.cumsum(uneven_parts(own, 8, LEN, LEN // 2, 1)), jnp.arange(LEN), side="right"))(jax.random.split(streams_of[1], ROWS)).reshape((ROWS, LEN)).astype(jnp.int32),
        "gain_one": jnp.clip(1.0 + 0.1 * jax.random.normal(streams_of[2], (D,), jnp.float32), 0.5, 1.5),
        "bias_one": centred(streams_of[3], (D,), 0.3, 1.75, (), jnp.float32),
        "query_weight": centred(streams_of[4], (D, D), (D // 2) ** -0.5, 0.3125, ((1, 4),)),
        "query_bias": centred(streams_of[5], (D,), 0.5, 3.0, ((0, 4),), jnp.float32),
        "key_weight": centred(streams_of[6], (D, D), D ** -0.5, 0.21875, ((1, 4),)),
        "value_weight": centred(streams_of[7], (D, D), D ** -0.5, 0.21875, ((1, 4),)),
        "value_bias": centred(streams_of[8], (D,), 0.5, 3.0, ((0, 4),), jnp.float32),
        "output_weight": centred(streams_of[9], (D, D), (D // 16) ** -0.5, 0.875, ((0, 4),)),
        "output_bias": centred(streams_of[10], (D,), 0.5, 3.0, (), jnp.float32),
        "gain_two": jnp.clip(1.0 + 0.1 * jax.random.normal(streams_of[11], (D,), jnp.float32), 0.5, 1.5),
        "bias_two": centred(streams_of[12], (D,), 0.3, 1.75, (), jnp.float32),
        "inner_weight": centred(streams_of[13], (D, FF), D ** -0.5, 0.21875, ((1, 4),)),
        "inner_bias": centred(streams_of[14], (FF,), 0.5, 3.0, ((0, 4),), jnp.float32),
        "outer_weight": centred(streams_of[15], (FF, D), FF ** -0.5, 0.109375, ((0, 4),)),
        "outer_bias": centred(streams_of[16], (D,), 0.5, 3.0, (), jnp.float32),
        "cotangent": centred(streams_of[17], (ROWS, LEN, D), 1.0, 6.0, ((0, 8),)),
    }


@jax.custom_vjp
def low(v):
    return lax.optimization_barrier(v.astype(jnp.bfloat16)).astype(jnp.float32)

@jax.custom_vjp
def low_back(v):
    return v

def low_keep(v):
    return (low(v), None)

def low_pass(kept, grad):
    return (grad,)

def back_keep(v):
    return (v, None)

def back_low(kept, grad):
    return (low(grad),)
low.defvjp(low_keep, low_pass)
low_back.defvjp(back_keep, back_low)

def product(left, right):
    return jnp.dot(left, right, precision=lax.Precision.HIGHEST, preferred_element_type=jnp.float32)

def layer_norm(values, gain, shift):
    center = values - lax.optimization_barrier(jnp.mean(values, axis=-1, keepdims=True))
    scale = lax.rsqrt(lax.optimization_barrier(jnp.mean(center * center, axis=-1, keepdims=True)) + 1e-05)
    return center * scale * gain + shift

def forward_row(weights, values, segments):
    gain_one, bias_one, query_weight, query_bias, key_weight, value_weight, value_bias, output_weight, output_bias, gain_two, bias_two, inner_weight, inner_bias, outer_weight, outer_bias = weights
    length = values.shape[0]
    block = min(512, length)
    factor = HEAD ** (-0.5)
    attend_in = low(layer_norm(values, gain_one, bias_one))
    queries = low(low_back(product(attend_in, query_weight) + query_bias))
    keys_all = low(low_back(product(attend_in, key_weight)))
    values_all = low(low_back(product(attend_in, value_weight) + value_bias))
    query_blocks = queries.reshape(length // block, block, HEADS, HEAD)
    segment_blocks = segments.reshape(length // block, block)
    key_heads = keys_all.reshape(length, HEADS, HEAD)
    value_heads = values_all.reshape(length, HEADS, HEAD)

    def attend_block(item):
        query_block, segment_block = item
        scores = low_back(jnp.einsum('qhd,khd->hqk', query_block, key_heads, precision=lax.Precision.HIGHEST) * factor)
        allowed = segment_block[:, None] == segments[None, :]
        scores = jnp.where(allowed[None], scores, -1e+30)
        chances = low(jax.nn.softmax(scores, axis=-1))
        return jnp.einsum('hqk,khd->qhd', chances, value_heads, precision=lax.Precision.HIGHEST)
    context = lax.map(jax.checkpoint(attend_block), (query_blocks, segment_blocks))
    attended = low(low_back(context.reshape(length, HEADS * HEAD)))
    residual = values + low_back(product(attended, output_weight)) + output_bias
    expand_in = low(layer_norm(residual, gain_two, bias_two))
    hidden = low_back(product(expand_in, inner_weight) + inner_bias)
    activated = low(jax.nn.gelu(hidden, approximate=False))
    return residual + low_back(product(activated, outer_weight)) + outer_bias

def reference(tokens, segment_ids, gain_one, bias_one, query_weight, query_bias, key_weight, value_weight, value_bias, output_weight, output_bias, gain_two, bias_two, inner_weight, inner_bias, outer_weight, outer_bias, cotangent):
    params = tuple((entry.astype(jnp.float32) for entry in (gain_one, bias_one, query_weight, query_bias, key_weight, value_weight, value_bias, output_weight, output_bias, gain_two, bias_two, inner_weight, inner_bias, outer_weight, outer_bias)))
    inputs = tokens.astype(jnp.float32)
    upstream = cotangent.astype(jnp.float32)

    def step(carry, item):
        row_values, row_segments, row_upstream = item
        result, pullback = jax.vjp(lambda weights, values: forward_row(weights, values, row_segments), params, row_values)
        grads, grad_row = pullback(row_upstream)
        carry = tuple((first + second for first, second in zip(carry, grads)))
        return (carry, (result, grad_row))
    start_sums = tuple((jnp.zeros_like(entry) for entry in params))
    totals, (results, grad_rows) = lax.scan(step, start_sums, (inputs, segment_ids, upstream))
    return (results.astype(jnp.bfloat16), grad_rows, totals[0], totals[1], totals[2], totals[3], totals[4], totals[5], totals[6], totals[7], totals[8], totals[9], totals[10], totals[11], totals[12], totals[13], totals[14])
```

```python
import functools

import jax
import jax.numpy as jnp
from jax import lax
from jax.experimental import pallas as pl
from jax.experimental.pallas import tpu as pltpu
from jax.sharding import Mesh
from jax.sharding import PartitionSpec as P

HEAD = 64
WIDE = 128
TILE = 256
MASKED = 1e30
F32 = jnp.float32
BF16 = jnp.bfloat16
MP = ("y", "core")
SWAP = [(0, 1), (1, 0)]


def nn(left, right):
    return lax.dot_general(left, right, (((1,), (0,)), ((), ())), preferred_element_type=F32)


def nt(left, right):
    return lax.dot_general(left, right, (((1,), (1,)), ((), ())), preferred_element_type=F32)


def tn(left, right):
    return lax.dot_general(left, right, (((0,), (0,)), ((), ())), preferred_element_type=F32)


def stats(values):
    center = values - jnp.mean(values, axis=-1, keepdims=True)
    scale = lax.rsqrt(jnp.mean(center * center, axis=-1, keepdims=True) + 1e-05)
    return center * scale, scale


def norm_back(grad_out, normed, scale, gain):
    upstream = grad_out * gain
    return scale * (
        upstream
        - jnp.mean(upstream, axis=-1, keepdims=True)
        - normed * jnp.mean(upstream * normed, axis=-1, keepdims=True)
    )


def project_body(x_ref, seg_ref, gain_ref, bias_ref, wt_ref, wn_ref, qb_ref, vb_ref, vbn_ref,
                 ai_ref, qt_ref, kt_ref, vt_ref, kn_ref, vn_ref):
    heads = kn_ref.shape[0]
    width = heads * HEAD
    normed, _ = stats(x_ref[...].astype(F32))
    ai = (normed * gain_ref[...] + bias_ref[...]).astype(BF16)
    ai_ref[...] = ai
    low = nt(wt_ref[...], ai)
    queries = ((low[:width] + qb_ref[...]).astype(BF16)).astype(F32) * HEAD ** -0.5
    kt_ref[...] = low[width:2 * width].astype(BF16)
    vt_ref[...] = (low[2 * width:] + vb_ref[...]).astype(BF16)
    tile = x_ref.shape[0]
    row = lax.broadcasted_iota(jnp.int32, (WIDE, tile), 0) - HEAD
    same = jnp.where(row == seg_ref[...], 1.0, 0.0)
    same = jnp.where(row >= 0, same, 0.0)
    for h in range(heads):
        qt_ref[h, :HEAD, :] = queries[h * HEAD:(h + 1) * HEAD].astype(BF16)
        qt_ref[h, HEAD:, :] = same[HEAD:].astype(BF16)
    lane = lax.broadcasted_iota(jnp.int32, (tile, WIDE), 1)
    mask = jnp.where((lane >= HEAD) & (lane < HEAD + 8), (same.T - 1.0) * MASKED, 0.0)
    mask = jnp.where((lane >= HEAD + 8) & (lane < HEAD + 11), 1.0, mask)
    ones = jnp.where((lane >= HEAD) & (lane < HEAD + 2), 1.0, 0.0)
    natural = nn(ai, wn_ref[...])
    for h in range(heads):
        kn_ref[h] = (natural[:, h * WIDE:(h + 1) * WIDE] + mask).astype(BF16)
        at = (heads + h) * WIDE
        vn_ref[h] = (natural[:, at:at + WIDE] + vbn_ref[:, h * WIDE:(h + 1) * WIDE] + ones).astype(BF16)


def project(tokens, seg_row, gain, bias, wt, wn, qb, vb, vbn, heads):
    length, features = tokens.shape
    width = heads * HEAD
    const = lambda shape: pl.BlockSpec(shape, lambda i: (0,) * len(shape))
    return pl.pallas_call(
        project_body,
        grid=(length // TILE,),
        in_specs=[
            pl.BlockSpec((TILE, features), lambda i: (i, 0)),
            pl.BlockSpec((1, TILE), lambda i: (0, i)),
            const((1, features)), const((1, features)),
            const(wt.shape), const(wn.shape), const(qb.shape), const(vb.shape), const(vbn.shape),
        ],
        out_specs=[
            pl.BlockSpec((TILE, features), lambda i: (i, 0)),
            pl.BlockSpec((heads, WIDE, TILE), lambda i: (0, 0, i)),
            pl.BlockSpec((width, TILE), lambda i: (0, i)),
            pl.BlockSpec((width, TILE), lambda i: (0, i)),
            pl.BlockSpec((heads, TILE, WIDE), lambda i: (0, i, 0)),
            pl.BlockSpec((heads, TILE, WIDE), lambda i: (0, i, 0)),
        ],
        out_shape=[
            jax.ShapeDtypeStruct((length, features), BF16),
            jax.ShapeDtypeStruct((heads, WIDE, length), BF16),
            jax.ShapeDtypeStruct((width, length), BF16),
            jax.ShapeDtypeStruct((width, length), BF16),
            jax.ShapeDtypeStruct((heads, length, WIDE), BF16),
            jax.ShapeDtypeStruct((heads, length, WIDE), BF16),
        ],
        compiler_params=pltpu.CompilerParams(vmem_limit_bytes=48 << 20),
        name="project",
    )(tokens, seg_row, gain, bias, wt, wn, qb, vb, vbn)


def key_range(seg_ref, seg_all, i):
    first = seg_ref[0, i * TILE]
    last = seg_ref[0, i * TILE + TILE - 1]
    before = jnp.sum(jnp.where(seg_all < first, 1.0, 0.0)).astype(jnp.int32)
    until = jnp.sum(jnp.where(seg_all <= last, 1.0, 0.0)).astype(jnp.int32)
    return before // TILE, (until + TILE - 1) // TILE


def split(value, parts):
    out = []
    for _ in range(parts):
        piece = value.astype(BF16).astype(F32)
        out.append(piece)
        value = value - piece
    return out


def forward_body(segs_ref, seg_ref, qt_ref, kn_ref, vt_ref, out_ref, extra_ref, acc_ref):
    heads = qt_ref.shape[0]
    low, high = key_range(segs_ref, seg_ref[...], pl.program_id(0))
    acc_ref[...] = jnp.zeros_like(acc_ref)

    def step(kb, carry):
        at = pl.multiple_of(kb * TILE, TILE)
        result = []
        for h in range(heads):
            top, total = carry[2 * h], carry[2 * h + 1]
            scores = nn(kn_ref[h, pl.ds(at, TILE), :], qt_ref[h])
            new_top = jnp.maximum(top, jnp.max(scores, axis=0, keepdims=True))
            powered = jnp.exp(scores - new_top)
            fade = jnp.exp(top - new_top)
            result += [new_top, total * fade + jnp.sum(powered, axis=0, keepdims=True)]
            rows = slice(h * HEAD, (h + 1) * HEAD)
            acc_ref[rows] = acc_ref[rows] * fade + nn(vt_ref[rows, pl.ds(at, TILE)], powered.astype(BF16))
        return tuple(result)

    tile = qt_ref.shape[2]
    start = (jnp.full((1, tile), -jnp.inf, F32), jnp.zeros((1, tile), F32)) * heads
    carry = lax.fori_loop(low, high, step, start)
    for h in range(heads):
        top, total = carry[2 * h], carry[2 * h + 1]
        rows = slice(h * HEAD, (h + 1) * HEAD)
        out_ref[rows] = (acc_ref[rows] / total).astype(BF16)
        pieces = split(-(top + jnp.log(total)), 3)
        one_hot = qt_ref[h, HEAD:HEAD + 16, :].astype(F32)
        row = lax.broadcasted_iota(jnp.int32, (16, tile), 0)
        value = one_hot
        for n, piece in enumerate(pieces):
            value = jnp.where(row == 8 + n, piece, value)
        extra_ref[h] = value.astype(BF16)


def attend_forward(seg_row, qt, kn, vt):
    heads, _, length = qt.shape
    width = heads * HEAD
    const = lambda shape: pl.BlockSpec(shape, lambda i: (0,) * len(shape))
    return pl.pallas_call(
        forward_body,
        grid=(length // TILE,),
        in_specs=[
            pl.BlockSpec(memory_space=pltpu.SMEM),
            const((1, length)),
            pl.BlockSpec((heads, WIDE, TILE), lambda i: (0, 0, i)),
            const(kn.shape), const(vt.shape),
        ],
        out_specs=[
            pl.BlockSpec((width, TILE), lambda i: (0, i)),
            pl.BlockSpec((heads, 16, TILE), lambda i: (0, 0, i)),
        ],
        out_shape=[
            jax.ShapeDtypeStruct((width, length), BF16),
            jax.ShapeDtypeStruct((heads, 16, length), BF16),
        ],
        scratch_shapes=[pltpu.VMEM((width, TILE), F32)],
        compiler_params=pltpu.CompilerParams(vmem_limit_bytes=48 << 20),
        name="attend_forward",
    )(seg_row, seg_row, qt, kn, vt)


def backward_body(segs_ref, seg_ref, qt_ref, extra_ref, kn_ref, kt_ref, vn_ref, out_ref, grad_ref,
                  grads_ref, qa_ref, da_ref, dq_ref, dk_ref, dv_ref):
    heads = qt_ref.shape[0]
    width = heads * HEAD
    tile = qt_ref.shape[2]
    i = pl.program_id(0)
    low, high = key_range(segs_ref, seg_ref[...], i)

    @pl.when(i == 0)
    def _():
        dk_ref[...] = jnp.zeros_like(dk_ref)
        dv_ref[...] = jnp.zeros_like(dv_ref)
        qa_ref[...] = jnp.zeros_like(qa_ref)
        da_ref[...] = jnp.zeros_like(da_ref)

    dq_ref[...] = jnp.zeros_like(dq_ref)
    row = lax.broadcasted_iota(jnp.int32, (16, tile), 0)
    for h in range(heads):
        rows = slice(h * HEAD, (h + 1) * HEAD)
        qa_ref[h, :HEAD, :] = qt_ref[h, :HEAD, :]
        qa_ref[h, HEAD:HEAD + 16, :] = extra_ref[h]
        grad = grad_ref[rows]
        da_ref[h, :HEAD, :] = grad
        inner = jnp.sum(grad.astype(F32) * out_ref[rows].astype(F32), axis=0, keepdims=True)
        first, second = split(-inner, 2)
        value = jnp.where(row == 0, first, jnp.where(row == 1, second, 0.0))
        da_ref[h, HEAD:HEAD + 16, :] = value.astype(BF16)

    def step(kb, carry):
        at = pl.multiple_of(kb * TILE, TILE)
        keys = pl.ds(at, TILE)
        for h in range(heads):
            rows = slice(h * HEAD, (h + 1) * HEAD)
            probs = jnp.exp(nn(kn_ref[h, keys, :], qa_ref[h]))
            ds = (probs * nn(vn_ref[h, keys, :], da_ref[h])).astype(BF16)
            dv_ref[rows, keys] += nt(grad_ref[rows], probs.astype(BF16))
            dk_ref[rows, keys] += nt(qa_ref[h, :HEAD, :], ds)
            dq_ref[rows] += nn(kt_ref[rows, keys], ds)
        return carry

    lax.fori_loop(low, high, step, 0)
    here = pl.ds(pl.multiple_of(i * TILE, TILE), TILE)
    grads_ref[:width, here] = (dq_ref[...] * HEAD ** -0.5).astype(BF16)

    @pl.when(i == pl.num_programs(0) - 1)
    def _():
        grads_ref[width:2 * width] = dk_ref[...].astype(BF16)
        grads_ref[2 * width:] = dv_ref[...].astype(BF16)


def attend_backward(seg_row, qt, extra, kn, kt, vn, out, grad):
    heads, _, length = qt.shape
    width = heads * HEAD
    const = lambda shape: pl.BlockSpec(shape, lambda i: (0,) * len(shape))
    return pl.pallas_call(
        backward_body,
        grid=(length // TILE,),
        in_specs=[
            pl.BlockSpec(memory_space=pltpu.SMEM),
            const((1, length)),
            pl.BlockSpec((heads, WIDE, TILE), lambda i: (0, 0, i)),
            pl.BlockSpec((heads, 16, TILE), lambda i: (0, 0, i)),
            const(kn.shape), const(kt.shape), const(vn.shape),
            pl.BlockSpec((width, TILE), lambda i: (0, i)),
            pl.BlockSpec((width, TILE), lambda i: (0, i)),
        ],
        out_specs=const((3 * width, length)),
        out_shape=jax.ShapeDtypeStruct((3 * width, length), BF16),
        scratch_shapes=[
            pltpu.VMEM((heads, WIDE, TILE), BF16),
            pltpu.VMEM((heads, WIDE, TILE), BF16),
            pltpu.VMEM((width, TILE), F32),
            pltpu.VMEM((width, length), F32),
            pltpu.VMEM((width, length), F32),
        ],
        compiler_params=pltpu.CompilerParams(vmem_limit_bytes=48 << 20),
        name="attend_backward",
    )(seg_row, seg_row, qt, extra, kn, kt, vn, out, grad)


def feed_body(order_ref, x_ref, g_ref, inner_ref, bias_ref, outer_ref, act_ref, dh_ref, out_ref, back_ref):
    hidden = nn(x_ref[...], inner_ref[...]) + bias_ref[...]
    half = 0.5 + 0.5 * lax.erf(hidden * 0.5 ** 0.5)
    act = (hidden * half).astype(BF16)
    act_ref[...] = act
    slope = half + hidden * (jnp.exp(-0.5 * hidden * hidden) * 0.3989422804014327)
    dh = (nt(g_ref[...], outer_ref[...]) * slope).astype(BF16)
    dh_ref[...] = dh
    out_ref[...] = nn(act, outer_ref[...]).astype(BF16)
    back_ref[...] = nt(dh, inner_ref[...]).astype(BF16)


def feed(order, x, cot, inner, bias, outer):
    total, features = x.shape
    units = inner.shape[1]
    const = lambda shape: pl.BlockSpec(shape, lambda i, o: (0,) * len(shape))
    rows = lambda n: pl.BlockSpec((TILE, n), lambda i, o: (i, 0))
    shape = lambda n: jax.ShapeDtypeStruct((total, n), BF16)
    return pl.pallas_call(
        feed_body,
        grid_spec=pltpu.PrefetchScalarGridSpec(
            num_scalar_prefetch=1,
            grid=(total // TILE,),
            in_specs=[
                rows(features),
                pl.BlockSpec((TILE, features), lambda i, o: (o[i], 0)),
                const(inner.shape), const(bias.shape), const(outer.shape),
            ],
            out_specs=[rows(units), rows(units), rows(features), rows(features)],
        ),
        out_shape=[shape(units), shape(units), shape(features), shape(features)],
        compiler_params=pltpu.CompilerParams(vmem_limit_bytes=48 << 20),
        name="feed",
    )(order, x, cot, inner, bias, outer)


def other_core(value):
    return lax.ppermute(value, "core", SWAP)


def other_chip(value):
    return lax.ppermute(value, "y", SWAP)


def local(
    tokens,
    segment_ids,
    gain_one,
    bias_one,
    query_weight,
    query_bias,
    key_weight,
    value_weight,
    value_bias,
    output_weight,
    output_bias,
    gain_two,
    bias_two,
    inner_weight,
    inner_bias,
    outer_weight,
    outer_bias,
    cotangent,
):
    _, length, features = tokens.shape
    width = query_weight.shape[1]
    heads = width // HEAD
    tokens = tokens.reshape(length, features)
    cot = cotangent.reshape(length, features)
    share = length // 4
    me = lax.axis_index(MP)
    begin = me * share

    output_full = lax.all_gather(output_weight, MP, axis=0, tiled=True)
    pad = lambda w: jnp.pad(w.reshape(-1, heads, HEAD), ((0, 0), (0, 0), (0, WIDE - HEAD))).reshape(-1, heads * WIDE)
    wt = jnp.concatenate([query_weight, key_weight, value_weight], axis=1).T
    wn = jnp.concatenate([pad(key_weight), pad(value_weight)], axis=1)
    attend_in, qt, kt, vt, kn, vn = project(
        tokens, segment_ids, gain_one[None], bias_one[None], wt, wn,
        query_bias[:, None], value_bias[:, None], pad(value_bias[None]), heads,
    )
    attended, extra = attend_forward(segment_ids, qt, kn, vt)

    mine = lax.all_to_all(attended, MP, 1, 0, tiled=True)
    inputs = lax.dynamic_slice_in_dim(tokens, begin, share, 0).astype(F32)
    residual = inputs + tn(mine, output_full) + output_bias
    normed_two, scale_two = stats(residual)
    own = (normed_two * gain_two + bias_two).astype(BF16)
    near = other_core(own)
    far = other_chip(own)
    across = other_core(far)

    blocks = share // TILE
    order = lambda who: who * blocks + jnp.arange(blocks, dtype=jnp.int32)
    x_one = jnp.concatenate([own, near], axis=0)
    x_two = jnp.concatenate([far, across], axis=0)
    cot_one = jnp.concatenate([order(me), order(me ^ 1)])
    cot_two = jnp.concatenate([order(me ^ 2), order(me ^ 3)])
    inner_row = inner_bias[None]
    act_one, dh_one, out_one, back_one = feed(cot_one, x_one, cot, inner_weight, inner_row, outer_weight)
    act_two, dh_two, out_two, back_two = feed(cot_two, x_two, cot, inner_weight, inner_row, outer_weight)

    def gather_sum(one, two):
        low = lambda v: v.astype(BF16)
        wide = lambda v: v.astype(F32)
        far_sum = low(wide(two[:share]) + wide(other_core(two[share:])))
        near_sum = wide(one[:share]) + wide(other_core(one[share:]))
        return near_sum + wide(other_chip(far_sum))

    grad_mid = gather_sum(back_one, back_two)
    cot_share = lax.dynamic_slice_in_dim(cot, begin, share, 0).astype(F32)
    grad_residual = cot_share + norm_back(grad_mid, normed_two, scale_two, gain_two)
    residual_low = grad_residual.astype(BF16)
    grad_attended = lax.all_to_all(nt(output_full, residual_low).astype(BF16), MP, 0, 1, tiled=True)

    cot_of = lambda who: lax.dynamic_slice_in_dim(cot, who * share, share, 0)
    g_one = jnp.concatenate([cot_of(me), cot_of(me ^ 1)], axis=0)
    g_two = jnp.concatenate([cot_of(me ^ 2), cot_of(me ^ 3)], axis=0)
    grad_outer = (tn(act_one, g_one) + tn(act_two, g_two)).astype(BF16)
    grad_inner = (tn(x_one, dh_one) + tn(x_two, dh_two)).astype(BF16)
    colsum = lambda v: jnp.sum(v.astype(F32), axis=0)
    vectors = jnp.stack([
        colsum(dh_one) + colsum(dh_two),
        jnp.sum(grad_mid * normed_two, axis=0),
        jnp.sum(grad_mid, axis=0),
        colsum(grad_residual),
        colsum(cot_share),
    ]).astype(BF16)
    grad_outer, grad_inner, vectors = lax.psum((grad_outer, grad_inner, vectors), "dp")

    result = residual + gather_sum(out_one, out_two) + outer_bias

    def spread(value):
        near, far = other_core(value), other_chip(value)
        across = other_core(far)
        whole = jnp.zeros((length, features), value.dtype)
        for n, part in enumerate((value, near, far, across)):
            whole = lax.dynamic_update_slice_in_dim(whole, part, (me ^ n) * share, 0)
        return whole

    layer_out = spread(result.astype(BF16))

    grads = attend_backward(segment_ids, qt, extra, kn, kt, vn, attended, grad_attended)
    part_of = lambda who: tn(lax.dynamic_slice_in_dim(grads, who * share, share, 1), wt)
    piece = [part_of(me ^ n) for n in (2, 3, 0, 1)]
    far_sum = (piece[0] + other_core(piece[1].astype(BF16)).astype(F32)).astype(BF16)
    grad_attend = piece[2] + other_core(piece[3].astype(BF16)).astype(F32) + other_chip(far_sum).astype(F32)
    normed_one, scale_one = stats(inputs)
    input_share = grad_residual + norm_back(grad_attend, normed_one, scale_one, gain_one)
    input_grad = spread(input_share.astype(BF16)).astype(F32)

    grad_weights = nn(grads, attend_in).astype(BF16)
    low_all = spread(residual_low)
    grad_output = nn(attended, low_all).astype(BF16)
    rowsum = jnp.sum(grads.astype(F32), axis=1).reshape(3, width)
    more = jnp.stack([
        jnp.pad(rowsum[0], (0, features - width)),
        jnp.pad(rowsum[2], (0, features - width)),
        jnp.sum(grad_attend * normed_one, axis=0),
        jnp.sum(grad_attend, axis=0),
    ]).astype(BF16)
    grad_weights, grad_output, more = lax.psum((grad_weights, grad_output, more), "dp")

    vectors, more = vectors.astype(F32), more.astype(F32)
    shared = lax.psum(jnp.concatenate([vectors[1:], more[2:]]), MP)
    weights = grad_weights.astype(F32).T
    return (
        layer_out.reshape(1, length, features),
        input_grad.reshape(1, length, features),
        shared[4],
        shared[5],
        weights[:, :width],
        more[0, :width],
        weights[:, width:2 * width],
        weights[:, 2 * width:],
        more[1, :width],
        grad_output.astype(F32),
        shared[2],
        shared[0],
        shared[1],
        grad_inner.astype(F32),
        vectors[0],
        grad_outer.astype(F32),
        shared[3],
    )


def solution(mesh):
    rows = mesh.shape["dp"]
    inner = Mesh(mesh.devices.reshape(rows, 2, 2), ("dp", "y", "core"))
    placed = (
        P("dp", None, None),
        P("dp", None),
        P(),
        P(),
        P(None, MP),
        P(MP),
        P(None, MP),
        P(None, MP),
        P(MP),
        P(MP, None),
        P(),
        P(),
        P(),
        P(None, MP),
        P(MP),
        P(MP, None),
        P(),
        P("dp", None, None),
    )
    return jax.shard_map(
        local,
        mesh=inner,
        in_specs=placed,
        out_specs=(
            P("dp", None, None),
            P("dp", None, None),
            P(),
            P(),
            P(None, MP),
            P(MP),
            P(None, MP),
            P(None, MP),
            P(MP),
            P(MP, None),
            P(),
            P(),
            P(),
            P(None, MP),
            P(MP),
            P(MP, None),
            P(),
        ),
        check_vma=False,
    )
```

```python
import jax
import jax.numpy as jnp
from jax import lax
from jax.experimental import pallas as pl
from jax.experimental.pallas import tpu as pltpu
from jax.sharding import Mesh
from jax.sharding import PartitionSpec as P

HEAD = 64
WIDE = 128
TILE = 256
PARTS = 2
MASKED = 1e30
F32 = jnp.float32
BF16 = jnp.bfloat16
DP = ("z", "x")
MP = ("y", "core")
SWAP = [(0, 1), (1, 0)]


def nn(left, right):
    return lax.dot_general(left, right, (((1,), (0,)), ((), ())), preferred_element_type=F32)


def nt(left, right):
    return lax.dot_general(left, right, (((1,), (1,)), ((), ())), preferred_element_type=F32)


def tn(left, right):
    return lax.dot_general(left, right, (((0,), (0,)), ((), ())), preferred_element_type=F32)


def stats(values):
    center = values - jnp.mean(values, axis=-1, keepdims=True)
    scale = lax.rsqrt(jnp.mean(center * center, axis=-1, keepdims=True) + 1e-05)
    return center * scale, scale


def norm_back(grad_out, normed, scale, gain):
    upstream = grad_out * gain
    return scale * (
        upstream
        - jnp.mean(upstream, axis=-1, keepdims=True)
        - normed * jnp.mean(upstream * normed, axis=-1, keepdims=True)
    )


def fold(values):
    return jnp.sum(values.reshape(-1, 8, values.shape[-1]), axis=0)


def split(value, parts):
    out = []
    for _ in range(parts):
        piece = value.astype(BF16).astype(F32)
        out.append(piece)
        value = value - piece
    return out


def const(shape):
    return pl.BlockSpec(shape, lambda *_: (0,) * len(shape))


def shape_of(*dims, dtype=BF16):
    return jax.ShapeDtypeStruct(dims, dtype)


def params():
    return pltpu.CompilerParams(vmem_limit_bytes=48 << 20)


def cost(flops, moved, special=0):
    return pl.CostEstimate(flops=int(flops), bytes_accessed=int(moved), transcendentals=int(special))


def project_body(x_ref, seg_ref, gain_ref, bias_ref, wt_ref, wn_ref, qb_ref, vb_ref, vbn_ref,
                 ai_ref, qt_ref, kt_ref, vt_ref, kn_ref, vn_ref):
    heads = kn_ref.shape[0]
    width = heads * HEAD
    normed, _ = stats(x_ref[...].astype(F32))
    ai = (normed * gain_ref[...] + bias_ref[...]).astype(BF16)
    ai_ref[...] = ai
    low = nt(wt_ref[...], ai)
    queries = ((low[:width] + qb_ref[...]).astype(BF16)).astype(F32) * HEAD ** -0.5
    kt_ref[...] = low[width:2 * width].astype(BF16)
    values = (low[2 * width:] + vb_ref[...]).astype(BF16)
    tile = x_ref.shape[0]
    row = lax.broadcasted_iota(jnp.int32, (WIDE, tile), 0) - HEAD
    same = jnp.where(row == seg_ref[...], 1.0, 0.0)
    same = jnp.where(row >= 0, same, 0.0)
    first = jnp.where(lax.broadcasted_iota(jnp.int32, (16, tile), 0) == 0, 1.0, 0.0).astype(BF16)
    for h in range(heads):
        rows = slice(h * HEAD, (h + 1) * HEAD)
        qt_ref[h, :HEAD, :] = queries[rows].astype(BF16)
        qt_ref[h, HEAD:, :] = same[HEAD:].astype(BF16)
        vt_ref[h, :HEAD, :] = values[rows]
        vt_ref[h, HEAD:, :] = first
    lane = lax.broadcasted_iota(jnp.int32, (tile, WIDE), 1)
    mask = jnp.where((lane >= HEAD) & (lane < HEAD + 8), (same.T - 1.0) * MASKED, 0.0)
    mask = jnp.where((lane >= HEAD + 8) & (lane < HEAD + 11), 1.0, mask)
    ones = jnp.where((lane >= HEAD) & (lane < HEAD + 2), 1.0, 0.0)
    natural = nn(ai, wn_ref[...])
    for h in range(heads):
        kn_ref[h] = (natural[:, h * WIDE:(h + 1) * WIDE] + mask).astype(BF16)
        at = (heads + h) * WIDE
        vn_ref[h] = (natural[:, at:at + WIDE] + vbn_ref[:, h * WIDE:(h + 1) * WIDE] + ones).astype(BF16)


def project(tokens, seg_row, gain, bias, wt, wn, qb, vb, vbn, heads):
    length, features = tokens.shape
    width = heads * HEAD
    return pl.pallas_call(
        project_body,
        grid=(length // TILE,),
        in_specs=[
            pl.BlockSpec((TILE, features), lambda i: (i, 0)),
            pl.BlockSpec((1, TILE), lambda i: (0, i)),
            const((1, features)), const((1, features)),
            const(wt.shape), const(wn.shape), const(qb.shape), const(vb.shape), const(vbn.shape),
        ],
        out_specs=[
            pl.BlockSpec((TILE, features), lambda i: (i, 0)),
            pl.BlockSpec((heads, WIDE, TILE), lambda i: (0, 0, i)),
            pl.BlockSpec((width, TILE), lambda i: (0, i)),
            pl.BlockSpec((heads, HEAD + 16, TILE), lambda i: (0, 0, i)),
            pl.BlockSpec((heads, TILE, WIDE), lambda i: (0, i, 0)),
            pl.BlockSpec((heads, TILE, WIDE), lambda i: (0, i, 0)),
        ],
        out_shape=[
            shape_of(length, features),
            shape_of(heads, WIDE, length),
            shape_of(width, length),
            shape_of(heads, HEAD + 16, length),
            shape_of(heads, length, WIDE),
            shape_of(heads, length, WIDE),
        ],
        compiler_params=params(),
        cost_estimate=cost(6e9, 14e6),
        name="project",
    )(tokens, seg_row, gain, bias, wt, wn, qb, vb, vbn)


def key_range(seg_ref, seg_all, i):
    first = seg_ref[0, i * TILE]
    last = seg_ref[0, i * TILE + TILE - 1]
    before = jnp.sum(jnp.where(seg_all < first, 1.0, 0.0)).astype(jnp.int32)
    until = jnp.sum(jnp.where(seg_all <= last, 1.0, 0.0)).astype(jnp.int32)
    return before // TILE, (until + TILE - 1) // TILE


def shifted(one_hot, pieces):
    row = lax.broadcasted_iota(jnp.int32, one_hot.shape, 0)
    value = one_hot
    for n, piece in enumerate(pieces):
        value = jnp.where(row == 8 + n, piece, value)
    return value.astype(BF16)


def forward_body(offset, segs_ref, seg_ref, qt_ref, kn_ref, vt_ref, out_ref, extra_ref, qa_ref, acc_ref):
    heads, _, tile = qt_ref.shape
    low, high = key_range(segs_ref, seg_ref[...], pl.program_id(0) + offset)
    acc_ref[...] = jnp.zeros_like(acc_ref)
    qa_ref[...] = qt_ref[...]

    def look(kb, tops):
        keys = pl.ds(pl.multiple_of(kb * TILE, TILE), TILE)
        return tuple(
            jnp.maximum(tops[h], jnp.max(nn(kn_ref[h, keys, :], qa_ref[h]).reshape(-1, 8, tile), axis=0))
            for h in range(heads)
        )

    tops = lax.fori_loop(low, high, look, (jnp.full((8, tile), -jnp.inf, F32),) * heads)
    tops = [jnp.max(top, axis=0, keepdims=True) for top in tops]
    one_hots = [qt_ref[h, HEAD:HEAD + 16, :].astype(F32) for h in range(heads)]
    for h in range(heads):
        qa_ref[h, HEAD:HEAD + 16, :] = shifted(one_hots[h], split(-tops[h], 3))

    def step(kb, carry):
        keys = pl.ds(pl.multiple_of(kb * TILE, TILE), TILE)
        for h in range(heads):
            powered = jnp.exp(nn(kn_ref[h, keys, :], qa_ref[h])).astype(BF16)
            acc_ref[h] += nn(vt_ref[h, :, keys], powered)
        return carry

    lax.fori_loop(low, high, step, 0)
    for h in range(heads):
        total = acc_ref[h, HEAD:HEAD + 1, :]
        out_ref[0, h * HEAD:(h + 1) * HEAD, :] = (acc_ref[h, :HEAD, :] / total).astype(BF16)
        extra_ref[h] = shifted(one_hots[h], split(-(tops[h] + jnp.log(total)), 3))


def attend_forward(part, seg_row, qt, kn, vt):
    heads, _, length = qt.shape
    width = heads * HEAD
    count = length // TILE // PARTS
    offset = part * count

    def body(*refs):
        forward_body(offset, *refs)

    return pl.pallas_call(
        body,
        grid=(count,),
        in_specs=[
            pl.BlockSpec(memory_space=pltpu.SMEM),
            const((1, length)),
            pl.BlockSpec((heads, WIDE, TILE), lambda i: (0, 0, i + offset)),
            const(kn.shape), const(vt.shape),
        ],
        out_specs=[
            pl.BlockSpec((1, width, TILE), lambda i: (i, 0, 0)),
            pl.BlockSpec((heads, 16, TILE), lambda i: (0, 0, i)),
        ],
        out_shape=[
            shape_of(count, width, TILE),
            shape_of(heads, 16, count * TILE),
        ],
        scratch_shapes=[
            pltpu.VMEM((heads, WIDE, TILE), BF16),
            pltpu.VMEM((heads, HEAD + 16, TILE), F32),
        ],
        compiler_params=params(),
        cost_estimate=cost(9e9, 5e6, 4e6),
        name="attend_forward",
    )(seg_row, seg_row, qt, kn, vt)


def backward_body(part, me_ref, segs_ref, seg_ref, qt_ref, extra_ref, kn_ref, kt_ref, vn_ref, out_ref,
                  g0_ref, g1_ref, g2_ref, g3_ref, *rest):
    heads, _, tile = qt_ref.shape
    width = heads * HEAD
    length = kt_ref.shape[1]
    if part == 0:
        dq_out, dk_ref, dv_ref, qa_ref, da_ref, dq_ref = rest
    else:
        dq_in, dk_in, dv_in, grads_ref, qa_ref, da_ref, dq_ref, dk_ref, dv_ref = rest
    i = pl.program_id(0)
    count = length // TILE // PARTS
    at_here = i + part * count
    low, high = key_range(segs_ref, seg_ref[...], at_here)

    @pl.when(i == 0)
    def _():
        if part == 0:
            dk_ref[...] = jnp.zeros_like(dk_ref)
            dv_ref[...] = jnp.zeros_like(dv_ref)
        else:
            dk_ref[...] = dk_in[...]
            dv_ref[...] = dv_in[...]
            grads_ref[:width, :count * TILE] = dq_in[...]
        qa_ref[...] = jnp.zeros_like(qa_ref)
        da_ref[...] = jnp.zeros_like(da_ref)

    source = i ^ me_ref[0]
    for n, g_ref in enumerate((g0_ref, g1_ref, g2_ref, g3_ref)):
        @pl.when(source == n)
        def _(g_ref=g_ref):
            for h in range(heads):
                da_ref[h, :HEAD, :] = g_ref[h * HEAD:(h + 1) * HEAD]

    dq_ref[...] = jnp.zeros_like(dq_ref)
    row = lax.broadcasted_iota(jnp.int32, (16, tile), 0)
    for h in range(heads):
        rows = slice(h * HEAD, (h + 1) * HEAD)
        qa_ref[h, :HEAD, :] = qt_ref[h, :HEAD, :]
        qa_ref[h, HEAD:HEAD + 16, :] = extra_ref[h]
        inner = jnp.sum(da_ref[h, :HEAD, :].astype(F32) * out_ref[0, rows].astype(F32), axis=0, keepdims=True)
        first, second = split(-inner, 2)
        value = jnp.where(row == 0, first, jnp.where(row == 1, second, 0.0))
        da_ref[h, HEAD:HEAD + 16, :] = value.astype(BF16)

    def step(kb, carry):
        keys = pl.ds(pl.multiple_of(kb * TILE, TILE), TILE)
        for h in range(heads):
            rows = slice(h * HEAD, (h + 1) * HEAD)
            probs = jnp.exp(nn(kn_ref[h, keys, :], qa_ref[h]))
            ds = (probs * nn(vn_ref[h, keys, :], da_ref[h])).astype(BF16)
            dv_ref[rows, keys] += nt(da_ref[h, :HEAD, :], probs.astype(BF16))
            dk_ref[rows, keys] += nt(qa_ref[h, :HEAD, :], ds)
            dq_ref[rows] += nn(kt_ref[rows, keys], ds)
        return carry

    lax.fori_loop(low, high, step, 0)
    dq = (dq_ref[...] * HEAD ** -0.5).astype(BF16)
    if part == 0:
        dq_out[...] = dq
    else:
        grads_ref[:width, pl.ds(pl.multiple_of(at_here * TILE, TILE), TILE)] = dq

        @pl.when(i == pl.num_programs(0) - 1)
        def _():
            grads_ref[width:2 * width] = dk_ref[...].astype(BF16)
            grads_ref[2 * width:] = dv_ref[...].astype(BF16)


def attend_backward(part, me, seg_row, qt, extra, kn, kt, vn, out, grad, earlier):
    heads, _, length = qt.shape
    width = heads * HEAD
    count = length // TILE // PARTS
    offset = part * count

    def body(*refs):
        backward_body(part, *refs)

    in_specs = [
        pl.BlockSpec(memory_space=pltpu.SMEM),
        const((1, length)),
        pl.BlockSpec((heads, WIDE, TILE), lambda i, m: (0, 0, i + offset)),
        pl.BlockSpec((heads, 16, TILE), lambda i, m: (0, 0, i)),
        const(kn.shape), const(kt.shape), const(vn.shape),
        pl.BlockSpec((1, width, TILE), lambda i, m: (i, 0, 0)),
        const(grad[0].shape), const(grad[1].shape), const(grad[2].shape), const(grad[3].shape),
    ]
    scratch = [
        pltpu.VMEM((heads, WIDE, TILE), BF16),
        pltpu.VMEM((heads, WIDE, TILE), BF16),
        pltpu.VMEM((width, TILE), F32),
    ]
    if part == 0:
        out_specs = [pl.BlockSpec((width, TILE), lambda i, m: (0, i)), const((width, length)), const((width, length))]
        out_shape = [shape_of(width, count * TILE), shape_of(width, length, dtype=F32), shape_of(width, length, dtype=F32)]
    else:
        in_specs += [const(v.shape) for v in earlier]
        out_specs = const((3 * width, length))
        out_shape = shape_of(3 * width, length)
        scratch += [pltpu.VMEM((width, length), F32), pltpu.VMEM((width, length), F32)]
    return pl.pallas_call(
        body,
        grid_spec=pltpu.PrefetchScalarGridSpec(
            num_scalar_prefetch=1, grid=(count,), in_specs=in_specs, out_specs=out_specs, scratch_shapes=scratch,
        ),
        out_shape=out_shape,
        compiler_params=params(),
        cost_estimate=cost(16e9, 10e6, 4e6),
        name="attend_backward",
    )(me, seg_row, seg_row, qt, extra, kn, kt, vn, out, *grad, *earlier)


def middle_body(me_ref, x_ref, m0_ref, m1_ref, m2_ref, m3_ref, w0_ref, w1_ref, w2_ref, w3_ref,
                ob_ref, gain_ref, bias_ref, residual_ref, own_ref):
    total = x_ref[...].astype(F32) + ob_ref[...]
    for m_ref, w_ref in ((m0_ref, w0_ref), (m1_ref, w1_ref), (m2_ref, w2_ref), (m3_ref, w3_ref)):
        total = total + tn(m_ref[...], w_ref[...])
    residual_ref[...] = total
    normed, _ = stats(total)
    own_ref[...] = (normed * gain_ref[...] + bias_ref[...]).astype(BF16)


def middle(part, me, tokens, mixed, weights, output_bias, gain, bias):
    features = tokens.shape[1]
    vector = const((1, features))
    return pl.pallas_call(
        middle_body,
        grid_spec=pltpu.PrefetchScalarGridSpec(
            num_scalar_prefetch=1,
            grid=(1,),
            in_specs=[pl.BlockSpec((TILE, features), lambda i, m: (4 * part + m[0], 0))]
            + [const(v.shape) for v in mixed] + [const(v.shape) for v in weights] + [vector] * 3,
            out_specs=[const((TILE, features)), const((TILE, features))],
        ),
        out_shape=[shape_of(TILE, features, dtype=F32), shape_of(TILE, features)],
        compiler_params=params(),
        cost_estimate=cost(2e9, 3e6),
        name="middle",
    )(me, tokens, *mixed, *weights, output_bias, gain, bias)


def feed_body(me_ref, x0_ref, x1_ref, g_ref, inner_ref, bias_ref, outer_ref, *rest):
    act_ref, dh_ref, xs_ref, gs_ref, out0_ref, out1_ref, back0_ref, back1_ref, sum_ref = rest[-9:]
    i = pl.program_id(0)

    @pl.when(i == 0)
    def _():
        xs_ref[...] = x0_ref[...]

    @pl.when(i == 1)
    def _():
        xs_ref[...] = x1_ref[...]

    gs_ref[...] = g_ref[...]
    hidden = nn(xs_ref[...], inner_ref[...]) + bias_ref[...]
    half = 0.5 + 0.5 * lax.erf(hidden * 0.5 ** 0.5)
    act = (hidden * half).astype(BF16)
    act_ref[...] = act
    slope = half + hidden * (jnp.exp(-0.5 * hidden * hidden) * 0.3989422804014327)
    dh = (nt(g_ref[...], outer_ref[...]) * slope).astype(BF16)
    dh_ref[...] = dh
    sums = fold(dh.astype(F32))
    out = nn(act, outer_ref[...]).astype(BF16)
    back = nt(dh, inner_ref[...]).astype(BF16)

    @pl.when(i == 0)
    def _():
        sum_ref[...] = sums
        out0_ref[...] = out
        back0_ref[...] = back

    @pl.when(i == 1)
    def _():
        sum_ref[...] += sums
        out1_ref[...] = out
        back1_ref[...] = back


def feed(part, base, me, first, second, cot, inner, bias, outer, kept):
    length, features = cot.shape
    units = inner.shape[1]
    at = 4 * part + base
    rows = lambda n: pl.BlockSpec((TILE, n), lambda i, m: (at + i, 0))
    piece = const((TILE, features))
    return pl.pallas_call(
        feed_body,
        grid_spec=pltpu.PrefetchScalarGridSpec(
            num_scalar_prefetch=1,
            grid=(2,),
            in_specs=[
                piece, piece,
                pl.BlockSpec((TILE, features), lambda i, m: (4 * part + (m[0] ^ (base + i)), 0)),
                const(inner.shape), const(bias.shape), const(outer.shape),
            ] + [pl.BlockSpec(memory_space=pl.ANY)] * len(kept),
            out_specs=[rows(units), rows(units), rows(features), rows(features)] + [piece] * 4 + [const((8, units))],
        ),
        out_shape=[shape_of(length, units), shape_of(length, units), shape_of(length, features),
                   shape_of(length, features)] + [shape_of(TILE, features)] * 4 + [shape_of(8, units, dtype=F32)],
        input_output_aliases={7 + n: n for n in range(len(kept))},
        compiler_params=params(),
        cost_estimate=cost(5e9, 8e6, 1e6),
        name="feed",
    )(me, first, second, cot, inner, bias, outer, *kept)


def back_body(me_ref, b0_ref, b1_ref, b2_ref, residual_ref, g_ref, gain_ref, w0_ref, w1_ref, w2_ref, w3_ref,
              grad_ref, low_ref, a0_ref, a1_ref, a2_ref, a3_ref, sum_ref):
    grad_mid = b0_ref[...].astype(F32) + b1_ref[...].astype(F32) + b2_ref[...].astype(F32)
    normed, scale = stats(residual_ref[...])
    upstream = g_ref[...].astype(F32)
    grad = upstream + norm_back(grad_mid, normed, scale, gain_ref[...])
    grad_ref[...] = grad
    low = grad.astype(BF16)
    low_ref[...] = low
    for w_ref, a_ref in ((w0_ref, a0_ref), (w1_ref, a1_ref), (w2_ref, a2_ref), (w3_ref, a3_ref)):
        a_ref[...] = nt(w_ref[...], low).astype(BF16)
    for n, value in enumerate((grad_mid * normed, grad_mid, grad, upstream)):
        sum_ref[8 * n:8 * n + 8] = fold(value)


def middle_back(part, me, sums, residual, cot, gain, weights):
    features = cot.shape[1]
    piece = const((TILE, features))
    width = weights[0].shape[0]
    return pl.pallas_call(
        back_body,
        grid_spec=pltpu.PrefetchScalarGridSpec(
            num_scalar_prefetch=1,
            grid=(1,),
            in_specs=[piece] * 4
            + [pl.BlockSpec((TILE, features), lambda i, m: (4 * part + m[0], 0)), const((1, features))]
            + [const(v.shape) for v in weights],
            out_specs=[piece, piece] + [const((width, TILE))] * 4 + [const((32, features))],
        ),
        out_shape=[shape_of(TILE, features, dtype=F32), shape_of(TILE, features)]
        + [shape_of(width, TILE)] * 4 + [shape_of(32, features, dtype=F32)],
        compiler_params=params(),
        cost_estimate=cost(2e9, 4e6),
        name="middle_back",
    )(me, *sums, residual, cot, gain, *weights)


def output_body(*refs):
    mixed, lows, outs = refs[:4 * PARTS], refs[4 * PARTS:5 * PARTS], refs[5 * PARTS:]
    for n in range(4):
        total = nn(mixed[n][...], lows[0][...])
        for p in range(1, PARTS):
            total = total + nn(mixed[4 * p + n][...], lows[p][...])
        outs[n][...] = total.astype(BF16)


def output_grad(mixed, lows):
    width, features = mixed[0].shape[0], lows[0].shape[1]
    return pl.pallas_call(
        output_body,
        out_shape=[shape_of(width, features)] * 4,
        compiler_params=params(),
        cost_estimate=cost(2e9, 4e6),
        name="output_grad",
    )(*mixed, *lows)


def tail_body(me_ref, g_ref, wt_ref, o0_ref, o1_ref, o2_ref, o3_ref, sum_ref):
    i = pl.program_id(0)
    grads = g_ref[...]
    value = tn(grads, wt_ref[...]).astype(BF16)
    sums = nt(jnp.ones((8, grads.shape[1]), BF16), grads)
    for step, o_ref in enumerate((o3_ref, o2_ref, o1_ref, o0_ref)):
        @pl.when(i == step)
        def _(o_ref=o_ref, step=step):
            o_ref[...] = value
            sum_ref[...] = sums if step == 0 else sum_ref[...] + sums


def tail(part, me, grads, wt):
    deep = grads.shape[0]
    features = wt.shape[1]
    piece = const((TILE, features))
    return pl.pallas_call(
        tail_body,
        grid_spec=pltpu.PrefetchScalarGridSpec(
            num_scalar_prefetch=1,
            grid=(4,),
            in_specs=[pl.BlockSpec((deep, TILE), lambda i, m: (0, 4 * part + (m[0] ^ (3 - i)))), const(wt.shape)],
            out_specs=[piece] * 4 + [const((8, deep))],
        ),
        out_shape=[shape_of(TILE, features)] * 4 + [shape_of(8, deep, dtype=F32)],
        compiler_params=params(),
        cost_estimate=cost(2e9, 4e6),
        name="tail",
    )(me, grads, wt)


def final_body(me_ref, b0_ref, b1_ref, b2_ref, x_ref, grad_ref, gain_ref, out_ref, sum_ref):
    grad_attend = b0_ref[...].astype(F32) + b1_ref[...].astype(F32) + b2_ref[...].astype(F32)
    normed, scale = stats(x_ref[...].astype(F32))
    out_ref[...] = (grad_ref[...] + norm_back(grad_attend, normed, scale, gain_ref[...])).astype(BF16)
    sum_ref[:8] = fold(grad_attend * normed)
    sum_ref[8:] = fold(grad_attend)


def final(part, me, sums, tokens, grad, gain):
    features = tokens.shape[1]
    piece = const((TILE, features))
    return pl.pallas_call(
        final_body,
        grid_spec=pltpu.PrefetchScalarGridSpec(
            num_scalar_prefetch=1,
            grid=(1,),
            in_specs=[piece] * 3
            + [pl.BlockSpec((TILE, features), lambda i, m: (4 * part + m[0], 0)), piece, const((1, features))],
            out_specs=[piece, const((16, features))],
        ),
        out_shape=[shape_of(TILE, features), shape_of(16, features, dtype=F32)],
        compiler_params=params(),
        cost_estimate=cost(1e8, 3e6),
        name="final",
    )(me, *sums, tokens, grad, gain)


def place_body(me_ref, p0_ref, p1_ref, p2_ref, p3_ref, *rest):
    out_ref = rest[-1]
    for step, p_ref in enumerate((p0_ref, p1_ref, p2_ref, p3_ref)):
        @pl.when(pl.program_id(0) == step)
        def _(p_ref=p_ref):
            out_ref[...] = p_ref[...].astype(out_ref.dtype)


def place(part, me, pieces, length, dtype, kept):
    features = pieces[0].shape[1]
    return pl.pallas_call(
        place_body,
        grid_spec=pltpu.PrefetchScalarGridSpec(
            num_scalar_prefetch=1,
            grid=(4,),
            in_specs=[const((TILE, features))] * 4 + [pl.BlockSpec(memory_space=pl.ANY)] * len(kept),
            out_specs=pl.BlockSpec((TILE, features), lambda i, m: (4 * part + (m[0] ^ i), 0)),
        ),
        out_shape=shape_of(length, features, dtype=dtype),
        input_output_aliases={5 + n: n for n in range(len(kept))},
        compiler_params=params(),
        cost_estimate=cost(1e6, 5e6),
        name="place",
    )(me, *pieces, *kept)


def other_core(value):
    return lax.ppermute(value, "core", SWAP)


def other_chip(value):
    return lax.ppermute(value, "y", SWAP)


def crosswise(value):
    return lax.ppermute(value, MP, [(n, n ^ 3) for n in range(4)])


def exchange(pieces):
    return [pieces[0], other_core(pieces[1]), other_chip(pieces[2]), crosswise(pieces[3])]


def gather_sum(pieces):
    near = other_core(pieces[1])
    far = (pieces[2].astype(F32) + other_core(pieces[3]).astype(F32)).astype(BF16)
    return [pieces[0], near, other_chip(far)]


def spread(value):
    far = other_chip(value)
    return [value, other_core(value), far, other_core(far)]


def pick(values, at):
    return lax.dynamic_index_in_dim(values, at, 0, keepdims=False)


def turned(values, way):
    size = lax.axis_size("z")
    return lax.ppermute(values, "z", [(n, (n + way) % size) for n in range(size)])


def sum_rows(value):
    size = lax.axis_size("z")
    if size > 4:
        return lax.psum(value, DP)
    rows, features = value.shape
    x, z = lax.axis_index("x"), lax.axis_index("z")
    halves = value.reshape(2, rows // 2, features)
    got = lax.ppermute(pick(halves, 1 - x), "x", SWAP)
    half = (pick(halves, x).astype(F32) + got.astype(F32)).astype(BF16)
    parts = half.reshape(size, -1, features)
    total = pick(parts, z).astype(F32)
    for way in range(1, size):
        total = total + turned(pick(parts, (z + way) % size), way).astype(F32)
    total = total.astype(BF16)
    whole = jnp.zeros_like(parts)
    for way in range(size):
        part = turned(total, way) if way else total
        whole = lax.dynamic_update_index_in_dim(whole, part, (z - way) % size, 0)
    half = whole.reshape(rows // 2, features)
    other = lax.ppermute(half, "x", SWAP)
    return jnp.where(x == 0, jnp.concatenate([half, other]), jnp.concatenate([other, half]))


def sum_small(value):
    size = lax.axis_size("z")
    if size > 4:
        return lax.psum(value, DP)
    value = value + lax.ppermute(value, "x", SWAP)
    total = value
    for way in range(1, size):
        total = total + turned(value, way)
    return total


def local(
    tokens,
    segment_ids,
    gain_one,
    bias_one,
    query_weight,
    query_bias,
    key_weight,
    value_weight,
    value_bias,
    output_weight,
    output_bias,
    gain_two,
    bias_two,
    inner_weight,
    inner_bias,
    outer_weight,
    outer_bias,
    cotangent,
):
    _, length, features = tokens.shape
    width = query_weight.shape[1]
    heads = width // HEAD
    tokens = tokens.reshape(length, features)
    cot = cotangent.reshape(length, features)
    at = lax.axis_index(MP).astype(jnp.int32)
    me = at[None]
    gain_one, bias_one, gain_two, bias_two = gain_one[None], bias_one[None], gain_two[None], bias_two[None]

    output_weights = exchange([output_weight] * 4)
    pad = lambda w: jnp.pad(w.reshape(-1, heads, HEAD), ((0, 0), (0, 0), (0, WIDE - HEAD))).reshape(-1, heads * WIDE)
    wt = jnp.concatenate([query_weight, key_weight, value_weight], axis=1).T
    wn = jnp.concatenate([pad(key_weight), pad(value_weight)], axis=1)
    attend_in, qt, kt, vt, kn, vn = project(
        tokens, segment_ids, gain_one, bias_one, wt, wn,
        query_bias[:, None], value_bias[:, None], pad(value_bias[None]), heads,
    )

    parts = range(PARTS)
    attended, extras, mixed, residuals, pieces = [], [], [], [], []
    for p in parts:
        out, extra = attend_forward(p, segment_ids, qt, kn, vt)
        attended.append(out)
        extras.append(extra)
        mixed.append(exchange([pick(out, at ^ n) for n in range(4)]))
        residual, own = middle(p, me, tokens, mixed[p], output_weights, output_bias[None], gain_two, bias_two)
        residuals.append(residual)
        pieces.append(spread(own))

    outs, backs, sums, kept = {}, {}, [], ()
    for base in (0, 2):
        for p in parts:
            result = feed(p, base, me, pieces[p][base], pieces[p][base + 1], cot,
                          inner_weight, inner_bias[None], outer_weight, kept)
            kept = result[:4]
            outs[p, base], outs[p, base + 1] = result[4:6]
            backs[p, base], backs[p, base + 1] = result[6:8]
            sums.append(result[8])
    acts, dhs, xs, gs = kept

    grad_residuals, lows, grads_attended, vectors = [], [], [], []
    for p in parts:
        grad, low, a0, a1, a2, a3, vector = middle_back(
            p, me, gather_sum([backs[p, n] for n in range(4)]), residuals[p], cot, gain_two, output_weights
        )
        grad_residuals.append(grad)
        lows.append(low)
        vectors.append(vector)
        grads_attended.append(exchange([a0, a1, a2, a3]))

    grad_outer = tn(acts, gs).astype(BF16)
    grad_inner = tn(xs, dhs).astype(BF16)
    grad_outer, grad_inner = lax.psum((grad_outer, grad_inner), DP)

    earlier = ()
    for p in parts:
        earlier = attend_backward(p, me, segment_ids, qt, extras[p], kn, kt, vn, attended[p], grads_attended[p], earlier)
    grads = earlier

    held, _ = lax.optimization_barrier((outs, grads_attended))
    layer_out = ()
    for p in parts:
        one, two, three = gather_sum([held[p, n] for n in range(4)])
        result = residuals[p] + one.astype(F32) + two.astype(F32) + three.astype(F32) + outer_bias
        layer_out = (place(p, me, spread(result.astype(BF16)), length, BF16, layer_out),)
    one, two, three = gather_sum(output_grad([m for p in parts for m in mixed[p]], lows))
    grad_output = (one.astype(F32) + two.astype(F32) + three.astype(F32)).astype(BF16)

    input_grad, finals, row_sums = (), [], []
    tails = [tail(p, me, grads, wt) for p in parts]
    grad_weights = nn(grads, attend_in).astype(BF16)
    for p in parts:
        share, vector = final(p, me, gather_sum(tails[p][:4]), tokens, grad_residuals[p], gain_one)
        finals.append(vector)
        row_sums.append(tails[p][4])
        input_grad = (place(p, me, spread(share), length, F32, input_grad),)

    weights = sum_rows(jnp.concatenate([grad_weights, grad_output], axis=0)).astype(F32)

    fold_rows = lambda v: jnp.sum(v.reshape(-1, 8, v.shape[-1]), axis=1)
    shared = jnp.concatenate([fold_rows(sum(vectors)), fold_rows(sum(finals)), jnp.zeros((2, features), F32)])
    shared = shared + other_core(shared)
    shared = shared + other_chip(shared)
    row_sum = sum(row_sums)[:1]
    apart = jnp.concatenate([
        jnp.sum(sum(sums), axis=0, keepdims=True),
        jnp.pad(row_sum, ((0, 0), (0, features - row_sum.shape[1]))),
        jnp.zeros((6, features), F32),
    ])
    small = sum_small(jnp.concatenate([shared, apart]))
    turned_weights = weights[:3 * width].T
    return (
        layer_out[0].reshape(1, length, features),
        input_grad[0].reshape(1, length, features),
        small[4],
        small[5],
        turned_weights[:, :width],
        small[9, :width],
        turned_weights[:, width:2 * width],
        turned_weights[:, 2 * width:],
        small[9, 2 * width:3 * width],
        weights[3 * width:],
        small[2],
        small[0],
        small[1],
        grad_inner.astype(F32),
        small[8],
        grad_outer.astype(F32),
        small[3],
    )


def solution(mesh):
    rows = mesh.shape["dp"]
    inner = Mesh(mesh.devices.reshape(rows // 2, 2, 2, 2), DP + MP)
    placed = (
        P(DP, None, None),
        P(DP, None),
        P(),
        P(),
        P(None, MP),
        P(MP),
        P(None, MP),
        P(None, MP),
        P(MP),
        P(MP, None),
        P(),
        P(),
        P(),
        P(None, MP),
        P(MP),
        P(MP, None),
        P(),
        P(DP, None, None),
    )
    return jax.shard_map(
        local,
        mesh=inner,
        in_specs=placed,
        out_specs=(
            P(DP, None, None),
            P(DP, None, None),
            P(),
            P(),
            P(None, MP),
            P(MP),
            P(None, MP),
            P(None, MP),
            P(MP),
            P(MP, None),
            P(),
            P(),
            P(),
            P(None, MP),
            P(MP),
            P(MP, None),
            P(),
        ),
        check_vma=False,
    )
```

```python
import jax
import jax.numpy as jnp
from jax import lax
from jax.experimental import pallas as pl
from jax.experimental.pallas import tpu as pltpu
from jax.sharding import Mesh
from jax.sharding import PartitionSpec as P

HEAD = 64
WIDE = 128
TILE = 256
PARTS = 2
MASKED = 1e30
SCALE = 1
F32 = jnp.float32
BF16 = jnp.bfloat16
DP = ("z", "x")
MP = ("y", "core")
SWAP = [(0, 1), (1, 0)]


def nn(left, right):
    return lax.dot_general(left, right, (((1,), (0,)), ((), ())), preferred_element_type=F32)


def nt(left, right):
    return lax.dot_general(left, right, (((1,), (1,)), ((), ())), preferred_element_type=F32)


def tn(left, right):
    return lax.dot_general(left, right, (((0,), (0,)), ((), ())), preferred_element_type=F32)


def stats(values):
    center = values - jnp.mean(values, axis=-1, keepdims=True)
    scale = lax.rsqrt(jnp.mean(center * center, axis=-1, keepdims=True) + 1e-05)
    return center * scale, scale


def norm_back(grad_out, normed, scale, gain):
    upstream = grad_out * gain
    return scale * (
        upstream
        - jnp.mean(upstream, axis=-1, keepdims=True)
        - normed * jnp.mean(upstream * normed, axis=-1, keepdims=True)
    )


def fold(values):
    return jnp.sum(values.reshape(-1, 8, values.shape[-1]), axis=0)


def split(value, parts):
    out = []
    for _ in range(parts):
        piece = value.astype(BF16).astype(F32)
        out.append(piece)
        value = value - piece
    return out


def const(shape):
    return pl.BlockSpec(shape, lambda *_: (0,) * len(shape))


def shape_of(*dims, dtype=BF16):
    return jax.ShapeDtypeStruct(dims, dtype)


def params():
    return pltpu.CompilerParams(vmem_limit_bytes=40 << 20)


def kernel_call(body, values, free_in=(), free_out=(), **options):
    shapes = options.pop("out_shape")
    many = isinstance(shapes, (list, tuple))
    shapes = [s if n in free_out else pltpu.HBM(s.shape, s.dtype) for n, s in enumerate(shapes if many else [shapes])]
    values = [
        v if n in free_in or v.dtype == jnp.int32 else pltpu.with_memory_space_constraint(v, pltpu.HBM)
        for n, v in enumerate(values)
    ]
    return pl.pallas_call(
        body, out_shape=shapes if many else shapes[0], compiler_params=params(), **options
    )(*values)


def cost(flops, moved, special=0):
    return pl.CostEstimate(flops=int(flops * SCALE), bytes_accessed=int(moved * SCALE), transcendentals=0)


def project_body(x_ref, seg_ref, vec_ref, wq_ref, wk_ref, wv_ref,
                 ai_ref, qt_ref, kt_ref, vt_ref, kn_ref, vn_ref):
    heads = kn_ref.shape[0]
    width = heads * HEAD
    tile = x_ref.shape[0]
    normed, _ = stats(x_ref[...].astype(F32))
    ai = (normed * vec_ref[0:1, :] + vec_ref[1:2, :]).astype(BF16)
    ai_ref[...] = ai
    column = vec_ref[...].T[:2 * width, 6:7]
    queries = ((nt(wq_ref[...], ai) + column[:width]).astype(BF16)).astype(F32) * HEAD ** -0.5
    keys = nt(wk_ref[...], ai)
    kt_ref[...] = keys.astype(BF16)
    values = nt(wv_ref[...], ai) + column[width:]
    row = lax.broadcasted_iota(jnp.int32, (HEAD, tile), 0)
    same = jnp.where(row == seg_ref[...], 1.0, 0.0)
    mask = jnp.where(row < 8, (same - 1.0) * MASKED, jnp.where(row < 11, 1.0, 0.0))
    ones = jnp.where(row < 2, 1.0, 0.0)
    first = jnp.where(row[:16] == 0, 1.0, 0.0).astype(BF16)
    for h in range(heads):
        rows = slice(h * HEAD, (h + 1) * HEAD)
        qt_ref[h, :HEAD, :] = queries[rows].astype(BF16)
        qt_ref[h, HEAD:, :] = same.astype(BF16)
        vt_ref[h, :HEAD, :] = values[rows].astype(BF16)
        vt_ref[h, HEAD:, :] = first
        kn_ref[h] = jnp.concatenate([keys[rows], mask], axis=0).T.astype(BF16)
        vn_ref[h] = jnp.concatenate([values[rows], ones], axis=0).T.astype(BF16)


def project(tokens, seg_row, vectors, wq, wk, wv, heads):
    length, features = tokens.shape
    width = heads * HEAD
    return kernel_call(
        project_body,
        (tokens, seg_row, vectors, wq, wk, wv),
        grid=(length // TILE,),
        in_specs=[
            pl.BlockSpec((TILE, features), lambda i: (i, 0)),
            pl.BlockSpec((1, TILE), lambda i: (0, i)),
            const(vectors.shape), const(wq.shape), const(wk.shape), const(wv.shape),
        ],
        out_specs=[
            pl.BlockSpec((TILE, features), lambda i: (i, 0)),
            pl.BlockSpec((heads, WIDE, TILE), lambda i: (0, 0, i)),
            pl.BlockSpec((width, TILE), lambda i: (0, i)),
            pl.BlockSpec((heads, HEAD + 16, TILE), lambda i: (0, 0, i)),
            pl.BlockSpec((heads, TILE, WIDE), lambda i: (0, i, 0)),
            pl.BlockSpec((heads, TILE, WIDE), lambda i: (0, i, 0)),
        ],
        out_shape=[
            shape_of(length, features),
            shape_of(heads, WIDE, length),
            shape_of(width, length),
            shape_of(heads, HEAD + 16, length),
            shape_of(heads, length, WIDE),
            shape_of(heads, length, WIDE),
        ],
        cost_estimate=cost(6e9, 14e6),
        name="project",
    )


def key_range(seg_ref, seg_all, i):
    first = seg_ref[0, i * TILE]
    last = seg_ref[0, i * TILE + TILE - 1]
    before = jnp.sum(jnp.where(seg_all < first, 1.0, 0.0)).astype(jnp.int32)
    until = jnp.sum(jnp.where(seg_all <= last, 1.0, 0.0)).astype(jnp.int32)
    return before // TILE, (until + TILE - 1) // TILE


def shifted(one_hot, pieces):
    row = lax.broadcasted_iota(jnp.int32, one_hot.shape, 0)
    value = one_hot
    for n, piece in enumerate(pieces):
        value = jnp.where(row == 8 + n, piece, value)
    return value.astype(BF16)


def forward_body(offset, segs_ref, seg_ref, qt_ref, kn_ref, vt_ref, out_ref, extra_ref, qa_ref, acc_ref):
    heads, _, tile = qt_ref.shape
    low, high = key_range(segs_ref, seg_ref[...], pl.program_id(0) + offset)
    acc_ref[...] = jnp.zeros_like(acc_ref)
    qa_ref[...] = qt_ref[...]

    def look(kb, tops):
        keys = pl.ds(pl.multiple_of(kb * TILE, TILE), TILE)
        return tuple(
            jnp.maximum(tops[h], jnp.max(nn(kn_ref[h, keys, :], qa_ref[h]).reshape(-1, 8, tile), axis=0))
            for h in range(heads)
        )

    tops = lax.fori_loop(low, high, look, (jnp.full((8, tile), -jnp.inf, F32),) * heads)
    tops = [jnp.max(top, axis=0, keepdims=True) for top in tops]
    one_hots = [qt_ref[h, HEAD:HEAD + 16, :].astype(F32) for h in range(heads)]
    for h in range(heads):
        qa_ref[h, HEAD:HEAD + 16, :] = shifted(one_hots[h], split(-tops[h], 3))

    def step(kb, carry):
        keys = pl.ds(pl.multiple_of(kb * TILE, TILE), TILE)
        for h in range(heads):
            powered = jnp.exp(nn(kn_ref[h, keys, :], qa_ref[h])).astype(BF16)
            acc_ref[h] += nn(vt_ref[h, :, keys], powered)
        return carry

    lax.fori_loop(low, high, step, 0)
    for h in range(heads):
        total = acc_ref[h, HEAD:HEAD + 1, :]
        out_ref[0, h * HEAD:(h + 1) * HEAD, :] = (acc_ref[h, :HEAD, :] / total).astype(BF16)
        extra_ref[h] = shifted(one_hots[h], split(-(tops[h] + jnp.log(total)), 3))


def attend_forward(part, seg_row, qt, kn, vt):
    heads, _, length = qt.shape
    width = heads * HEAD
    count = length // TILE // PARTS
    offset = part * count

    def body(*refs):
        forward_body(offset, *refs)

    return kernel_call(
        body,
        (seg_row, seg_row, qt, kn, vt),
        grid=(count,),
        in_specs=[
            pl.BlockSpec(memory_space=pltpu.SMEM),
            const((1, length)),
            pl.BlockSpec((heads, WIDE, TILE), lambda i: (0, 0, i + offset)),
            const(kn.shape), const(vt.shape),
        ],
        out_specs=[
            pl.BlockSpec((1, width, TILE), lambda i: (i, 0, 0)),
            pl.BlockSpec((heads, 16, TILE), lambda i: (0, 0, i)),
        ],
        out_shape=[
            shape_of(count, width, TILE),
            shape_of(heads, 16, count * TILE),
        ],
        scratch_shapes=[
            pltpu.VMEM((heads, WIDE, TILE), BF16),
            pltpu.VMEM((heads, HEAD + 16, TILE), F32),
        ],
        cost_estimate=cost(9e9, 5e6, 4e6),
        name="attend_forward",
    )


def backward_body(part, me_ref, segs_ref, seg_ref, qt_ref, extra_ref, kn_ref, kt_ref, vn_ref, out_ref,
                  g0_ref, g1_ref, g2_ref, g3_ref, *rest):
    heads, _, tile = qt_ref.shape
    width = heads * HEAD
    length = kt_ref.shape[1]
    if part == 0:
        dq_out, dk_ref, dv_ref, qa_ref, da_ref, dq_ref = rest[-6:]
    else:
        dq_in, dk_in, dv_in = rest[:3]
        grads_ref, qa_ref, da_ref, dq_ref, dk_ref, dv_ref = rest[-6:]
    i = pl.program_id(0)
    count = length // TILE // PARTS
    at_here = i + part * count
    low, high = key_range(segs_ref, seg_ref[...], at_here)

    @pl.when(i == 0)
    def _():
        if part == 0:
            dk_ref[...] = jnp.zeros_like(dk_ref)
            dv_ref[...] = jnp.zeros_like(dv_ref)
        else:
            dk_ref[...] = dk_in[...]
            dv_ref[...] = dv_in[...]
            grads_ref[:width, :count * TILE] = dq_in[...]
        qa_ref[...] = jnp.zeros_like(qa_ref)
        da_ref[...] = jnp.zeros_like(da_ref)

    source = i ^ me_ref[0]
    for n, g_ref in enumerate((g0_ref, g1_ref, g2_ref, g3_ref)):
        @pl.when(source == n)
        def _(g_ref=g_ref):
            for h in range(heads):
                da_ref[h, :HEAD, :] = g_ref[h * HEAD:(h + 1) * HEAD]

    dq_ref[...] = jnp.zeros_like(dq_ref)
    row = lax.broadcasted_iota(jnp.int32, (16, tile), 0)
    for h in range(heads):
        rows = slice(h * HEAD, (h + 1) * HEAD)
        qa_ref[h, :HEAD, :] = qt_ref[h, :HEAD, :]
        qa_ref[h, HEAD:HEAD + 16, :] = extra_ref[h]
        inner = jnp.sum(da_ref[h, :HEAD, :].astype(F32) * out_ref[0, rows].astype(F32), axis=0, keepdims=True)
        first, second = split(-inner, 2)
        value = jnp.where(row == 0, first, jnp.where(row == 1, second, 0.0))
        da_ref[h, HEAD:HEAD + 16, :] = value.astype(BF16)

    def step(kb, carry):
        keys = pl.ds(pl.multiple_of(kb * TILE, TILE), TILE)
        for h in range(heads):
            rows = slice(h * HEAD, (h + 1) * HEAD)
            probs = jnp.exp(nn(kn_ref[h, keys, :], qa_ref[h]))
            ds = (probs * nn(vn_ref[h, keys, :], da_ref[h])).astype(BF16)
            dv_ref[rows, keys] += nt(da_ref[h, :HEAD, :], probs.astype(BF16))
            dk_ref[rows, keys] += nt(qa_ref[h, :HEAD, :], ds)
            dq_ref[rows] += nn(kt_ref[rows, keys], ds)
        return carry

    lax.fori_loop(low, high, step, 0)
    dq = (dq_ref[...] * HEAD ** -0.5).astype(BF16)
    if part == 0:
        dq_out[...] = dq
    else:
        grads_ref[:width, pl.ds(pl.multiple_of(at_here * TILE, TILE), TILE)] = dq

        @pl.when(i == pl.num_programs(0) - 1)
        def _():
            grads_ref[width:2 * width] = dk_ref[...].astype(BF16)
            grads_ref[2 * width:] = dv_ref[...].astype(BF16)


def attend_backward(part, me, seg_row, qt, extra, kn, kt, vn, out, grad, earlier, after):
    heads, _, length = qt.shape
    width = heads * HEAD
    count = length // TILE // PARTS
    offset = part * count

    def body(*refs):
        backward_body(part, *refs)

    in_specs = [
        pl.BlockSpec(memory_space=pltpu.SMEM),
        const((1, length)),
        pl.BlockSpec((heads, WIDE, TILE), lambda i, m: (0, 0, i + offset)),
        pl.BlockSpec((heads, 16, TILE), lambda i, m: (0, 0, i)),
        const(kn.shape), const(kt.shape), const(vn.shape),
        pl.BlockSpec((1, width, TILE), lambda i, m: (i, 0, 0)),
        const(grad[0].shape), const(grad[1].shape), const(grad[2].shape), const(grad[3].shape),
    ] + [const(v.shape) for v in earlier] + [pl.BlockSpec(memory_space=pl.ANY)] * len(after)
    scratch = [
        pltpu.VMEM((heads, WIDE, TILE), BF16),
        pltpu.VMEM((heads, WIDE, TILE), BF16),
        pltpu.VMEM((width, TILE), F32),
    ]
    if part == 0:
        out_specs = [pl.BlockSpec((width, TILE), lambda i, m: (0, i)), const((width, length)), const((width, length))]
        out_shape = [shape_of(width, count * TILE), shape_of(width, length, dtype=F32), shape_of(width, length, dtype=F32)]
    else:
        out_specs = const((3 * width, length))
        out_shape = shape_of(3 * width, length)
        scratch += [pltpu.VMEM((width, length), F32), pltpu.VMEM((width, length), F32)]
    return kernel_call(
        body,
        (me, seg_row, seg_row, qt, extra, kn, kt, vn, out, *grad, *earlier, *after),
        free_in=(10, 11, 12) + tuple(range(13 + len(earlier), 13 + len(earlier) + len(after))),
        grid_spec=pltpu.PrefetchScalarGridSpec(
            num_scalar_prefetch=1, grid=(count,), in_specs=in_specs, out_specs=out_specs, scratch_shapes=scratch,
        ),
        out_shape=out_shape,
        cost_estimate=cost(16e9, 10e6, 4e6),
        name="attend_backward",
    )


def middle_body(me_ref, x_ref, m0_ref, m1_ref, m2_ref, m3_ref, w0_ref, w1_ref, w2_ref, w3_ref,
                vec_ref, residual_ref, own_ref, mixed_ref):
    total = x_ref[...].astype(F32) + vec_ref[2:3, :]
    pairs = ((m0_ref, w0_ref), (m1_ref, w1_ref), (m2_ref, w2_ref), (m3_ref, w3_ref))
    for n, (m_ref, w_ref) in enumerate(pairs):
        total = total + tn(m_ref[...], w_ref[...])
        mixed_ref[n] = m_ref[...]
    residual_ref[...] = total
    normed, _ = stats(total)
    own_ref[...] = (normed * vec_ref[3:4, :] + vec_ref[4:5, :]).astype(BF16)


def middle(part, me, tokens, mixed, weights, vectors):
    features = tokens.shape[1]
    width = weights[0].shape[0]
    return kernel_call(
        middle_body,
        (me, tokens, *mixed, *weights, vectors),
        free_in=(3, 4, 5),
        free_out=(1,),
        grid_spec=pltpu.PrefetchScalarGridSpec(
            num_scalar_prefetch=1,
            grid=(1,),
            in_specs=[pl.BlockSpec((TILE, features), lambda i, m: (4 * part + m[0], 0))]
            + [const(v.shape) for v in mixed] + [const(v.shape) for v in weights] + [const(vectors.shape)],
            out_specs=[const((TILE, features)), const((TILE, features)), const((4, width, TILE))],
        ),
        out_shape=[shape_of(TILE, features, dtype=F32), shape_of(TILE, features), shape_of(4, width, TILE)],
        cost_estimate=cost(2e9, 3e6),
        name="middle",
    )


def feed_body(me_ref, x0_ref, x1_ref, g_ref, inner_ref, vec_ref, outer_ref, *rest):
    act_ref, dh_ref, xs_ref, gs_ref, out0_ref, out1_ref, back0_ref, back1_ref, sum_ref = rest[-9:]
    i = pl.program_id(0)

    @pl.when(i == 0)
    def _():
        xs_ref[...] = x0_ref[...]

    @pl.when(i == 1)
    def _():
        xs_ref[...] = x1_ref[...]

    gs_ref[...] = g_ref[...]
    hidden = nn(xs_ref[...], inner_ref[...]) + vec_ref[7:8, :]
    half = 0.5 + 0.5 * lax.erf(hidden * 0.5 ** 0.5)
    act = (hidden * half).astype(BF16)
    act_ref[...] = act
    slope = half + hidden * (jnp.exp(-0.5 * hidden * hidden) * 0.3989422804014327)
    dh = (nt(g_ref[...], outer_ref[...]) * slope).astype(BF16)
    dh_ref[...] = dh
    sums = fold(dh.astype(F32))
    out = nn(act, outer_ref[...]).astype(BF16)
    back = nt(dh, inner_ref[...]).astype(BF16)

    @pl.when(i == 0)
    def _():
        sum_ref[...] = sums
        out0_ref[...] = out
        back0_ref[...] = back

    @pl.when(i == 1)
    def _():
        sum_ref[...] += sums
        out1_ref[...] = out
        back1_ref[...] = back


def feed(part, base, me, first, second, cot, inner, vectors, outer, kept, outs):
    length, features = cot.shape
    units = inner.shape[1]
    at = 4 * part + base
    rows = lambda n: pl.BlockSpec((TILE, n), lambda i, m: (at + i, 0))
    piece = const((TILE, features))
    half = pl.BlockSpec((TILE, features), lambda i, m: (part, 0))
    kept = (*kept, *outs)
    targets = list(range(4)) * (len(kept) >= 4) + [4, 5] * (len(outs) > 0)
    return kernel_call(
        feed_body,
        (me, first, second, cot, inner, vectors, outer, *kept),
        free_in=(1, 2),
        free_out=(7,),
        grid_spec=pltpu.PrefetchScalarGridSpec(
            num_scalar_prefetch=1,
            grid=(2,),
            in_specs=[
                piece, piece,
                pl.BlockSpec((TILE, features), lambda i, m: (4 * part + (m[0] ^ (base + i)), 0)),
                const(inner.shape), const(vectors.shape), const(outer.shape),
            ] + [pl.BlockSpec(memory_space=pl.ANY)] * len(kept),
            out_specs=[rows(units), rows(units), rows(features), rows(features), half, half, piece, piece,
                       const((8, units))],
        ),
        out_shape=[shape_of(length, units), shape_of(length, units), shape_of(length, features),
                   shape_of(length, features)] + [shape_of(PARTS * TILE, features)] * 2
        + [shape_of(TILE, features)] * 2 + [shape_of(8, units, dtype=F32)],
        input_output_aliases={7 + n: target for n, target in enumerate(targets)},
        cost_estimate=cost(5e9, 8e6, 1e6),
        name="feed",
    )


def back_body(me_ref, b0_ref, b1_ref, b2_ref, residual_ref, g_ref, vec_ref, w0_ref, w1_ref, w2_ref, w3_ref,
              grad_ref, low_ref, a0_ref, a1_ref, a2_ref, a3_ref, sum_ref):
    grad_mid = b0_ref[...].astype(F32) + b1_ref[...].astype(F32) + b2_ref[...].astype(F32)
    normed, scale = stats(residual_ref[...])
    upstream = g_ref[...].astype(F32)
    grad = upstream + norm_back(grad_mid, normed, scale, vec_ref[3:4, :])
    grad_ref[...] = grad
    low = grad.astype(BF16)
    low_ref[...] = low
    for w_ref, a_ref in ((w0_ref, a0_ref), (w1_ref, a1_ref), (w2_ref, a2_ref), (w3_ref, a3_ref)):
        a_ref[...] = nt(w_ref[...], low).astype(BF16)
    for n, value in enumerate((grad_mid * normed, grad_mid, grad, upstream)):
        sum_ref[8 * n:8 * n + 8] = fold(value)


def middle_back(part, me, sums, residual, cot, vectors, weights):
    features = cot.shape[1]
    piece = const((TILE, features))
    width = weights[0].shape[0]
    return kernel_call(
        back_body,
        (me, *sums, residual, cot, vectors, *weights),
        free_in=(2, 3),
        free_out=(3, 4, 5),
        grid_spec=pltpu.PrefetchScalarGridSpec(
            num_scalar_prefetch=1,
            grid=(1,),
            in_specs=[piece] * 4
            + [pl.BlockSpec((TILE, features), lambda i, m: (4 * part + m[0], 0)), const(vectors.shape)]
            + [const(v.shape) for v in weights],
            out_specs=[piece, piece] + [const((width, TILE))] * 4 + [const((32, features))],
        ),
        out_shape=[shape_of(TILE, features, dtype=F32), shape_of(TILE, features)]
        + [shape_of(width, TILE)] * 4 + [shape_of(32, features, dtype=F32)],
        cost_estimate=cost(2e9, 4e6),
        name="middle_back",
    )


def output_body(*refs):
    mixed, lows, outs = refs[:PARTS], refs[PARTS:2 * PARTS], refs[2 * PARTS:]
    for n in range(4):
        total = nn(mixed[0][n], lows[0][...])
        for p in range(1, PARTS):
            total = total + nn(mixed[p][n], lows[p][...])
        outs[n][...] = total.astype(BF16)


def output_grad(mixed, lows):
    width, features = mixed[0].shape[1], lows[0].shape[1]
    return kernel_call(
        output_body,
        (*mixed, *lows),
        free_out=(1, 3),
        out_shape=[shape_of(width, features)] * 4,
        cost_estimate=cost(2e9, 4e6),
        name="output_grad",
    )


def tail_body(me_ref, g_ref, wq_ref, wk_ref, wv_ref, *rest):
    o0_ref, o1_ref, sum_ref = rest[-3:]
    i, p = pl.program_id(0), pl.program_id(1)
    grads = g_ref[...]
    width = wq_ref.shape[0]
    value = tn(grads[:width], wq_ref[...]) + tn(grads[width:2 * width], wk_ref[...])
    value = (value + tn(grads[2 * width:], wv_ref[...])).astype(BF16)
    sums = nt(jnp.ones((8, grads.shape[1]), BF16), grads)

    @pl.when((i == 0) & (p == 0))
    def _():
        sum_ref[...] = jnp.zeros_like(sum_ref)

    sum_ref[...] += sums
    for step, o_ref in enumerate((o1_ref, o0_ref)):
        @pl.when(i == step)
        def _(o_ref=o_ref):
            o_ref[pl.ds(pl.multiple_of(p * TILE, TILE), TILE), :] = value


def tail(base, me, grads, wq, wk, wv, after):
    deep = grads.shape[0]
    features = wq.shape[1]
    share = const((PARTS * TILE, features))
    return kernel_call(
        tail_body,
        (me, grads, wq, wk, wv, *after),
        free_in=tuple(range(5, 5 + len(after))),
        free_out=(1,),
        grid_spec=pltpu.PrefetchScalarGridSpec(
            num_scalar_prefetch=1,
            grid=(2, PARTS),
            in_specs=[pl.BlockSpec((deep, TILE), lambda i, p, m: (0, 4 * p + (m[0] ^ (base + 1 - i)))),
                      const(wq.shape), const(wk.shape), const(wv.shape)]
            + [pl.BlockSpec(memory_space=pl.ANY)] * len(after),
            out_specs=[share] * 2 + [const((8, deep))],
        ),
        out_shape=[shape_of(PARTS * TILE, features)] * 2 + [shape_of(8, deep, dtype=F32)],
        cost_estimate=cost(2e9, 4e6),
        name="tail",
    )


def weights_body(xz_ref, g_ref, ai_ref, go_ref, keep_ref, send_ref):
    i = pl.program_id(0)
    count = pl.num_programs(0)
    mine = i // (count // 2) == xz_ref[0]
    rows = g_ref.shape[0]
    at = pl.ds(pl.multiple_of(i % (count // 2) * rows, rows), rows)
    for inside in (True, False):
        for to_ref, chosen in ((keep_ref, mine), (send_ref, jnp.logical_not(mine))):
            @pl.when(chosen & ((i < count * 3 // 4) == inside))
            def _(to_ref=to_ref, inside=inside):
                to_ref[at, :] = nn(g_ref[...], ai_ref[...]).astype(BF16) if inside else go_ref[...]


def weight_grads(xz, grads, attend_in, grad_output):
    deep, length = grads.shape
    width, features = grad_output.shape
    rows = width // 2
    half = const((2 * width, features))
    return kernel_call(
        weights_body,
        (xz, grads, attend_in, grad_output),
        free_in=(3,),
        free_out=(0, 1),
        grid_spec=pltpu.PrefetchScalarGridSpec(
            num_scalar_prefetch=1,
            grid=(8,),
            in_specs=[pl.BlockSpec((rows, length), lambda i, m: (jnp.minimum(i, 5), 0)), const(attend_in.shape),
                      pl.BlockSpec((rows, features), lambda i, m: (jnp.maximum(i - 6, 0), 0))],
            out_specs=[half, half],
        ),
        out_shape=[shape_of(2 * width, features)] * 2,
        cost_estimate=cost(2e9, 8e6),
        name="weight_grads",
    )


def quarter_body(xz_ref, one_ref, two_ref, *outs):
    for n, out_ref in enumerate(outs):
        @pl.when(pl.program_id(0) == n)
        def _(out_ref=out_ref):
            out_ref[...] = (one_ref[...].astype(F32) + two_ref[...].astype(F32)).astype(BF16)


def quarters(xz, one, two, count):
    rows, features = one.shape
    block = pl.BlockSpec((rows // count, features), lambda i, m: ((m[1] + i) % count, 0))
    return kernel_call(
        quarter_body,
        (xz, one, two),
        free_in=(1, 2),
        free_out=tuple(range(count)),
        grid_spec=pltpu.PrefetchScalarGridSpec(
            num_scalar_prefetch=1,
            grid=(count,),
            in_specs=[block, block],
            out_specs=[const((rows // count, features))] * count,
        ),
        out_shape=[shape_of(rows // count, features)] * count,
        cost_estimate=cost(1e6, 2e6),
        name="quarters",
    )


def whole_body(xz_ref, *refs):
    out_ref = refs[-1]
    for n, in_ref in enumerate(refs[:-1]):
        @pl.when(pl.program_id(0) == n)
        def _(in_ref=in_ref):
            out_ref[...] = in_ref[...]


def whole(xz, pieces):
    count = len(pieces)
    rows, features = pieces[0].shape
    return kernel_call(
        whole_body,
        (xz, *pieces),
        free_in=tuple(range(1, count + 1)),
        free_out=(0,),
        grid_spec=pltpu.PrefetchScalarGridSpec(
            num_scalar_prefetch=1,
            grid=(count,),
            in_specs=[const((rows, features))] * count,
            out_specs=pl.BlockSpec((rows, features), lambda i, m: ((m[1] + count - i) % count, 0)),
        ),
        out_shape=shape_of(rows * count, features),
        cost_estimate=cost(1e6, 2e6),
        name="whole",
    )


def ready_body(xz_ref, mine_ref, other_ref, *outs):
    width = outs[0].shape[0]
    for n, out_ref in enumerate(outs):
        rows = slice(n % 2 * width, (n % 2 + 1) * width)
        for to_ref, chosen in ((mine_ref, xz_ref[0] == n // 2), (other_ref, xz_ref[0] != n // 2)):
            @pl.when(chosen)
            def _(to_ref=to_ref, out_ref=out_ref, rows=rows):
                out_ref[...] = to_ref[rows].astype(F32)


def ready(xz, mine, other):
    rows, features = mine.shape
    width = rows // 2
    return kernel_call(
        ready_body,
        (xz, mine, other),
        free_in=(1, 2),
        grid_spec=pltpu.PrefetchScalarGridSpec(
            num_scalar_prefetch=1,
            grid=(1,),
            in_specs=[const(mine.shape), const(other.shape)],
            out_specs=[const((width, features))] * 4,
        ),
        out_shape=[shape_of(width, features, dtype=F32)] * 4,
        cost_estimate=cost(1e6, 4e6),
        name="ready",
    )


def final_body(me_ref, b0_ref, b1_ref, b2_ref, x_ref, *rest):
    grad_refs, (vec_ref, out_ref, sum_ref) = rest[:PARTS], rest[PARTS:]
    p = pl.program_id(0)
    grad_attend = b0_ref[...].astype(F32) + b1_ref[...].astype(F32) + b2_ref[...].astype(F32)
    normed, scale = stats(x_ref[...].astype(F32))
    back = norm_back(grad_attend, normed, scale, vec_ref[0:1, :])
    for n, grad_ref in enumerate(grad_refs):
        @pl.when(p == n)
        def _(grad_ref=grad_ref):
            out_ref[...] = (grad_ref[...] + back).astype(BF16)

    @pl.when(p == 0)
    def _():
        sum_ref[...] = jnp.zeros_like(sum_ref)

    sum_ref[:8] += fold(grad_attend * normed)
    sum_ref[8:] += fold(grad_attend)


def final(me, sums, tokens, grads, vectors):
    features = tokens.shape[1]
    rows = pl.BlockSpec((TILE, features), lambda p, m: (p, 0))
    return kernel_call(
        final_body,
        (me, *sums, tokens, *grads, vectors),
        free_in=(2, 3),
        free_out=(0,),
        grid_spec=pltpu.PrefetchScalarGridSpec(
            num_scalar_prefetch=1,
            grid=(PARTS,),
            in_specs=[rows] * 3 + [pl.BlockSpec((TILE, features), lambda p, m: (4 * p + m[0], 0))]
            + [const((TILE, features))] * PARTS + [const(vectors.shape)],
            out_specs=[rows, const((16, features))],
        ),
        out_shape=[shape_of(PARTS * TILE, features), shape_of(16, features, dtype=F32)],
        cost_estimate=cost(1e8, 5e6),
        name="final",
    )


def place_body(me_ref, p0_ref, p1_ref, p2_ref, p3_ref, out_ref):
    for step, p_ref in enumerate((p0_ref, p1_ref, p2_ref, p3_ref)):
        @pl.when(pl.program_id(0) == step)
        def _(p_ref=p_ref):
            at = pl.ds(pl.multiple_of(pl.program_id(1) * TILE, TILE), TILE)
            out_ref[...] = p_ref[at, :].astype(out_ref.dtype)


def place(me, shares, dtype):
    rows, features = shares[0].shape
    return kernel_call(
        place_body,
        (me, *shares),
        free_in=(1, 2, 3, 4),
        grid_spec=pltpu.PrefetchScalarGridSpec(
            num_scalar_prefetch=1,
            grid=(4, PARTS),
            in_specs=[const((rows, features))] * 4,
            out_specs=pl.BlockSpec((TILE, features), lambda i, p, m: (4 * p + (m[0] ^ i), 0)),
        ),
        out_shape=shape_of(4 * rows, features, dtype=dtype),
        cost_estimate=cost(1e6, 9e6),
        name="place",
    )


def fence_body(*refs):
    pass


def fence(value, *after, space=pltpu.HBM):
    anywhere = pl.BlockSpec(memory_space=pl.ANY)
    return pl.pallas_call(
        fence_body,
        in_specs=[anywhere] * (1 + len(after)),
        out_specs=anywhere,
        out_shape=space(value.shape, value.dtype),
        input_output_aliases={0: 0},
        name="fence",
    )(pltpu.with_memory_space_constraint(value, space), *after)


def other_core(value):
    return lax.ppermute(value, "core", SWAP)


def other_chip(value):
    return lax.ppermute(value, "y", SWAP)


def crosswise(value):
    return lax.ppermute(value, MP, [(n, n ^ 3) for n in range(4)])


def exchange(pieces):
    return [pieces[0], other_core(pieces[1]), other_chip(pieces[2]), crosswise(pieces[3])]


def gather_sum(pieces):
    near = other_core(pieces[1])
    far = (pieces[2].astype(F32) + other_core(pieces[3]).astype(F32)).astype(BF16)
    return [pieces[0], near, other_chip(far)], far


def spread(value):
    far = other_chip(value)
    return [value, other_core(value), far, other_core(far)]


def pick(values, at):
    return lax.dynamic_index_in_dim(values, at, 0, keepdims=False)


def turned(values, way):
    size = lax.axis_size("z")
    return lax.ppermute(values, "z", [(n, (n + way) % size) for n in range(size)])


def sum_weights(grads, attend_in, grad_output):
    size = lax.axis_size("z")
    x, z = lax.axis_index("x"), lax.axis_index("z")
    xz = jnp.stack([x, z]).astype(jnp.int32)
    keep, send = weight_grads(xz, grads, attend_in, grad_output)
    if size > 4:
        keep = lax.psum(keep + lax.ppermute(send, "x", SWAP), "z")
    else:
        parts = quarters(xz, keep, lax.ppermute(send, "x", SWAP), size)
        total = parts[0].astype(F32)
        for way in range(1, size):
            total = total + turned(parts[way], way).astype(F32)
        total = total.astype(BF16)
        keep = whole(xz, [turned(total, way) if way else total for way in range(size)])
    return ready(xz, keep, lax.ppermute(keep, "x", SWAP))


def sum_small(value):
    size = lax.axis_size("z")
    if size > 4:
        return lax.psum(value, DP)
    value = value + lax.ppermute(value, "x", SWAP)
    total = value
    for way in range(1, size):
        total = total + turned(value, way)
    return total


def local(
    tokens,
    segment_ids,
    gain_one,
    bias_one,
    query_weight,
    query_bias,
    key_weight,
    value_weight,
    value_bias,
    output_weight,
    output_bias,
    gain_two,
    bias_two,
    inner_weight,
    inner_bias,
    outer_weight,
    outer_bias,
    cotangent,
):
    _, length, features = tokens.shape
    width = query_weight.shape[1]
    heads = width // HEAD
    tokens = tokens.reshape(length, features)
    cot = cotangent.reshape(length, features)
    at = lax.axis_index(MP).astype(jnp.int32)
    me = at[None]
    apart = jnp.concatenate([query_bias, value_bias, jnp.zeros((features - 2 * width,), F32)])
    vectors = jnp.stack([gain_one, bias_one, output_bias, gain_two, bias_two, outer_bias, apart, inner_bias])
    wq, wk, wv = query_weight.T, key_weight.T, value_weight.T

    output_weights = exchange([output_weight] * 4)
    attend_in, qt, kt, vt, kn, vn = project(tokens, segment_ids, vectors, wq, wk, wv, heads)

    parts = range(PARTS)
    attended, extras, mixed, residuals, pieces = [], [], [], [], []
    for p in parts:
        out, extra = attend_forward(p, segment_ids, qt, kn, vt)
        attended.append(out)
        extras.append(extra)
        arrived = exchange([pick(out, at ^ n) for n in range(4)])
        residual, own, together = middle(p, me, tokens, arrived, output_weights, vectors)
        mixed.append(together)
        residuals.append(residual)
        pieces.append([own, other_core(own), other_chip(own)])

    outs, backs, sums, kept = [], {}, [], ()
    for base in (0, 2):
        held = ()
        for p in parts:
            if base:
                far = fence(pieces[p][2], backs[p, 0], space=pltpu.VMEM)
                pieces[p] = [None, None, far, other_core(far)]
            result = feed(p, base, me, pieces[p][base], pieces[p][base + 1], cot,
                          inner_weight, vectors, outer_weight, kept, held)
            kept, held = result[:4], result[4:6]
            backs[p, base], backs[p, base + 1] = result[6:8]
            sums.append(result[8])
        outs += held
    acts, dhs, xs, gs = kept

    gathered, far_sums = zip(*[gather_sum([backs[p, n] for n in range(4)]) for p in parts])
    grad_residuals, lows, grads_attended, inner_sums = [], [], [], []
    for p in parts:
        grad, low, a0, a1, a2, a3, vector = middle_back(
            p, me, gathered[p], residuals[p], cot, vectors, output_weights
        )
        grad_residuals.append(grad)
        lows.append(low)
        inner_sums.append(vector)
        grads_attended.append(exchange([a0, a1, a2, a3]))

    grad_outer = tn(fence(acts, *far_sums), gs).astype(BF16)
    grad_inner = tn(fence(xs, *far_sums), dhs).astype(BF16)
    feed_sum = lax.psum_scatter(jnp.concatenate([grad_outer, grad_inner]), DP, scatter_dimension=0, tiled=True)

    last = fence(outs[3], lows[-1])
    near = other_core(fence(outs[1], lows[-1]))
    far = (outs[2].astype(F32) + other_core(last).astype(F32)).astype(BF16)
    earlier = attend_backward(0, me, segment_ids, qt, extras[0], kn, kt, vn, attended[0], grads_attended[0], (),
                              (far, near))
    result = jnp.concatenate(residuals) + outs[0].astype(F32) + near.astype(F32)
    result = (result + other_chip(far).astype(F32) + outer_bias).astype(BF16)
    (one, two, three), _ = gather_sum(output_grad(mixed, lows))
    grad_output = (one.astype(F32) + two.astype(F32) + three.astype(F32)).astype(BF16)
    grads = attend_backward(1, me, segment_ids, qt, extras[1], kn, kt, vn, attended[1], grads_attended[1], earlier,
                            (result, grad_output))

    feed_sum = lax.all_gather(fence(feed_sum, grads), DP, axis=0, tiled=True).astype(F32)
    wide = sum_weights(grads, attend_in, grad_output)
    near, far = other_core(result), other_chip(result)
    back_far, back_across, sum_far = tail(2, me, grads, wq, wk, wv, (near, far))
    back_own, back_near, sum_near = tail(0, me, grads, wq, wk, wv, ())
    arrived, _ = gather_sum([back_own, back_near, back_far, back_across])
    share, outer_sums = final(me, arrived, tokens, grad_residuals, vectors)
    layer_out = place(me, [result, near, far, other_core(far)], BF16)
    input_grad = place(me, spread(share), F32)

    fold_rows = lambda v: jnp.sum(v.reshape(-1, 8, v.shape[-1]), axis=1)
    shared = jnp.concatenate([fold_rows(sum(inner_sums)), fold_rows(outer_sums), jnp.zeros((2, features), F32)])
    shared = shared + other_core(shared)
    shared = shared + other_chip(shared)
    row_sum = (sum_far + sum_near)[:1]
    apart = jnp.concatenate([
        jnp.sum(sum(sums), axis=0, keepdims=True),
        jnp.pad(row_sum, ((0, 0), (0, features - row_sum.shape[1]))),
        jnp.zeros((6, features), F32),
    ])
    small = sum_small(jnp.concatenate([shared, apart]))
    return (
        layer_out.reshape(1, length, features),
        input_grad.reshape(1, length, features),
        small[4],
        small[5],
        wide[0].T,
        small[9, :width],
        wide[1].T,
        wide[2].T,
        small[9, 2 * width:3 * width],
        wide[3],
        small[2],
        small[0],
        small[1],
        feed_sum[features:],
        small[8],
        feed_sum[:features],
        small[3],
    )


def solution(mesh):
    rows = mesh.shape["dp"]
    inner = Mesh(mesh.devices.reshape(rows // 2, 2, 2, 2), DP + MP)
    placed = (
        P(DP, None, None),
        P(DP, None),
        P(),
        P(),
        P(None, MP),
        P(MP),
        P(None, MP),
        P(None, MP),
        P(MP),
        P(MP, None),
        P(),
        P(),
        P(),
        P(None, MP),
        P(MP),
        P(MP, None),
        P(),
        P(DP, None, None),
    )
    return jax.shard_map(
        local,
        mesh=inner,
        in_specs=placed,
        out_specs=(
            P(DP, None, None),
            P(DP, None, None),
            P(),
            P(),
            P(None, MP),
            P(MP),
            P(None, MP),
            P(None, MP),
            P(MP),
            P(MP, None),
            P(),
            P(),
            P(),
            P(None, MP),
            P(MP),
            P(MP, None),
            P(),
        ),
        check_vma=False,
    )
```

```python
import jax
import jax.numpy as jnp
from jax import lax
from jax.experimental import pallas as pl
from jax.experimental.pallas import tpu as pltpu
from jax.sharding import Mesh
from jax.sharding import PartitionSpec as P

HEAD = 64
WIDE = 128
TILE = 256
PARTS = 2
MASKED = 1e30
SCALE = 1
F32 = jnp.float32
BF16 = jnp.bfloat16
DP = ("z", "x")
MP = ("y", "core")
SWAP = [(0, 1), (1, 0)]


def nn(left, right):
    return lax.dot_general(left, right, (((1,), (0,)), ((), ())), preferred_element_type=F32)


def nt(left, right):
    return lax.dot_general(left, right, (((1,), (1,)), ((), ())), preferred_element_type=F32)


def tn(left, right):
    return lax.dot_general(left, right, (((0,), (0,)), ((), ())), preferred_element_type=F32)


def stats(values):
    center = values - jnp.mean(values, axis=-1, keepdims=True)
    scale = lax.rsqrt(jnp.mean(center * center, axis=-1, keepdims=True) + 1e-05)
    return center * scale, scale


def norm_back(grad_out, normed, scale, gain):
    upstream = grad_out * gain
    return scale * (
        upstream
        - jnp.mean(upstream, axis=-1, keepdims=True)
        - normed * jnp.mean(upstream * normed, axis=-1, keepdims=True)
    )


def fold(values):
    return jnp.sum(values.reshape(-1, 8, values.shape[-1]), axis=0)


def split(value, parts):
    out = []
    for _ in range(parts):
        piece = value.astype(BF16).astype(F32)
        out.append(piece)
        value = value - piece
    return out


def const(shape):
    return pl.BlockSpec(shape, lambda *_: (0,) * len(shape))


def shape_of(*dims, dtype=BF16):
    return jax.ShapeDtypeStruct(dims, dtype)


def params(mib=40):
    return pltpu.CompilerParams(vmem_limit_bytes=mib << 20)


def kernel_call(body, values, free_in=(), free_out=(), **options):
    shapes = options.pop("out_shape")
    many = isinstance(shapes, (list, tuple))
    shapes = [s if n in free_out else pltpu.HBM(s.shape, s.dtype) for n, s in enumerate(shapes if many else [shapes])]
    values = [
        v if n in free_in or v.dtype == jnp.int32 else pltpu.with_memory_space_constraint(v, pltpu.HBM)
        for n, v in enumerate(values)
    ]
    return pl.pallas_call(
        body, out_shape=shapes if many else shapes[0], compiler_params=params(), **options
    )(*values)


def cost(flops, moved, special=0):
    return pl.CostEstimate(flops=int(flops * SCALE), bytes_accessed=int(moved * SCALE), transcendentals=0)


def project_body(x_ref, seg_ref, vec_ref, wq_ref, wk_ref, wv_ref,
                 ai_ref, qt_ref, kt_ref, vt_ref, kn_ref, vn_ref):
    heads = kn_ref.shape[0]
    width = heads * HEAD
    tile = x_ref.shape[0]
    normed, _ = stats(x_ref[...].astype(F32))
    ai = (normed * vec_ref[0:1, :] + vec_ref[1:2, :]).astype(BF16)
    ai_ref[...] = ai
    column = vec_ref[...].T[:2 * width, 6:7]
    queries = ((nt(wq_ref[...], ai) + column[:width]).astype(BF16)).astype(F32) * HEAD ** -0.5
    keys = nt(wk_ref[...], ai)
    kt_ref[...] = keys.astype(BF16)
    values = nt(wv_ref[...], ai) + column[width:]
    row = lax.broadcasted_iota(jnp.int32, (HEAD, tile), 0)
    same = jnp.where(row == seg_ref[...], 1.0, 0.0)
    mask = jnp.where(row < 8, (same - 1.0) * MASKED, jnp.where(row < 11, 1.0, 0.0))
    ones = jnp.where(row < 2, 1.0, 0.0)
    first = jnp.where(row[:16] == 0, 1.0, 0.0).astype(BF16)
    for h in range(heads):
        rows = slice(h * HEAD, (h + 1) * HEAD)
        qt_ref[h, :HEAD, :] = queries[rows].astype(BF16)
        qt_ref[h, HEAD:, :] = same.astype(BF16)
        vt_ref[h, :HEAD, :] = values[rows].astype(BF16)
        vt_ref[h, HEAD:, :] = first
        kn_ref[h] = jnp.concatenate([keys[rows], mask], axis=0).T.astype(BF16)
        vn_ref[h] = jnp.concatenate([values[rows], ones], axis=0).T.astype(BF16)


def project(tokens, seg_row, vectors, wq, wk, wv, heads):
    length, features = tokens.shape
    width = heads * HEAD
    return kernel_call(
        project_body,
        (tokens, seg_row, vectors, wq, wk, wv),
        grid=(length // TILE,),
        in_specs=[
            pl.BlockSpec((TILE, features), lambda i: (i, 0)),
            pl.BlockSpec((1, TILE), lambda i: (0, i)),
            const(vectors.shape), const(wq.shape), const(wk.shape), const(wv.shape),
        ],
        out_specs=[
            pl.BlockSpec((TILE, features), lambda i: (i, 0)),
            pl.BlockSpec((heads, WIDE, TILE), lambda i: (0, 0, i)),
            pl.BlockSpec((width, TILE), lambda i: (0, i)),
            pl.BlockSpec((heads, HEAD + 16, TILE), lambda i: (0, 0, i)),
            pl.BlockSpec((heads, TILE, WIDE), lambda i: (0, i, 0)),
            pl.BlockSpec((heads, TILE, WIDE), lambda i: (0, i, 0)),
        ],
        out_shape=[
            shape_of(length, features),
            shape_of(heads, WIDE, length),
            shape_of(width, length),
            shape_of(heads, HEAD + 16, length),
            shape_of(heads, length, WIDE),
            shape_of(heads, length, WIDE),
        ],
        cost_estimate=cost(6e9, 14e6),
        name="project",
    )


def key_range(seg_ref, seg_all, i):
    first = seg_ref[0, i * TILE]
    last = seg_ref[0, i * TILE + TILE - 1]
    before = jnp.sum(jnp.where(seg_all < first, 1.0, 0.0)).astype(jnp.int32)
    until = jnp.sum(jnp.where(seg_all <= last, 1.0, 0.0)).astype(jnp.int32)
    return before // TILE, (until + TILE - 1) // TILE


def by_pairs(low, high, step, carry):
    keys = lambda kb: pl.ds(pl.multiple_of(kb * TILE, TILE), TILE)
    pairs = (high - low) // 2
    carry = lax.fori_loop(0, pairs, lambda n, c: step([keys(low + 2 * n), keys(low + 2 * n + 1)], c), carry)
    return lax.fori_loop(low + 2 * pairs, high, lambda kb, c: step([keys(kb)], c), carry)


def shifted(one_hot, pieces):
    row = lax.broadcasted_iota(jnp.int32, one_hot.shape, 0)
    value = one_hot
    for n, piece in enumerate(pieces):
        value = jnp.where(row == 8 + n, piece, value)
    return value.astype(BF16)


def forward_body(offset, me_ref, segs_ref, seg_ref, qt_ref, kn_ref, vt_ref,
                 out_ref, extra_ref, o0_ref, o1_ref, o2_ref, o3_ref, acc_ref):
    heads, _, tile = qt_ref.shape
    i = pl.program_id(0)
    low, high = key_range(segs_ref, seg_ref[...], i + offset)
    acc_ref[...] = jnp.zeros_like(acc_ref)

    def step(keys, tops):
        scores = [[nn(kn_ref[h, at, :], qt_ref[h]) for at in keys] for h in range(heads)]
        new_tops = []
        for h in range(heads):
            top = tops[h]
            for score in scores[h]:
                top = jnp.maximum(top, jnp.max(score, axis=0, keepdims=True))
            new_tops.append(top)
        powered = [[jnp.exp(score - new_tops[h]).astype(BF16) for score in scores[h]] for h in range(heads)]
        for h in range(heads):
            total = acc_ref[h] * jnp.exp(tops[h] - new_tops[h])
            for at, power in zip(keys, powered[h]):
                total = total + nn(vt_ref[h, :, at], power)
            acc_ref[h] = total
        return tuple(new_tops)

    tops = by_pairs(low, high, step, (jnp.full((1, tile), -jnp.inf, F32),) * heads)
    for h in range(heads):
        total = acc_ref[h, HEAD:HEAD + 1, :]
        out_ref[0, h * HEAD:(h + 1) * HEAD, :] = (acc_ref[h, :HEAD, :] / total).astype(BF16)
        one_hot = qt_ref[h, HEAD:HEAD + 16, :].astype(F32)
        extra_ref[h] = shifted(one_hot, split(-(tops[h] + jnp.log(total)), 3))
    for n, o_ref in enumerate((o0_ref, o1_ref, o2_ref, o3_ref)):
        @pl.when((i ^ me_ref[0]) == n)
        def _(o_ref=o_ref):
            o_ref[...] = out_ref[0]


def attend_forward(part, me, seg_row, qt, kn, vt):
    heads, _, length = qt.shape
    width = heads * HEAD
    count = length // TILE // PARTS
    offset = part * count

    def body(*refs):
        forward_body(offset, *refs)

    return kernel_call(
        body,
        (me, seg_row, seg_row, qt, kn, vt),
        free_out=(3, 4, 5),
        grid_spec=pltpu.PrefetchScalarGridSpec(
            num_scalar_prefetch=1,
            grid=(count,),
            in_specs=[
                pl.BlockSpec(memory_space=pltpu.SMEM),
                const((1, length)),
                pl.BlockSpec((heads, WIDE, TILE), lambda i, m: (0, 0, i + offset)),
                const(kn.shape), const(vt.shape),
            ],
            out_specs=[
                pl.BlockSpec((1, width, TILE), lambda i, m: (i, 0, 0)),
                pl.BlockSpec((heads, 16, TILE), lambda i, m: (0, 0, i)),
            ] + [const((width, TILE))] * 4,
            scratch_shapes=[pltpu.VMEM((heads, HEAD + 16, TILE), F32)],
        ),
        out_shape=[shape_of(count, width, TILE), shape_of(heads, 16, count * TILE)] + [shape_of(width, TILE)] * 4,
        cost_estimate=cost(9e9, 5e6, 4e6),
        name="attend_forward",
    )


def backward_body(part, me_ref, segs_ref, seg_ref, qt_ref, extra_ref, kn_ref, kt_ref, vn_ref, out_ref,
                  g0_ref, g1_ref, g2_ref, g3_ref, *rest):
    heads, _, tile = qt_ref.shape
    width = heads * HEAD
    length = kt_ref.shape[1]
    if part == 0:
        dq_out, dk_ref, dv_ref, qa_ref, da_ref, dq_ref = rest[-6:]
    else:
        dq_in, dk_in, dv_in = rest[:3]
        grads_ref, qa_ref, da_ref, dq_ref, dk_ref, dv_ref = rest[-6:]
    i = pl.program_id(0)
    count = length // TILE // PARTS
    at_here = i + part * count
    low, high = key_range(segs_ref, seg_ref[...], at_here)

    @pl.when(i == 0)
    def _():
        if part == 0:
            dk_ref[...] = jnp.zeros_like(dk_ref)
            dv_ref[...] = jnp.zeros_like(dv_ref)
        else:
            dk_ref[...] = dk_in[...]
            dv_ref[...] = dv_in[...]
            grads_ref[:width, :count * TILE] = dq_in[...]
        qa_ref[...] = jnp.zeros_like(qa_ref)
        da_ref[...] = jnp.zeros_like(da_ref)

    source = i ^ me_ref[0]
    for n, g_ref in enumerate((g0_ref, g1_ref, g2_ref, g3_ref)):
        @pl.when(source == n)
        def _(g_ref=g_ref):
            for h in range(heads):
                da_ref[h, :HEAD, :] = g_ref[h * HEAD:(h + 1) * HEAD]

    dq_ref[...] = jnp.zeros_like(dq_ref)
    row = lax.broadcasted_iota(jnp.int32, (16, tile), 0)
    for h in range(heads):
        rows = slice(h * HEAD, (h + 1) * HEAD)
        qa_ref[h, :HEAD, :] = qt_ref[h, :HEAD, :]
        qa_ref[h, HEAD:HEAD + 16, :] = extra_ref[h]
        inner = jnp.sum(da_ref[h, :HEAD, :].astype(F32) * out_ref[0, rows].astype(F32), axis=0, keepdims=True)
        first, second = split(-inner, 2)
        value = jnp.where(row == 0, first, jnp.where(row == 1, second, 0.0))
        da_ref[h, HEAD:HEAD + 16, :] = value.astype(BF16)

    def step(keys, carry):
        every = range(heads)
        rows = [slice(h * HEAD, (h + 1) * HEAD) for h in every]
        scores = [[nn(kn_ref[h, at, :], qa_ref[h]) for at in keys] for h in every]
        slopes = [[nn(vn_ref[h, at, :], da_ref[h]) for at in keys] for h in every]
        probs = [[jnp.exp(score) for score in scores[h]] for h in every]
        ds = [[(p * s).astype(BF16) for p, s in zip(probs[h], slopes[h])] for h in every]
        probs = [[p.astype(BF16) for p in probs[h]] for h in every]
        for h in every:
            total = dq_ref[rows[h]]
            for n, at in enumerate(keys):
                dv_ref[rows[h], at] += nt(da_ref[h, :HEAD, :], probs[h][n])
                dk_ref[rows[h], at] += nt(qa_ref[h, :HEAD, :], ds[h][n])
                total = total + nn(kt_ref[rows[h], at], ds[h][n])
            dq_ref[rows[h]] = total
        return carry

    by_pairs(low, high, step, 0)
    dq = (dq_ref[...] * HEAD ** -0.5).astype(BF16)
    if part == 0:
        dq_out[...] = dq
    else:
        grads_ref[:width, pl.ds(pl.multiple_of(at_here * TILE, TILE), TILE)] = dq

        @pl.when(i == pl.num_programs(0) - 1)
        def _():
            grads_ref[width:2 * width] = dk_ref[...].astype(BF16)
            grads_ref[2 * width:] = dv_ref[...].astype(BF16)


def attend_backward(part, me, seg_row, qt, extra, kn, kt, vn, out, grad, earlier, after):
    heads, _, length = qt.shape
    width = heads * HEAD
    count = length // TILE // PARTS
    offset = part * count

    def body(*refs):
        backward_body(part, *refs)

    in_specs = [
        pl.BlockSpec(memory_space=pltpu.SMEM),
        const((1, length)),
        pl.BlockSpec((heads, WIDE, TILE), lambda i, m: (0, 0, i + offset)),
        pl.BlockSpec((heads, 16, TILE), lambda i, m: (0, 0, i)),
        const(kn.shape), const(kt.shape), const(vn.shape),
        pl.BlockSpec((1, width, TILE), lambda i, m: (i, 0, 0)),
        const(grad[0].shape), const(grad[1].shape), const(grad[2].shape), const(grad[3].shape),
    ] + [const(v.shape) for v in earlier] + [pl.BlockSpec(memory_space=pl.ANY)] * len(after)
    scratch = [
        pltpu.VMEM((heads, WIDE, TILE), BF16),
        pltpu.VMEM((heads, WIDE, TILE), BF16),
        pltpu.VMEM((width, TILE), F32),
    ]
    if part == 0:
        out_specs = [pl.BlockSpec((width, TILE), lambda i, m: (0, i)), const((width, length)), const((width, length))]
        out_shape = [shape_of(width, count * TILE), shape_of(width, length, dtype=F32), shape_of(width, length, dtype=F32)]
    else:
        out_specs = const((3 * width, length))
        out_shape = shape_of(3 * width, length)
        scratch += [pltpu.VMEM((width, length), F32), pltpu.VMEM((width, length), F32)]
    return kernel_call(
        body,
        (me, seg_row, seg_row, qt, extra, kn, kt, vn, out, *grad, *earlier, *after),
        free_in=(10, 11, 12) + tuple(range(13 + len(earlier), 13 + len(earlier) + len(after))),
        grid_spec=pltpu.PrefetchScalarGridSpec(
            num_scalar_prefetch=1, grid=(count,), in_specs=in_specs, out_specs=out_specs, scratch_shapes=scratch,
        ),
        out_shape=out_shape,
        cost_estimate=cost(16e9, 10e6, 4e6),
        name="attend_backward",
    )


def middle_body(me_ref, x_ref, m0_ref, m1_ref, m2_ref, m3_ref, w0_ref, w1_ref, w2_ref, w3_ref,
                vec_ref, *rest):
    residual_ref, own_ref, mixed_ref = rest[-3:]
    total = x_ref[...].astype(F32) + vec_ref[2:3, :]
    pairs = ((m0_ref, w0_ref), (m1_ref, w1_ref), (m2_ref, w2_ref), (m3_ref, w3_ref))
    for n, (m_ref, w_ref) in enumerate(pairs):
        total = total + tn(m_ref[...], w_ref[...])
        mixed_ref[n] = m_ref[...]
    residual_ref[...] = total
    normed, _ = stats(total)
    own_ref[...] = (normed * vec_ref[3:4, :] + vec_ref[4:5, :]).astype(BF16)


def middle(part, me, tokens, mixed, weights, vectors, after):
    features = tokens.shape[1]
    width = weights[0].shape[0]
    return kernel_call(
        middle_body,
        (me, tokens, *mixed, *weights, vectors, *after),
        free_in=(3, 4, 5),
        free_out=(1,),
        grid_spec=pltpu.PrefetchScalarGridSpec(
            num_scalar_prefetch=1,
            grid=(1,),
            in_specs=[pl.BlockSpec((TILE, features), lambda i, m: (4 * part + m[0], 0))]
            + [const(v.shape) for v in mixed] + [const(v.shape) for v in weights] + [const(vectors.shape)]
            + [pl.BlockSpec(memory_space=pl.ANY)] * len(after),
            out_specs=[const((TILE, features)), const((TILE, features)), const((4, width, TILE))],
        ),
        out_shape=[shape_of(TILE, features, dtype=F32), shape_of(TILE, features), shape_of(4, width, TILE)],
        cost_estimate=cost(2e9, 3e6),
        name="middle",
    )


def feed_body(me_ref, x0_ref, x1_ref, g_ref, inner_ref, vec_ref, outer_ref, *rest):
    left_ref, right_ref, out0_ref, out1_ref, back0_ref, back1_ref, sum_ref = rest[-7:]
    i = pl.program_id(0)

    @pl.when(i == 0)
    def _():
        left_ref[1] = x0_ref[...]

    @pl.when(i == 1)
    def _():
        left_ref[1] = x1_ref[...]

    right_ref[0] = g_ref[...]
    hidden = nn(left_ref[1], inner_ref[...]) + vec_ref[7:8, :]
    half = 0.5 + 0.5 * lax.erf(hidden * 0.5 ** 0.5)
    act = (hidden * half).astype(BF16)
    left_ref[0] = act
    slope = half + hidden * (jnp.exp(-0.5 * hidden * hidden) * 0.3989422804014327)
    dh = (nt(g_ref[...], outer_ref[...]) * slope).astype(BF16)
    right_ref[1] = dh
    sums = fold(dh.astype(F32))
    out = nn(act, outer_ref[...]).astype(BF16)
    back = nt(dh, inner_ref[...]).astype(BF16)

    @pl.when(i == 0)
    def _():
        sum_ref[...] = sums
        out0_ref[...] = out
        back0_ref[...] = back

    @pl.when(i == 1)
    def _():
        sum_ref[...] += sums
        out1_ref[...] = out
        back1_ref[...] = back


def feed(part, base, me, first, second, cot, inner, vectors, outer, kept, outs):
    length, features = cot.shape
    units = inner.shape[1]
    at = 4 * part + base
    rows = pl.BlockSpec((2, TILE, features), lambda i, m: (0, at + i, 0))
    piece = const((TILE, features))
    half = pl.BlockSpec((TILE, features), lambda i, m: (part, 0))
    kept = (*kept, *outs)
    targets = list(range(2)) * (len(kept) >= 2) + [2, 3] * (len(outs) > 0)
    return kernel_call(
        feed_body,
        (me, first, second, cot, inner, vectors, outer, *kept),
        free_in=(1, 2),
        free_out=(5,),
        grid_spec=pltpu.PrefetchScalarGridSpec(
            num_scalar_prefetch=1,
            grid=(2,),
            in_specs=[
                piece, piece,
                pl.BlockSpec((TILE, features), lambda i, m: (4 * part + (m[0] ^ (base + i)), 0)),
                const(inner.shape), const(vectors.shape), const(outer.shape),
            ] + [pl.BlockSpec(memory_space=pl.ANY)] * len(kept),
            out_specs=[rows, rows, half, half, piece, piece, const((8, units))],
        ),
        out_shape=[shape_of(2, length, features)] * 2 + [shape_of(PARTS * TILE, features)] * 2
        + [shape_of(TILE, features)] * 2 + [shape_of(8, units, dtype=F32)],
        input_output_aliases={7 + n: target for n, target in enumerate(targets)},
        cost_estimate=cost(5e9, 8e6, 1e6),
        name="feed",
    )


def back_body(me_ref, b0_ref, b1_ref, b2_ref, residual_ref, g_ref, vec_ref, w0_ref, w1_ref, w2_ref, w3_ref,
              grad_ref, low_ref, a0_ref, a1_ref, a2_ref, a3_ref, sum_ref):
    grad_mid = b0_ref[...].astype(F32) + b1_ref[...].astype(F32) + b2_ref[...].astype(F32)
    normed, scale = stats(residual_ref[...])
    upstream = g_ref[...].astype(F32)
    grad = upstream + norm_back(grad_mid, normed, scale, vec_ref[3:4, :])
    grad_ref[...] = grad
    low = grad.astype(BF16)
    low_ref[...] = low
    for w_ref, a_ref in ((w0_ref, a0_ref), (w1_ref, a1_ref), (w2_ref, a2_ref), (w3_ref, a3_ref)):
        a_ref[...] = nt(w_ref[...], low).astype(BF16)
    for n, value in enumerate((grad_mid * normed, grad_mid, grad, upstream)):
        sum_ref[8 * n:8 * n + 8] = fold(value)


def middle_back(part, me, sums, residual, cot, vectors, weights):
    features = cot.shape[1]
    piece = const((TILE, features))
    width = weights[0].shape[0]
    return kernel_call(
        back_body,
        (me, *sums, residual, cot, vectors, *weights),
        free_in=(2, 3),
        free_out=(3, 4, 5),
        grid_spec=pltpu.PrefetchScalarGridSpec(
            num_scalar_prefetch=1,
            grid=(1,),
            in_specs=[piece] * 4
            + [pl.BlockSpec((TILE, features), lambda i, m: (4 * part + m[0], 0)), const(vectors.shape)]
            + [const(v.shape) for v in weights],
            out_specs=[piece, piece] + [const((width, TILE))] * 4 + [const((32, features))],
        ),
        out_shape=[shape_of(TILE, features, dtype=F32), shape_of(TILE, features)]
        + [shape_of(width, TILE)] * 4 + [shape_of(32, features, dtype=F32)],
        cost_estimate=cost(2e9, 4e6),
        name="middle_back",
    )


def output_body(*refs):
    mixed, lows, outs = refs[:PARTS], refs[PARTS:2 * PARTS], refs[2 * PARTS:]
    for n in range(4):
        total = nn(mixed[0][n], lows[0][...])
        for p in range(1, PARTS):
            total = total + nn(mixed[p][n], lows[p][...])
        outs[n][...] = total.astype(BF16)


def output_grad(mixed, lows):
    width, features = mixed[0].shape[1], lows[0].shape[1]
    return kernel_call(
        output_body,
        (*mixed, *lows),
        free_out=(1, 3),
        out_shape=[shape_of(width, features)] * 4,
        cost_estimate=cost(2e9, 4e6),
        name="output_grad",
    )


def tail_body(me_ref, g_ref, wq_ref, wk_ref, wv_ref, *rest):
    o0_ref, o1_ref, sum_ref = rest[-3:]
    i, p = pl.program_id(0), pl.program_id(1)
    grads = g_ref[...]
    width = wq_ref.shape[0]
    value = tn(grads[:width], wq_ref[...]) + tn(grads[width:2 * width], wk_ref[...])
    value = (value + tn(grads[2 * width:], wv_ref[...])).astype(BF16)
    sums = nt(jnp.ones((8, grads.shape[1]), BF16), grads)

    @pl.when((i == 0) & (p == 0))
    def _():
        sum_ref[...] = jnp.zeros_like(sum_ref)

    sum_ref[...] += sums
    for step, o_ref in enumerate((o1_ref, o0_ref)):
        @pl.when(i == step)
        def _(o_ref=o_ref):
            o_ref[pl.ds(pl.multiple_of(p * TILE, TILE), TILE), :] = value


def tail(base, me, grads, wq, wk, wv, after):
    deep = grads.shape[0]
    features = wq.shape[1]
    share = const((PARTS * TILE, features))
    return kernel_call(
        tail_body,
        (me, grads, wq, wk, wv, *after),
        free_in=tuple(range(5, 5 + len(after))),
        free_out=(1,),
        grid_spec=pltpu.PrefetchScalarGridSpec(
            num_scalar_prefetch=1,
            grid=(2, PARTS),
            in_specs=[pl.BlockSpec((deep, TILE), lambda i, p, m: (0, 4 * p + (m[0] ^ (base + 1 - i)))),
                      const(wq.shape), const(wk.shape), const(wv.shape)]
            + [pl.BlockSpec(memory_space=pl.ANY)] * len(after),
            out_specs=[share] * 2 + [const((8, deep))],
        ),
        out_shape=[shape_of(PARTS * TILE, features)] * 2 + [shape_of(8, deep, dtype=F32)],
        cost_estimate=cost(2e9, 4e6),
        name="tail",
    )


def halves_body(xz_ref, g_ref, go_ref, keep_ref, send_ref):
    width = go_ref.shape[0]
    for to_ref, half in ((keep_ref, xz_ref[0]), (send_ref, 1 - xz_ref[0])):
        @pl.when(half == 0)
        def _(to_ref=to_ref):
            to_ref[...] = g_ref[:2 * width]

        @pl.when(half == 1)
        def _(to_ref=to_ref):
            to_ref[:width] = g_ref[2 * width:]
            to_ref[width:] = go_ref[...]


def halves(xz, grad_weights, grad_output):
    width, features = grad_output.shape
    half = const((2 * width, features))
    return kernel_call(
        halves_body,
        (xz, grad_weights, grad_output),
        free_in=(1, 2),
        free_out=(1,),
        grid_spec=pltpu.PrefetchScalarGridSpec(
            num_scalar_prefetch=1,
            grid=(1,),
            in_specs=[const(grad_weights.shape), const(grad_output.shape)],
            out_specs=[half, half],
        ),
        out_shape=[shape_of(2 * width, features)] * 2,
        cost_estimate=cost(1e6, 4e6),
        name="halves",
    )


def quarter_body(count, xz_ref, one_ref, two_ref, *rest):
    for n, out_ref in enumerate(rest[-count:]):
        @pl.when(pl.program_id(0) == n)
        def _(out_ref=out_ref):
            out_ref[...] = (one_ref[...].astype(F32) + two_ref[...].astype(F32)).astype(BF16)


def quarters(xz, one, two, count, after):
    rows, features = one.shape

    def body(*refs):
        quarter_body(count, *refs)

    block = pl.BlockSpec((rows // count, features), lambda i, m: ((m[1] + i) % count, 0))
    return kernel_call(
        body,
        (xz, one, two, *after),
        free_in=(2,) + tuple(range(3, 3 + len(after))),
        free_out=tuple(range(count)),
        grid_spec=pltpu.PrefetchScalarGridSpec(
            num_scalar_prefetch=1,
            grid=(count,),
            in_specs=[block, block] + [pl.BlockSpec(memory_space=pl.ANY)] * len(after),
            out_specs=[const((rows // count, features))] * count,
        ),
        out_shape=[shape_of(rows // count, features)] * count,
        cost_estimate=cost(1e6, 2e6),
        name="quarters",
    )


def whole_body(xz_ref, *refs):
    out_ref = refs[-1]
    for n, in_ref in enumerate(refs[:-1]):
        @pl.when(pl.program_id(0) == n)
        def _(in_ref=in_ref):
            out_ref[...] = in_ref[...]


def whole(xz, pieces):
    count = len(pieces)
    rows, features = pieces[0].shape
    return kernel_call(
        whole_body,
        (xz, *pieces),
        free_in=tuple(range(1, count + 1)),
        free_out=(0,),
        grid_spec=pltpu.PrefetchScalarGridSpec(
            num_scalar_prefetch=1,
            grid=(count,),
            in_specs=[const((rows, features))] * count,
            out_specs=pl.BlockSpec((rows, features), lambda i, m: ((m[1] + count - i) % count, 0)),
        ),
        out_shape=shape_of(rows * count, features),
        cost_estimate=cost(1e6, 2e6),
        name="whole",
    )


def ready_body(xz_ref, mine_ref, other_ref, *rest):
    outs = rest[-4:]
    width = outs[0].shape[0]
    for n, out_ref in enumerate(outs):
        rows = slice(n % 2 * width, (n % 2 + 1) * width)
        for to_ref, chosen in ((mine_ref, xz_ref[0] == n // 2), (other_ref, xz_ref[0] != n // 2)):
            @pl.when(chosen)
            def _(to_ref=to_ref, out_ref=out_ref, rows=rows):
                out_ref[...] = to_ref[rows].astype(F32)


def ready(xz, mine, other, after):
    rows, features = mine.shape
    width = rows // 2
    return kernel_call(
        ready_body,
        (xz, mine, other, *after),
        free_in=(1, 2) + tuple(range(3, 3 + len(after))),
        grid_spec=pltpu.PrefetchScalarGridSpec(
            num_scalar_prefetch=1,
            grid=(1,),
            in_specs=[const(mine.shape), const(other.shape)] + [pl.BlockSpec(memory_space=pl.ANY)] * len(after),
            out_specs=[const((width, features))] * 4,
        ),
        out_shape=[shape_of(width, features, dtype=F32)] * 4,
        cost_estimate=cost(1e6, 4e6),
        name="ready",
    )


def final_body(me_ref, b0_ref, b1_ref, b2_ref, x_ref, *rest):
    grad_refs, vec_ref, (out_ref, sum_ref) = rest[:PARTS], rest[PARTS], rest[-2:]
    p = pl.program_id(0)
    grad_attend = b0_ref[...].astype(F32) + b1_ref[...].astype(F32) + b2_ref[...].astype(F32)
    normed, scale = stats(x_ref[...].astype(F32))
    back = norm_back(grad_attend, normed, scale, vec_ref[0:1, :])
    for n, grad_ref in enumerate(grad_refs):
        @pl.when(p == n)
        def _(grad_ref=grad_ref):
            out_ref[...] = (grad_ref[...] + back).astype(BF16)

    @pl.when(p == 0)
    def _():
        sum_ref[...] = jnp.zeros_like(sum_ref)

    sum_ref[:8] += fold(grad_attend * normed)
    sum_ref[8:] += fold(grad_attend)


def final(me, sums, tokens, grads, vectors, after):
    features = tokens.shape[1]
    rows = pl.BlockSpec((TILE, features), lambda p, m: (p, 0))
    return kernel_call(
        final_body,
        (me, *sums, tokens, *grads, vectors, *after),
        free_in=(2, 3) + tuple(range(6 + PARTS, 6 + PARTS + len(after))),
        free_out=(0,),
        grid_spec=pltpu.PrefetchScalarGridSpec(
            num_scalar_prefetch=1,
            grid=(PARTS,),
            in_specs=[rows] * 3 + [pl.BlockSpec((TILE, features), lambda p, m: (4 * p + m[0], 0))]
            + [const((TILE, features))] * PARTS + [const(vectors.shape)]
            + [pl.BlockSpec(memory_space=pl.ANY)] * len(after),
            out_specs=[rows, const((16, features))],
        ),
        out_shape=[shape_of(PARTS * TILE, features), shape_of(16, features, dtype=F32)],
        cost_estimate=cost(1e8, 5e6),
        name="final",
    )


def place_body(me_ref, p0_ref, p1_ref, p2_ref, p3_ref, out_ref):
    for step, p_ref in enumerate((p0_ref, p1_ref, p2_ref, p3_ref)):
        @pl.when(pl.program_id(0) == step)
        def _(p_ref=p_ref):
            at = pl.ds(pl.multiple_of(pl.program_id(1) * TILE, TILE), TILE)
            out_ref[...] = p_ref[at, :].astype(out_ref.dtype)


def place(me, shares, dtype):
    rows, features = shares[0].shape
    return kernel_call(
        place_body,
        (me, *shares),
        free_in=(1, 2, 3, 4),
        grid_spec=pltpu.PrefetchScalarGridSpec(
            num_scalar_prefetch=1,
            grid=(4, PARTS),
            in_specs=[const((rows, features))] * 4,
            out_specs=pl.BlockSpec((TILE, features), lambda i, p, m: (4 * p + (m[0] ^ i), 0)),
        ),
        out_shape=shape_of(4 * rows, features, dtype=dtype),
        cost_estimate=cost(1e6, 9e6),
        name="place",
    )


def fence_body(*refs):
    pass


def fence(value, *after, space=pltpu.HBM):
    anywhere = pl.BlockSpec(memory_space=pl.ANY)
    return pl.pallas_call(
        fence_body,
        in_specs=[anywhere] * (1 + len(after)),
        out_specs=anywhere,
        out_shape=space(value.shape, value.dtype),
        input_output_aliases={0: 0},
        name="fence",
    )(pltpu.with_memory_space_constraint(value, space), *after)


def other_core(value):
    return lax.ppermute(value, "core", SWAP)


def other_chip(value):
    return lax.ppermute(value, "y", SWAP)


def crosswise(value):
    return lax.ppermute(value, MP, [(n, n ^ 3) for n in range(4)])


def exchange(pieces):
    return [pieces[0], other_core(pieces[1]), other_chip(pieces[2]), crosswise(pieces[3])]


def gather_sum(pieces):
    near = other_core(pieces[1])
    far = (pieces[2].astype(F32) + other_core(pieces[3]).astype(F32)).astype(BF16)
    return [pieces[0], near, other_chip(far)], far


def spread(value):
    far = other_chip(value)
    return [value, other_core(value), far, other_core(far)]


def pick(values, at):
    return lax.dynamic_index_in_dim(values, at, 0, keepdims=False)


def turned(values, way):
    size = lax.axis_size("z")
    return lax.ppermute(values, "z", [(n, (n + way) % size) for n in range(size)])


def sum_first(xz, keep, send, after):
    size = lax.axis_size("z")
    got = lax.ppermute(send, "x", SWAP)
    if size > 4:
        return [lax.psum(keep + got, "z")]
    return quarters(xz, keep, got, size, after)


def sum_second(parts):
    total = parts[0].astype(F32)
    for way in range(1, len(parts)):
        total = total + turned(parts[way], way).astype(F32)
    return total.astype(BF16)


def sum_third(xz, total):
    size = lax.axis_size("z")
    if size > 4:
        keep = total
    else:
        keep = whole(xz, [turned(total, way) if way else total for way in range(size)])
    return keep, lax.ppermute(keep, "x", SWAP)


def sum_small(value):
    size = lax.axis_size("z")
    if size > 4:
        return lax.psum(value, DP)
    value = value + lax.ppermute(value, "x", SWAP)
    total = value
    for way in range(1, size):
        total = total + turned(value, way)
    return total


def local(
    tokens,
    segment_ids,
    gain_one,
    bias_one,
    query_weight,
    query_bias,
    key_weight,
    value_weight,
    value_bias,
    output_weight,
    output_bias,
    gain_two,
    bias_two,
    inner_weight,
    inner_bias,
    outer_weight,
    outer_bias,
    cotangent,
):
    _, length, features = tokens.shape
    width = query_weight.shape[1]
    heads = width // HEAD
    tokens = tokens.reshape(length, features)
    cot = cotangent.reshape(length, features)
    at = lax.axis_index(MP).astype(jnp.int32)
    me = at[None]
    apart = jnp.concatenate([query_bias, value_bias, jnp.zeros((features - 2 * width,), F32)])
    vectors = jnp.concatenate([gain_one, bias_one, output_bias, gain_two, bias_two, outer_bias, apart, inner_bias])
    vectors = vectors.reshape(8, features)
    wq, wk, wv = query_weight.T, key_weight.T, value_weight.T

    output_weights = exchange([output_weight] * 4)
    attend_in, qt, kt, vt, kn, vn = project(tokens, segment_ids, vectors, wq, wk, wv, heads)

    parts = range(PARTS)
    attended, extras, fours = [], [], []
    for p in parts:
        out, extra, *four = attend_forward(p, me, segment_ids, qt, kn, vt)
        attended.append(out)
        extras.append(extra)
        fours.append(exchange(four))
    mixed, residuals, pieces = [], [], []
    for p in parts:
        residual, own, together = middle(p, me, tokens, fours[p], output_weights, vectors, extras[p + 1:])
        mixed.append(together)
        residuals.append(residual)
        pieces.append([own, other_core(own), other_chip(own)])

    outs, backs, sums, kept = [], {}, [], ()
    for base in (0, 2):
        held = ()
        for p in parts:
            if base:
                far = fence(pieces[p][2], backs[p, 0], space=pltpu.VMEM)
                pieces[p] = [None, None, far, other_core(far)]
            result = feed(p, base, me, pieces[p][base], pieces[p][base + 1], cot,
                          inner_weight, vectors, outer_weight, kept, held)
            kept, held = result[:2], result[2:4]
            backs[p, base], backs[p, base + 1] = result[4:6]
            sums.append(result[6])
        outs += held
    left, right = kept

    gathered, far_sums = zip(*[gather_sum([backs[p, n] for n in range(4)]) for p in parts])
    grad_residuals, lows, grads_attended, inner_sums = [], [], [], []
    for p in parts:
        grad, low, a0, a1, a2, a3, vector = middle_back(
            p, me, gathered[p], residuals[p], cot, vectors, output_weights
        )
        grad_residuals.append(grad)
        lows.append(low)
        inner_sums.append(vector)
        grads_attended.append(exchange([a0, a1, a2, a3]))

    grad_feed = lax.dot_general(fence(left, *far_sums), right, (((1,), (1,)), ((0,), (0,))), preferred_element_type=F32)
    grad_feed = grad_feed.astype(BF16).reshape(2 * features, features)
    feed_sum = lax.psum_scatter(grad_feed, DP, scatter_dimension=0, tiled=True)

    near = other_core(fence(outs[1], *far_sums))
    far = (outs[2].astype(F32) + other_core(fence(outs[3], *far_sums)).astype(F32)).astype(BF16)
    far = fence(far, lows[-1], space=pltpu.VMEM)
    part = output_grad(mixed, lows)
    earlier = attend_backward(0, me, segment_ids, qt, extras[0], kn, kt, vn, attended[0], grads_attended[0], (),
                              (far, near, part[0]))
    result = jnp.concatenate(residuals) + outs[0].astype(F32) + near.astype(F32)
    result = (result + other_chip(far).astype(F32) + outer_bias).astype(BF16)
    part_far = fence(part[2], earlier[0])
    part_far = (part_far.astype(F32) + other_core(part[3]).astype(F32)).astype(BF16)
    part_near = other_core(part[1])
    grads = attend_backward(1, me, segment_ids, qt, extras[1], kn, kt, vn, attended[1], grads_attended[1], earlier,
                            (result, part_far, part_near))

    xz = jnp.stack([lax.axis_index("x"), lax.axis_index("z")]).astype(jnp.int32)
    grad_output = fence(part[0], grads).astype(F32) + part_near.astype(F32) + other_chip(part_far).astype(F32)
    keep, send = halves(xz, nn(grads, attend_in).astype(BF16), grad_output.astype(BF16))
    near, far = other_core(result), other_chip(result)
    back_far, back_across, sum_far = tail(2, me, grads, wq, wk, wv, (near, far, send))
    back_far = (back_far.astype(F32) + other_core(back_across).astype(F32)).astype(BF16)
    quarter = sum_first(xz, keep, send, (back_far,))
    back_own, back_near, sum_near = tail(0, me, grads, wq, wk, wv, quarter[-1:])
    layer_out = place(me, [result, near, far, other_core(far)], BF16)
    feed_sum = lax.all_gather(fence(feed_sum, layer_out), DP, axis=0, tiled=True).astype(F32)
    total = fence(sum_second(quarter), layer_out, back_own, space=pltpu.VMEM)
    arrived = [back_own, other_core(back_near), other_chip(back_far)]
    share, outer_sums = final(me, arrived, tokens, grad_residuals, vectors, (total,))
    mine, other = sum_third(xz, total)
    wide = ready(xz, mine, other, ())
    input_grad = place(me, spread(share), F32)

    fold_rows = lambda v: jnp.sum(v.reshape(-1, 8, v.shape[-1]), axis=1)
    shared = jnp.concatenate([fold_rows(sum(inner_sums)), fold_rows(outer_sums), jnp.zeros((2, features), F32)])
    shared = shared + other_core(shared)
    shared = shared + other_chip(shared)
    row_sum = (sum_far + sum_near)[:1]
    apart = jnp.concatenate([
        jnp.sum(sum(sums), axis=0, keepdims=True),
        jnp.pad(row_sum, ((0, 0), (0, features - row_sum.shape[1]))),
        jnp.zeros((6, features), F32),
    ])
    small = sum_small(jnp.concatenate([shared, apart]))
    return (
        layer_out.reshape(1, length, features),
        input_grad.reshape(1, length, features),
        small[4],
        small[5],
        wide[0].T,
        small[9, :width],
        wide[1].T,
        wide[2].T,
        small[9, 2 * width:3 * width],
        wide[3],
        small[2],
        small[0],
        small[1],
        feed_sum[features:],
        small[8],
        feed_sum[:features],
        small[3],
    )


def solution(mesh):
    rows = mesh.shape["dp"]
    inner = Mesh(mesh.devices.reshape(rows // 2, 2, 2, 2), DP + MP)
    placed = (
        P(DP, None, None),
        P(DP, None),
        P(),
        P(),
        P(None, MP),
        P(MP),
        P(None, MP),
        P(None, MP),
        P(MP),
        P(MP, None),
        P(),
        P(),
        P(),
        P(None, MP),
        P(MP),
        P(MP, None),
        P(),
        P(DP, None, None),
    )
    return jax.shard_map(
        local,
        mesh=inner,
        in_specs=placed,
        out_specs=(
            P(DP, None, None),
            P(DP, None, None),
            P(),
            P(),
            P(None, MP),
            P(MP),
            P(None, MP),
            P(None, MP),
            P(MP),
            P(MP, None),
            P(),
            P(),
            P(),
            P(None, MP),
            P(MP),
            P(MP, None),
            P(),
        ),
        check_vma=False,
    )
```

```python
import jax
import jax.numpy as jnp
from jax import lax
from jax.experimental import pallas as pl
from jax.experimental.pallas import tpu as pltpu
from jax.sharding import Mesh
from jax.sharding import PartitionSpec as P

HEAD = 64
WIDE = 128
TILE = 256
PARTS = 2
MASKED = 1e30
SCALE = 1
F32 = jnp.float32
BF16 = jnp.bfloat16
DP = ("z", "x")
MP = ("y", "core")
SWAP = [(0, 1), (1, 0)]


def nn(left, right):
    return lax.dot_general(left, right, (((1,), (0,)), ((), ())), preferred_element_type=F32)


def nt(left, right):
    return lax.dot_general(left, right, (((1,), (1,)), ((), ())), preferred_element_type=F32)


def tn(left, right):
    return lax.dot_general(left, right, (((0,), (0,)), ((), ())), preferred_element_type=F32)


def stats(values):
    mean = jnp.mean(values, axis=-1, keepdims=True)
    center = values - mean
    scale = lax.rsqrt(jnp.mean(center * center, axis=-1, keepdims=True) + 1e-05)
    return center * scale, scale, mean


def norm_back(grad_out, normed, scale, gain):
    upstream = grad_out * gain
    return scale * (
        upstream
        - jnp.mean(upstream, axis=-1, keepdims=True)
        - normed * jnp.mean(upstream * normed, axis=-1, keepdims=True)
    )


def fold(values):
    return jnp.sum(values.reshape(-1, 8, values.shape[-1]), axis=0)


def split(value, parts):
    out = []
    for _ in range(parts):
        piece = value.astype(BF16).astype(F32)
        out.append(piece)
        value = value - piece
    return out


def const(shape):
    return pl.BlockSpec(shape, lambda *_: (0,) * len(shape))


def shape_of(*dims, dtype=BF16):
    return jax.ShapeDtypeStruct(dims, dtype)


def params(mib=40):
    return pltpu.CompilerParams(vmem_limit_bytes=mib << 20)


def kernel_call(body, values, free_in=(), free_out=(), **options):
    shapes = options.pop("out_shape")
    many = isinstance(shapes, (list, tuple))
    shapes = [s if n in free_out else pltpu.HBM(s.shape, s.dtype) for n, s in enumerate(shapes if many else [shapes])]
    values = [
        v if n in free_in or v.dtype == jnp.int32 else pltpu.with_memory_space_constraint(v, pltpu.HBM)
        for n, v in enumerate(values)
    ]
    return pl.pallas_call(
        body, out_shape=shapes if many else shapes[0], compiler_params=params(), **options
    )(*values)


def cost(flops, moved, special=0):
    return pl.CostEstimate(flops=int(flops * SCALE), bytes_accessed=int(moved * SCALE), transcendentals=0)


def project_body(x_ref, seg_ref, vec_ref, wq_ref, wk_ref, wv_ref,
                 ai_ref, qt_ref, kt_ref, vt_ref, kn_ref, vn_ref, stat_ref):
    heads = kn_ref.shape[0]
    width = heads * HEAD
    tile = x_ref.shape[0]
    normed, scale, mean = stats(x_ref[...].astype(F32))
    lane = lax.broadcasted_iota(jnp.int32, stat_ref.shape, 1)
    stat_ref[...] = jnp.where(lane == 0, mean, scale)
    ai = (normed * vec_ref[0:1, :] + vec_ref[1:2, :]).astype(BF16)
    ai_ref[...] = ai
    column = vec_ref[...].T[:2 * width, 6:7]
    queries = ((nt(wq_ref[...], ai) + column[:width]).astype(BF16)).astype(F32) * HEAD ** -0.5
    keys = nt(wk_ref[...], ai)
    kt_ref[...] = keys.astype(BF16)
    values = nt(wv_ref[...], ai) + column[width:]
    row = lax.broadcasted_iota(jnp.int32, (HEAD, tile), 0)
    same = jnp.where(row == seg_ref[...], 1.0, 0.0)
    mask = jnp.where(row < 8, (same - 1.0) * MASKED, jnp.where(row < 11, 1.0, 0.0))
    ones = jnp.where(row < 2, 1.0, 0.0)
    first = jnp.where(row[:16] == 0, 1.0, 0.0).astype(BF16)
    for h in range(heads):
        rows = slice(h * HEAD, (h + 1) * HEAD)
        qt_ref[h, :HEAD, :] = queries[rows].astype(BF16)
        qt_ref[h, HEAD:, :] = same.astype(BF16)
        vt_ref[h, :HEAD, :] = values[rows].astype(BF16)
        vt_ref[h, HEAD:, :] = first
        kn_ref[h] = jnp.concatenate([keys[rows], mask], axis=0).T.astype(BF16)
        vn_ref[h] = jnp.concatenate([values[rows], ones], axis=0).T.astype(BF16)


def project(tokens, seg_row, vectors, wq, wk, wv, heads):
    length, features = tokens.shape
    width = heads * HEAD
    return kernel_call(
        project_body,
        (tokens, seg_row, vectors, wq, wk, wv),
        grid=(length // TILE,),
        in_specs=[
            pl.BlockSpec((TILE, features), lambda i: (i, 0)),
            pl.BlockSpec((1, TILE), lambda i: (0, i)),
            const(vectors.shape), const(wq.shape), const(wk.shape), const(wv.shape),
        ],
        out_specs=[
            pl.BlockSpec((TILE, features), lambda i: (i, 0)),
            pl.BlockSpec((heads, WIDE, TILE), lambda i: (0, 0, i)),
            pl.BlockSpec((width, TILE), lambda i: (0, i)),
            pl.BlockSpec((heads, HEAD + 16, TILE), lambda i: (0, 0, i)),
            pl.BlockSpec((heads, TILE, WIDE), lambda i: (0, i, 0)),
            pl.BlockSpec((heads, TILE, WIDE), lambda i: (0, i, 0)),
            pl.BlockSpec((TILE, WIDE), lambda i: (i, 0)),
        ],
        out_shape=[
            shape_of(length, features),
            shape_of(heads, WIDE, length),
            shape_of(width, length),
            shape_of(heads, HEAD + 16, length),
            shape_of(heads, length, WIDE),
            shape_of(heads, length, WIDE),
            shape_of(length, WIDE, dtype=F32),
        ],
        cost_estimate=cost(6e9, 14e6),
        name="project",
    )


def key_range(seg_ref, seg_all, i):
    first = seg_ref[0, i * TILE]
    last = seg_ref[0, i * TILE + TILE - 1]
    before = jnp.sum(jnp.where(seg_all < first, 1.0, 0.0)).astype(jnp.int32)
    until = jnp.sum(jnp.where(seg_all <= last, 1.0, 0.0)).astype(jnp.int32)
    return before // TILE, (until + TILE - 1) // TILE


def by_pairs(low, high, step, carry):
    keys = lambda kb: pl.ds(pl.multiple_of(kb * TILE, TILE), TILE)
    pairs = (high - low) // 2
    carry = lax.fori_loop(0, pairs, lambda n, c: step([keys(low + 2 * n), keys(low + 2 * n + 1)], c), carry)
    return lax.fori_loop(low + 2 * pairs, high, lambda kb, c: step([keys(kb)], c), carry)


def shifted(one_hot, pieces):
    row = lax.broadcasted_iota(jnp.int32, one_hot.shape, 0)
    value = one_hot
    for n, piece in enumerate(pieces):
        value = jnp.where(row == 8 + n, piece, value)
    return value.astype(BF16)


def forward_body(offset, me_ref, segs_ref, seg_ref, qt_ref, kn_ref, vt_ref,
                 out_ref, extra_ref, o0_ref, o1_ref, o2_ref, o3_ref, acc_ref):
    heads, _, tile = qt_ref.shape
    i = pl.program_id(0)
    low, high = key_range(segs_ref, seg_ref[...], i + offset)
    acc_ref[...] = jnp.zeros_like(acc_ref)

    def step(keys, tops):
        scores = [[nn(kn_ref[h, at, :], qt_ref[h]) for at in keys] for h in range(heads)]
        new_tops = []
        for h in range(heads):
            top = tops[h]
            for score in scores[h]:
                top = jnp.maximum(top, jnp.max(score, axis=0, keepdims=True))
            new_tops.append(top)
        powered = [[jnp.exp(score - new_tops[h]).astype(BF16) for score in scores[h]] for h in range(heads)]
        for h in range(heads):
            total = acc_ref[h] * jnp.exp(tops[h] - new_tops[h])
            for at, power in zip(keys, powered[h]):
                total = total + nn(vt_ref[h, :, at], power)
            acc_ref[h] = total
        return tuple(new_tops)

    tops = by_pairs(low, high, step, (jnp.full((1, tile), -jnp.inf, F32),) * heads)
    for h in range(heads):
        total = acc_ref[h, HEAD:HEAD + 1, :]
        out_ref[0, h * HEAD:(h + 1) * HEAD, :] = (acc_ref[h, :HEAD, :] / total).astype(BF16)
        one_hot = qt_ref[h, HEAD:HEAD + 16, :].astype(F32)
        extra_ref[h] = shifted(one_hot, split(-(tops[h] + jnp.log(total)), 3))
    for n, o_ref in enumerate((o0_ref, o1_ref, o2_ref, o3_ref)):
        @pl.when((i ^ me_ref[0]) == n)
        def _(o_ref=o_ref):
            o_ref[...] = out_ref[0]


def attend_forward(part, me, seg_row, qt, kn, vt):
    heads, _, length = qt.shape
    width = heads * HEAD
    count = length // TILE // PARTS
    offset = part * count

    def body(*refs):
        forward_body(offset, *refs)

    return kernel_call(
        body,
        (me, seg_row, seg_row, qt, kn, vt),
        free_out=(3, 4, 5),
        grid_spec=pltpu.PrefetchScalarGridSpec(
            num_scalar_prefetch=1,
            grid=(count,),
            in_specs=[
                pl.BlockSpec(memory_space=pltpu.SMEM),
                const((1, length)),
                pl.BlockSpec((heads, WIDE, TILE), lambda i, m: (0, 0, i + offset)),
                const(kn.shape), const(vt.shape),
            ],
            out_specs=[
                pl.BlockSpec((1, width, TILE), lambda i, m: (i, 0, 0)),
                pl.BlockSpec((heads, 16, TILE), lambda i, m: (0, 0, i)),
            ] + [const((width, TILE))] * 4,
            scratch_shapes=[pltpu.VMEM((heads, HEAD + 16, TILE), F32)],
        ),
        out_shape=[shape_of(count, width, TILE), shape_of(heads, 16, count * TILE)] + [shape_of(width, TILE)] * 4,
        cost_estimate=cost(9e9, 5e6, 4e6),
        name="attend_forward",
    )


def backward_body(part, me_ref, segs_ref, seg_ref, qt_ref, extra_ref, kn_ref, kt_ref, vn_ref, out_ref,
                  g0_ref, g1_ref, g2_ref, g3_ref, *rest):
    heads, _, tile = qt_ref.shape
    width = heads * HEAD
    length = kt_ref.shape[1]
    if part == 0:
        dq_out, dk_ref, dv_ref, qa_ref, da_ref, dq_ref = rest[-6:]
    else:
        dq_in, dk_in, dv_in = rest[:3]
        grads_ref, qa_ref, da_ref, dq_ref, dk_ref, dv_ref = rest[-6:]
    i = pl.program_id(0)
    count = length // TILE // PARTS
    at_here = i + part * count
    low, high = key_range(segs_ref, seg_ref[...], at_here)

    @pl.when(i == 0)
    def _():
        if part == 0:
            dk_ref[...] = jnp.zeros_like(dk_ref)
            dv_ref[...] = jnp.zeros_like(dv_ref)
        else:
            dk_ref[...] = dk_in[...]
            dv_ref[...] = dv_in[...]
            grads_ref[:width, :count * TILE] = dq_in[...]
        qa_ref[...] = jnp.zeros_like(qa_ref)
        da_ref[...] = jnp.zeros_like(da_ref)

    source = i ^ me_ref[0]
    for n, g_ref in enumerate((g0_ref, g1_ref, g2_ref, g3_ref)):
        @pl.when(source == n)
        def _(g_ref=g_ref):
            for h in range(heads):
                da_ref[h, :HEAD, :] = g_ref[h * HEAD:(h + 1) * HEAD]

    dq_ref[...] = jnp.zeros_like(dq_ref)
    row = lax.broadcasted_iota(jnp.int32, (16, tile), 0)
    for h in range(heads):
        rows = slice(h * HEAD, (h + 1) * HEAD)
        qa_ref[h, :HEAD, :] = qt_ref[h, :HEAD, :]
        qa_ref[h, HEAD:HEAD + 16, :] = extra_ref[h]
        inner = jnp.sum(da_ref[h, :HEAD, :].astype(F32) * out_ref[0, rows].astype(F32), axis=0, keepdims=True)
        first, second = split(-inner, 2)
        value = jnp.where(row == 0, first, jnp.where(row == 1, second, 0.0))
        da_ref[h, HEAD:HEAD + 16, :] = value.astype(BF16)

    def step(keys, carry):
        every = range(heads)
        rows = [slice(h * HEAD, (h + 1) * HEAD) for h in every]
        scores = [[nn(kn_ref[h, at, :], qa_ref[h]) for at in keys] for h in every]
        slopes = [[nn(vn_ref[h, at, :], da_ref[h]) for at in keys] for h in every]
        probs = [[jnp.exp(score) for score in scores[h]] for h in every]
        ds = [[(p * s).astype(BF16) for p, s in zip(probs[h], slopes[h])] for h in every]
        probs = [[p.astype(BF16) for p in probs[h]] for h in every]
        for h in every:
            total = dq_ref[rows[h]]
            for n, at in enumerate(keys):
                dv_ref[rows[h], at] += nt(da_ref[h, :HEAD, :], probs[h][n])
                dk_ref[rows[h], at] += nt(qa_ref[h, :HEAD, :], ds[h][n])
                total = total + nn(kt_ref[rows[h], at], ds[h][n])
            dq_ref[rows[h]] = total
        return carry

    by_pairs(low, high, step, 0)
    dq = (dq_ref[...] * HEAD ** -0.5).astype(BF16)
    if part == 0:
        dq_out[...] = dq
    else:
        grads_ref[:width, pl.ds(pl.multiple_of(at_here * TILE, TILE), TILE)] = dq

        @pl.when(i == pl.num_programs(0) - 1)
        def _():
            grads_ref[width:2 * width] = dk_ref[...].astype(BF16)
            grads_ref[2 * width:] = dv_ref[...].astype(BF16)


def attend_backward(part, me, seg_row, qt, extra, kn, kt, vn, out, grad, earlier, after):
    heads, _, length = qt.shape
    width = heads * HEAD
    count = length // TILE // PARTS
    offset = part * count

    def body(*refs):
        backward_body(part, *refs)

    in_specs = [
        pl.BlockSpec(memory_space=pltpu.SMEM),
        const((1, length)),
        pl.BlockSpec((heads, WIDE, TILE), lambda i, m: (0, 0, i + offset)),
        pl.BlockSpec((heads, 16, TILE), lambda i, m: (0, 0, i)),
        const(kn.shape), const(kt.shape), const(vn.shape),
        pl.BlockSpec((1, width, TILE), lambda i, m: (i, 0, 0)),
        const(grad[0].shape), const(grad[1].shape), const(grad[2].shape), const(grad[3].shape),
    ] + [const(v.shape) for v in earlier] + [pl.BlockSpec(memory_space=pl.ANY)] * len(after)
    scratch = [
        pltpu.VMEM((heads, WIDE, TILE), BF16),
        pltpu.VMEM((heads, WIDE, TILE), BF16),
        pltpu.VMEM((width, TILE), F32),
    ]
    if part == 0:
        out_specs = [pl.BlockSpec((width, TILE), lambda i, m: (0, i)), const((width, length)), const((width, length))]
        out_shape = [shape_of(width, count * TILE), shape_of(width, length, dtype=F32), shape_of(width, length, dtype=F32)]
    else:
        out_specs = const((3 * width, length))
        out_shape = shape_of(3 * width, length)
        scratch += [pltpu.VMEM((width, length), F32), pltpu.VMEM((width, length), F32)]
    return kernel_call(
        body,
        (me, seg_row, seg_row, qt, extra, kn, kt, vn, out, *grad, *earlier, *after),
        free_in=(10, 11, 12) + tuple(range(13 + len(earlier), 13 + len(earlier) + len(after))),
        grid_spec=pltpu.PrefetchScalarGridSpec(
            num_scalar_prefetch=1, grid=(count,), in_specs=in_specs, out_specs=out_specs, scratch_shapes=scratch,
        ),
        out_shape=out_shape,
        cost_estimate=cost(16e9, 10e6, 4e6),
        name="attend_backward",
    )


def middle_body(me_ref, x_ref, m0_ref, m1_ref, m2_ref, m3_ref, w0_ref, w1_ref, w2_ref, w3_ref,
                vec_ref, *rest):
    residual_ref, own_ref, mixed_ref = rest[-3:]
    total = x_ref[...].astype(F32) + vec_ref[2:3, :]
    pairs = ((m0_ref, w0_ref), (m1_ref, w1_ref), (m2_ref, w2_ref), (m3_ref, w3_ref))
    for n, (m_ref, w_ref) in enumerate(pairs):
        total = total + tn(m_ref[...], w_ref[...])
        mixed_ref[n] = m_ref[...]
    residual_ref[...] = total
    normed, _, _ = stats(total)
    own_ref[...] = (normed * vec_ref[3:4, :] + vec_ref[4:5, :]).astype(BF16)


def middle(part, me, tokens, mixed, weights, vectors, after):
    features = tokens.shape[1]
    width = weights[0].shape[0]
    return kernel_call(
        middle_body,
        (me, tokens, *mixed, *weights, vectors, *after),
        free_in=(3, 4, 5),
        free_out=(1,),
        grid_spec=pltpu.PrefetchScalarGridSpec(
            num_scalar_prefetch=1,
            grid=(1,),
            in_specs=[pl.BlockSpec((TILE, features), lambda i, m: (4 * part + m[0], 0))]
            + [const(v.shape) for v in mixed] + [const(v.shape) for v in weights] + [const(vectors.shape)]
            + [pl.BlockSpec(memory_space=pl.ANY)] * len(after),
            out_specs=[const((TILE, features)), const((TILE, features)), const((4, width, TILE))],
        ),
        out_shape=[shape_of(TILE, features, dtype=F32), shape_of(TILE, features), shape_of(4, width, TILE)],
        cost_estimate=cost(2e9, 3e6),
        name="middle",
    )


def feed_body(me_ref, x0_ref, x1_ref, g_ref, inner_ref, vec_ref, outer_ref, *rest):
    left_ref, right_ref, out0_ref, out1_ref, back0_ref, back1_ref, sum_ref = rest[-7:]
    i = pl.program_id(0)

    @pl.when(i == 0)
    def _():
        left_ref[1] = x0_ref[...]

    @pl.when(i == 1)
    def _():
        left_ref[1] = x1_ref[...]

    right_ref[0] = g_ref[...]
    hidden = nn(left_ref[1], inner_ref[...]) + vec_ref[7:8, :]
    half = 0.5 + 0.5 * lax.erf(hidden * 0.5 ** 0.5)
    act = (hidden * half).astype(BF16)
    left_ref[0] = act
    slope = half + hidden * (jnp.exp(-0.5 * hidden * hidden) * 0.3989422804014327)
    dh = (nt(g_ref[...], outer_ref[...]) * slope).astype(BF16)
    right_ref[1] = dh
    sums = fold(dh.astype(F32))
    out = nn(act, outer_ref[...]).astype(BF16)
    back = nt(dh, inner_ref[...]).astype(BF16)

    @pl.when(i == 0)
    def _():
        sum_ref[...] = sums
        out0_ref[...] = out
        back0_ref[...] = back

    @pl.when(i == 1)
    def _():
        sum_ref[...] += sums
        out1_ref[...] = out
        back1_ref[...] = back


def feed(part, base, me, first, second, cot, inner, vectors, outer, kept, outs):
    length, features = cot.shape
    units = inner.shape[1]
    at = 4 * part + base
    rows = pl.BlockSpec((2, TILE, features), lambda i, m: (0, at + i, 0))
    piece = const((TILE, features))
    half = pl.BlockSpec((TILE, features), lambda i, m: (part, 0))
    kept = (*kept, *outs)
    targets = list(range(2)) * (len(kept) >= 2) + [2, 3] * (len(outs) > 0)
    return kernel_call(
        feed_body,
        (me, first, second, cot, inner, vectors, outer, *kept),
        free_in=(1, 2),
        free_out=(5,),
        grid_spec=pltpu.PrefetchScalarGridSpec(
            num_scalar_prefetch=1,
            grid=(2,),
            in_specs=[
                piece, piece,
                pl.BlockSpec((TILE, features), lambda i, m: (4 * part + (m[0] ^ (base + i)), 0)),
                const(inner.shape), const(vectors.shape), const(outer.shape),
            ] + [pl.BlockSpec(memory_space=pl.ANY)] * len(kept),
            out_specs=[rows, rows, half, half, piece, piece, const((8, units))],
        ),
        out_shape=[shape_of(2, length, features)] * 2 + [shape_of(PARTS * TILE, features)] * 2
        + [shape_of(TILE, features)] * 2 + [shape_of(8, units, dtype=F32)],
        input_output_aliases={7 + n: target for n, target in enumerate(targets)},
        cost_estimate=cost(5e9, 8e6, 1e6),
        name="feed",
    )


def back_body(me_ref, b0_ref, b1_ref, b2_ref, residual_ref, g_ref, vec_ref, w0_ref, w1_ref, w2_ref, w3_ref,
              grad_ref, low_ref, a0_ref, a1_ref, a2_ref, a3_ref, sum_ref):
    grad_mid = b0_ref[...].astype(F32) + b1_ref[...].astype(F32) + b2_ref[...].astype(F32)
    normed, scale, _ = stats(residual_ref[...])
    upstream = g_ref[...].astype(F32)
    grad = upstream + norm_back(grad_mid, normed, scale, vec_ref[3:4, :])
    grad_ref[...] = grad
    low = grad.astype(BF16)
    low_ref[...] = low
    for w_ref, a_ref in ((w0_ref, a0_ref), (w1_ref, a1_ref), (w2_ref, a2_ref), (w3_ref, a3_ref)):
        a_ref[...] = nt(w_ref[...], low).astype(BF16)
    for n, value in enumerate((grad_mid * normed, grad_mid, grad, upstream)):
        sum_ref[8 * n:8 * n + 8] = fold(value)


def middle_back(part, me, sums, residual, cot, vectors, weights):
    features = cot.shape[1]
    piece = const((TILE, features))
    width = weights[0].shape[0]
    return kernel_call(
        back_body,
        (me, *sums, residual, cot, vectors, *weights),
        free_in=(2, 3),
        free_out=(3, 4, 5),
        grid_spec=pltpu.PrefetchScalarGridSpec(
            num_scalar_prefetch=1,
            grid=(1,),
            in_specs=[piece] * 4
            + [pl.BlockSpec((TILE, features), lambda i, m: (4 * part + m[0], 0)), const(vectors.shape)]
            + [const(v.shape) for v in weights],
            out_specs=[piece, piece] + [const((width, TILE))] * 4 + [const((32, features))],
        ),
        out_shape=[shape_of(TILE, features, dtype=F32), shape_of(TILE, features)]
        + [shape_of(width, TILE)] * 4 + [shape_of(32, features, dtype=F32)],
        cost_estimate=cost(2e9, 4e6),
        name="middle_back",
    )


def output_body(*refs):
    mixed, lows, outs = refs[:PARTS], refs[PARTS:2 * PARTS], refs[2 * PARTS:]
    for n in range(4):
        total = nn(mixed[0][n], lows[0][...])
        for p in range(1, PARTS):
            total = total + nn(mixed[p][n], lows[p][...])
        outs[n][...] = total.astype(BF16)


def output_grad(mixed, lows):
    width, features = mixed[0].shape[1], lows[0].shape[1]
    return kernel_call(
        output_body,
        (*mixed, *lows),
        free_out=(1, 3),
        out_shape=[shape_of(width, features)] * 4,
        cost_estimate=cost(2e9, 4e6),
        name="output_grad",
    )


def tail_body(me_ref, g_ref, wq_ref, wk_ref, wv_ref, x_ref, stat_ref, *rest):
    early = rest[:PARTS]
    o0_ref, o1_ref, o2_ref, o3_ref, row_ref, vec_ref, sum_ref = rest[-7:]
    i, p = pl.program_id(0), pl.program_id(1)
    grads = g_ref[...]
    width = wq_ref.shape[0]
    value = tn(grads[:width], wq_ref[...]) + tn(grads[width:2 * width], wk_ref[...])
    value = value + tn(grads[2 * width:], wv_ref[...])

    @pl.when((i == 0) & (p == 0))
    def _():
        row_ref[...] = jnp.zeros_like(row_ref)
        sum_ref[...] = jnp.zeros_like(sum_ref)

    row_ref[...] += nt(jnp.ones((8, grads.shape[1]), BF16), grads)
    normed = (x_ref[...].astype(F32) - stat_ref[:, 0:1]) * stat_ref[:, 1:2]
    sum_ref[:8] += fold(value * normed)
    sum_ref[8:] += fold(value)
    value = value.astype(BF16)
    for step, o_ref in enumerate((o3_ref, o2_ref, o1_ref, o0_ref)):
        @pl.when(i == step)
        def _(o_ref=o_ref):
            o_ref[pl.ds(pl.multiple_of(p * TILE, TILE), TILE), :] = value

    @pl.when((i == 3) & (p == PARTS - 1))
    def _():
        row = lax.broadcasted_iota(jnp.int32, vec_ref.shape, 0)
        vectors = jnp.zeros(vec_ref.shape, F32)
        before = early[0][...]
        for ref in early[1:]:
            before = before + ref[...]
        parts = [before[8 * n:8 * n + 8] for n in range(4)] + [sum_ref[:8], sum_ref[8:]]
        for n, part in enumerate(parts):
            vectors = jnp.where(row == n, jnp.sum(part, axis=0, keepdims=True), vectors)
        vec_ref[...] = vectors
        o3_ref[PARTS * TILE:] = paired(vectors)


def tail(me, grads, wq, wk, wv, tokens, stat, early, after):
    deep = grads.shape[0]
    features = wq.shape[1]
    share = const((PARTS * TILE, features))
    more = const((PARTS * TILE + 16, features))
    at = lambda i, p, m: 4 * p + (m[0] ^ (3 - i))
    return kernel_call(
        tail_body,
        (me, grads, wq, wk, wv, tokens, stat, *early, *after),
        free_in=tuple(range(7 + PARTS, 7 + PARTS + len(after))),
        free_out=(1, 3),
        grid_spec=pltpu.PrefetchScalarGridSpec(
            num_scalar_prefetch=1,
            grid=(4, PARTS),
            in_specs=[pl.BlockSpec((deep, TILE), lambda i, p, m: (0, at(i, p, m))),
                      const(wq.shape), const(wk.shape), const(wv.shape),
                      pl.BlockSpec((TILE, features), lambda i, p, m: (at(i, p, m), 0)),
                      pl.BlockSpec((TILE, WIDE), lambda i, p, m: (at(i, p, m), 0))]
            + [const(v.shape) for v in early] + [pl.BlockSpec(memory_space=pl.ANY)] * len(after),
            out_specs=[share, share, share, more, const((8, deep)), const((8, features))],
            scratch_shapes=[pltpu.VMEM((16, features), F32)],
        ),
        out_shape=[shape_of(PARTS * TILE, features)] * 3 + [shape_of(PARTS * TILE + 16, features)]
        + [shape_of(8, deep, dtype=F32), shape_of(8, features, dtype=F32)],
        cost_estimate=cost(4e9, 10e6),
        name="tail",
    )


def chip_body(one_ref, two_ref, vec_ref, out_ref):
    rows = one_ref.shape[0]
    out_ref[:rows] = (one_ref[...].astype(F32) + two_ref[:rows].astype(F32)).astype(BF16)
    out_ref[rows:] = paired(vec_ref[...] + joined(two_ref[rows:]))


def chip_sum(one, two, vectors):
    return kernel_call(
        chip_body,
        (one, two, vectors),
        free_in=(1,),
        free_out=(0,),
        grid=(1,),
        in_specs=[const(one.shape), const(two.shape), const(vectors.shape)],
        out_specs=[const(two.shape)],
        out_shape=[shape_of(*two.shape)],
        name="chip_sum",
    )[0]


def halves_body(xz_ref, g_ref, go_ref, keep_ref, send_ref):
    width = go_ref.shape[0]
    for to_ref, half in ((keep_ref, xz_ref[0]), (send_ref, 1 - xz_ref[0])):
        @pl.when(half == 0)
        def _(to_ref=to_ref):
            to_ref[...] = g_ref[:2 * width]

        @pl.when(half == 1)
        def _(to_ref=to_ref):
            to_ref[:width] = g_ref[2 * width:]
            to_ref[width:] = go_ref[...]


def halves(xz, grad_weights, grad_output):
    width, features = grad_output.shape
    half = const((2 * width, features))
    return kernel_call(
        halves_body,
        (xz, grad_weights, grad_output),
        free_in=(1, 2),
        free_out=(1,),
        grid_spec=pltpu.PrefetchScalarGridSpec(
            num_scalar_prefetch=1,
            grid=(1,),
            in_specs=[const(grad_weights.shape), const(grad_output.shape)],
            out_specs=[half, half],
        ),
        out_shape=[shape_of(2 * width, features)] * 2,
        cost_estimate=cost(1e6, 4e6),
        name="halves",
    )


def quarter_body(count, xz_ref, one_ref, two_ref, *rest):
    for n, out_ref in enumerate(rest[-count:]):
        @pl.when(pl.program_id(0) == n)
        def _(out_ref=out_ref):
            out_ref[...] = (one_ref[...].astype(F32) + two_ref[...].astype(F32)).astype(BF16)


def quarters(xz, one, two, count, after):
    rows, features = one.shape

    def body(*refs):
        quarter_body(count, *refs)

    block = pl.BlockSpec((rows // count, features), lambda i, m: ((m[1] + i) % count, 0))
    return kernel_call(
        body,
        (xz, one, two, *after),
        free_in=(2,) + tuple(range(3, 3 + len(after))),
        grid_spec=pltpu.PrefetchScalarGridSpec(
            num_scalar_prefetch=1,
            grid=(count,),
            in_specs=[block, block] + [pl.BlockSpec(memory_space=pl.ANY)] * len(after),
            out_specs=[const((rows // count, features))] * count,
        ),
        out_shape=[shape_of(rows // count, features)] * count,
        cost_estimate=cost(1e6, 2e6),
        name="quarters",
    )


def paired(value):
    return jnp.concatenate(split(value, 2), axis=0).astype(BF16)


def joined(both):
    both = both.astype(F32)
    half = both.shape[0] // 2
    return both[:half] + both[half:]


def second_body(total_ref, one_ref, two_ref, apart_ref, out_ref):
    rows = total_ref.shape[0]
    out_ref[:rows] = total_ref[...]
    shared = joined(one_ref[...]) + joined(two_ref[...])
    out_ref[rows:] = paired(jnp.concatenate([shared, apart_ref[...]], axis=0))


def second(total, one, two, apart):
    rows, features = total.shape
    last = pl.BlockSpec((16, features), lambda i: (one.shape[0] // 16 - 1, 0))
    return kernel_call(
        second_body,
        (total, one, two, apart),
        free_in=(0, 1, 2),
        free_out=(0,),
        grid=(1,),
        in_specs=[const(total.shape), last, last, const(apart.shape)],
        out_specs=[const((rows + 32, features))],
        out_shape=[shape_of(rows + 32, features)],
        name="second",
    )[0]


def third_body(count, xz_ref, *refs):
    out_ref = refs[-1]
    step = out_ref.shape[0] - (refs[0].shape[0] * count - out_ref.shape[0]) // (count - 1)
    rows = step // count
    sums = None
    for n, ref in enumerate(refs[:count]):
        place_at = lax.rem(xz_ref[1] + count - n, count)
        out_ref[pl.ds(pl.multiple_of(place_at * rows, rows), rows), :] = ref[:rows]
        value = joined(ref[rows:])
        sums = value if sums is None else sums + value
    out_ref[step:] = paired(sums)


def third(xz, pieces, extra):
    count = len(pieces)
    rows, features = pieces[0].shape
    total = (rows - extra) * count + extra

    def body(*refs):
        third_body(count, *refs)

    return kernel_call(
        body,
        (xz, *pieces),
        free_in=tuple(range(1, count + 1)),
        grid_spec=pltpu.PrefetchScalarGridSpec(
            num_scalar_prefetch=1,
            grid=(1,),
            in_specs=[const((rows, features))] * count,
            out_specs=[const((total, features))],
        ),
        out_shape=[shape_of(total, features)],
        name="third",
    )[0]


def ready_body(xz_ref, mine_ref, other_ref, *rest):
    outs = rest[-5:]
    small_ref = outs[4]
    width = outs[0].shape[0]
    for n, out_ref in enumerate(outs[:4]):
        rows = slice(n % 2 * width, (n % 2 + 1) * width)
        for to_ref, chosen in ((mine_ref, xz_ref[0] == n // 2), (other_ref, xz_ref[0] != n // 2)):
            @pl.when(chosen)
            def _(to_ref=to_ref, out_ref=out_ref, rows=rows):
                out_ref[...] = to_ref[rows].astype(F32)

    small_ref[...] = joined(mine_ref[2 * width:]) + joined(other_ref[2 * width:])


def ready(xz, mine, other, width, count, after):
    rows, features = mine.shape
    return kernel_call(
        ready_body,
        (xz, mine, other, *after),
        free_in=(1, 2) + tuple(range(3, 3 + len(after))),
        grid_spec=pltpu.PrefetchScalarGridSpec(
            num_scalar_prefetch=1,
            grid=(1,),
            in_specs=[const(mine.shape), const(other.shape)] + [pl.BlockSpec(memory_space=pl.ANY)] * len(after),
            out_specs=[const((width, features))] * 4 + [const((count, features))],
        ),
        out_shape=[shape_of(width, features, dtype=F32)] * 4 + [shape_of(count, features, dtype=F32)],
        cost_estimate=cost(1e6, 4e6),
        name="ready",
    )


def final_body(me_ref, b0_ref, b1_ref, b2_ref, x_ref, *rest):
    grad_refs, vec_ref, out_ref = rest[:PARTS], rest[PARTS], rest[-1]
    p = pl.program_id(0)
    grad_attend = b0_ref[...].astype(F32) + b1_ref[...].astype(F32) + b2_ref[...].astype(F32)
    normed, scale, _ = stats(x_ref[...].astype(F32))
    back = norm_back(grad_attend, normed, scale, vec_ref[0:1, :])
    for n, grad_ref in enumerate(grad_refs):
        @pl.when(p == n)
        def _(grad_ref=grad_ref):
            out_ref[...] = (grad_ref[...] + back).astype(BF16)


def final(me, sums, tokens, grads, vectors, after):
    features = tokens.shape[1]
    rows = pl.BlockSpec((TILE, features), lambda p, m: (p, 0))
    return kernel_call(
        final_body,
        (me, *sums, tokens, *grads, vectors, *after),
        free_in=(2, 3) + tuple(range(6 + PARTS, 6 + PARTS + len(after))),
        free_out=(0,),
        grid_spec=pltpu.PrefetchScalarGridSpec(
            num_scalar_prefetch=1,
            grid=(PARTS,),
            in_specs=[rows] * 3 + [pl.BlockSpec((TILE, features), lambda p, m: (4 * p + m[0], 0))]
            + [const((TILE, features))] * PARTS + [const(vectors.shape)]
            + [pl.BlockSpec(memory_space=pl.ANY)] * len(after),
            out_specs=[rows],
        ),
        out_shape=[shape_of(PARTS * TILE, features)],
        cost_estimate=cost(1e8, 5e6),
        name="final",
    )[0]


def place_body(me_ref, p0_ref, p1_ref, p2_ref, p3_ref, *rest):
    out_ref = rest[-1]
    for step, p_ref in enumerate((p0_ref, p1_ref, p2_ref, p3_ref)):
        @pl.when(pl.program_id(0) == step)
        def _(p_ref=p_ref):
            at = pl.ds(pl.multiple_of(pl.program_id(1) * TILE, TILE), TILE)
            out_ref[...] = p_ref[at, :].astype(out_ref.dtype)


def place(me, shares, dtype, after):
    rows, features = shares[0].shape
    return kernel_call(
        place_body,
        (me, *shares, *after),
        free_in=tuple(range(1, 5 + len(after))),
        grid_spec=pltpu.PrefetchScalarGridSpec(
            num_scalar_prefetch=1,
            grid=(4, PARTS),
            in_specs=[const((rows, features))] * 4 + [pl.BlockSpec(memory_space=pl.ANY)] * len(after),
            out_specs=pl.BlockSpec((TILE, features), lambda i, p, m: (4 * p + (m[0] ^ i), 0)),
        ),
        out_shape=shape_of(4 * rows, features, dtype=dtype),
        cost_estimate=cost(1e6, 9e6),
        name="place",
    )


def fence_body(*refs):
    pass


def fence(value, *after, space=pltpu.HBM):
    anywhere = pl.BlockSpec(memory_space=pl.ANY)
    return pl.pallas_call(
        fence_body,
        in_specs=[anywhere] * (1 + len(after)),
        out_specs=anywhere,
        out_shape=space(value.shape, value.dtype),
        input_output_aliases={0: 0},
        name="fence",
    )(pltpu.with_memory_space_constraint(value, space), *after)


def other_core(value):
    return lax.ppermute(value, "core", SWAP)


def other_chip(value):
    return lax.ppermute(value, "y", SWAP)


def crosswise(value):
    return lax.ppermute(value, MP, [(n, n ^ 3) for n in range(4)])


def exchange(pieces):
    return [pieces[0], other_core(pieces[1]), other_chip(pieces[2]), crosswise(pieces[3])]


def gather_sum(pieces):
    near = other_core(pieces[1])
    far = (pieces[2].astype(F32) + other_core(pieces[3]).astype(F32)).astype(BF16)
    return [pieces[0], near, other_chip(far)], far


def spread(value):
    far = other_chip(value)
    return [value, other_core(value), far, other_core(far)]


def pick(values, at):
    return lax.dynamic_index_in_dim(values, at, 0, keepdims=False)


def turned(values, way):
    size = lax.axis_size("z")
    return lax.ppermute(values, "z", [(n, (n + way) % size) for n in range(size)])


def sum_first(xz, keep, got, after):
    size = lax.axis_size("z")
    if size > 4:
        return [lax.psum(keep + got, "z")]
    return quarters(xz, keep, got, size, after)


def sum_second(parts):
    total = parts[0].astype(F32)
    for way in range(1, len(parts)):
        total = total + turned(parts[way], way).astype(F32)
    return total.astype(BF16)


def gather_z(value):
    size = lax.axis_size("z")
    if size > 4:
        return [lax.all_gather(value, "z", axis=0, tiled=True)]
    return [turned(value, way) if way else value for way in range(size)]


def local(
    tokens,
    segment_ids,
    gain_one,
    bias_one,
    query_weight,
    query_bias,
    key_weight,
    value_weight,
    value_bias,
    output_weight,
    output_bias,
    gain_two,
    bias_two,
    inner_weight,
    inner_bias,
    outer_weight,
    outer_bias,
    cotangent,
):
    _, length, features = tokens.shape
    width = query_weight.shape[1]
    heads = width // HEAD
    tokens = tokens.reshape(length, features)
    cot = cotangent.reshape(length, features)
    at = lax.axis_index(MP).astype(jnp.int32)
    me = at[None]
    apart = jnp.concatenate([query_bias, value_bias, jnp.zeros((features - 2 * width,), F32)])
    vectors = jnp.concatenate([gain_one, bias_one, output_bias, gain_two, bias_two, outer_bias, apart, inner_bias])
    vectors = vectors.reshape(8, features)
    wq, wk, wv = query_weight.T, key_weight.T, value_weight.T

    output_weights = exchange([output_weight] * 4)
    attend_in, qt, kt, vt, kn, vn, stat = project(tokens, segment_ids, vectors, wq, wk, wv, heads)

    parts = range(PARTS)
    attended, extras, fours = [], [], []
    for p in parts:
        out, extra, *four = attend_forward(p, me, segment_ids, qt, kn, vt)
        attended.append(out)
        extras.append(extra)
        fours.append(exchange(four))
    mixed, residuals, pieces = [], [], []
    for p in parts:
        residual, own, together = middle(p, me, tokens, fours[p], output_weights, vectors, extras[p + 1:])
        mixed.append(together)
        residuals.append(residual)
        pieces.append([own, other_core(own), other_chip(own)])

    outs, backs, sums, kept = [], {}, [], ()
    for base in (0, 2):
        held = ()
        for p in parts:
            if base:
                far = fence(pieces[p][2], backs[p, 0], space=pltpu.VMEM)
                pieces[p] = [None, None, far, other_core(far)]
            result = feed(p, base, me, pieces[p][base], pieces[p][base + 1], cot,
                          inner_weight, vectors, outer_weight, kept, held)
            kept, held = result[:2], result[2:4]
            backs[p, base], backs[p, base + 1] = result[4:6]
            sums.append(result[6])
        outs += held
    left, right = kept

    gathered, far_sums = zip(*[gather_sum([backs[p, n] for n in range(4)]) for p in parts])
    grad_residuals, lows, grads_attended, inner_sums = [], [], [], []
    for p in parts:
        grad, low, a0, a1, a2, a3, vector = middle_back(
            p, me, gathered[p], residuals[p], cot, vectors, output_weights
        )
        grad_residuals.append(grad)
        lows.append(low)
        inner_sums.append(vector)
        grads_attended.append(exchange([a0, a1, a2, a3]))

    grad_feed = lax.dot_general(fence(left, *far_sums), right, (((1,), (1,)), ((0,), (0,))), preferred_element_type=F32)
    grad_feed = grad_feed.astype(BF16).reshape(2 * features, features)
    feed_sum = lax.psum_scatter(grad_feed, DP, scatter_dimension=0, tiled=True)

    near = other_core(fence(outs[1], *far_sums))
    far = (outs[2].astype(F32) + other_core(fence(outs[3], *far_sums)).astype(F32)).astype(BF16)
    far = fence(far, lows[-1], space=pltpu.VMEM)
    part = output_grad(mixed, lows)
    earlier = attend_backward(0, me, segment_ids, qt, extras[0], kn, kt, vn, attended[0], grads_attended[0], (),
                              (far, near, part[0]))
    result = jnp.concatenate(residuals) + outs[0].astype(F32) + near.astype(F32)
    result = (result + other_chip(far).astype(F32) + outer_bias).astype(BF16)
    part_far = fence(part[2], earlier[0])
    part_far = (part_far.astype(F32) + other_core(part[3]).astype(F32)).astype(BF16)
    part_near = other_core(part[1])
    grads = attend_backward(1, me, segment_ids, qt, extras[1], kn, kt, vn, attended[1], grads_attended[1], earlier,
                            (result, part_far, part_near))

    xz = jnp.stack([lax.axis_index("x"), lax.axis_index("z")]).astype(jnp.int32)
    near, far = other_core(result), other_chip(result)
    part_across = other_chip(part_far)
    back_own, back_near, back_far, back_across, row_sum, summed = tail(
        me, grads, wq, wk, wv, tokens, stat, inner_sums, (near, far, part_across)
    )
    grads = fence(grads, row_sum)
    feed_sum = lax.all_gather(fence(feed_sum, row_sum), DP, axis=0, tiled=True)
    feed_sum = (feed_sum[:features].astype(F32), feed_sum[features:].astype(F32))
    grad_output = fence(part[0], row_sum).astype(F32) + part_near.astype(F32) + part_across.astype(F32)
    keep, send = halves(xz, nn(grads, attend_in).astype(BF16), grad_output.astype(BF16))
    back_far = chip_sum(back_far, other_core(back_across), summed)
    back_there = other_chip(back_far)
    got = lax.ppermute(send, "x", SWAP)
    quarter = sum_first(xz, keep, got, (back_far,))
    layer_out = place(me, [result, near, far, other_core(far)], BF16, quarter[-1:])
    row_sum = row_sum[:1]
    apart = jnp.concatenate([
        jnp.sum(sum(sums), axis=0, keepdims=True),
        jnp.pad(row_sum, ((0, 0), (0, features - row_sum.shape[1]))),
        jnp.zeros((6, features), F32),
    ])
    total = sum_second(quarter)
    if len(quarter) > 1:
        held = second(total, back_far, back_there, apart)
        mine = third(xz, gather_z(held), 32)
    else:
        small = jnp.concatenate([joined(back_far[-16:]) + joined(back_there[-16:]), apart])
        held = mine = jnp.concatenate([total, paired(lax.psum(small, "z"))])
    share = final(me, [back_own, other_core(back_near), back_there], tokens, grad_residuals, vectors, (layer_out, held))
    near, far = other_core(share), fence(other_chip(share), mine, space=pltpu.VMEM)
    input_grad = place(me, [share, near, far, other_core(far)], F32, (mine,))
    *wide, small = ready(xz, mine, lax.ppermute(mine, "x", SWAP), width, 16, feed_sum)
    return (
        layer_out.reshape(1, length, features),
        input_grad.reshape(1, length, features),
        small[4],
        small[5],
        wide[0].T,
        small[9, :width],
        wide[1].T,
        wide[2].T,
        small[9, 2 * width:3 * width],
        wide[3],
        small[2],
        small[0],
        small[1],
        feed_sum[1],
        small[8],
        feed_sum[0],
        small[3],
    )


def solution(mesh):
    rows = mesh.shape["dp"]
    inner = Mesh(mesh.devices.reshape(rows // 2, 2, 2, 2), DP + MP)
    placed = (
        P(DP, None, None),
        P(DP, None),
        P(),
        P(),
        P(None, MP),
        P(MP),
        P(None, MP),
        P(None, MP),
        P(MP),
        P(MP, None),
        P(),
        P(),
        P(),
        P(None, MP),
        P(MP),
        P(MP, None),
        P(),
        P(DP, None, None),
    )
    return jax.shard_map(
        local,
        mesh=inner,
        in_specs=placed,
        out_specs=(
            P(DP, None, None),
            P(DP, None, None),
            P(),
            P(),
            P(None, MP),
            P(MP),
            P(None, MP),
            P(None, MP),
            P(MP),
            P(MP, None),
            P(),
            P(),
            P(),
            P(None, MP),
            P(MP),
            P(MP, None),
            P(),
        ),
        check_vma=False,
    )
```

```python
import jax
import jax.numpy as jnp
from jax import lax
from jax.experimental import pallas as pl
from jax.experimental.pallas import tpu as pltpu
from jax.sharding import Mesh
from jax.sharding import PartitionSpec as P

HEAD = 64
WIDE = 128
TILE = 256
PARTS = 2
MASKED = 1e30
SCALE = 1
F32 = jnp.float32
BF16 = jnp.bfloat16
DP = ("z", "x")
MP = ("y", "core")
SWAP = [(0, 1), (1, 0)]


def nn(left, right):
    return lax.dot_general(left, right, (((1,), (0,)), ((), ())), preferred_element_type=F32)


def nt(left, right):
    return lax.dot_general(left, right, (((1,), (1,)), ((), ())), preferred_element_type=F32)


def tn(left, right):
    return lax.dot_general(left, right, (((0,), (0,)), ((), ())), preferred_element_type=F32)


def stats(values):
    mean = jnp.mean(values, axis=-1, keepdims=True)
    center = values - mean
    scale = lax.rsqrt(jnp.mean(center * center, axis=-1, keepdims=True) + 1e-05)
    return center * scale, scale, mean


def norm_back(grad_out, normed, scale, gain):
    upstream = grad_out * gain
    return scale * (
        upstream
        - jnp.mean(upstream, axis=-1, keepdims=True)
        - normed * jnp.mean(upstream * normed, axis=-1, keepdims=True)
    )


def fold(values):
    return jnp.sum(values.reshape(-1, 8, values.shape[-1]), axis=0)


def split(value, parts):
    out = []
    for _ in range(parts):
        piece = value.astype(BF16).astype(F32)
        out.append(piece)
        value = value - piece
    return out


def const(shape):
    return pl.BlockSpec(shape, lambda *_: (0,) * len(shape))


def shape_of(*dims, dtype=BF16):
    return jax.ShapeDtypeStruct(dims, dtype)


def params(mib=40):
    return pltpu.CompilerParams(vmem_limit_bytes=mib << 20)


def kernel_call(body, values, free_in=(), free_out=(), **options):
    shapes = options.pop("out_shape")
    many = isinstance(shapes, (list, tuple))
    shapes = [s if n in free_out else pltpu.HBM(s.shape, s.dtype) for n, s in enumerate(shapes if many else [shapes])]
    values = [
        v if n in free_in or v.dtype == jnp.int32 else pltpu.with_memory_space_constraint(v, pltpu.HBM)
        for n, v in enumerate(values)
    ]
    return pl.pallas_call(
        body, out_shape=shapes if many else shapes[0], compiler_params=params(), **options
    )(*values)


def cost(flops, moved, special=0):
    return pl.CostEstimate(flops=int(flops * SCALE), bytes_accessed=int(moved * SCALE), transcendentals=0)


def project_body(x_ref, seg_ref, vec_ref, wq_ref, wk_ref, wv_ref,
                 ai_ref, qt_ref, kt_ref, vt_ref, kn_ref, vn_ref, stat_ref):
    heads = kn_ref.shape[0]
    width = heads * HEAD
    tile = x_ref.shape[0]
    normed, scale, mean = stats(x_ref[...].astype(F32))
    lane = lax.broadcasted_iota(jnp.int32, stat_ref.shape, 1)
    stat_ref[...] = jnp.where(lane == 0, mean, scale)
    ai = (normed * vec_ref[0:1, :] + vec_ref[1:2, :]).astype(BF16)
    ai_ref[...] = ai
    column = vec_ref[...].T[:2 * width, 6:7]
    queries = ((nt(wq_ref[...], ai) + column[:width]).astype(BF16)).astype(F32) * HEAD ** -0.5
    keys = nt(wk_ref[...], ai)
    kt_ref[...] = keys.astype(BF16)
    values = nt(wv_ref[...], ai) + column[width:]
    row = lax.broadcasted_iota(jnp.int32, (HEAD, tile), 0)
    same = jnp.where(row == seg_ref[...], 1.0, 0.0)
    mask = jnp.where(row < 8, (same - 1.0) * MASKED, jnp.where(row < 11, 1.0, 0.0))
    ones = jnp.where(row < 2, 1.0, 0.0)
    first = jnp.where(row[:16] == 0, 1.0, 0.0).astype(BF16)
    for h in range(heads):
        rows = slice(h * HEAD, (h + 1) * HEAD)
        qt_ref[h, :HEAD, :] = queries[rows].astype(BF16)
        qt_ref[h, HEAD:, :] = same.astype(BF16)
        vt_ref[h, :HEAD, :] = values[rows].astype(BF16)
        vt_ref[h, HEAD:, :] = first
        kn_ref[h] = jnp.concatenate([keys[rows], mask], axis=0).T.astype(BF16)
        vn_ref[h] = jnp.concatenate([values[rows], ones], axis=0).T.astype(BF16)


def project(tokens, seg_row, vectors, wq, wk, wv, heads):
    length, features = tokens.shape
    width = heads * HEAD
    return kernel_call(
        project_body,
        (tokens, seg_row, vectors, wq, wk, wv),
        grid=(length // TILE,),
        in_specs=[
            pl.BlockSpec((TILE, features), lambda i: (i, 0)),
            pl.BlockSpec((1, TILE), lambda i: (0, i)),
            const(vectors.shape), const(wq.shape), const(wk.shape), const(wv.shape),
        ],
        out_specs=[
            pl.BlockSpec((TILE, features), lambda i: (i, 0)),
            pl.BlockSpec((heads, WIDE, TILE), lambda i: (0, 0, i)),
            pl.BlockSpec((width, TILE), lambda i: (0, i)),
            pl.BlockSpec((heads, HEAD + 16, TILE), lambda i: (0, 0, i)),
            pl.BlockSpec((heads, TILE, WIDE), lambda i: (0, i, 0)),
            pl.BlockSpec((heads, TILE, WIDE), lambda i: (0, i, 0)),
            pl.BlockSpec((TILE, WIDE), lambda i: (i, 0)),
        ],
        out_shape=[
            shape_of(length, features),
            shape_of(heads, WIDE, length),
            shape_of(width, length),
            shape_of(heads, HEAD + 16, length),
            shape_of(heads, length, WIDE),
            shape_of(heads, length, WIDE),
            shape_of(length, WIDE, dtype=F32),
        ],
        cost_estimate=cost(6e9, 14e6),
        name="project",
    )


def key_range(seg_ref, seg_all, i):
    first = seg_ref[0, i * TILE]
    last = seg_ref[0, i * TILE + TILE - 1]
    before = jnp.sum(jnp.where(seg_all < first, 1.0, 0.0)).astype(jnp.int32)
    until = jnp.sum(jnp.where(seg_all <= last, 1.0, 0.0)).astype(jnp.int32)
    return before // TILE, (until + TILE - 1) // TILE


def by_pairs(low, high, step, carry):
    keys = lambda kb: pl.ds(pl.multiple_of(kb * TILE, TILE), TILE)
    pairs = (high - low) // 2
    carry = lax.fori_loop(0, pairs, lambda n, c: step([keys(low + 2 * n), keys(low + 2 * n + 1)], c), carry)
    return lax.fori_loop(low + 2 * pairs, high, lambda kb, c: step([keys(kb)], c), carry)


def shifted(one_hot, pieces):
    row = lax.broadcasted_iota(jnp.int32, one_hot.shape, 0)
    value = one_hot
    for n, piece in enumerate(pieces):
        value = jnp.where(row == 8 + n, piece, value)
    return value.astype(BF16)


def forward_body(offset, me_ref, segs_ref, seg_ref, qt_ref, kn_ref, vt_ref,
                 out_ref, extra_ref, o0_ref, o1_ref, o2_ref, o3_ref, acc_ref):
    heads, _, tile = qt_ref.shape
    i = pl.program_id(0)
    low, high = key_range(segs_ref, seg_ref[...], i + offset)
    acc_ref[...] = jnp.zeros_like(acc_ref)

    def step(keys, tops):
        scores = [[nn(kn_ref[h, at, :], qt_ref[h]) for at in keys] for h in range(heads)]
        new_tops = []
        for h in range(heads):
            top = tops[h]
            for score in scores[h]:
                top = jnp.maximum(top, jnp.max(score, axis=0, keepdims=True))
            new_tops.append(top)
        powered = [[jnp.exp(score - new_tops[h]).astype(BF16) for score in scores[h]] for h in range(heads)]
        for h in range(heads):
            total = acc_ref[h] * jnp.exp(tops[h] - new_tops[h])
            for at, power in zip(keys, powered[h]):
                total = total + nn(vt_ref[h, :, at], power)
            acc_ref[h] = total
        return tuple(new_tops)

    tops = by_pairs(low, high, step, (jnp.full((1, tile), -jnp.inf, F32),) * heads)
    for h in range(heads):
        total = acc_ref[h, HEAD:HEAD + 1, :]
        out_ref[0, h * HEAD:(h + 1) * HEAD, :] = (acc_ref[h, :HEAD, :] / total).astype(BF16)
        one_hot = qt_ref[h, HEAD:HEAD + 16, :].astype(F32)
        extra_ref[h] = shifted(one_hot, split(-(tops[h] + jnp.log(total)), 3))
    for n, o_ref in enumerate((o0_ref, o1_ref, o2_ref, o3_ref)):
        @pl.when((i ^ me_ref[0]) == n)
        def _(o_ref=o_ref):
            o_ref[...] = out_ref[0]


def attend_forward(part, me, seg_row, qt, kn, vt):
    heads, _, length = qt.shape
    width = heads * HEAD
    count = length // TILE // PARTS
    offset = part * count

    def body(*refs):
        forward_body(offset, *refs)

    return kernel_call(
        body,
        (me, seg_row, seg_row, qt, kn, vt),
        free_out=(3, 4, 5),
        grid_spec=pltpu.PrefetchScalarGridSpec(
            num_scalar_prefetch=1,
            grid=(count,),
            in_specs=[
                pl.BlockSpec(memory_space=pltpu.SMEM),
                const((1, length)),
                pl.BlockSpec((heads, WIDE, TILE), lambda i, m: (0, 0, i + offset)),
                const(kn.shape), const(vt.shape),
            ],
            out_specs=[
                pl.BlockSpec((1, width, TILE), lambda i, m: (i, 0, 0)),
                pl.BlockSpec((heads, 16, TILE), lambda i, m: (0, 0, i)),
            ] + [const((width, TILE))] * 4,
            scratch_shapes=[pltpu.VMEM((heads, HEAD + 16, TILE), F32)],
        ),
        out_shape=[shape_of(count, width, TILE), shape_of(heads, 16, count * TILE)] + [shape_of(width, TILE)] * 4,
        cost_estimate=cost(9e9, 5e6, 4e6),
        name="attend_forward",
    )


def backward_body(part, me_ref, segs_ref, seg_ref, qt_ref, extra_ref, kn_ref, kt_ref, vn_ref, out_ref,
                  g0_ref, g1_ref, g2_ref, g3_ref, *rest):
    heads, _, tile = qt_ref.shape
    width = heads * HEAD
    length = kt_ref.shape[1]
    if part == 0:
        dq_out, dk_ref, dv_ref, qa_ref, da_ref, dq_ref = rest[-6:]
    else:
        dq_in, dk_in, dv_in = rest[:3]
        grads_ref, qa_ref, da_ref, dq_ref, dk_ref, dv_ref = rest[-6:]
    i = pl.program_id(0)
    count = length // TILE // PARTS
    at_here = i + part * count
    low, high = key_range(segs_ref, seg_ref[...], at_here)

    @pl.when(i == 0)
    def _():
        if part == 0:
            dk_ref[...] = jnp.zeros_like(dk_ref)
            dv_ref[...] = jnp.zeros_like(dv_ref)
        else:
            dk_ref[...] = dk_in[...]
            dv_ref[...] = dv_in[...]
            grads_ref[:width, :count * TILE] = dq_in[...]
        qa_ref[...] = jnp.zeros_like(qa_ref)
        da_ref[...] = jnp.zeros_like(da_ref)

    source = i ^ me_ref[0]
    for n, g_ref in enumerate((g0_ref, g1_ref, g2_ref, g3_ref)):
        @pl.when(source == n)
        def _(g_ref=g_ref):
            for h in range(heads):
                da_ref[h, :HEAD, :] = g_ref[h * HEAD:(h + 1) * HEAD]

    dq_ref[...] = jnp.zeros_like(dq_ref)
    row = lax.broadcasted_iota(jnp.int32, (16, tile), 0)
    for h in range(heads):
        rows = slice(h * HEAD, (h + 1) * HEAD)
        qa_ref[h, :HEAD, :] = qt_ref[h, :HEAD, :]
        qa_ref[h, HEAD:HEAD + 16, :] = extra_ref[h]
        inner = jnp.sum(da_ref[h, :HEAD, :].astype(F32) * out_ref[0, rows].astype(F32), axis=0, keepdims=True)
        first, second = split(-inner, 2)
        value = jnp.where(row == 0, first, jnp.where(row == 1, second, 0.0))
        da_ref[h, HEAD:HEAD + 16, :] = value.astype(BF16)

    def step(keys, carry):
        every = range(heads)
        rows = [slice(h * HEAD, (h + 1) * HEAD) for h in every]
        scores = [[nn(kn_ref[h, at, :], qa_ref[h]) for at in keys] for h in every]
        slopes = [[nn(vn_ref[h, at, :], da_ref[h]) for at in keys] for h in every]
        probs = [[jnp.exp(score) for score in scores[h]] for h in every]
        ds = [[(p * s).astype(BF16) for p, s in zip(probs[h], slopes[h])] for h in every]
        probs = [[p.astype(BF16) for p in probs[h]] for h in every]
        for h in every:
            total = dq_ref[rows[h]]
            for n, at in enumerate(keys):
                dv_ref[rows[h], at] += nt(da_ref[h, :HEAD, :], probs[h][n])
                dk_ref[rows[h], at] += nt(qa_ref[h, :HEAD, :], ds[h][n])
                total = total + nn(kt_ref[rows[h], at], ds[h][n])
            dq_ref[rows[h]] = total
        return carry

    by_pairs(low, high, step, 0)
    dq = (dq_ref[...] * HEAD ** -0.5).astype(BF16)
    if part == 0:
        dq_out[...] = dq
    else:
        grads_ref[:width, pl.ds(pl.multiple_of(at_here * TILE, TILE), TILE)] = dq

        @pl.when(i == pl.num_programs(0) - 1)
        def _():
            grads_ref[width:2 * width] = dk_ref[...].astype(BF16)
            grads_ref[2 * width:] = dv_ref[...].astype(BF16)


def attend_backward(part, me, seg_row, qt, extra, kn, kt, vn, out, grad, earlier, after):
    heads, _, length = qt.shape
    width = heads * HEAD
    count = length // TILE // PARTS
    offset = part * count

    def body(*refs):
        backward_body(part, *refs)

    in_specs = [
        pl.BlockSpec(memory_space=pltpu.SMEM),
        const((1, length)),
        pl.BlockSpec((heads, WIDE, TILE), lambda i, m: (0, 0, i + offset)),
        pl.BlockSpec((heads, 16, TILE), lambda i, m: (0, 0, i)),
        const(kn.shape), const(kt.shape), const(vn.shape),
        pl.BlockSpec((1, width, TILE), lambda i, m: (i, 0, 0)),
        const(grad[0].shape), const(grad[1].shape), const(grad[2].shape), const(grad[3].shape),
    ] + [const(v.shape) for v in earlier] + [pl.BlockSpec(memory_space=pl.ANY)] * len(after)
    scratch = [
        pltpu.VMEM((heads, WIDE, TILE), BF16),
        pltpu.VMEM((heads, WIDE, TILE), BF16),
        pltpu.VMEM((width, TILE), F32),
    ]
    if part == 0:
        out_specs = [pl.BlockSpec((width, TILE), lambda i, m: (0, i)), const((width, length)), const((width, length))]
        out_shape = [shape_of(width, count * TILE), shape_of(width, length, dtype=F32), shape_of(width, length, dtype=F32)]
    else:
        out_specs = const((3 * width, length))
        out_shape = shape_of(3 * width, length)
        scratch += [pltpu.VMEM((width, length), F32), pltpu.VMEM((width, length), F32)]
    return kernel_call(
        body,
        (me, seg_row, seg_row, qt, extra, kn, kt, vn, out, *grad, *earlier, *after),
        free_in=(10, 11, 12) + tuple(range(13 + len(earlier), 13 + len(earlier) + 2)),
        grid_spec=pltpu.PrefetchScalarGridSpec(
            num_scalar_prefetch=1, grid=(count,), in_specs=in_specs, out_specs=out_specs, scratch_shapes=scratch,
        ),
        out_shape=out_shape,
        cost_estimate=cost(16e9, 10e6, 4e6),
        name="attend_backward",
    )


def middle_body(me_ref, x_ref, m0_ref, m1_ref, m2_ref, m3_ref, w0_ref, w1_ref, w2_ref, w3_ref,
                vec_ref, *rest):
    residual_ref, own_ref, mixed_ref = rest[-3:]
    total = x_ref[...].astype(F32) + vec_ref[2:3, :]
    pairs = ((m0_ref, w0_ref), (m1_ref, w1_ref), (m2_ref, w2_ref), (m3_ref, w3_ref))
    for n, (m_ref, w_ref) in enumerate(pairs):
        total = total + tn(m_ref[...], w_ref[...])
        mixed_ref[n] = m_ref[...]
    residual_ref[...] = total
    normed, _, _ = stats(total)
    own_ref[...] = (normed * vec_ref[3:4, :] + vec_ref[4:5, :]).astype(BF16)


def middle(part, me, tokens, mixed, weights, vectors, after):
    features = tokens.shape[1]
    width = weights[0].shape[0]
    return kernel_call(
        middle_body,
        (me, tokens, *mixed, *weights, vectors, *after),
        free_in=(3, 4, 5),
        free_out=(1,),
        grid_spec=pltpu.PrefetchScalarGridSpec(
            num_scalar_prefetch=1,
            grid=(1,),
            in_specs=[pl.BlockSpec((TILE, features), lambda i, m: (4 * part + m[0], 0))]
            + [const(v.shape) for v in mixed] + [const(v.shape) for v in weights] + [const(vectors.shape)]
            + [pl.BlockSpec(memory_space=pl.ANY)] * len(after),
            out_specs=[const((TILE, features)), const((TILE, features)), const((4, width, TILE))],
        ),
        out_shape=[shape_of(TILE, features, dtype=F32), shape_of(TILE, features), shape_of(4, width, TILE)],
        cost_estimate=cost(2e9, 3e6),
        name="middle",
    )


def feed_body(me_ref, x0_ref, x1_ref, g_ref, inner_ref, vec_ref, outer_ref, *rest):
    left_ref, right_ref, out0_ref, out1_ref, back0_ref, back1_ref, sum_ref = rest[-7:]
    i = pl.program_id(0)

    @pl.when(i == 0)
    def _():
        left_ref[1] = x0_ref[...]

    @pl.when(i == 1)
    def _():
        left_ref[1] = x1_ref[...]

    right_ref[0] = g_ref[...]
    hidden = nn(left_ref[1], inner_ref[...]) + vec_ref[7:8, :]
    half = 0.5 + 0.5 * lax.erf(hidden * 0.5 ** 0.5)
    act = (hidden * half).astype(BF16)
    left_ref[0] = act
    slope = half + hidden * (jnp.exp(-0.5 * hidden * hidden) * 0.3989422804014327)
    dh = (nt(g_ref[...], outer_ref[...]) * slope).astype(BF16)
    right_ref[1] = dh
    sums = fold(dh.astype(F32))
    out = nn(act, outer_ref[...]).astype(BF16)
    back = nt(dh, inner_ref[...]).astype(BF16)

    @pl.when(i == 0)
    def _():
        sum_ref[...] = sums
        out0_ref[...] = out
        back0_ref[...] = back

    @pl.when(i == 1)
    def _():
        sum_ref[...] += sums
        out1_ref[...] = out
        back1_ref[...] = back


def feed(part, base, me, first, second, cot, inner, vectors, outer, kept, outs):
    length, features = cot.shape
    units = inner.shape[1]
    at = 4 * part + base
    rows = pl.BlockSpec((2, TILE, features), lambda i, m: (0, at + i, 0))
    piece = const((TILE, features))
    half = pl.BlockSpec((TILE, features), lambda i, m: (part, 0))
    kept = (*kept, *outs)
    targets = list(range(2)) * (len(kept) >= 2) + [2, 3] * (len(outs) > 0)
    return kernel_call(
        feed_body,
        (me, first, second, cot, inner, vectors, outer, *kept),
        free_in=(1, 2),
        free_out=(5,),
        grid_spec=pltpu.PrefetchScalarGridSpec(
            num_scalar_prefetch=1,
            grid=(2,),
            in_specs=[
                piece, piece,
                pl.BlockSpec((TILE, features), lambda i, m: (4 * part + (m[0] ^ (base + i)), 0)),
                const(inner.shape), const(vectors.shape), const(outer.shape),
            ] + [pl.BlockSpec(memory_space=pl.ANY)] * len(kept),
            out_specs=[rows, rows, half, half, piece, piece, const((8, units))],
        ),
        out_shape=[shape_of(2, length, features)] * 2 + [shape_of(PARTS * TILE, features)] * 2
        + [shape_of(TILE, features)] * 2 + [shape_of(8, units, dtype=F32)],
        input_output_aliases={7 + n: target for n, target in enumerate(targets)},
        cost_estimate=cost(5e9, 8e6, 1e6),
        name="feed",
    )


def back_body(me_ref, b0_ref, b1_ref, b2_ref, residual_ref, g_ref, vec_ref, w0_ref, w1_ref, w2_ref, w3_ref,
              grad_ref, low_ref, a0_ref, a1_ref, a2_ref, a3_ref, sum_ref):
    grad_mid = b0_ref[...].astype(F32) + b1_ref[...].astype(F32) + b2_ref[...].astype(F32)
    normed, scale, _ = stats(residual_ref[...])
    upstream = g_ref[...].astype(F32)
    grad = upstream + norm_back(grad_mid, normed, scale, vec_ref[3:4, :])
    grad_ref[...] = grad
    low = grad.astype(BF16)
    low_ref[...] = low
    for w_ref, a_ref in ((w0_ref, a0_ref), (w1_ref, a1_ref), (w2_ref, a2_ref), (w3_ref, a3_ref)):
        a_ref[...] = nt(w_ref[...], low).astype(BF16)
    for n, value in enumerate((grad_mid * normed, grad_mid, grad, upstream)):
        sum_ref[8 * n:8 * n + 8] = fold(value)


def middle_back(part, me, sums, residual, cot, vectors, weights):
    features = cot.shape[1]
    piece = const((TILE, features))
    width = weights[0].shape[0]
    return kernel_call(
        back_body,
        (me, *sums, residual, cot, vectors, *weights),
        free_in=(2, 3),
        free_out=(3, 4, 5),
        grid_spec=pltpu.PrefetchScalarGridSpec(
            num_scalar_prefetch=1,
            grid=(1,),
            in_specs=[piece] * 4
            + [pl.BlockSpec((TILE, features), lambda i, m: (4 * part + m[0], 0)), const(vectors.shape)]
            + [const(v.shape) for v in weights],
            out_specs=[piece, piece] + [const((width, TILE))] * 4 + [const((32, features))],
        ),
        out_shape=[shape_of(TILE, features, dtype=F32), shape_of(TILE, features)]
        + [shape_of(width, TILE)] * 4 + [shape_of(32, features, dtype=F32)],
        cost_estimate=cost(2e9, 4e6),
        name="middle_back",
    )


def output_body(*refs):
    mixed, lows, outs = refs[:PARTS], refs[PARTS:2 * PARTS], refs[2 * PARTS:]
    for n in range(4):
        total = nn(mixed[0][n], lows[0][...])
        for p in range(1, PARTS):
            total = total + nn(mixed[p][n], lows[p][...])
        outs[n][...] = total.astype(BF16)


def output_grad(mixed, lows):
    width, features = mixed[0].shape[1], lows[0].shape[1]
    return kernel_call(
        output_body,
        (*mixed, *lows),
        free_out=(1, 3),
        out_shape=[shape_of(width, features)] * 4,
        cost_estimate=cost(2e9, 4e6),
        name="output_grad",
    )


def tail_body(me_ref, g_ref, wq_ref, wk_ref, wv_ref, x_ref, stat_ref, *rest):
    early, units = rest[:PARTS], rest[PARTS:3 * PARTS]
    o0_ref, o1_ref, o2_ref, o3_ref, apart_ref, vec_ref, sum_ref, row_ref = rest[-8:]
    i, p = pl.program_id(0), pl.program_id(1)
    grads = g_ref[...]
    width = wq_ref.shape[0]
    value = tn(grads[:width], wq_ref[...]) + tn(grads[width:2 * width], wk_ref[...])
    value = value + tn(grads[2 * width:], wv_ref[...])

    @pl.when((i == 0) & (p == 0))
    def _():
        row_ref[...] = jnp.zeros_like(row_ref)
        sum_ref[...] = jnp.zeros_like(sum_ref)

    row_ref[...] += nt(jnp.ones((8, grads.shape[1]), BF16), grads)
    normed = (x_ref[...].astype(F32) - stat_ref[:, 0:1]) * stat_ref[:, 1:2]
    sum_ref[:8] += fold(value * normed)
    sum_ref[8:] += fold(value)
    value = value.astype(BF16)
    for step, o_ref in enumerate((o3_ref, o2_ref, o1_ref, o0_ref)):
        @pl.when(i == step)
        def _(o_ref=o_ref):
            o_ref[pl.ds(pl.multiple_of(p * TILE, TILE), TILE), :] = value

    @pl.when((i == 3) & (p == PARTS - 1))
    def _():
        row = lax.broadcasted_iota(jnp.int32, vec_ref.shape, 0)
        vectors = jnp.zeros(vec_ref.shape, F32)
        before = early[0][...]
        for ref in early[1:]:
            before = before + ref[...]
        parts = [before[8 * n:8 * n + 8] for n in range(4)] + [sum_ref[:8], sum_ref[8:]]
        for n, part in enumerate(parts):
            vectors = jnp.where(row == n, jnp.sum(part, axis=0, keepdims=True), vectors)
        vec_ref[...] = vectors
        inside = units[0][...]
        for ref in units[1:]:
            inside = inside + ref[...]
        apart_ref[0:1] = jnp.sum(inside, axis=0, keepdims=True)
        apart_ref[1:] = jnp.zeros((7, apart_ref.shape[1]), F32)
        apart_ref[1:2, :row_ref.shape[1]] = row_ref[0:1]
        o3_ref[PARTS * TILE:] = paired(vectors)


def tail(me, grads, wq, wk, wv, tokens, stat, early, units, after):
    deep = grads.shape[0]
    features = wq.shape[1]
    share = const((PARTS * TILE, features))
    more = const((PARTS * TILE + 16, features))
    at = lambda i, p, m: 4 * p + (m[0] ^ (3 - i))
    return kernel_call(
        tail_body,
        (me, grads, wq, wk, wv, tokens, stat, *early, *units, *after),
        free_in=tuple(range(7 + 3 * PARTS, 9 + 3 * PARTS)),
        free_out=(1, 3),
        grid_spec=pltpu.PrefetchScalarGridSpec(
            num_scalar_prefetch=1,
            grid=(4, PARTS),
            in_specs=[pl.BlockSpec((deep, TILE), lambda i, p, m: (0, at(i, p, m))),
                      const(wq.shape), const(wk.shape), const(wv.shape),
                      pl.BlockSpec((TILE, features), lambda i, p, m: (at(i, p, m), 0)),
                      pl.BlockSpec((TILE, WIDE), lambda i, p, m: (at(i, p, m), 0))]
            + [const(v.shape) for v in (*early, *units)] + [pl.BlockSpec(memory_space=pl.ANY)] * len(after),
            out_specs=[share, share, share, more, const((8, features)), const((8, features))],
            scratch_shapes=[pltpu.VMEM((16, features), F32), pltpu.VMEM((8, deep), F32)],
        ),
        out_shape=[shape_of(PARTS * TILE, features)] * 3 + [shape_of(PARTS * TILE + 16, features)]
        + [shape_of(8, features, dtype=F32)] * 2,
        cost_estimate=cost(4e9, 10e6),
        name="tail",
    )


def chip_body(one_ref, two_ref, vec_ref, *rest):
    out_ref = rest[-1]
    rows = one_ref.shape[0]
    out_ref[:rows] = (one_ref[...].astype(F32) + two_ref[:rows].astype(F32)).astype(BF16)
    out_ref[rows:] = paired(vec_ref[...] + joined(two_ref[rows:]))


def chip_sum(one, two, vectors, after):
    return kernel_call(
        chip_body,
        (one, two, vectors, *after),
        free_in=(1,) + tuple(range(3, 3 + len(after))),
        free_out=(0,),
        grid=(1,),
        in_specs=[const(one.shape), const(two.shape), const(vectors.shape)]
        + [pl.BlockSpec(memory_space=pl.ANY)] * len(after),
        out_specs=[const(two.shape)],
        out_shape=[shape_of(*two.shape)],
        name="chip_sum",
    )[0]


def halves_body(xz_ref, g_ref, go_ref, keep_ref, send_ref):
    width = go_ref.shape[0]
    for to_ref, half in ((keep_ref, xz_ref[0]), (send_ref, 1 - xz_ref[0])):
        @pl.when(half == 0)
        def _(to_ref=to_ref):
            to_ref[...] = g_ref[:2 * width]

        @pl.when(half == 1)
        def _(to_ref=to_ref):
            to_ref[:width] = g_ref[2 * width:]
            to_ref[width:] = go_ref[...]


def halves(xz, grad_weights, grad_output):
    width, features = grad_output.shape
    half = const((2 * width, features))
    return kernel_call(
        halves_body,
        (xz, grad_weights, grad_output),
        free_in=(1, 2),
        grid_spec=pltpu.PrefetchScalarGridSpec(
            num_scalar_prefetch=1,
            grid=(1,),
            in_specs=[const(grad_weights.shape), const(grad_output.shape)],
            out_specs=[half, half],
        ),
        out_shape=[shape_of(2 * width, features)] * 2,
        cost_estimate=cost(1e6, 4e6),
        name="halves",
    )


def quarter_body(count, xz_ref, one_ref, two_ref, *rest):
    rows = one_ref.shape[0] // count
    for n, out_ref in enumerate(rest[-count:]):
        at = pl.ds(pl.multiple_of(lax.rem(xz_ref[1] + n, count) * rows, rows), rows)
        out_ref[...] = (one_ref[at, :].astype(F32) + two_ref[at, :].astype(F32)).astype(BF16)


def quarters(xz, one, two, count, after):
    rows, features = one.shape

    def body(*refs):
        quarter_body(count, *refs)

    return kernel_call(
        body,
        (xz, one, two, *after),
        free_in=(2,),
        grid_spec=pltpu.PrefetchScalarGridSpec(
            num_scalar_prefetch=1,
            grid=(1,),
            in_specs=[const(one.shape), const(two.shape)] + [pl.BlockSpec(memory_space=pl.ANY)] * len(after),
            out_specs=[const((rows // count, features))] * count,
        ),
        out_shape=[shape_of(rows // count, features)] * count,
        cost_estimate=cost(1e6, 2e6),
        name="quarters",
    )


def paired(value):
    return jnp.concatenate(split(value, 2), axis=0).astype(BF16)


def joined(both):
    both = both.astype(F32)
    half = both.shape[0] // 2
    return both[:half] + both[half:]


def second_body(count, *refs):
    one_ref, two_ref, apart_ref, out_ref = refs[count], refs[count + 1], refs[count + 2], refs[-1]
    rows = refs[0].shape[0]
    total = refs[0][...].astype(F32)
    for ref in refs[1:count]:
        total = total + ref[...].astype(F32)
    out_ref[:rows] = total.astype(BF16)
    shared = joined(one_ref[...]) + joined(two_ref[...])
    out_ref[rows:] = paired(jnp.concatenate([shared, apart_ref[...]], axis=0))


def second(parts, one, two, apart, after):
    count = len(parts)
    rows, features = parts[0].shape
    last = pl.BlockSpec((16, features), lambda i: (one.shape[0] // 16 - 1, 0))

    def body(*refs):
        second_body(count, *refs)

    return kernel_call(
        body,
        (*parts, one, two, apart, *after),
        free_in=tuple(range(1, count + 2)) + tuple(range(count + 3, count + 3 + len(after))),
        grid=(1,),
        in_specs=[const((rows, features))] * count + [last, last, const(apart.shape)]
        + [pl.BlockSpec(memory_space=pl.ANY)] * len(after),
        out_specs=[const((rows + 32, features))],
        out_shape=[shape_of(rows + 32, features)],
        name="second",
    )[0]


def third_body(count, xz_ref, *refs):
    out_ref = refs[-1]
    step = out_ref.shape[0] - (refs[0].shape[0] * count - out_ref.shape[0]) // (count - 1)
    rows = step // count
    sums = None
    for n, ref in enumerate(refs[:count]):
        place_at = lax.rem(xz_ref[1] + count - n, count)
        out_ref[pl.ds(pl.multiple_of(place_at * rows, rows), rows), :] = ref[:rows]
        value = joined(ref[rows:])
        sums = value if sums is None else sums + value
    out_ref[step:] = paired(sums)


def third(xz, pieces, extra, after):
    count = len(pieces)
    rows, features = pieces[0].shape
    total = (rows - extra) * count + extra

    def body(*refs):
        third_body(count, *refs)

    return kernel_call(
        body,
        (xz, *pieces, *after),
        free_in=tuple(range(1, count + 1)),
        grid_spec=pltpu.PrefetchScalarGridSpec(
            num_scalar_prefetch=1,
            grid=(1,),
            in_specs=[const((rows, features))] * count + [pl.BlockSpec(memory_space=pl.ANY)] * len(after),
            out_specs=[const((total, features))],
        ),
        out_shape=[shape_of(total, features)],
        name="third",
    )[0]


def ready_body(xz_ref, mine_ref, other_ref, *rest):
    outs = rest[-16:]
    width = outs[0].shape[0]
    for n, out_ref in enumerate(outs[:4]):
        rows = slice(n % 2 * width, (n % 2 + 1) * width)
        for to_ref, chosen in ((mine_ref, xz_ref[0] == n // 2), (other_ref, xz_ref[0] != n // 2)):
            @pl.when(chosen)
            def _(to_ref=to_ref, out_ref=out_ref, rows=rows):
                out_ref[...] = to_ref[rows].astype(F32)

    small = joined(mine_ref[2 * width:]) + joined(other_ref[2 * width:])
    for n, out_ref in enumerate(outs[4:13]):
        out_ref[...] = small[n]
    for n, out_ref in enumerate(outs[13:]):
        out_ref[...] = small[9, n * width:(n + 1) * width]


def ready(xz, mine, other, width, after):
    rows, features = mine.shape
    sizes = [(features,)] * 9 + [(width,)] * 3
    return kernel_call(
        ready_body,
        (xz, mine, other, *after),
        free_in=(2,),
        grid_spec=pltpu.PrefetchScalarGridSpec(
            num_scalar_prefetch=1,
            grid=(1,),
            in_specs=[const(mine.shape), const(other.shape)] + [pl.BlockSpec(memory_space=pl.ANY)] * len(after),
            out_specs=[const((width, features))] * 4 + [const(size) for size in sizes],
        ),
        out_shape=[shape_of(width, features, dtype=F32)] * 4 + [shape_of(*size, dtype=F32) for size in sizes],
        cost_estimate=cost(1e6, 4e6),
        name="ready",
    )


def final_body(me_ref, b0_ref, b1_ref, b2_ref, x_ref, *rest):
    grad_refs, vec_ref, out_ref = rest[:PARTS], rest[PARTS], rest[-1]
    p = pl.program_id(0)
    grad_attend = b0_ref[...].astype(F32) + b1_ref[...].astype(F32) + b2_ref[...].astype(F32)
    normed, scale, _ = stats(x_ref[...].astype(F32))
    back = norm_back(grad_attend, normed, scale, vec_ref[0:1, :])
    for n, grad_ref in enumerate(grad_refs):
        @pl.when(p == n)
        def _(grad_ref=grad_ref):
            out_ref[...] = (grad_ref[...] + back).astype(BF16)


def final(me, sums, tokens, grads, vectors, after):
    features = tokens.shape[1]
    rows = pl.BlockSpec((TILE, features), lambda p, m: (p, 0))
    return kernel_call(
        final_body,
        (me, *sums, tokens, *grads, vectors, *after),
        free_in=(2, 3) + tuple(range(6 + PARTS, 6 + PARTS + len(after))),
        free_out=(0,),
        grid_spec=pltpu.PrefetchScalarGridSpec(
            num_scalar_prefetch=1,
            grid=(PARTS,),
            in_specs=[rows] * 3 + [pl.BlockSpec((TILE, features), lambda p, m: (4 * p + m[0], 0))]
            + [const((TILE, features))] * PARTS + [const(vectors.shape)]
            + [pl.BlockSpec(memory_space=pl.ANY)] * len(after),
            out_specs=[rows],
        ),
        out_shape=[shape_of(PARTS * TILE, features)],
        cost_estimate=cost(1e8, 5e6),
        name="final",
    )[0]


def place_body(me_ref, p0_ref, p1_ref, p2_ref, p3_ref, *rest):
    out_ref = rest[-1]
    for step, p_ref in enumerate((p0_ref, p1_ref, p2_ref, p3_ref)):
        @pl.when(pl.program_id(0) == step)
        def _(p_ref=p_ref):
            at = pl.ds(pl.multiple_of(pl.program_id(1) * TILE, TILE), TILE)
            out_ref[...] = p_ref[at, :].astype(out_ref.dtype)


def place(me, shares, dtype, after):
    rows, features = shares[0].shape
    return kernel_call(
        place_body,
        (me, *shares, *after),
        free_in=(1, 2, 3, 4),
        grid_spec=pltpu.PrefetchScalarGridSpec(
            num_scalar_prefetch=1,
            grid=(4, PARTS),
            in_specs=[const((rows, features))] * 4 + [pl.BlockSpec(memory_space=pl.ANY)] * len(after),
            out_specs=pl.BlockSpec((TILE, features), lambda i, p, m: (4 * p + (m[0] ^ i), 0)),
        ),
        out_shape=shape_of(4 * rows, features, dtype=dtype),
        cost_estimate=cost(1e6, 9e6),
        name="place",
    )


def fence_body(*refs):
    pass


def fence(value, *after, space=pltpu.HBM):
    anywhere = pl.BlockSpec(memory_space=pl.ANY)
    return pl.pallas_call(
        fence_body,
        in_specs=[anywhere] * (1 + len(after)),
        out_specs=anywhere,
        out_shape=space(value.shape, value.dtype),
        input_output_aliases={0: 0},
        name="fence",
    )(pltpu.with_memory_space_constraint(value, space), *after)


def other_core(value):
    return lax.ppermute(value, "core", SWAP)


def other_chip(value):
    return lax.ppermute(value, "y", SWAP)


def crosswise(value):
    return lax.ppermute(value, MP, [(n, n ^ 3) for n in range(4)])


def exchange(pieces):
    return [pieces[0], other_core(pieces[1]), other_chip(pieces[2]), crosswise(pieces[3])]


def gather_sum(pieces):
    near = other_core(pieces[1])
    far = (pieces[2].astype(F32) + other_core(pieces[3]).astype(F32)).astype(BF16)
    return [pieces[0], near, other_chip(far)], far


def spread(value):
    far = other_chip(value)
    return [value, other_core(value), far, other_core(far)]


def pick(values, at):
    return lax.dynamic_index_in_dim(values, at, 0, keepdims=False)


def turned(values, way):
    size = lax.axis_size("z")
    return lax.ppermute(values, "z", [(n, (n + way) % size) for n in range(size)])


def sum_first(xz, keep, got, after):
    size = lax.axis_size("z")
    if size > 4:
        return [lax.psum(keep + got, "z")]
    return quarters(xz, keep, got, size, after)


def gather_z(value):
    size = lax.axis_size("z")
    if size > 4:
        return [lax.all_gather(value, "z", axis=0, tiled=True)]
    return [turned(value, way) if way else value for way in range(size)]


def local(
    tokens,
    segment_ids,
    gain_one,
    bias_one,
    query_weight,
    query_bias,
    key_weight,
    value_weight,
    value_bias,
    output_weight,
    output_bias,
    gain_two,
    bias_two,
    inner_weight,
    inner_bias,
    outer_weight,
    outer_bias,
    cotangent,
):
    _, length, features = tokens.shape
    width = query_weight.shape[1]
    heads = width // HEAD
    tokens = tokens.reshape(length, features)
    cot = cotangent.reshape(length, features)
    at = lax.axis_index(MP).astype(jnp.int32)
    me = at[None]
    apart = jnp.concatenate([query_bias, value_bias, jnp.zeros((features - 2 * width,), F32)])
    vectors = jnp.concatenate([gain_one, bias_one, output_bias, gain_two, bias_two, outer_bias, apart, inner_bias])
    vectors = vectors.reshape(8, features)
    wq, wk, wv = query_weight.T, key_weight.T, value_weight.T

    output_weights = exchange([output_weight] * 4)
    attend_in, qt, kt, vt, kn, vn, stat = project(tokens, segment_ids, vectors, wq, wk, wv, heads)

    parts = range(PARTS)
    attended, extras, fours = [], [], []
    for p in parts:
        out, extra, *four = attend_forward(p, me, segment_ids, qt, kn, vt)
        attended.append(out)
        extras.append(extra)
        fours.append(exchange(four))
    mixed, residuals, pieces = [], [], []
    for p in parts:
        residual, own, together = middle(p, me, tokens, fours[p], output_weights, vectors, extras[p + 1:])
        mixed.append(together)
        residuals.append(residual)
        pieces.append([own, other_core(own), other_chip(own)])

    outs, backs, sums, kept = [], {}, [], ()
    for base in (0, 2):
        held = ()
        for p in parts:
            if base:
                far = fence(pieces[p][2], backs[p, 0], space=pltpu.VMEM)
                pieces[p] = [None, None, far, other_core(far)]
            result = feed(p, base, me, pieces[p][base], pieces[p][base + 1], cot,
                          inner_weight, vectors, outer_weight, kept, held)
            kept, held = result[:2], result[2:4]
            backs[p, base], backs[p, base + 1] = result[4:6]
            sums.append(result[6])
        outs += held
    left, right = kept

    gathered, far_sums = zip(*[gather_sum([backs[p, n] for n in range(4)]) for p in parts])
    grad_residuals, lows, grads_attended, inner_sums = [], [], [], []
    for p in parts:
        grad, low, a0, a1, a2, a3, vector = middle_back(
            p, me, gathered[p], residuals[p], cot, vectors, output_weights
        )
        grad_residuals.append(grad)
        lows.append(low)
        inner_sums.append(vector)
        grads_attended.append(exchange([a0, a1, a2, a3]))

    grad_feed = lax.dot_general(fence(left, *far_sums), right, (((1,), (1,)), ((0,), (0,))), preferred_element_type=F32)
    grad_feed = grad_feed.astype(BF16).reshape(2 * features, features)
    feed_sum = lax.psum_scatter(grad_feed, DP, scatter_dimension=0, tiled=True)

    near = other_core(fence(outs[1], *far_sums))
    far = (outs[2].astype(F32) + other_core(fence(outs[3], *far_sums)).astype(F32)).astype(BF16)
    far = fence(far, lows[-1], space=pltpu.VMEM)
    part = output_grad(mixed, lows)
    earlier = attend_backward(0, me, segment_ids, qt, extras[0], kn, kt, vn, attended[0], grads_attended[0], (),
                              (far, near, part[0]))
    result = jnp.concatenate(residuals) + outs[0].astype(F32) + near.astype(F32)
    result = (result + other_chip(far).astype(F32) + outer_bias).astype(BF16)
    part_far = fence(part[2], earlier[0])
    part_far = (part_far.astype(F32) + other_core(part[3]).astype(F32)).astype(BF16)
    part_near = other_core(part[1])
    grads = attend_backward(1, me, segment_ids, qt, extras[1], kn, kt, vn, attended[1], grads_attended[1], earlier,
                            (part_near, part_far, result))

    xz = jnp.stack([lax.axis_index("x"), lax.axis_index("z")]).astype(jnp.int32)
    near, far = other_core(result), other_chip(result)
    part_across = other_chip(part_far)
    grad_output = fence(part[0], grads).astype(F32) + part_near.astype(F32) + part_across.astype(F32)
    keep, send = halves(xz, nn(grads, attend_in).astype(BF16), grad_output.astype(BF16))
    near, far = other_core(result), other_chip(result)
    got = lax.ppermute(send, "x", SWAP)
    back_own, back_near, back_far, back_across, apart, summed = tail(
        me, grads, wq, wk, wv, tokens, stat, inner_sums, sums, (near, far, send)
    )
    feed_sum = lax.all_gather(fence(feed_sum, send), DP, axis=0, tiled=True)
    feed_sum = (feed_sum[:features].astype(F32), feed_sum[features:].astype(F32))
    quarter = sum_first(xz, keep, got, (apart,))
    back_across = other_core(fence(back_across, quarter[-1], space=pltpu.VMEM))
    back_far = chip_sum(back_far, back_across, summed, ())
    back_there = other_chip(back_far)
    share = final(me, [back_own, other_core(back_near), back_there], tokens, grad_residuals, vectors, ())
    if len(quarter) > 1:
        turns = [quarter[0]] + [turned(part, n + 1) for n, part in enumerate(quarter[1:])]
        held = second(turns, back_far, back_there, apart, (share,))
        layer_out = place(me, [result, near, far, other_core(far)], BF16, (held,))
        mine = third(xz, gather_z(held), 32, (layer_out,))
    else:
        small = jnp.concatenate([joined(back_far[-16:]) + joined(back_there[-16:]), apart])
        layer_out = place(me, [result, near, far, other_core(far)], BF16, ())
        mine = jnp.concatenate([quarter[0], paired(lax.psum(small, "z"))])
    share = fence(share, held if len(quarter) > 1 else mine, space=pltpu.VMEM)
    near, far = other_core(share), fence(other_chip(share), mine, space=pltpu.VMEM)
    input_grad = place(me, [share, near, far, other_core(far)], F32, (mine,))
    *wide, two_gain, two_bias, output_sum, outer_bias, one_gain, one_bias, _, _, inner_bias, query, _, value = ready(
        xz, mine, lax.ppermute(mine, "x", SWAP), width, feed_sum
    )
    return (
        layer_out.reshape(1, length, features),
        input_grad.reshape(1, length, features),
        one_gain,
        one_bias,
        wide[0].T,
        query,
        wide[1].T,
        wide[2].T,
        value,
        wide[3],
        output_sum,
        two_gain,
        two_bias,
        feed_sum[1],
        inner_bias,
        feed_sum[0],
        outer_bias,
    )


def solution(mesh):
    rows = mesh.shape["dp"]
    inner = Mesh(mesh.devices.reshape(rows // 2, 2, 2, 2), DP + MP)
    placed = (
        P(DP, None, None),
        P(DP, None),
        P(),
        P(),
        P(None, MP),
        P(MP),
        P(None, MP),
        P(None, MP),
        P(MP),
        P(MP, None),
        P(),
        P(),
        P(),
        P(None, MP),
        P(MP),
        P(MP, None),
        P(),
        P(DP, None, None),
    )
    return jax.shard_map(
        local,
        mesh=inner,
        in_specs=placed,
        out_specs=(
            P(DP, None, None),
            P(DP, None, None),
            P(),
            P(),
            P(None, MP),
            P(MP),
            P(None, MP),
            P(None, MP),
            P(MP),
            P(MP, None),
            P(),
            P(),
            P(),
            P(None, MP),
            P(MP),
            P(MP, None),
            P(),
        ),
        check_vma=False,
    )
```

```python
import jax
import jax.numpy as jnp
from jax import lax
from jax.experimental import pallas as pl
from jax.experimental.pallas import tpu as pltpu
from jax.sharding import Mesh
from jax.sharding import PartitionSpec as P

HEAD = 64
WIDE = 128
TILE = 256
PARTS = 2
MASKED = 1e30
SCALE = 1
F32 = jnp.float32
BF16 = jnp.bfloat16
DP = ("z", "x")
MP = ("y", "core")
SWAP = [(0, 1), (1, 0)]


def nn(left, right):
    return lax.dot_general(left, right, (((1,), (0,)), ((), ())), preferred_element_type=F32)


def nt(left, right):
    return lax.dot_general(left, right, (((1,), (1,)), ((), ())), preferred_element_type=F32)


def tn(left, right):
    return lax.dot_general(left, right, (((0,), (0,)), ((), ())), preferred_element_type=F32)


def stats(values):
    mean = jnp.mean(values, axis=-1, keepdims=True)
    center = values - mean
    scale = lax.rsqrt(jnp.mean(center * center, axis=-1, keepdims=True) + 1e-05)
    return center * scale, scale, mean


def norm_back(grad_out, normed, scale, gain):
    upstream = grad_out * gain
    return scale * (
        upstream
        - jnp.mean(upstream, axis=-1, keepdims=True)
        - normed * jnp.mean(upstream * normed, axis=-1, keepdims=True)
    )


def fold(values):
    return jnp.sum(values.reshape(-1, 8, values.shape[-1]), axis=0)


def split(value, parts):
    out = []
    for _ in range(parts):
        piece = value.astype(BF16).astype(F32)
        out.append(piece)
        value = value - piece
    return out


def const(shape):
    return pl.BlockSpec(shape, lambda *_: (0,) * len(shape))


def shape_of(*dims, dtype=BF16):
    return jax.ShapeDtypeStruct(dims, dtype)


def params(mib=40):
    return pltpu.CompilerParams(vmem_limit_bytes=mib << 20)


def kernel_call(body, values, free_in=(), free_out=(), **options):
    shapes = options.pop("out_shape")
    many = isinstance(shapes, (list, tuple))
    shapes = [s if n in free_out else pltpu.HBM(s.shape, s.dtype) for n, s in enumerate(shapes if many else [shapes])]
    values = [
        v if n in free_in or v.dtype == jnp.int32 else pltpu.with_memory_space_constraint(v, pltpu.HBM)
        for n, v in enumerate(values)
    ]
    return pl.pallas_call(
        body, out_shape=shapes if many else shapes[0], compiler_params=params(), **options
    )(*values)


def cost(flops, moved, special=0):
    return pl.CostEstimate(flops=int(flops * SCALE), bytes_accessed=int(moved * SCALE), transcendentals=0)


def project_body(x_ref, seg_ref, vec_ref, wq_ref, wk_ref, wv_ref,
                 ai_ref, qt_ref, kt_ref, vt_ref, kn_ref, vn_ref, stat_ref):
    heads = kn_ref.shape[0]
    width = heads * HEAD
    tile = x_ref.shape[0]
    normed, scale, mean = stats(x_ref[...].astype(F32))
    lane = lax.broadcasted_iota(jnp.int32, stat_ref.shape, 1)
    stat_ref[...] = jnp.where(lane == 0, mean, scale)
    ai = (normed * vec_ref[0:1, :] + vec_ref[1:2, :]).astype(BF16)
    ai_ref[...] = ai
    column = vec_ref[...].T[:2 * width, 6:7]
    queries = ((nt(wq_ref[...], ai) + column[:width]).astype(BF16)).astype(F32) * HEAD ** -0.5
    keys = nt(wk_ref[...], ai)
    kt_ref[...] = keys.astype(BF16)
    values = nt(wv_ref[...], ai) + column[width:]
    row = lax.broadcasted_iota(jnp.int32, (HEAD, tile), 0)
    same = jnp.where(row == seg_ref[...], 1.0, 0.0)
    mask = jnp.where(row < 8, (same - 1.0) * MASKED, jnp.where(row < 11, 1.0, 0.0))
    ones = jnp.where(row < 2, 1.0, 0.0)
    first = jnp.where(row[:16] == 0, 1.0, 0.0).astype(BF16)
    for h in range(heads):
        rows = slice(h * HEAD, (h + 1) * HEAD)
        qt_ref[h, :HEAD, :] = queries[rows].astype(BF16)
        qt_ref[h, HEAD:, :] = same.astype(BF16)
        vt_ref[h, :HEAD, :] = values[rows].astype(BF16)
        vt_ref[h, HEAD:, :] = first
        kn_ref[h] = jnp.concatenate([keys[rows], mask], axis=0).T.astype(BF16)
        vn_ref[h] = jnp.concatenate([values[rows], ones], axis=0).T.astype(BF16)


def project(tokens, seg_row, vectors, wq, wk, wv, heads):
    length, features = tokens.shape
    width = heads * HEAD
    return kernel_call(
        project_body,
        (tokens, seg_row, vectors, wq, wk, wv),
        grid=(length // TILE,),
        in_specs=[
            pl.BlockSpec((TILE, features), lambda i: (i, 0)),
            pl.BlockSpec((1, TILE), lambda i: (0, i)),
            const(vectors.shape), const(wq.shape), const(wk.shape), const(wv.shape),
        ],
        out_specs=[
            pl.BlockSpec((TILE, features), lambda i: (i, 0)),
            pl.BlockSpec((heads, WIDE, TILE), lambda i: (0, 0, i)),
            pl.BlockSpec((width, TILE), lambda i: (0, i)),
            pl.BlockSpec((heads, HEAD + 16, TILE), lambda i: (0, 0, i)),
            pl.BlockSpec((heads, TILE, WIDE), lambda i: (0, i, 0)),
            pl.BlockSpec((heads, TILE, WIDE), lambda i: (0, i, 0)),
            pl.BlockSpec((TILE, WIDE), lambda i: (i, 0)),
        ],
        out_shape=[
            shape_of(length, features),
            shape_of(heads, WIDE, length),
            shape_of(width, length),
            shape_of(heads, HEAD + 16, length),
            shape_of(heads, length, WIDE),
            shape_of(heads, length, WIDE),
            shape_of(length, WIDE, dtype=F32),
        ],
        cost_estimate=cost(6e9, 14e6),
        name="project",
    )


def key_range(seg_ref, seg_all, i):
    first = seg_ref[0, i * TILE]
    last = seg_ref[0, i * TILE + TILE - 1]
    before = jnp.sum(jnp.where(seg_all < first, 1.0, 0.0)).astype(jnp.int32)
    until = jnp.sum(jnp.where(seg_all <= last, 1.0, 0.0)).astype(jnp.int32)
    return before // TILE, (until + TILE - 1) // TILE


def by_pairs(low, high, step, carry):
    keys = lambda kb: pl.ds(pl.multiple_of(kb * TILE, TILE), TILE)
    pairs = (high - low) // 2
    carry = lax.fori_loop(0, pairs, lambda n, c: step([keys(low + 2 * n), keys(low + 2 * n + 1)], c), carry)
    return lax.fori_loop(low + 2 * pairs, high, lambda kb, c: step([keys(kb)], c), carry)


def shifted(one_hot, pieces):
    row = lax.broadcasted_iota(jnp.int32, one_hot.shape, 0)
    value = one_hot
    for n, piece in enumerate(pieces):
        value = jnp.where(row == 8 + n, piece, value)
    return value.astype(BF16)


def forward_body(offset, me_ref, segs_ref, seg_ref, qt_ref, kn_ref, vt_ref,
                 out_ref, extra_ref, o0_ref, o1_ref, o2_ref, o3_ref, acc_ref):
    heads, _, tile = qt_ref.shape
    i = pl.program_id(0)
    low, high = key_range(segs_ref, seg_ref[...], i + offset)
    acc_ref[...] = jnp.zeros_like(acc_ref)

    def step(keys, tops):
        scores = [[nn(kn_ref[h, at, :], qt_ref[h]) for at in keys] for h in range(heads)]
        new_tops = []
        for h in range(heads):
            top = tops[h]
            for score in scores[h]:
                top = jnp.maximum(top, jnp.max(score, axis=0, keepdims=True))
            new_tops.append(top)
        powered = [[jnp.exp(score - new_tops[h]).astype(BF16) for score in scores[h]] for h in range(heads)]
        for h in range(heads):
            total = acc_ref[h] * jnp.exp(tops[h] - new_tops[h])
            for at, power in zip(keys, powered[h]):
                total = total + nn(vt_ref[h, :, at], power)
            acc_ref[h] = total
        return tuple(new_tops)

    tops = by_pairs(low, high, step, (jnp.full((1, tile), -jnp.inf, F32),) * heads)
    for h in range(heads):
        total = acc_ref[h, HEAD:HEAD + 1, :]
        out_ref[0, h * HEAD:(h + 1) * HEAD, :] = (acc_ref[h, :HEAD, :] / total).astype(BF16)
        one_hot = qt_ref[h, HEAD:HEAD + 16, :].astype(F32)
        extra_ref[h] = shifted(one_hot, split(-(tops[h] + jnp.log(total)), 3))
    for n, o_ref in enumerate((o0_ref, o1_ref, o2_ref, o3_ref)):
        @pl.when((i ^ me_ref[0]) == n)
        def _(o_ref=o_ref):
            o_ref[...] = out_ref[0]


def attend_forward(part, me, seg_row, qt, kn, vt):
    heads, _, length = qt.shape
    width = heads * HEAD
    count = length // TILE // PARTS
    offset = part * count

    def body(*refs):
        forward_body(offset, *refs)

    return kernel_call(
        body,
        (me, seg_row, seg_row, qt, kn, vt),
        free_out=(3, 4, 5),
        grid_spec=pltpu.PrefetchScalarGridSpec(
            num_scalar_prefetch=1,
            grid=(count,),
            in_specs=[
                pl.BlockSpec(memory_space=pltpu.SMEM),
                const((1, length)),
                pl.BlockSpec((heads, WIDE, TILE), lambda i, m: (0, 0, i + offset)),
                const(kn.shape), const(vt.shape),
            ],
            out_specs=[
                pl.BlockSpec((1, width, TILE), lambda i, m: (i, 0, 0)),
                pl.BlockSpec((heads, 16, TILE), lambda i, m: (0, 0, i)),
            ] + [const((width, TILE))] * 4,
            scratch_shapes=[pltpu.VMEM((heads, HEAD + 16, TILE), F32)],
        ),
        out_shape=[shape_of(count, width, TILE), shape_of(heads, 16, count * TILE)] + [shape_of(width, TILE)] * 4,
        cost_estimate=cost(9e9, 5e6, 4e6),
        name="attend_forward",
    )


def backward_body(part, me_ref, segs_ref, seg_ref, qt_ref, extra_ref, kn_ref, kt_ref, vn_ref, out_ref,
                  g0_ref, g1_ref, g2_ref, g3_ref, *rest):
    heads, _, tile = qt_ref.shape
    width = heads * HEAD
    length = kt_ref.shape[1]
    if part == 0:
        dq_out, dk_ref, dv_ref, qa_ref, da_ref, dq_ref = rest[-6:]
    else:
        dq_in, dk_in, dv_in = rest[:3]
        grads_ref, qa_ref, da_ref, dq_ref, dk_ref, dv_ref = rest[-6:]
    i = pl.program_id(0)
    count = length // TILE // PARTS
    at_here = i + part * count
    low, high = key_range(segs_ref, seg_ref[...], at_here)

    @pl.when(i == 0)
    def _():
        if part == 0:
            dk_ref[...] = jnp.zeros_like(dk_ref)
            dv_ref[...] = jnp.zeros_like(dv_ref)
        else:
            dk_ref[...] = dk_in[...]
            dv_ref[...] = dv_in[...]
            grads_ref[:width, :count * TILE] = dq_in[...]
        qa_ref[...] = jnp.zeros_like(qa_ref)
        da_ref[...] = jnp.zeros_like(da_ref)

    source = i ^ me_ref[0]
    for n, g_ref in enumerate((g0_ref, g1_ref, g2_ref, g3_ref)):
        @pl.when(source == n)
        def _(g_ref=g_ref):
            for h in range(heads):
                da_ref[h, :HEAD, :] = g_ref[h * HEAD:(h + 1) * HEAD]

    dq_ref[...] = jnp.zeros_like(dq_ref)
    row = lax.broadcasted_iota(jnp.int32, (16, tile), 0)
    for h in range(heads):
        rows = slice(h * HEAD, (h + 1) * HEAD)
        qa_ref[h, :HEAD, :] = qt_ref[h, :HEAD, :]
        qa_ref[h, HEAD:HEAD + 16, :] = extra_ref[h]
        inner = jnp.sum(da_ref[h, :HEAD, :].astype(F32) * out_ref[0, rows].astype(F32), axis=0, keepdims=True)
        first, second = split(-inner, 2)
        value = jnp.where(row == 0, first, jnp.where(row == 1, second, 0.0))
        da_ref[h, HEAD:HEAD + 16, :] = value.astype(BF16)

    def step(keys, carry):
        every = range(heads)
        rows = [slice(h * HEAD, (h + 1) * HEAD) for h in every]
        scores = [[nn(kn_ref[h, at, :], qa_ref[h]) for at in keys] for h in every]
        slopes = [[nn(vn_ref[h, at, :], da_ref[h]) for at in keys] for h in every]
        probs = [[jnp.exp(score) for score in scores[h]] for h in every]
        ds = [[(p * s).astype(BF16) for p, s in zip(probs[h], slopes[h])] for h in every]
        probs = [[p.astype(BF16) for p in probs[h]] for h in every]
        for h in every:
            total = dq_ref[rows[h]]
            for n, at in enumerate(keys):
                dv_ref[rows[h], at] += nt(da_ref[h, :HEAD, :], probs[h][n])
                dk_ref[rows[h], at] += nt(qa_ref[h, :HEAD, :], ds[h][n])
                total = total + nn(kt_ref[rows[h], at], ds[h][n])
            dq_ref[rows[h]] = total
        return carry

    by_pairs(low, high, step, 0)
    dq = (dq_ref[...] * HEAD ** -0.5).astype(BF16)
    if part == 0:
        dq_out[...] = dq
    else:
        grads_ref[:width, pl.ds(pl.multiple_of(at_here * TILE, TILE), TILE)] = dq

        @pl.when(i == pl.num_programs(0) - 1)
        def _():
            grads_ref[width:2 * width] = dk_ref[...].astype(BF16)
            grads_ref[2 * width:] = dv_ref[...].astype(BF16)


def attend_backward(part, me, seg_row, qt, extra, kn, kt, vn, out, grad, earlier, after):
    heads, _, length = qt.shape
    width = heads * HEAD
    count = length // TILE // PARTS
    offset = part * count

    def body(*refs):
        backward_body(part, *refs)

    in_specs = [
        pl.BlockSpec(memory_space=pltpu.SMEM),
        const((1, length)),
        pl.BlockSpec((heads, WIDE, TILE), lambda i, m: (0, 0, i + offset)),
        pl.BlockSpec((heads, 16, TILE), lambda i, m: (0, 0, i)),
        const(kn.shape), const(kt.shape), const(vn.shape),
        pl.BlockSpec((1, width, TILE), lambda i, m: (i, 0, 0)),
        const(grad[0].shape), const(grad[1].shape), const(grad[2].shape), const(grad[3].shape),
    ] + [const(v.shape) for v in earlier] + [pl.BlockSpec(memory_space=pl.ANY)] * len(after)
    scratch = [
        pltpu.VMEM((heads, WIDE, TILE), BF16),
        pltpu.VMEM((heads, WIDE, TILE), BF16),
        pltpu.VMEM((width, TILE), F32),
    ]
    if part == 0:
        out_specs = [pl.BlockSpec((width, TILE), lambda i, m: (0, i)), const((width, length)), const((width, length))]
        out_shape = [shape_of(width, count * TILE), shape_of(width, length, dtype=F32), shape_of(width, length, dtype=F32)]
    else:
        out_specs = const((3 * width, length))
        out_shape = shape_of(3 * width, length)
        scratch += [pltpu.VMEM((width, length), F32), pltpu.VMEM((width, length), F32)]
    return kernel_call(
        body,
        (me, seg_row, seg_row, qt, extra, kn, kt, vn, out, *grad, *earlier, *after),
        free_in=(10, 11, 12) + tuple(range(13 + len(earlier), 13 + len(earlier) + 2)),
        grid_spec=pltpu.PrefetchScalarGridSpec(
            num_scalar_prefetch=1, grid=(count,), in_specs=in_specs, out_specs=out_specs, scratch_shapes=scratch,
        ),
        out_shape=out_shape,
        cost_estimate=cost(16e9, 10e6, 4e6),
        name="attend_backward",
    )


def middle_body(me_ref, x_ref, m0_ref, m1_ref, m2_ref, m3_ref, w0_ref, w1_ref, w2_ref, w3_ref,
                vec_ref, *rest):
    residual_ref, own_ref, mixed_ref = rest[-3:]
    total = x_ref[...].astype(F32) + vec_ref[2:3, :]
    pairs = ((m0_ref, w0_ref), (m1_ref, w1_ref), (m2_ref, w2_ref), (m3_ref, w3_ref))
    for n, (m_ref, w_ref) in enumerate(pairs):
        total = total + tn(m_ref[...], w_ref[...])
        mixed_ref[n] = m_ref[...]
    residual_ref[...] = total
    normed, _, _ = stats(total)
    own_ref[...] = (normed * vec_ref[3:4, :] + vec_ref[4:5, :]).astype(BF16)


def middle(part, me, tokens, mixed, weights, vectors, after):
    features = tokens.shape[1]
    width = weights[0].shape[0]
    return kernel_call(
        middle_body,
        (me, tokens, *mixed, *weights, vectors, *after),
        free_in=(3, 4, 5),
        free_out=(1,),
        grid_spec=pltpu.PrefetchScalarGridSpec(
            num_scalar_prefetch=1,
            grid=(1,),
            in_specs=[pl.BlockSpec((TILE, features), lambda i, m: (4 * part + m[0], 0))]
            + [const(v.shape) for v in mixed] + [const(v.shape) for v in weights] + [const(vectors.shape)]
            + [pl.BlockSpec(memory_space=pl.ANY)] * len(after),
            out_specs=[const((TILE, features)), const((TILE, features)), const((4, width, TILE))],
        ),
        out_shape=[shape_of(TILE, features, dtype=F32), shape_of(TILE, features), shape_of(4, width, TILE)],
        cost_estimate=cost(2e9, 3e6),
        name="middle",
    )


def feed_body(me_ref, *refs):
    count = 2 * PARTS
    x_refs = refs[:count]
    g_ref, inner_ref, vec_ref, outer_ref = refs[count:count + 4]
    before = refs[count + 4:-(count + 8)]
    out_refs, back_refs = refs[-(count + 8):-(count + 6)], refs[-(count + 6):-6]
    sum_ref, grad_ref, x_all, g_all, act_all, dh_all = refs[-6:]
    i = pl.program_id(0)
    at = pl.ds(pl.multiple_of(i * TILE, TILE), TILE)
    for n, x_ref in enumerate(x_refs):
        @pl.when(i == n)
        def _(n=n, x_ref=x_ref):
            x_all[n * TILE:(n + 1) * TILE] = x_ref[...]

    g_all[at] = g_ref[...]
    hidden = nn(x_all[at], inner_ref[...]) + vec_ref[7:8, :]
    half = 0.5 + 0.5 * lax.erf(hidden * 0.5 ** 0.5)
    act = (hidden * half).astype(BF16)
    act_all[at] = act
    slope = half + hidden * (jnp.exp(-0.5 * hidden * hidden) * 0.3989422804014327)
    dh = (nt(g_ref[...], outer_ref[...]) * slope).astype(BF16)
    dh_all[at] = dh
    sums = fold(dh.astype(F32))
    out = nn(act, outer_ref[...]).astype(BF16)
    back = nt(dh, inner_ref[...]).astype(BF16)

    @pl.when(i == 0)
    def _():
        sum_ref[...] = jnp.zeros_like(sum_ref)

    sum_ref[...] += sums
    for n in range(count):
        @pl.when(i == n)
        def _(n=n):
            out_refs[n % 2][n // 2 * TILE:(n // 2 + 1) * TILE] = out
            back_refs[n][...] = back

    @pl.when(i == count - 1)
    def _():
        for n, (left, right) in enumerate(((act_all, g_all), (x_all, dh_all))):
            grad = tn(left[...], right[...])
            for ref in before:
                grad = grad + ref[n].astype(F32)
            grad_ref[n] = grad.astype(BF16)


def feed(base, me, pieces, cot, inner, vectors, outer, before):
    features = cot.shape[1]
    units = inner.shape[1]
    count = 2 * PARTS
    piece = const((TILE, features))
    scratch = lambda n: pltpu.VMEM((count * TILE, n), BF16)
    return kernel_call(
        feed_body,
        (me, *pieces, cot, inner, vectors, outer, *before),
        free_in=tuple(range(1, count + 1)),
        free_out=(3, 5),
        grid_spec=pltpu.PrefetchScalarGridSpec(
            num_scalar_prefetch=1,
            grid=(count,),
            in_specs=[piece] * count
            + [pl.BlockSpec((TILE, features), lambda i, m: (4 * (i // 2) + (m[0] ^ (base + i % 2)), 0)),
               const(inner.shape), const(vectors.shape), const(outer.shape)]
            + [const(v.shape) for v in before],
            out_specs=[const((PARTS * TILE, features))] * 2 + [piece] * count
            + [const((8, units)), const((2, units, features))],
            scratch_shapes=[scratch(features), scratch(features), scratch(units), scratch(units)],
        ),
        out_shape=[shape_of(PARTS * TILE, features)] * 2 + [shape_of(TILE, features)] * count
        + [shape_of(8, units, dtype=F32), shape_of(2, units, features)],
        cost_estimate=cost(15e9, 12e6, 2e6),
        name="feed",
    )


def back_body(me_ref, b0_ref, b1_ref, b2_ref, residual_ref, g_ref, vec_ref, w0_ref, w1_ref, w2_ref, w3_ref,
              grad_ref, low_ref, a0_ref, a1_ref, a2_ref, a3_ref, sum_ref):
    grad_mid = b0_ref[...].astype(F32) + b1_ref[...].astype(F32) + b2_ref[...].astype(F32)
    normed, scale, _ = stats(residual_ref[...])
    upstream = g_ref[...].astype(F32)
    grad = upstream + norm_back(grad_mid, normed, scale, vec_ref[3:4, :])
    grad_ref[...] = grad
    low = grad.astype(BF16)
    low_ref[...] = low
    for w_ref, a_ref in ((w0_ref, a0_ref), (w1_ref, a1_ref), (w2_ref, a2_ref), (w3_ref, a3_ref)):
        a_ref[...] = nt(w_ref[...], low).astype(BF16)
    for n, value in enumerate((grad_mid * normed, grad_mid, grad, upstream)):
        sum_ref[8 * n:8 * n + 8] = fold(value)


def middle_back(part, me, sums, residual, cot, vectors, weights):
    features = cot.shape[1]
    piece = const((TILE, features))
    width = weights[0].shape[0]
    return kernel_call(
        back_body,
        (me, *sums, residual, cot, vectors, *weights),
        free_in=(2, 3),
        free_out=(3, 4, 5),
        grid_spec=pltpu.PrefetchScalarGridSpec(
            num_scalar_prefetch=1,
            grid=(1,),
            in_specs=[piece] * 4
            + [pl.BlockSpec((TILE, features), lambda i, m: (4 * part + m[0], 0)), const(vectors.shape)]
            + [const(v.shape) for v in weights],
            out_specs=[piece, piece] + [const((width, TILE))] * 4 + [const((32, features))],
        ),
        out_shape=[shape_of(TILE, features, dtype=F32), shape_of(TILE, features)]
        + [shape_of(width, TILE)] * 4 + [shape_of(32, features, dtype=F32)],
        cost_estimate=cost(2e9, 4e6),
        name="middle_back",
    )


def output_body(*refs):
    mixed, lows, outs = refs[:PARTS], refs[PARTS:2 * PARTS], refs[2 * PARTS:]
    for n in range(4):
        total = nn(mixed[0][n], lows[0][...])
        for p in range(1, PARTS):
            total = total + nn(mixed[p][n], lows[p][...])
        outs[n][...] = total.astype(BF16)


def output_grad(mixed, lows):
    width, features = mixed[0].shape[1], lows[0].shape[1]
    return kernel_call(
        output_body,
        (*mixed, *lows),
        free_out=(1, 3),
        out_shape=[shape_of(width, features)] * 4,
        cost_estimate=cost(2e9, 4e6),
        name="output_grad",
    )


def tail_body(me_ref, g_ref, wq_ref, wk_ref, wv_ref, x_ref, stat_ref, *rest):
    early, units = rest[:PARTS], rest[PARTS:PARTS + 2]
    o0_ref, o1_ref, o2_ref, o3_ref, apart_ref, vec_ref, sum_ref, row_ref = rest[-8:]
    i, p = pl.program_id(0), pl.program_id(1)
    grads = g_ref[...]
    width = wq_ref.shape[0]
    value = tn(grads[:width], wq_ref[...]) + tn(grads[width:2 * width], wk_ref[...])
    value = value + tn(grads[2 * width:], wv_ref[...])

    @pl.when((i == 0) & (p == 0))
    def _():
        row_ref[...] = jnp.zeros_like(row_ref)
        sum_ref[...] = jnp.zeros_like(sum_ref)

    row_ref[...] += nt(jnp.ones((8, grads.shape[1]), BF16), grads)
    normed = (x_ref[...].astype(F32) - stat_ref[:, 0:1]) * stat_ref[:, 1:2]
    sum_ref[:8] += fold(value * normed)
    sum_ref[8:] += fold(value)
    value = value.astype(BF16)
    for step, o_ref in enumerate((o3_ref, o2_ref, o1_ref, o0_ref)):
        @pl.when(i == step)
        def _(o_ref=o_ref):
            o_ref[pl.ds(pl.multiple_of(p * TILE, TILE), TILE), :] = value

    @pl.when((i == 3) & (p == PARTS - 1))
    def _():
        row = lax.broadcasted_iota(jnp.int32, vec_ref.shape, 0)
        vectors = jnp.zeros(vec_ref.shape, F32)
        before = early[0][...]
        for ref in early[1:]:
            before = before + ref[...]
        parts = [before[8 * n:8 * n + 8] for n in range(4)] + [sum_ref[:8], sum_ref[8:]]
        for n, part in enumerate(parts):
            vectors = jnp.where(row == n, jnp.sum(part, axis=0, keepdims=True), vectors)
        vec_ref[...] = vectors
        inside = units[0][...]
        for ref in units[1:]:
            inside = inside + ref[...]
        apart_ref[0:1] = jnp.sum(inside, axis=0, keepdims=True)
        apart_ref[1:] = jnp.zeros((7, apart_ref.shape[1]), F32)
        apart_ref[1:2, :row_ref.shape[1]] = row_ref[0:1]
        o3_ref[PARTS * TILE:] = paired(vectors)


def tail(me, grads, wq, wk, wv, tokens, stat, early, units, after):
    deep = grads.shape[0]
    features = wq.shape[1]
    share = const((PARTS * TILE, features))
    more = const((PARTS * TILE + 16, features))
    at = lambda i, p, m: 4 * p + (m[0] ^ (3 - i))
    return kernel_call(
        tail_body,
        (me, grads, wq, wk, wv, tokens, stat, *early, *units, *after),
        free_out=(1, 3),
        grid_spec=pltpu.PrefetchScalarGridSpec(
            num_scalar_prefetch=1,
            grid=(4, PARTS),
            in_specs=[pl.BlockSpec((deep, TILE), lambda i, p, m: (0, at(i, p, m))),
                      const(wq.shape), const(wk.shape), const(wv.shape),
                      pl.BlockSpec((TILE, features), lambda i, p, m: (at(i, p, m), 0)),
                      pl.BlockSpec((TILE, WIDE), lambda i, p, m: (at(i, p, m), 0))]
            + [const(v.shape) for v in (*early, *units)] + [pl.BlockSpec(memory_space=pl.ANY)] * len(after),
            out_specs=[share, share, share, more, const((8, features)), const((8, features))],
            scratch_shapes=[pltpu.VMEM((16, features), F32), pltpu.VMEM((8, deep), F32)],
        ),
        out_shape=[shape_of(PARTS * TILE, features)] * 3 + [shape_of(PARTS * TILE + 16, features)]
        + [shape_of(8, features, dtype=F32)] * 2,
        cost_estimate=cost(4e9, 10e6),
        name="tail",
    )


def chip_body(one_ref, two_ref, vec_ref, *rest):
    out_ref = rest[-1]
    rows = one_ref.shape[0]
    out_ref[:rows] = (one_ref[...].astype(F32) + two_ref[:rows].astype(F32)).astype(BF16)
    out_ref[rows:] = paired(vec_ref[...] + joined(two_ref[rows:]))


def chip_sum(one, two, vectors, after):
    return kernel_call(
        chip_body,
        (one, two, vectors, *after),
        free_in=(1,) + tuple(range(3, 3 + len(after))),
        free_out=(0,),
        grid=(1,),
        in_specs=[const(one.shape), const(two.shape), const(vectors.shape)]
        + [pl.BlockSpec(memory_space=pl.ANY)] * len(after),
        out_specs=[const(two.shape)],
        out_shape=[shape_of(*two.shape)],
        name="chip_sum",
    )[0]


def halves_body(xz_ref, g_ref, go_ref, *rest):
    keep_ref, send_ref = rest[-2:]
    width = go_ref.shape[0]
    for to_ref, half in ((keep_ref, xz_ref[0]), (send_ref, 1 - xz_ref[0])):
        @pl.when(half == 0)
        def _(to_ref=to_ref):
            to_ref[...] = g_ref[:2 * width]

        @pl.when(half == 1)
        def _(to_ref=to_ref):
            to_ref[:width] = g_ref[2 * width:]
            to_ref[width:] = go_ref[...]


def halves(xz, grad_weights, grad_output, after):
    width, features = grad_output.shape
    half = const((2 * width, features))
    return kernel_call(
        halves_body,
        (xz, grad_weights, grad_output, *after),
        free_in=(1, 2, 3),
        grid_spec=pltpu.PrefetchScalarGridSpec(
            num_scalar_prefetch=1,
            grid=(1,),
            in_specs=[const(grad_weights.shape), const(grad_output.shape)]
            + [pl.BlockSpec(memory_space=pl.ANY)] * len(after),
            out_specs=[half, half],
        ),
        out_shape=[shape_of(2 * width, features)] * 2,
        cost_estimate=cost(1e6, 4e6),
        name="halves",
    )


def quarter_body(count, xz_ref, one_ref, two_ref, *rest):
    rows = one_ref.shape[0] // count
    for n, out_ref in enumerate(rest[-count:]):
        at = pl.ds(pl.multiple_of(lax.rem(xz_ref[1] + n, count) * rows, rows), rows)
        out_ref[...] = (one_ref[at, :].astype(F32) + two_ref[at, :].astype(F32)).astype(BF16)


def quarters(xz, one, two, count, after):
    rows, features = one.shape

    def body(*refs):
        quarter_body(count, *refs)

    return kernel_call(
        body,
        (xz, one, two, *after),
        free_in=(2, 3, 4),
        grid_spec=pltpu.PrefetchScalarGridSpec(
            num_scalar_prefetch=1,
            grid=(1,),
            in_specs=[const(one.shape), const(two.shape)] + [pl.BlockSpec(memory_space=pl.ANY)] * len(after),
            out_specs=[const((rows // count, features))] * count,
        ),
        out_shape=[shape_of(rows // count, features)] * count,
        cost_estimate=cost(1e6, 2e6),
        name="quarters",
    )


def paired(value):
    return jnp.concatenate(split(value, 2), axis=0).astype(BF16)


def joined(both):
    both = both.astype(F32)
    half = both.shape[0] // 2
    return both[:half] + both[half:]


def second_body(count, *refs):
    one_ref, two_ref, apart_ref, out_ref = refs[count], refs[count + 1], refs[count + 2], refs[-1]
    rows = refs[0].shape[0]
    total = refs[0][...].astype(F32)
    for ref in refs[1:count]:
        total = total + ref[...].astype(F32)
    out_ref[:rows] = total.astype(BF16)
    shared = joined(one_ref[...]) + joined(two_ref[...])
    out_ref[rows:] = paired(jnp.concatenate([shared, apart_ref[...]], axis=0))


def second(parts, one, two, apart, after):
    count = len(parts)
    rows, features = parts[0].shape
    last = pl.BlockSpec((16, features), lambda i: (one.shape[0] // 16 - 1, 0))

    def body(*refs):
        second_body(count, *refs)

    return kernel_call(
        body,
        (*parts, one, two, apart, *after),
        free_in=tuple(range(1, count + 2)) + tuple(range(count + 3, count + 3 + len(after))),
        grid=(1,),
        in_specs=[const((rows, features))] * count + [last, last, const(apart.shape)]
        + [pl.BlockSpec(memory_space=pl.ANY)] * len(after),
        out_specs=[const((rows + 32, features))],
        out_shape=[shape_of(rows + 32, features)],
        name="second",
    )[0]


def third_body(count, xz_ref, *refs):
    out_ref = refs[-1]
    step = out_ref.shape[0] - (refs[0].shape[0] * count - out_ref.shape[0]) // (count - 1)
    rows = step // count
    sums = None
    for n, ref in enumerate(refs[:count]):
        place_at = lax.rem(xz_ref[1] + count - n, count)
        out_ref[pl.ds(pl.multiple_of(place_at * rows, rows), rows), :] = ref[:rows]
        value = joined(ref[rows:])
        sums = value if sums is None else sums + value
    out_ref[step:] = paired(sums)


def third(xz, pieces, extra, after):
    count = len(pieces)
    rows, features = pieces[0].shape
    total = (rows - extra) * count + extra

    def body(*refs):
        third_body(count, *refs)

    return kernel_call(
        body,
        (xz, *pieces, *after),
        free_in=tuple(range(1, count + 1)),
        grid_spec=pltpu.PrefetchScalarGridSpec(
            num_scalar_prefetch=1,
            grid=(1,),
            in_specs=[const((rows, features))] * count + [pl.BlockSpec(memory_space=pl.ANY)] * len(after),
            out_specs=[const((total, features))],
        ),
        out_shape=[shape_of(total, features)],
        name="third",
    )[0]


def ready_body(xz_ref, mine_ref, other_ref, *rest):
    outs = rest[-16:]
    width = outs[0].shape[0]
    for n, out_ref in enumerate(outs[:4]):
        rows = slice(n % 2 * width, (n % 2 + 1) * width)
        for to_ref, chosen in ((mine_ref, xz_ref[0] == n // 2), (other_ref, xz_ref[0] != n // 2)):
            @pl.when(chosen)
            def _(to_ref=to_ref, out_ref=out_ref, rows=rows):
                out_ref[...] = to_ref[rows].astype(F32)

    small = joined(mine_ref[2 * width:]) + joined(other_ref[2 * width:])
    for n, out_ref in enumerate(outs[4:13]):
        out_ref[...] = small[n]
    for n, out_ref in enumerate(outs[13:]):
        out_ref[...] = small[9, n * width:(n + 1) * width]


def ready(xz, mine, other, width, after):
    rows, features = mine.shape
    sizes = [(features,)] * 9 + [(width,)] * 3
    return kernel_call(
        ready_body,
        (xz, mine, other, *after),
        free_in=(2,),
        grid_spec=pltpu.PrefetchScalarGridSpec(
            num_scalar_prefetch=1,
            grid=(1,),
            in_specs=[const(mine.shape), const(other.shape)] + [pl.BlockSpec(memory_space=pl.ANY)] * len(after),
            out_specs=[const((width, features))] * 4 + [const(size) for size in sizes],
        ),
        out_shape=[shape_of(width, features, dtype=F32)] * 4 + [shape_of(*size, dtype=F32) for size in sizes],
        cost_estimate=cost(1e6, 4e6),
        name="ready",
    )


def final_body(me_ref, b0_ref, b1_ref, b2_ref, x_ref, *rest):
    grad_refs, vec_ref, out_ref = rest[:PARTS], rest[PARTS], rest[-1]
    p = pl.program_id(0)
    grad_attend = b0_ref[...].astype(F32) + b1_ref[...].astype(F32) + b2_ref[...].astype(F32)
    normed, scale, _ = stats(x_ref[...].astype(F32))
    back = norm_back(grad_attend, normed, scale, vec_ref[0:1, :])
    for n, grad_ref in enumerate(grad_refs):
        @pl.when(p == n)
        def _(grad_ref=grad_ref):
            out_ref[...] = (grad_ref[...] + back).astype(BF16)


def final(me, sums, tokens, grads, vectors, after):
    features = tokens.shape[1]
    rows = pl.BlockSpec((TILE, features), lambda p, m: (p, 0))
    return kernel_call(
        final_body,
        (me, *sums, tokens, *grads, vectors, *after),
        free_in=(2, 3) + tuple(range(6 + PARTS, 6 + PARTS + len(after))),
        free_out=(0,),
        grid_spec=pltpu.PrefetchScalarGridSpec(
            num_scalar_prefetch=1,
            grid=(PARTS,),
            in_specs=[rows] * 3 + [pl.BlockSpec((TILE, features), lambda p, m: (4 * p + m[0], 0))]
            + [const((TILE, features))] * PARTS + [const(vectors.shape)]
            + [pl.BlockSpec(memory_space=pl.ANY)] * len(after),
            out_specs=[rows],
        ),
        out_shape=[shape_of(PARTS * TILE, features)],
        cost_estimate=cost(1e8, 5e6),
        name="final",
    )[0]


def place_body(me_ref, p0_ref, p1_ref, p2_ref, p3_ref, *rest):
    out_ref = rest[-1]
    for step, p_ref in enumerate((p0_ref, p1_ref, p2_ref, p3_ref)):
        @pl.when(pl.program_id(0) == step)
        def _(p_ref=p_ref):
            at = pl.ds(pl.multiple_of(pl.program_id(1) * TILE, TILE), TILE)
            out_ref[...] = p_ref[at, :].astype(out_ref.dtype)


def place(me, shares, dtype, after):
    rows, features = shares[0].shape
    return kernel_call(
        place_body,
        (me, *shares, *after),
        free_in=(1, 2, 3, 4),
        grid_spec=pltpu.PrefetchScalarGridSpec(
            num_scalar_prefetch=1,
            grid=(4, PARTS),
            in_specs=[const((rows, features))] * 4 + [pl.BlockSpec(memory_space=pl.ANY)] * len(after),
            out_specs=pl.BlockSpec((TILE, features), lambda i, p, m: (4 * p + (m[0] ^ i), 0)),
        ),
        out_shape=shape_of(4 * rows, features, dtype=dtype),
        cost_estimate=cost(1e6, 9e6),
        name="place",
    )


def fence_body(*refs):
    pass


def fence(value, *after, space=pltpu.HBM):
    anywhere = pl.BlockSpec(memory_space=pl.ANY)
    return pl.pallas_call(
        fence_body,
        in_specs=[anywhere] * (1 + len(after)),
        out_specs=anywhere,
        out_shape=space(value.shape, value.dtype),
        input_output_aliases={0: 0},
        name="fence",
    )(pltpu.with_memory_space_constraint(value, space), *after)


def other_core(value):
    return lax.ppermute(value, "core", SWAP)


def other_chip(value):
    return lax.ppermute(value, "y", SWAP)


def crosswise(value):
    return lax.ppermute(value, MP, [(n, n ^ 3) for n in range(4)])


def exchange(pieces):
    return [pieces[0], other_core(pieces[1]), other_chip(pieces[2]), crosswise(pieces[3])]


def gather_sum(pieces):
    near = other_core(pieces[1])
    far = (pieces[2].astype(F32) + other_core(pieces[3]).astype(F32)).astype(BF16)
    return [pieces[0], near, other_chip(far)], far


def spread(value):
    far = other_chip(value)
    return [value, other_core(value), far, other_core(far)]


def pick(values, at):
    return lax.dynamic_index_in_dim(values, at, 0, keepdims=False)


def turned(values, way):
    size = lax.axis_size("z")
    return lax.ppermute(values, "z", [(n, (n + way) % size) for n in range(size)])


def sum_first(xz, keep, got, after):
    size = lax.axis_size("z")
    if size > 4:
        return [lax.psum(keep + got, "z")]
    return quarters(xz, keep, got, size, after)


def gather_z(value):
    size = lax.axis_size("z")
    if size > 4:
        return [lax.all_gather(value, "z", axis=0, tiled=True)]
    return [turned(value, way) if way else value for way in range(size)]


def local(
    tokens,
    segment_ids,
    gain_one,
    bias_one,
    query_weight,
    query_bias,
    key_weight,
    value_weight,
    value_bias,
    output_weight,
    output_bias,
    gain_two,
    bias_two,
    inner_weight,
    inner_bias,
    outer_weight,
    outer_bias,
    cotangent,
):
    _, length, features = tokens.shape
    width = query_weight.shape[1]
    heads = width // HEAD
    tokens = tokens.reshape(length, features)
    cot = cotangent.reshape(length, features)
    at = lax.axis_index(MP).astype(jnp.int32)
    me = at[None]
    apart = jnp.concatenate([query_bias, value_bias, jnp.zeros((features - 2 * width,), F32)])
    vectors = jnp.concatenate([gain_one, bias_one, output_bias, gain_two, bias_two, outer_bias, apart, inner_bias])
    vectors = vectors.reshape(8, features)
    wq, wk, wv = query_weight.T, key_weight.T, value_weight.T

    output_weights = exchange([output_weight] * 4)
    attend_in, qt, kt, vt, kn, vn, stat = project(tokens, segment_ids, vectors, wq, wk, wv, heads)

    parts = range(PARTS)
    attended, extras, fours = [], [], []
    for p in parts:
        out, extra, *four = attend_forward(p, me, segment_ids, qt, kn, vt)
        attended.append(out)
        extras.append(extra)
        fours.append(exchange(four))
    mixed, residuals, pieces = [], [], []
    for p in parts:
        residual, own, together = middle(p, me, tokens, fours[p], output_weights, vectors, extras[p + 1:])
        mixed.append(together)
        residuals.append(residual)
        pieces.append([own, other_core(own), other_chip(own)])

    outs, backs, sums, before = [], {}, [], ()
    for base in (0, 2):
        for p in parts:
            if base:
                far = fence(pieces[p][2], backs[0, 0], space=pltpu.VMEM)
                pieces[p] = [None, None, far, other_core(far)]
        result = feed(base, me, [pieces[p][base + n] for p in parts for n in (0, 1)], cot,
                      inner_weight, vectors, outer_weight, before)
        outs += result[:2]
        for p in parts:
            backs[p, base], backs[p, base + 1] = result[2 + 2 * p:4 + 2 * p]
        sums.append(result[2 + 2 * PARTS])
        before = result[3 + 2 * PARTS:]
    feed_sum = lax.psum_scatter(before[0].reshape(-1, features), DP, scatter_dimension=0, tiled=True)

    gathered, far_sums = zip(*[gather_sum([backs[p, n] for n in range(4)]) for p in parts])
    grad_residuals, lows, grads_attended, inner_sums = [], [], [], []
    for p in parts:
        grad, low, a0, a1, a2, a3, vector = middle_back(
            p, me, gathered[p], residuals[p], cot, vectors, output_weights
        )
        grad_residuals.append(grad)
        lows.append(low)
        inner_sums.append(vector)
        grads_attended.append(exchange([a0, a1, a2, a3]))

    near = other_core(fence(outs[1], *far_sums))
    far = (outs[2].astype(F32) + other_core(fence(outs[3], *far_sums)).astype(F32)).astype(BF16)
    far = fence(far, lows[-1], space=pltpu.VMEM)
    part = output_grad(mixed, lows)
    earlier = attend_backward(0, me, segment_ids, qt, extras[0], kn, kt, vn, attended[0], grads_attended[0], (),
                              (far, near, part[0]))
    part_far = fence(part[2], earlier[0])
    part_far = (part_far.astype(F32) + other_core(part[3]).astype(F32)).astype(BF16)
    part_near = other_core(part[1])
    grads = attend_backward(1, me, segment_ids, qt, extras[1], kn, kt, vn, attended[1], grads_attended[1], earlier,
                            (part_near, part_far))

    xz = jnp.stack([lax.axis_index("x"), lax.axis_index("z")]).astype(jnp.int32)
    part_across = other_chip(part_far)
    grad_output = fence(part[0], grads).astype(F32) + part_near.astype(F32) + part_across.astype(F32)
    there = other_chip(far)
    keep, send = halves(xz, nn(grads, attend_in).astype(BF16), grad_output.astype(BF16), (there,))
    result = jnp.concatenate(residuals) + fence(outs[0], send).astype(F32) + near.astype(F32)
    result = (result + there.astype(F32) + outer_bias).astype(BF16)
    near, far = other_core(result), other_chip(result)
    got = lax.ppermute(send, "x", SWAP)
    back_own, back_near, back_far, back_across, apart, summed = tail(
        me, grads, wq, wk, wv, tokens, stat, inner_sums, sums, (send,)
    )
    feed_sum = lax.all_gather(fence(feed_sum, send), DP, axis=0, tiled=True)
    feed_sum = (feed_sum[:features].astype(F32), feed_sum[features:].astype(F32))
    quarter = sum_first(xz, keep, got, (near, far, apart))
    back_across = other_core(fence(back_across, quarter[-1], space=pltpu.VMEM))
    back_far = chip_sum(back_far, back_across, summed, ())
    back_there = other_chip(back_far)
    share = final(me, [back_own, other_core(back_near), back_there], tokens, grad_residuals, vectors, ())
    if len(quarter) > 1:
        turns = [quarter[0]] + [turned(part, n + 1) for n, part in enumerate(quarter[1:])]
        held = second(turns, back_far, back_there, apart, (share,))
        layer_out = place(me, [result, near, far, other_core(far)], BF16, (held,))
        mine = third(xz, gather_z(held), 32, (layer_out,))
    else:
        small = jnp.concatenate([joined(back_far[-16:]) + joined(back_there[-16:]), apart])
        layer_out = place(me, [result, near, far, other_core(far)], BF16, ())
        mine = jnp.concatenate([quarter[0], paired(lax.psum(small, "z"))])
    share = fence(share, held if len(quarter) > 1 else mine, space=pltpu.VMEM)
    near, far = other_core(share), fence(other_chip(share), mine, space=pltpu.VMEM)
    input_grad = place(me, [share, near, far, other_core(far)], F32, (mine,))
    *wide, two_gain, two_bias, output_sum, outer_bias, one_gain, one_bias, _, _, inner_bias, query, _, value = ready(
        xz, mine, lax.ppermute(mine, "x", SWAP), width, feed_sum
    )
    return (
        layer_out.reshape(1, length, features),
        input_grad.reshape(1, length, features),
        one_gain,
        one_bias,
        wide[0].T,
        query,
        wide[1].T,
        wide[2].T,
        value,
        wide[3],
        output_sum,
        two_gain,
        two_bias,
        feed_sum[1],
        inner_bias,
        feed_sum[0],
        outer_bias,
    )


def solution(mesh):
    rows = mesh.shape["dp"]
    inner = Mesh(mesh.devices.reshape(rows // 2, 2, 2, 2), DP + MP)
    placed = (
        P(DP, None, None),
        P(DP, None),
        P(),
        P(),
        P(None, MP),
        P(MP),
        P(None, MP),
        P(None, MP),
        P(MP),
        P(MP, None),
        P(),
        P(),
        P(),
        P(None, MP),
        P(MP),
        P(MP, None),
        P(),
        P(DP, None, None),
    )
    return jax.shard_map(
        local,
        mesh=inner,
        in_specs=placed,
        out_specs=(
            P(DP, None, None),
            P(DP, None, None),
            P(),
            P(),
            P(None, MP),
            P(MP),
            P(None, MP),
            P(None, MP),
            P(MP),
            P(MP, None),
            P(),
            P(),
            P(),
            P(None, MP),
            P(MP),
            P(MP, None),
            P(),
        ),
        check_vma=False,
    )
```

```python
import jax
import jax.numpy as jnp
from jax import lax
from jax.experimental import pallas as pl
from jax.experimental.pallas import tpu as pltpu
from jax.sharding import Mesh
from jax.sharding import PartitionSpec as P

HEAD = 64
WIDE = 128
TILE = 256
PARTS = 2
MASKED = 1e30
SCALE = 1
F32 = jnp.float32
BF16 = jnp.bfloat16
DP = ("z", "x")
MP = ("y", "core")
SWAP = [(0, 1), (1, 0)]


def nn(left, right):
    return lax.dot_general(left, right, (((1,), (0,)), ((), ())), preferred_element_type=F32)


def nt(left, right):
    return lax.dot_general(left, right, (((1,), (1,)), ((), ())), preferred_element_type=F32)


def tn(left, right):
    return lax.dot_general(left, right, (((0,), (0,)), ((), ())), preferred_element_type=F32)


def stats(values):
    mean = jnp.mean(values, axis=-1, keepdims=True)
    center = values - mean
    scale = lax.rsqrt(jnp.mean(center * center, axis=-1, keepdims=True) + 1e-05)
    return center * scale, scale, mean


def norm_back(grad_out, normed, scale, gain):
    upstream = grad_out * gain
    return scale * (
        upstream
        - jnp.mean(upstream, axis=-1, keepdims=True)
        - normed * jnp.mean(upstream * normed, axis=-1, keepdims=True)
    )


def fold(values):
    return jnp.sum(values.reshape(-1, 8, values.shape[-1]), axis=0)


def split(value, parts):
    out = []
    for _ in range(parts):
        piece = value.astype(BF16).astype(F32)
        out.append(piece)
        value = value - piece
    return out


def const(shape):
    return pl.BlockSpec(shape, lambda *_: (0,) * len(shape))


def shape_of(*dims, dtype=BF16):
    return jax.ShapeDtypeStruct(dims, dtype)


def params(mib=40):
    return pltpu.CompilerParams(vmem_limit_bytes=mib << 20)


def kernel_call(body, values, free_in=(), free_out=(), **options):
    shapes = options.pop("out_shape")
    many = isinstance(shapes, (list, tuple))
    shapes = [s if n in free_out else pltpu.HBM(s.shape, s.dtype) for n, s in enumerate(shapes if many else [shapes])]
    values = [
        v if n in free_in or v.dtype == jnp.int32 else pltpu.with_memory_space_constraint(v, pltpu.HBM)
        for n, v in enumerate(values)
    ]
    return pl.pallas_call(
        body, out_shape=shapes if many else shapes[0], compiler_params=params(), **options
    )(*values)


def cost(flops, moved, special=0):
    return pl.CostEstimate(flops=int(flops * SCALE), bytes_accessed=int(moved * SCALE), transcendentals=0)


def project_body(x_ref, seg_ref, vec_ref, wq_ref, wk_ref, wv_ref,
                 ai_ref, qt_ref, kt_ref, vt_ref, kn_ref, vn_ref, stat_ref):
    heads = kn_ref.shape[0]
    width = heads * HEAD
    tile = x_ref.shape[0]
    normed, scale, mean = stats(x_ref[...].astype(F32))
    lane = lax.broadcasted_iota(jnp.int32, stat_ref.shape, 1)
    stat_ref[...] = jnp.where(lane == 0, mean, scale)
    ai = (normed * vec_ref[0:1, :] + vec_ref[1:2, :]).astype(BF16)
    ai_ref[...] = ai
    column = vec_ref[...].T[:2 * width, 6:7]
    queries = ((nt(wq_ref[...], ai) + column[:width]).astype(BF16)).astype(F32) * HEAD ** -0.5
    keys = nt(wk_ref[...], ai)
    kt_ref[...] = keys.astype(BF16)
    values = nt(wv_ref[...], ai) + column[width:]
    row = lax.broadcasted_iota(jnp.int32, (HEAD, tile), 0)
    same = jnp.where(row == seg_ref[...], 1.0, 0.0)
    mask = jnp.where(row < 8, (same - 1.0) * MASKED, jnp.where(row < 11, 1.0, 0.0))
    ones = jnp.where(row < 2, 1.0, 0.0)
    first = jnp.where(row[:16] == 0, 1.0, 0.0).astype(BF16)
    for h in range(heads):
        rows = slice(h * HEAD, (h + 1) * HEAD)
        qt_ref[h, :HEAD, :] = queries[rows].astype(BF16)
        qt_ref[h, HEAD:, :] = same.astype(BF16)
        vt_ref[h, :HEAD, :] = values[rows].astype(BF16)
        vt_ref[h, HEAD:, :] = first
        kn_ref[h] = jnp.concatenate([keys[rows], mask], axis=0).T.astype(BF16)
        vn_ref[h] = jnp.concatenate([values[rows], ones], axis=0).T.astype(BF16)


def project(tokens, seg_row, vectors, wq, wk, wv, heads):
    length, features = tokens.shape
    width = heads * HEAD
    return kernel_call(
        project_body,
        (tokens, seg_row, vectors, wq, wk, wv),
        grid=(length // TILE,),
        in_specs=[
            pl.BlockSpec((TILE, features), lambda i: (i, 0)),
            pl.BlockSpec((1, TILE), lambda i: (0, i)),
            const(vectors.shape), const(wq.shape), const(wk.shape), const(wv.shape),
        ],
        out_specs=[
            pl.BlockSpec((TILE, features), lambda i: (i, 0)),
            pl.BlockSpec((heads, WIDE, TILE), lambda i: (0, 0, i)),
            pl.BlockSpec((width, TILE), lambda i: (0, i)),
            pl.BlockSpec((heads, HEAD + 16, TILE), lambda i: (0, 0, i)),
            pl.BlockSpec((heads, TILE, WIDE), lambda i: (0, i, 0)),
            pl.BlockSpec((heads, TILE, WIDE), lambda i: (0, i, 0)),
            pl.BlockSpec((TILE, WIDE), lambda i: (i, 0)),
        ],
        out_shape=[
            shape_of(length, features),
            shape_of(heads, WIDE, length),
            shape_of(width, length),
            shape_of(heads, HEAD + 16, length),
            shape_of(heads, length, WIDE),
            shape_of(heads, length, WIDE),
            shape_of(length, WIDE, dtype=F32),
        ],
        cost_estimate=cost(6e9, 14e6),
        name="project",
    )


def key_range(seg_ref, seg_all, i):
    first = seg_ref[0, i * TILE]
    last = seg_ref[0, i * TILE + TILE - 1]
    before = jnp.sum(jnp.where(seg_all < first, 1.0, 0.0)).astype(jnp.int32)
    until = jnp.sum(jnp.where(seg_all <= last, 1.0, 0.0)).astype(jnp.int32)
    return before // TILE, (until + TILE - 1) // TILE


def by_pairs(low, high, step, carry):
    keys = lambda kb: pl.ds(pl.multiple_of(kb * TILE, TILE), TILE)
    pairs = (high - low) // 2
    carry = lax.fori_loop(0, pairs, lambda n, c: step([keys(low + 2 * n), keys(low + 2 * n + 1)], c), carry)
    return lax.fori_loop(low + 2 * pairs, high, lambda kb, c: step([keys(kb)], c), carry)


def shifted(one_hot, pieces):
    row = lax.broadcasted_iota(jnp.int32, one_hot.shape, 0)
    value = one_hot
    for n, piece in enumerate(pieces):
        value = jnp.where(row == 8 + n, piece, value)
    return value.astype(BF16)


def forward_body(offset, me_ref, segs_ref, seg_ref, qt_ref, kn_ref, vt_ref, *rest):
    out_ref, extra_ref, o0_ref, o1_ref, o2_ref, o3_ref, acc_ref = rest[-7:]
    heads, _, tile = qt_ref.shape
    i = pl.program_id(0)
    low, high = key_range(segs_ref, seg_ref[...], i + offset)
    acc_ref[...] = jnp.zeros_like(acc_ref)

    def step(keys, tops):
        scores = [[nn(kn_ref[h, at, :], qt_ref[h]) for at in keys] for h in range(heads)]
        new_tops = []
        for h in range(heads):
            top = tops[h]
            for score in scores[h]:
                top = jnp.maximum(top, jnp.max(score, axis=0, keepdims=True))
            new_tops.append(top)
        powered = [[jnp.exp(score - new_tops[h]).astype(BF16) for score in scores[h]] for h in range(heads)]
        for h in range(heads):
            total = acc_ref[h] * jnp.exp(tops[h] - new_tops[h])
            for at, power in zip(keys, powered[h]):
                total = total + nn(vt_ref[h, :, at], power)
            acc_ref[h] = total
        return tuple(new_tops)

    tops = by_pairs(low, high, step, (jnp.full((1, tile), -jnp.inf, F32),) * heads)
    for h in range(heads):
        total = acc_ref[h, HEAD:HEAD + 1, :]
        out_ref[0, h * HEAD:(h + 1) * HEAD, :] = (acc_ref[h, :HEAD, :] / total).astype(BF16)
        one_hot = qt_ref[h, HEAD:HEAD + 16, :].astype(F32)
        extra_ref[h] = shifted(one_hot, split(-(tops[h] + jnp.log(total)), 3))
    for n, o_ref in enumerate((o0_ref, o1_ref, o2_ref, o3_ref)):
        @pl.when((i ^ me_ref[0]) == n)
        def _(o_ref=o_ref):
            o_ref[...] = out_ref[0]


def attend_forward(part, me, seg_row, qt, kn, vt, after):
    heads, _, length = qt.shape
    width = heads * HEAD
    count = length // TILE // PARTS
    offset = part * count

    def body(*refs):
        forward_body(offset, *refs)

    return kernel_call(
        body,
        (me, seg_row, seg_row, qt, kn, vt, *after),
        free_in=tuple(range(6, 6 + len(after))),
        free_out=(3, 4, 5),
        grid_spec=pltpu.PrefetchScalarGridSpec(
            num_scalar_prefetch=1,
            grid=(count,),
            in_specs=[
                pl.BlockSpec(memory_space=pltpu.SMEM),
                const((1, length)),
                pl.BlockSpec((heads, WIDE, TILE), lambda i, m: (0, 0, i + offset)),
                const(kn.shape), const(vt.shape),
            ] + [pl.BlockSpec(memory_space=pl.ANY)] * len(after),
            out_specs=[
                pl.BlockSpec((1, width, TILE), lambda i, m: (i, 0, 0)),
                pl.BlockSpec((heads, 16, TILE), lambda i, m: (0, 0, i)),
            ] + [const((width, TILE))] * 4,
            scratch_shapes=[pltpu.VMEM((heads, HEAD + 16, TILE), F32)],
        ),
        out_shape=[shape_of(count, width, TILE), shape_of(heads, 16, count * TILE)] + [shape_of(width, TILE)] * 4,
        cost_estimate=cost(9e9, 5e6, 4e6),
        name="attend_forward",
    )


def backward_body(part, me_ref, segs_ref, seg_ref, qt_ref, extra_ref, kn_ref, kt_ref, vn_ref, out_ref,
                  g0_ref, g1_ref, g2_ref, g3_ref, *rest):
    heads, _, tile = qt_ref.shape
    width = heads * HEAD
    length = kt_ref.shape[1]
    if part == 0:
        dq_out, dk_ref, dv_ref, qa_ref, da_ref, dq_ref = rest[-6:]
    else:
        dq_in, dk_in, dv_in = rest[:3]
        grads_ref, qa_ref, da_ref, dq_ref, dk_ref, dv_ref = rest[-6:]
    i = pl.program_id(0)
    count = length // TILE // PARTS
    at_here = i + part * count
    low, high = key_range(segs_ref, seg_ref[...], at_here)

    @pl.when(i == 0)
    def _():
        if part == 0:
            dk_ref[...] = jnp.zeros_like(dk_ref)
            dv_ref[...] = jnp.zeros_like(dv_ref)
        else:
            dk_ref[...] = dk_in[...]
            dv_ref[...] = dv_in[...]
            grads_ref[:width, :count * TILE] = dq_in[...]
        qa_ref[...] = jnp.zeros_like(qa_ref)
        da_ref[...] = jnp.zeros_like(da_ref)

    source = i ^ me_ref[0]
    for n, g_ref in enumerate((g0_ref, g1_ref, g2_ref, g3_ref)):
        @pl.when(source == n)
        def _(g_ref=g_ref):
            for h in range(heads):
                da_ref[h, :HEAD, :] = g_ref[h * HEAD:(h + 1) * HEAD]

    dq_ref[...] = jnp.zeros_like(dq_ref)
    row = lax.broadcasted_iota(jnp.int32, (16, tile), 0)
    for h in range(heads):
        rows = slice(h * HEAD, (h + 1) * HEAD)
        qa_ref[h, :HEAD, :] = qt_ref[h, :HEAD, :]
        qa_ref[h, HEAD:HEAD + 16, :] = extra_ref[h]
        inner = jnp.sum(da_ref[h, :HEAD, :].astype(F32) * out_ref[0, rows].astype(F32), axis=0, keepdims=True)
        first, second = split(-inner, 2)
        value = jnp.where(row == 0, first, jnp.where(row == 1, second, 0.0))
        da_ref[h, HEAD:HEAD + 16, :] = value.astype(BF16)

    def step(keys, carry):
        every = range(heads)
        rows = [slice(h * HEAD, (h + 1) * HEAD) for h in every]
        scores = [[nn(kn_ref[h, at, :], qa_ref[h]) for at in keys] for h in every]
        slopes = [[nn(vn_ref[h, at, :], da_ref[h]) for at in keys] for h in every]
        probs = [[jnp.exp(score) for score in scores[h]] for h in every]
        ds = [[(p * s).astype(BF16) for p, s in zip(probs[h], slopes[h])] for h in every]
        probs = [[p.astype(BF16) for p in probs[h]] for h in every]
        for h in every:
            total = dq_ref[rows[h]]
            for n, at in enumerate(keys):
                dv_ref[rows[h], at] += nt(da_ref[h, :HEAD, :], probs[h][n])
                dk_ref[rows[h], at] += nt(qa_ref[h, :HEAD, :], ds[h][n])
                total = total + nn(kt_ref[rows[h], at], ds[h][n])
            dq_ref[rows[h]] = total
        return carry

    by_pairs(low, high, step, 0)
    dq = (dq_ref[...] * HEAD ** -0.5).astype(BF16)
    if part == 0:
        dq_out[...] = dq
    else:
        grads_ref[:width, pl.ds(pl.multiple_of(at_here * TILE, TILE), TILE)] = dq

        @pl.when(i == pl.num_programs(0) - 1)
        def _():
            grads_ref[width:2 * width] = dk_ref[...].astype(BF16)
            grads_ref[2 * width:] = dv_ref[...].astype(BF16)


def attend_backward(part, me, seg_row, qt, extra, kn, kt, vn, out, grad, earlier, after):
    heads, _, length = qt.shape
    width = heads * HEAD
    count = length // TILE // PARTS
    offset = part * count

    def body(*refs):
        backward_body(part, *refs)

    in_specs = [
        pl.BlockSpec(memory_space=pltpu.SMEM),
        const((1, length)),
        pl.BlockSpec((heads, WIDE, TILE), lambda i, m: (0, 0, i + offset)),
        pl.BlockSpec((heads, 16, TILE), lambda i, m: (0, 0, i)),
        const(kn.shape), const(kt.shape), const(vn.shape),
        pl.BlockSpec((1, width, TILE), lambda i, m: (i, 0, 0)),
        const(grad[0].shape), const(grad[1].shape), const(grad[2].shape), const(grad[3].shape),
    ] + [const(v.shape) for v in earlier] + [pl.BlockSpec(memory_space=pl.ANY)] * len(after)
    scratch = [
        pltpu.VMEM((heads, WIDE, TILE), BF16),
        pltpu.VMEM((heads, WIDE, TILE), BF16),
        pltpu.VMEM((width, TILE), F32),
    ]
    if part == 0:
        out_specs = [pl.BlockSpec((width, TILE), lambda i, m: (0, i)), const((width, length)), const((width, length))]
        out_shape = [shape_of(width, count * TILE), shape_of(width, length, dtype=F32), shape_of(width, length, dtype=F32)]
    else:
        out_specs = const((3 * width, length))
        out_shape = shape_of(3 * width, length)
        scratch += [pltpu.VMEM((width, length), F32), pltpu.VMEM((width, length), F32)]
    return kernel_call(
        body,
        (me, seg_row, seg_row, qt, extra, kn, kt, vn, out, *grad, *earlier, *after),
        free_in=(10, 11, 12) + tuple(range(13 + len(earlier), 15 + len(earlier))),
        grid_spec=pltpu.PrefetchScalarGridSpec(
            num_scalar_prefetch=1, grid=(count,), in_specs=in_specs, out_specs=out_specs, scratch_shapes=scratch,
        ),
        out_shape=out_shape,
        cost_estimate=cost(16e9, 10e6, 4e6),
        name="attend_backward",
    )


def middle_body(me_ref, x_ref, m0_ref, m1_ref, m2_ref, m3_ref, w0_ref, w1_ref, w2_ref, w3_ref,
                vec_ref, *rest):
    residual_ref, own_ref, mixed_ref = rest[-3:]
    total = x_ref[...].astype(F32) + vec_ref[2:3, :]
    pairs = ((m0_ref, w0_ref), (m1_ref, w1_ref), (m2_ref, w2_ref), (m3_ref, w3_ref))
    for n, (m_ref, w_ref) in enumerate(pairs):
        total = total + tn(m_ref[...], w_ref[...])
        mixed_ref[n] = m_ref[...]
    residual_ref[...] = total
    normed, _, _ = stats(total)
    own_ref[...] = (normed * vec_ref[3:4, :] + vec_ref[4:5, :]).astype(BF16)


def middle(part, me, tokens, mixed, weights, vectors, after):
    features = tokens.shape[1]
    width = weights[0].shape[0]
    return kernel_call(
        middle_body,
        (me, tokens, *mixed, *weights, vectors, *after),
        free_in=(3, 4, 5),
        free_out=(1,),
        grid_spec=pltpu.PrefetchScalarGridSpec(
            num_scalar_prefetch=1,
            grid=(1,),
            in_specs=[pl.BlockSpec((TILE, features), lambda i, m: (4 * part + m[0], 0))]
            + [const(v.shape) for v in mixed] + [const(v.shape) for v in weights] + [const(vectors.shape)]
            + [pl.BlockSpec(memory_space=pl.ANY)] * len(after),
            out_specs=[const((TILE, features)), const((TILE, features)), const((4, width, TILE))],
        ),
        out_shape=[shape_of(TILE, features, dtype=F32), shape_of(TILE, features), shape_of(4, width, TILE)],
        cost_estimate=cost(2e9, 3e6),
        name="middle",
    )


def feed_piece(x, g, inner_ref, vec_ref, outer_ref):
    hidden = nn(x, inner_ref[...]) + vec_ref[7:8, :]
    half = 0.5 + 0.5 * lax.erf(hidden * 0.5 ** 0.5)
    act = (hidden * half).astype(BF16)
    slope = half + hidden * (jnp.exp(-0.5 * hidden * hidden) * 0.3989422804014327)
    dh = (nt(g, outer_ref[...]) * slope).astype(BF16)
    out = nn(act, outer_ref[...]).astype(BF16)
    return act, dh, out, nt(dh, inner_ref[...]).astype(BF16)


def near_body(me_ref, *refs):
    count = 2 * PARTS
    x_refs = refs[:count]
    g_ref, inner_ref, vec_ref, outer_ref = refs[count:count + 4]
    out_refs, back_refs = refs[count + 4:count + 6], refs[count + 6:-6]
    sum_ref, grad_ref, x_all, g_all, act_all, dh_all = refs[-6:]
    i = pl.program_id(0)
    at = pl.ds(pl.multiple_of(i * TILE, TILE), TILE)
    for n, x_ref in enumerate(x_refs):
        @pl.when(i == n)
        def _(n=n, x_ref=x_ref):
            x_all[n * TILE:(n + 1) * TILE] = x_ref[...]

    g_all[at] = g_ref[...]
    act, dh, out, back = feed_piece(x_all[at], g_ref[...], inner_ref, vec_ref, outer_ref)
    act_all[at] = act
    dh_all[at] = dh
    sums = fold(dh.astype(F32))

    @pl.when(i == 0)
    def _():
        sum_ref[...] = jnp.zeros_like(sum_ref)

    sum_ref[...] += sums
    for n in range(count):
        @pl.when(i == n)
        def _(n=n):
            out_refs[n % 2][n // 2 * TILE:(n // 2 + 1) * TILE] = out
            back_refs[n][...] = back

    @pl.when(i == count - 1)
    def _():
        grad_ref[0] = tn(act_all[...], g_all[...]).astype(BF16)
        grad_ref[1] = tn(x_all[...], dh_all[...]).astype(BF16)


def feed_near(me, pieces, cot, inner, vectors, outer):
    features = cot.shape[1]
    units = inner.shape[1]
    count = 2 * PARTS
    piece = const((TILE, features))
    scratch = lambda n: pltpu.VMEM((count * TILE, n), BF16)
    return kernel_call(
        near_body,
        (me, *pieces, cot, inner, vectors, outer),
        free_in=tuple(range(1, count + 1)),
        free_out=(3, 5),
        grid_spec=pltpu.PrefetchScalarGridSpec(
            num_scalar_prefetch=1,
            grid=(count,),
            in_specs=[piece] * count
            + [pl.BlockSpec((TILE, features), lambda i, m: (4 * (i // 2) + (m[0] ^ (i % 2)), 0)),
               const(inner.shape), const(vectors.shape), const(outer.shape)],
            out_specs=[const((PARTS * TILE, features))] * 2 + [piece] * count
            + [const((8, units)), const((2, units, features))],
            scratch_shapes=[scratch(features), scratch(features), scratch(units), scratch(units)],
        ),
        out_shape=[shape_of(PARTS * TILE, features)] * 2 + [shape_of(TILE, features)] * count
        + [shape_of(8, units, dtype=F32), shape_of(2, units, features)],
        cost_estimate=cost(15e9, 12e6, 2e6),
        name="feed_near",
    )


def far_body(me_ref, x0_ref, x1_ref, g_ref, inner_ref, vec_ref, outer_ref, *rest):
    left_ref, right_ref, out0_ref, out1_ref, back0_ref, back1_ref, sum_ref = rest[-7:]
    i = pl.program_id(0)
    for n, x_ref in enumerate((x0_ref, x1_ref)):
        @pl.when(i == n)
        def _(x_ref=x_ref):
            left_ref[1] = x_ref[...]

    right_ref[0] = g_ref[...]
    act, dh, out, back = feed_piece(left_ref[1], g_ref[...], inner_ref, vec_ref, outer_ref)
    left_ref[0] = act
    right_ref[1] = dh
    sums = fold(dh.astype(F32))
    for n, (out_ref, back_ref) in enumerate(((out0_ref, back0_ref), (out1_ref, back1_ref))):
        @pl.when(i == n)
        def _(n=n, out_ref=out_ref, back_ref=back_ref):
            sum_ref[...] = sum_ref[...] + sums if n else sums
            out_ref[...] = out
            back_ref[...] = back


def feed_far(part, me, first, second, cot, inner, vectors, outer, kept):
    features = cot.shape[1]
    units = inner.shape[1]
    rows = pl.BlockSpec((2, TILE, features), lambda i, m: (0, 2 * part + i, 0))
    piece = const((TILE, features))
    half = pl.BlockSpec((TILE, features), lambda i, m: (part, 0))
    return kernel_call(
        far_body,
        (me, first, second, cot, inner, vectors, outer, *kept),
        free_in=(1, 2),
        free_out=(5,),
        grid_spec=pltpu.PrefetchScalarGridSpec(
            num_scalar_prefetch=1,
            grid=(2,),
            in_specs=[
                piece, piece,
                pl.BlockSpec((TILE, features), lambda i, m: (4 * part + (m[0] ^ (2 + i)), 0)),
                const(inner.shape), const(vectors.shape), const(outer.shape),
            ] + [pl.BlockSpec(memory_space=pl.ANY)] * len(kept),
            out_specs=[rows, rows, half, half, piece, piece, const((8, units))],
        ),
        out_shape=[shape_of(2, 2 * PARTS * TILE, features)] * 2 + [shape_of(PARTS * TILE, features)] * 2
        + [shape_of(TILE, features)] * 2 + [shape_of(8, units, dtype=F32)],
        input_output_aliases={7 + n: n for n in range(len(kept))},
        cost_estimate=cost(5e9, 8e6, 1e6),
        name="feed_far",
    )


def feed_grad_body(left_ref, right_ref, before_ref, *rest):
    rest[-1][0] = (tn(left_ref[0], right_ref[0]) + before_ref[0].astype(F32)).astype(BF16)


def feed_grad(left, right, before, after):
    _, rows, features = left.shape
    both = pl.BlockSpec((1, rows, features), lambda i: (i, 0, 0))
    square = pl.BlockSpec((1, features, features), lambda i: (i, 0, 0))
    return kernel_call(
        feed_grad_body,
        (left, right, before, *after),
        free_in=tuple(range(3, 3 + len(after))),
        grid=(2,),
        in_specs=[both, both, square] + [pl.BlockSpec(memory_space=pl.ANY)] * len(after),
        out_specs=[square],
        out_shape=[shape_of(*before.shape)],
        cost_estimate=cost(5e9, 10e6),
        name="feed_grad",
    )[0]


def back_body(me_ref, b0_ref, b1_ref, b2_ref, residual_ref, g_ref, vec_ref, w0_ref, w1_ref, w2_ref, w3_ref,
              grad_ref, low_ref, a0_ref, a1_ref, a2_ref, a3_ref, sum_ref):
    grad_mid = b0_ref[...].astype(F32) + b1_ref[...].astype(F32) + b2_ref[...].astype(F32)
    normed, scale, _ = stats(residual_ref[...])
    upstream = g_ref[...].astype(F32)
    grad = upstream + norm_back(grad_mid, normed, scale, vec_ref[3:4, :])
    grad_ref[...] = grad
    low = grad.astype(BF16)
    low_ref[...] = low
    for w_ref, a_ref in ((w0_ref, a0_ref), (w1_ref, a1_ref), (w2_ref, a2_ref), (w3_ref, a3_ref)):
        a_ref[...] = nt(w_ref[...], low).astype(BF16)
    for n, value in enumerate((grad_mid * normed, grad_mid, grad, upstream)):
        sum_ref[8 * n:8 * n + 8] = fold(value)


def middle_back(part, me, sums, residual, cot, vectors, weights):
    features = cot.shape[1]
    piece = const((TILE, features))
    width = weights[0].shape[0]
    return kernel_call(
        back_body,
        (me, *sums, residual, cot, vectors, *weights),
        free_in=(2, 3),
        free_out=(3, 4, 5),
        grid_spec=pltpu.PrefetchScalarGridSpec(
            num_scalar_prefetch=1,
            grid=(1,),
            in_specs=[piece] * 4
            + [pl.BlockSpec((TILE, features), lambda i, m: (4 * part + m[0], 0)), const(vectors.shape)]
            + [const(v.shape) for v in weights],
            out_specs=[piece, piece] + [const((width, TILE))] * 4 + [const((32, features))],
        ),
        out_shape=[shape_of(TILE, features, dtype=F32), shape_of(TILE, features)]
        + [shape_of(width, TILE)] * 4 + [shape_of(32, features, dtype=F32)],
        cost_estimate=cost(2e9, 4e6),
        name="middle_back",
    )


def output_body(*refs):
    mixed, lows, outs = refs[:PARTS], refs[PARTS:2 * PARTS], refs[2 * PARTS:]
    for n in range(4):
        total = nn(mixed[0][n], lows[0][...])
        for p in range(1, PARTS):
            total = total + nn(mixed[p][n], lows[p][...])
        outs[n][...] = total.astype(BF16)


def output_grad(mixed, lows):
    width, features = mixed[0].shape[1], lows[0].shape[1]
    return kernel_call(
        output_body,
        (*mixed, *lows),
        free_out=(1, 3),
        out_shape=[shape_of(width, features)] * 4,
        cost_estimate=cost(2e9, 4e6),
        name="output_grad",
    )


def tail_body(me_ref, g_ref, wq_ref, wk_ref, wv_ref, x_ref, stat_ref, *rest):
    early, units = rest[:PARTS], rest[PARTS:2 * PARTS + 1]
    o0_ref, o1_ref, o2_ref, o3_ref, apart_ref, vec_ref, sum_ref, row_ref = rest[-8:]
    i, p = pl.program_id(0), pl.program_id(1)
    grads = g_ref[...]
    width = wq_ref.shape[0]
    value = tn(grads[:width], wq_ref[...]) + tn(grads[width:2 * width], wk_ref[...])
    value = value + tn(grads[2 * width:], wv_ref[...])

    @pl.when((i == 0) & (p == 0))
    def _():
        row_ref[...] = jnp.zeros_like(row_ref)
        sum_ref[...] = jnp.zeros_like(sum_ref)

    row_ref[...] += nt(jnp.ones((8, grads.shape[1]), BF16), grads)
    normed = (x_ref[...].astype(F32) - stat_ref[:, 0:1]) * stat_ref[:, 1:2]
    sum_ref[:8] += fold(value * normed)
    sum_ref[8:] += fold(value)
    value = value.astype(BF16)
    for step, o_ref in enumerate((o3_ref, o2_ref, o1_ref, o0_ref)):
        @pl.when(i == step)
        def _(o_ref=o_ref):
            o_ref[pl.ds(pl.multiple_of(p * TILE, TILE), TILE), :] = value

    @pl.when((i == 3) & (p == PARTS - 1))
    def _():
        row = lax.broadcasted_iota(jnp.int32, vec_ref.shape, 0)
        vectors = jnp.zeros(vec_ref.shape, F32)
        before = early[0][...]
        for ref in early[1:]:
            before = before + ref[...]
        parts = [before[8 * n:8 * n + 8] for n in range(4)] + [sum_ref[:8], sum_ref[8:]]
        for n, part in enumerate(parts):
            vectors = jnp.where(row == n, jnp.sum(part, axis=0, keepdims=True), vectors)
        vec_ref[...] = vectors
        inside = units[0][...]
        for ref in units[1:]:
            inside = inside + ref[...]
        apart_ref[0:1] = jnp.sum(inside, axis=0, keepdims=True)
        apart_ref[1:] = jnp.zeros((7, apart_ref.shape[1]), F32)
        apart_ref[1:2, :row_ref.shape[1]] = row_ref[0:1]
        o3_ref[PARTS * TILE:] = paired(vectors)


def tail(me, grads, wq, wk, wv, tokens, stat, early, units, after):
    deep = grads.shape[0]
    features = wq.shape[1]
    share = const((PARTS * TILE, features))
    more = const((PARTS * TILE + 16, features))
    at = lambda i, p, m: 4 * p + (m[0] ^ (3 - i))
    return kernel_call(
        tail_body,
        (me, grads, wq, wk, wv, tokens, stat, *early, *units, *after),
        free_out=(1, 3),
        grid_spec=pltpu.PrefetchScalarGridSpec(
            num_scalar_prefetch=1,
            grid=(4, PARTS),
            in_specs=[pl.BlockSpec((deep, TILE), lambda i, p, m: (0, at(i, p, m))),
                      const(wq.shape), const(wk.shape), const(wv.shape),
                      pl.BlockSpec((TILE, features), lambda i, p, m: (at(i, p, m), 0)),
                      pl.BlockSpec((TILE, WIDE), lambda i, p, m: (at(i, p, m), 0))]
            + [const(v.shape) for v in (*early, *units)] + [pl.BlockSpec(memory_space=pl.ANY)] * len(after),
            out_specs=[share, share, share, more, const((8, features)), const((8, features))],
            scratch_shapes=[pltpu.VMEM((16, features), F32), pltpu.VMEM((8, deep), F32)],
        ),
        out_shape=[shape_of(PARTS * TILE, features)] * 3 + [shape_of(PARTS * TILE + 16, features)]
        + [shape_of(8, features, dtype=F32)] * 2,
        cost_estimate=cost(4e9, 10e6),
        name="tail",
    )


def chip_body(one_ref, two_ref, vec_ref, *rest):
    out_ref = rest[-1]
    rows = one_ref.shape[0]
    out_ref[:rows] = (one_ref[...].astype(F32) + two_ref[:rows].astype(F32)).astype(BF16)
    out_ref[rows:] = paired(vec_ref[...] + joined(two_ref[rows:]))


def chip_sum(one, two, vectors, after):
    return kernel_call(
        chip_body,
        (one, two, vectors, *after),
        free_in=(1,) + tuple(range(3, 3 + len(after))),
        free_out=(0,),
        grid=(1,),
        in_specs=[const(one.shape), const(two.shape), const(vectors.shape)]
        + [pl.BlockSpec(memory_space=pl.ANY)] * len(after),
        out_specs=[const(two.shape)],
        out_shape=[shape_of(*two.shape)],
        name="chip_sum",
    )[0]


def halves_body(xz_ref, g_ref, go_ref, *rest):
    keep_ref, send_ref = rest[-2:]
    width = go_ref.shape[0]
    for to_ref, half in ((keep_ref, xz_ref[0]), (send_ref, 1 - xz_ref[0])):
        @pl.when(half == 0)
        def _(to_ref=to_ref):
            to_ref[...] = g_ref[:2 * width]

        @pl.when(half == 1)
        def _(to_ref=to_ref):
            to_ref[:width] = g_ref[2 * width:]
            to_ref[width:] = go_ref[...]


def halves(xz, grad_weights, grad_output, after):
    width, features = grad_output.shape
    half = const((2 * width, features))
    return kernel_call(
        halves_body,
        (xz, grad_weights, grad_output, *after),
        free_in=(1, 2, 3),
        grid_spec=pltpu.PrefetchScalarGridSpec(
            num_scalar_prefetch=1,
            grid=(1,),
            in_specs=[const(grad_weights.shape), const(grad_output.shape)]
            + [pl.BlockSpec(memory_space=pl.ANY)] * len(after),
            out_specs=[half, half],
        ),
        out_shape=[shape_of(2 * width, features)] * 2,
        cost_estimate=cost(1e6, 4e6),
        name="halves",
    )


def quarter_body(count, xz_ref, one_ref, two_ref, *rest):
    rows = one_ref.shape[0] // count
    for n, out_ref in enumerate(rest[-count:]):
        at = pl.ds(pl.multiple_of(lax.rem(xz_ref[1] + n, count) * rows, rows), rows)
        out_ref[...] = (one_ref[at, :].astype(F32) + two_ref[at, :].astype(F32)).astype(BF16)


def quarters(xz, one, two, count, after):
    rows, features = one.shape

    def body(*refs):
        quarter_body(count, *refs)

    return kernel_call(
        body,
        (xz, one, two, *after),
        free_in=(2, 3, 4),
        grid_spec=pltpu.PrefetchScalarGridSpec(
            num_scalar_prefetch=1,
            grid=(1,),
            in_specs=[const(one.shape), const(two.shape)] + [pl.BlockSpec(memory_space=pl.ANY)] * len(after),
            out_specs=[const((rows // count, features))] * count,
        ),
        out_shape=[shape_of(rows // count, features)] * count,
        cost_estimate=cost(1e6, 2e6),
        name="quarters",
    )


def paired(value):
    return jnp.concatenate(split(value, 2), axis=0).astype(BF16)


def joined(both):
    both = both.astype(F32)
    half = both.shape[0] // 2
    return both[:half] + both[half:]


def second_body(count, *refs):
    one_ref, two_ref, apart_ref, out_ref = refs[count], refs[count + 1], refs[count + 2], refs[-1]
    rows = refs[0].shape[0]
    total = refs[0][...].astype(F32)
    for ref in refs[1:count]:
        total = total + ref[...].astype(F32)
    out_ref[:rows] = total.astype(BF16)
    shared = joined(one_ref[...]) + joined(two_ref[...])
    out_ref[rows:] = paired(jnp.concatenate([shared, apart_ref[...]], axis=0))


def second(parts, one, two, apart, after):
    count = len(parts)
    rows, features = parts[0].shape
    last = pl.BlockSpec((16, features), lambda i: (one.shape[0] // 16 - 1, 0))

    def body(*refs):
        second_body(count, *refs)

    return kernel_call(
        body,
        (*parts, one, two, apart, *after),
        free_in=tuple(range(1, count + 2)) + tuple(range(count + 3, count + 3 + len(after))),
        grid=(1,),
        in_specs=[const((rows, features))] * count + [last, last, const(apart.shape)]
        + [pl.BlockSpec(memory_space=pl.ANY)] * len(after),
        out_specs=[const((rows + 32, features))],
        out_shape=[shape_of(rows + 32, features)],
        name="second",
    )[0]


def third_body(count, xz_ref, *refs):
    out_ref = refs[-1]
    step = out_ref.shape[0] - (refs[0].shape[0] * count - out_ref.shape[0]) // (count - 1)
    rows = step // count
    sums = None
    for n, ref in enumerate(refs[:count]):
        place_at = lax.rem(xz_ref[1] + count - n, count)
        out_ref[pl.ds(pl.multiple_of(place_at * rows, rows), rows), :] = ref[:rows]
        value = joined(ref[rows:])
        sums = value if sums is None else sums + value
    out_ref[step:] = paired(sums)


def third(xz, pieces, extra, after):
    count = len(pieces)
    rows, features = pieces[0].shape
    total = (rows - extra) * count + extra

    def body(*refs):
        third_body(count, *refs)

    return kernel_call(
        body,
        (xz, *pieces, *after),
        free_in=tuple(range(1, count + 1)),
        grid_spec=pltpu.PrefetchScalarGridSpec(
            num_scalar_prefetch=1,
            grid=(1,),
            in_specs=[const((rows, features))] * count + [pl.BlockSpec(memory_space=pl.ANY)] * len(after),
            out_specs=[const((total, features))],
        ),
        out_shape=[shape_of(total, features)],
        name="third",
    )[0]


def ready_body(xz_ref, mine_ref, other_ref, *rest):
    outs = rest[-16:]
    width = outs[0].shape[0]
    for n, out_ref in enumerate(outs[:4]):
        rows = slice(n % 2 * width, (n % 2 + 1) * width)
        for to_ref, chosen in ((mine_ref, xz_ref[0] == n // 2), (other_ref, xz_ref[0] != n // 2)):
            @pl.when(chosen)
            def _(to_ref=to_ref, out_ref=out_ref, rows=rows):
                out_ref[...] = to_ref[rows].astype(F32)

    small = joined(mine_ref[2 * width:]) + joined(other_ref[2 * width:])
    for n, out_ref in enumerate(outs[4:13]):
        out_ref[...] = small[n]
    for n, out_ref in enumerate(outs[13:]):
        out_ref[...] = small[9, n * width:(n + 1) * width]


def ready(xz, mine, other, width, after):
    rows, features = mine.shape
    sizes = [(features,)] * 9 + [(width,)] * 3
    return kernel_call(
        ready_body,
        (xz, mine, other, *after),
        free_in=(2,),
        grid_spec=pltpu.PrefetchScalarGridSpec(
            num_scalar_prefetch=1,
            grid=(1,),
            in_specs=[const(mine.shape), const(other.shape)] + [pl.BlockSpec(memory_space=pl.ANY)] * len(after),
            out_specs=[const((width, features))] * 4 + [const(size) for size in sizes],
        ),
        out_shape=[shape_of(width, features, dtype=F32)] * 4 + [shape_of(*size, dtype=F32) for size in sizes],
        cost_estimate=cost(1e6, 4e6),
        name="ready",
    )


def final_body(me_ref, b0_ref, b1_ref, b2_ref, x_ref, *rest):
    grad_refs, vec_ref, out_ref = rest[:PARTS], rest[PARTS], rest[-1]
    p = pl.program_id(0)
    grad_attend = b0_ref[...].astype(F32) + b1_ref[...].astype(F32) + b2_ref[...].astype(F32)
    normed, scale, _ = stats(x_ref[...].astype(F32))
    back = norm_back(grad_attend, normed, scale, vec_ref[0:1, :])
    for n, grad_ref in enumerate(grad_refs):
        @pl.when(p == n)
        def _(grad_ref=grad_ref):
            out_ref[...] = (grad_ref[...] + back).astype(BF16)


def final(me, sums, tokens, grads, vectors, after):
    features = tokens.shape[1]
    rows = pl.BlockSpec((TILE, features), lambda p, m: (p, 0))
    return kernel_call(
        final_body,
        (me, *sums, tokens, *grads, vectors, *after),
        free_in=(2, 3) + tuple(range(6 + PARTS, 6 + PARTS + len(after))),
        free_out=(0,),
        grid_spec=pltpu.PrefetchScalarGridSpec(
            num_scalar_prefetch=1,
            grid=(PARTS,),
            in_specs=[rows] * 3 + [pl.BlockSpec((TILE, features), lambda p, m: (4 * p + m[0], 0))]
            + [const((TILE, features))] * PARTS + [const(vectors.shape)]
            + [pl.BlockSpec(memory_space=pl.ANY)] * len(after),
            out_specs=[rows],
        ),
        out_shape=[shape_of(PARTS * TILE, features)],
        cost_estimate=cost(1e8, 5e6),
        name="final",
    )[0]


def place_body(me_ref, p0_ref, p1_ref, p2_ref, p3_ref, *rest):
    out_ref = rest[-1]
    for step, p_ref in enumerate((p0_ref, p1_ref, p2_ref, p3_ref)):
        @pl.when(pl.program_id(0) == step)
        def _(p_ref=p_ref):
            at = pl.ds(pl.multiple_of(pl.program_id(1) * TILE, TILE), TILE)
            out_ref[...] = p_ref[at, :].astype(out_ref.dtype)


def place(me, shares, dtype, after):
    rows, features = shares[0].shape
    return kernel_call(
        place_body,
        (me, *shares, *after),
        free_in=(1, 2, 3, 4),
        grid_spec=pltpu.PrefetchScalarGridSpec(
            num_scalar_prefetch=1,
            grid=(4, PARTS),
            in_specs=[const((rows, features))] * 4 + [pl.BlockSpec(memory_space=pl.ANY)] * len(after),
            out_specs=pl.BlockSpec((TILE, features), lambda i, p, m: (4 * p + (m[0] ^ i), 0)),
        ),
        out_shape=shape_of(4 * rows, features, dtype=dtype),
        cost_estimate=cost(1e6, 9e6),
        name="place",
    )


def fence_body(*refs):
    pass


def fence(value, *after, space=pltpu.HBM):
    anywhere = pl.BlockSpec(memory_space=pl.ANY)
    return pl.pallas_call(
        fence_body,
        in_specs=[anywhere] * (1 + len(after)),
        out_specs=anywhere,
        out_shape=space(value.shape, value.dtype),
        input_output_aliases={0: 0},
        name="fence",
    )(pltpu.with_memory_space_constraint(value, space), *after)


def other_core(value):
    return lax.ppermute(value, "core", SWAP)


def other_chip(value):
    return lax.ppermute(value, "y", SWAP)


def crosswise(value):
    return lax.ppermute(value, MP, [(n, n ^ 3) for n in range(4)])


def exchange(pieces):
    return [pieces[0], other_core(pieces[1]), other_chip(pieces[2]), crosswise(pieces[3])]


def gather_sum(pieces):
    near = other_core(pieces[1])
    far = (pieces[2].astype(F32) + other_core(pieces[3]).astype(F32)).astype(BF16)
    return [pieces[0], near, other_chip(far)], far


def spread(value):
    far = other_chip(value)
    return [value, other_core(value), far, other_core(far)]


def pick(values, at):
    return lax.dynamic_index_in_dim(values, at, 0, keepdims=False)


def turned(values, way):
    size = lax.axis_size("z")
    return lax.ppermute(values, "z", [(n, (n + way) % size) for n in range(size)])


def sum_first(xz, keep, got, after):
    size = lax.axis_size("z")
    if size > 4:
        return [lax.psum(keep + got, "z")]
    return quarters(xz, keep, got, size, after)


def gather_z(value):
    size = lax.axis_size("z")
    if size > 4:
        return [lax.all_gather(value, "z", axis=0, tiled=True)]
    return [turned(value, way) if way else value for way in range(size)]


def local(
    tokens,
    segment_ids,
    gain_one,
    bias_one,
    query_weight,
    query_bias,
    key_weight,
    value_weight,
    value_bias,
    output_weight,
    output_bias,
    gain_two,
    bias_two,
    inner_weight,
    inner_bias,
    outer_weight,
    outer_bias,
    cotangent,
):
    _, length, features = tokens.shape
    width = query_weight.shape[1]
    heads = width // HEAD
    tokens = tokens.reshape(length, features)
    cot = cotangent.reshape(length, features)
    at = lax.axis_index(MP).astype(jnp.int32)
    me = at[None]
    apart = jnp.concatenate([query_bias, value_bias, jnp.zeros((features - 2 * width,), F32)])
    vectors = jnp.concatenate([gain_one, bias_one, output_bias, gain_two, bias_two, outer_bias, apart, inner_bias])
    vectors = vectors.reshape(8, features)
    wq, wk, wv = query_weight.T, key_weight.T, value_weight.T

    output_weights = spread(output_weight)
    attend_in, qt, kt, vt, kn, vn, stat = project(tokens, segment_ids, vectors, wq, wk, wv, heads)

    parts = range(PARTS)
    attended, extras, fours = [], [], []
    for p in parts:
        out, extra, *four = attend_forward(p, me, segment_ids, qt, kn, vt, output_weights[1:3] if p == 0 else ())
        attended.append(out)
        extras.append(extra)
        fours.append(exchange(four))
    mixed, residuals, pieces = [], [], []
    for p in parts:
        residual, own, together = middle(p, me, tokens, fours[p], output_weights, vectors, extras[p + 1:])
        mixed.append(together)
        residuals.append(residual)
        pieces.append([own, other_core(own), other_chip(own)])

    backs = {}
    *outs, b00, b01, b10, b11, near_sum, near_grad = feed_near(
        me, [pieces[p][n] for p in parts for n in (0, 1)], cot, inner_weight, vectors, outer_weight
    )
    backs[0, 0], backs[0, 1], backs[1, 0], backs[1, 1] = b00, b01, b10, b11
    sums, kept = [near_sum], ()
    for p in parts:
        far = fence(pieces[p][2], b00, space=pltpu.VMEM)
        *kept, backs[p, 2], backs[p, 3], far_sum = feed_far(
            p, me, far, other_core(far), cot, inner_weight, vectors, outer_weight, kept
        )
        sums.append(far_sum)
    left, right, *far_outs = kept
    outs += far_outs
    gathered, far_sums = zip(*[gather_sum([backs[p, n] for n in range(4)]) for p in parts])
    feed_sum = feed_grad(left, right, near_grad, far_sums).reshape(-1, features)
    feed_sum = lax.psum_scatter(feed_sum, DP, scatter_dimension=0, tiled=True)
    grad_residuals, lows, grads_attended, inner_sums = [], [], [], []
    for p in parts:
        grad, low, a0, a1, a2, a3, vector = middle_back(
            p, me, gathered[p], residuals[p], cot, vectors, output_weights
        )
        grad_residuals.append(grad)
        lows.append(low)
        inner_sums.append(vector)
        grads_attended.append(exchange([a0, a1, a2, a3]))

    near = other_core(fence(outs[1], *far_sums))
    far = (outs[2].astype(F32) + other_core(fence(outs[3], *far_sums)).astype(F32)).astype(BF16)
    far = fence(far, lows[-1], space=pltpu.VMEM)
    part = output_grad(mixed, lows)
    earlier = attend_backward(0, me, segment_ids, qt, extras[0], kn, kt, vn, attended[0], grads_attended[0], (),
                              (far, near, part[0]))
    there = other_chip(far)
    part_far = fence(part[2], earlier[0])
    part_far = (part_far.astype(F32) + other_core(part[3]).astype(F32)).astype(BF16)
    part_near = other_core(part[1])
    grads = attend_backward(1, me, segment_ids, qt, extras[1], kn, kt, vn, attended[1], grads_attended[1], earlier,
                            (part_near, part_far, there))

    xz = jnp.stack([lax.axis_index("x"), lax.axis_index("z")]).astype(jnp.int32)
    part_across = other_chip(part_far)
    grad_output = fence(part[0], grads).astype(F32) + part_near.astype(F32) + part_across.astype(F32)
    keep, send = halves(xz, nn(grads, attend_in).astype(BF16), grad_output.astype(BF16), ())
    result = jnp.concatenate(residuals) + fence(outs[0], send).astype(F32) + near.astype(F32)
    result = (result + there.astype(F32) + outer_bias).astype(BF16)
    near, far = other_core(result), other_chip(result)
    got = lax.ppermute(send, "x", SWAP)
    back_own, back_near, back_far, back_across, apart, summed = tail(
        me, grads, wq, wk, wv, tokens, stat, inner_sums, sums, (send,)
    )
    feed_sum = lax.all_gather(fence(feed_sum, send), DP, axis=0, tiled=True)
    feed_sum = (feed_sum[:features].astype(F32), feed_sum[features:].astype(F32))
    quarter = sum_first(xz, keep, got, (near, far, apart))
    back_across = other_core(fence(back_across, quarter[-1], space=pltpu.VMEM))
    back_far = chip_sum(back_far, back_across, summed, ())
    back_there = other_chip(back_far)
    share = final(me, [back_own, other_core(back_near), back_there], tokens, grad_residuals, vectors, ())
    if len(quarter) > 1:
        turns = [quarter[0]] + [turned(part, n + 1) for n, part in enumerate(quarter[1:])]
        held = second(turns, back_far, back_there, apart, (share,))
        layer_out = place(me, [result, near, far, other_core(far)], BF16, (held,))
        mine = third(xz, gather_z(held), 32, (layer_out,))
    else:
        small = jnp.concatenate([joined(back_far[-16:]) + joined(back_there[-16:]), apart])
        layer_out = place(me, [result, near, far, other_core(far)], BF16, ())
        mine = jnp.concatenate([quarter[0], paired(lax.psum(small, "z"))])
    share = fence(share, held if len(quarter) > 1 else mine, space=pltpu.VMEM)
    near, far = other_core(share), fence(other_chip(share), mine, space=pltpu.VMEM)
    input_grad = place(me, [share, near, far, other_core(far)], F32, (mine,))
    *wide, two_gain, two_bias, output_sum, outer_bias, one_gain, one_bias, _, _, inner_bias, query, _, value = ready(
        xz, mine, lax.ppermute(mine, "x", SWAP), width, feed_sum
    )
    return (
        layer_out.reshape(1, length, features),
        input_grad.reshape(1, length, features),
        one_gain,
        one_bias,
        wide[0].T,
        query,
        wide[1].T,
        wide[2].T,
        value,
        wide[3],
        output_sum,
        two_gain,
        two_bias,
        feed_sum[1],
        inner_bias,
        feed_sum[0],
        outer_bias,
    )


def solution(mesh):
    rows = mesh.shape["dp"]
    inner = Mesh(mesh.devices.reshape(rows // 2, 2, 2, 2), DP + MP)
    placed = (
        P(DP, None, None),
        P(DP, None),
        P(),
        P(),
        P(None, MP),
        P(MP),
        P(None, MP),
        P(None, MP),
        P(MP),
        P(MP, None),
        P(),
        P(),
        P(),
        P(None, MP),
        P(MP),
        P(MP, None),
        P(),
        P(DP, None, None),
    )
    return jax.shard_map(
        local,
        mesh=inner,
        in_specs=placed,
        out_specs=(
            P(DP, None, None),
            P(DP, None, None),
            P(),
            P(),
            P(None, MP),
            P(MP),
            P(None, MP),
            P(None, MP),
            P(MP),
            P(MP, None),
            P(),
            P(),
            P(),
            P(None, MP),
            P(MP),
            P(MP, None),
            P(),
        ),
        check_vma=False,
    )
```

```python
import jax
import jax.numpy as jnp
from jax import lax
from jax.experimental import pallas as pl
from jax.experimental.pallas import tpu as pltpu
from jax.sharding import Mesh
from jax.sharding import PartitionSpec as P

HEAD = 64
WIDE = 128
TILE = 256
PARTS = 2
MASKED = 1e30
SCALE = 1
F32 = jnp.float32
BF16 = jnp.bfloat16
DP = ("z", "x")
MP = ("y", "core")
SWAP = [(0, 1), (1, 0)]


def nn(left, right):
    return lax.dot_general(left, right, (((1,), (0,)), ((), ())), preferred_element_type=F32)


def nt(left, right):
    return lax.dot_general(left, right, (((1,), (1,)), ((), ())), preferred_element_type=F32)


def tn(left, right):
    return lax.dot_general(left, right, (((0,), (0,)), ((), ())), preferred_element_type=F32)


def stats(values):
    mean = jnp.mean(values, axis=-1, keepdims=True)
    center = values - mean
    scale = lax.rsqrt(jnp.mean(center * center, axis=-1, keepdims=True) + 1e-05)
    return center * scale, scale, mean


def norm_back(grad_out, normed, scale, gain):
    upstream = grad_out * gain
    return scale * (
        upstream
        - jnp.mean(upstream, axis=-1, keepdims=True)
        - normed * jnp.mean(upstream * normed, axis=-1, keepdims=True)
    )


def fold(values):
    return jnp.sum(values.reshape(-1, 8, values.shape[-1]), axis=0)


def split(value, parts):
    out = []
    for _ in range(parts):
        piece = value.astype(BF16).astype(F32)
        out.append(piece)
        value = value - piece
    return out


def const(shape):
    return pl.BlockSpec(shape, lambda *_: (0,) * len(shape))


def shape_of(*dims, dtype=BF16):
    return jax.ShapeDtypeStruct(dims, dtype)


def params(mib=40):
    return pltpu.CompilerParams(vmem_limit_bytes=mib << 20)


def kernel_call(body, values, free_in=(), free_out=(), **options):
    shapes = options.pop("out_shape")
    many = isinstance(shapes, (list, tuple))
    shapes = [s if n in free_out else pltpu.HBM(s.shape, s.dtype) for n, s in enumerate(shapes if many else [shapes])]
    values = [
        v if n in free_in or v.dtype == jnp.int32 else pltpu.with_memory_space_constraint(v, pltpu.HBM)
        for n, v in enumerate(values)
    ]
    return pl.pallas_call(
        body, out_shape=shapes if many else shapes[0], compiler_params=params(), **options
    )(*values)


def cost(flops, moved, special=0):
    return pl.CostEstimate(flops=int(flops * SCALE), bytes_accessed=int(moved * SCALE), transcendentals=0)


def project_body(x_ref, seg_ref, vec_ref, wq_ref, wk_ref, wv_ref,
                 ai_ref, qt_ref, kt_ref, vt_ref, kn_ref, vn_ref, stat_ref):
    heads = kn_ref.shape[0]
    width = heads * HEAD
    tile = x_ref.shape[0]
    normed, scale, mean = stats(x_ref[...].astype(F32))
    lane = lax.broadcasted_iota(jnp.int32, stat_ref.shape, 1)
    stat_ref[...] = jnp.where(lane == 0, mean, scale)
    ai = (normed * vec_ref[0:1, :] + vec_ref[1:2, :]).astype(BF16)
    ai_ref[...] = ai
    column = vec_ref[...].T[:2 * width, 6:7]
    queries = ((nt(wq_ref[...], ai) + column[:width]).astype(BF16)).astype(F32) * HEAD ** -0.5
    keys = nt(wk_ref[...], ai)
    kt_ref[...] = keys.astype(BF16)
    values = nt(wv_ref[...], ai) + column[width:]
    row = lax.broadcasted_iota(jnp.int32, (HEAD, tile), 0)
    same = jnp.where(row == seg_ref[...], 1.0, 0.0)
    mask = jnp.where(row < 8, (same - 1.0) * MASKED, jnp.where(row < 11, 1.0, 0.0))
    ones = jnp.where(row < 2, 1.0, 0.0)
    first = jnp.where(row[:16] == 0, 1.0, 0.0).astype(BF16)
    for h in range(heads):
        rows = slice(h * HEAD, (h + 1) * HEAD)
        qt_ref[h, :HEAD, :] = queries[rows].astype(BF16)
        qt_ref[h, HEAD:, :] = same.astype(BF16)
        vt_ref[h, :HEAD, :] = values[rows].astype(BF16)
        vt_ref[h, HEAD:, :] = first
        kn_ref[h] = jnp.concatenate([keys[rows], mask], axis=0).T.astype(BF16)
        vn_ref[h] = jnp.concatenate([values[rows], ones], axis=0).T.astype(BF16)


def project(tokens, seg_row, vectors, wq, wk, wv, heads):
    length, features = tokens.shape
    width = heads * HEAD
    return kernel_call(
        project_body,
        (tokens, seg_row, vectors, wq, wk, wv),
        grid=(length // TILE,),
        in_specs=[
            pl.BlockSpec((TILE, features), lambda i: (i, 0)),
            pl.BlockSpec((1, TILE), lambda i: (0, i)),
            const(vectors.shape), const(wq.shape), const(wk.shape), const(wv.shape),
        ],
        out_specs=[
            pl.BlockSpec((TILE, features), lambda i: (i, 0)),
            pl.BlockSpec((heads, WIDE, TILE), lambda i: (0, 0, i)),
            pl.BlockSpec((width, TILE), lambda i: (0, i)),
            pl.BlockSpec((heads, HEAD + 16, TILE), lambda i: (0, 0, i)),
            pl.BlockSpec((heads, TILE, WIDE), lambda i: (0, i, 0)),
            pl.BlockSpec((heads, TILE, WIDE), lambda i: (0, i, 0)),
            pl.BlockSpec((TILE, WIDE), lambda i: (i, 0)),
        ],
        out_shape=[
            shape_of(length, features),
            shape_of(heads, WIDE, length),
            shape_of(width, length),
            shape_of(heads, HEAD + 16, length),
            shape_of(heads, length, WIDE),
            shape_of(heads, length, WIDE),
            shape_of(length, WIDE, dtype=F32),
        ],
        cost_estimate=cost(6e9, 14e6),
        name="project",
    )


def key_range(seg_ref, seg_all, i):
    first = seg_ref[0, i * TILE]
    last = seg_ref[0, i * TILE + TILE - 1]
    before = jnp.sum(jnp.where(seg_all < first, 1.0, 0.0)).astype(jnp.int32)
    until = jnp.sum(jnp.where(seg_all <= last, 1.0, 0.0)).astype(jnp.int32)
    return before // TILE, (until + TILE - 1) // TILE


def by_pairs(low, high, step, carry):
    keys = lambda kb: pl.ds(pl.multiple_of(kb * TILE, TILE), TILE)
    pairs = (high - low) // 2
    carry = lax.fori_loop(0, pairs, lambda n, c: step([keys(low + 2 * n), keys(low + 2 * n + 1)], c), carry)
    return lax.fori_loop(low + 2 * pairs, high, lambda kb, c: step([keys(kb)], c), carry)


def shifted(one_hot, pieces):
    row = lax.broadcasted_iota(jnp.int32, one_hot.shape, 0)
    value = one_hot
    for n, piece in enumerate(pieces):
        value = jnp.where(row == 8 + n, piece, value)
    return value.astype(BF16)


def forward_body(offset, me_ref, segs_ref, seg_ref, qt_ref, kn_ref, vt_ref, *rest):
    out_ref, extra_ref, o0_ref, o1_ref, o2_ref, o3_ref, acc_ref = rest[-7:]
    heads, _, tile = qt_ref.shape
    i = pl.program_id(0)
    low, high = key_range(segs_ref, seg_ref[...], i + offset)
    acc_ref[...] = jnp.zeros_like(acc_ref)

    def step(keys, tops):
        scores = [[nn(kn_ref[h, at, :], qt_ref[h]) for at in keys] for h in range(heads)]
        new_tops = []
        for h in range(heads):
            top = tops[h]
            for score in scores[h]:
                top = jnp.maximum(top, jnp.max(score, axis=0, keepdims=True))
            new_tops.append(top)
        powered = [[jnp.exp(score - new_tops[h]).astype(BF16) for score in scores[h]] for h in range(heads)]
        for h in range(heads):
            total = acc_ref[h] * jnp.exp(tops[h] - new_tops[h])
            for at, power in zip(keys, powered[h]):
                total = total + nn(vt_ref[h, :, at], power)
            acc_ref[h] = total
        return tuple(new_tops)

    tops = by_pairs(low, high, step, (jnp.full((1, tile), -jnp.inf, F32),) * heads)
    for h in range(heads):
        total = acc_ref[h, HEAD:HEAD + 1, :]
        out_ref[0, h * HEAD:(h + 1) * HEAD, :] = (acc_ref[h, :HEAD, :] / total).astype(BF16)
        one_hot = qt_ref[h, HEAD:HEAD + 16, :].astype(F32)
        extra_ref[h] = shifted(one_hot, split(-(tops[h] + jnp.log(total)), 3))
    for n, o_ref in enumerate((o0_ref, o1_ref, o2_ref, o3_ref)):
        @pl.when((i ^ me_ref[0]) == n)
        def _(o_ref=o_ref):
            o_ref[...] = out_ref[0]


def attend_forward(part, me, seg_row, qt, kn, vt, after):
    heads, _, length = qt.shape
    width = heads * HEAD
    count = length // TILE // PARTS
    offset = part * count

    def body(*refs):
        forward_body(offset, *refs)

    return kernel_call(
        body,
        (me, seg_row, seg_row, qt, kn, vt, *after),
        free_in=tuple(range(6, 6 + len(after))),
        free_out=(3, 4, 5),
        grid_spec=pltpu.PrefetchScalarGridSpec(
            num_scalar_prefetch=1,
            grid=(count,),
            in_specs=[
                pl.BlockSpec(memory_space=pltpu.SMEM),
                const((1, length)),
                pl.BlockSpec((heads, WIDE, TILE), lambda i, m: (0, 0, i + offset)),
                const(kn.shape), const(vt.shape),
            ] + [pl.BlockSpec(memory_space=pl.ANY)] * len(after),
            out_specs=[
                pl.BlockSpec((1, width, TILE), lambda i, m: (i, 0, 0)),
                pl.BlockSpec((heads, 16, TILE), lambda i, m: (0, 0, i)),
            ] + [const((width, TILE))] * 4,
            scratch_shapes=[pltpu.VMEM((heads, HEAD + 16, TILE), F32)],
        ),
        out_shape=[shape_of(count, width, TILE), shape_of(heads, 16, count * TILE)] + [shape_of(width, TILE)] * 4,
        cost_estimate=cost(9e9, 5e6, 4e6),
        name="attend_forward",
    )


def backward_body(part, me_ref, segs_ref, seg_ref, qt_ref, extra_ref, kn_ref, kt_ref, vn_ref, out_ref,
                  g0_ref, g1_ref, g2_ref, g3_ref, *rest):
    heads, _, tile = qt_ref.shape
    width = heads * HEAD
    length = kt_ref.shape[1]
    if part == 0:
        dq_out, dk_ref, dv_ref, qa_ref, da_ref, dq_ref = rest[-6:]
    else:
        dq_in, dk_in, dv_in = rest[:3]
        grads_ref, qa_ref, da_ref, dq_ref, dk_ref, dv_ref = rest[-6:]
    i = pl.program_id(0)
    count = length // TILE // PARTS
    at_here = i + part * count
    low, high = key_range(segs_ref, seg_ref[...], at_here)

    @pl.when(i == 0)
    def _():
        if part == 0:
            dk_ref[...] = jnp.zeros_like(dk_ref)
            dv_ref[...] = jnp.zeros_like(dv_ref)
        else:
            dk_ref[...] = dk_in[...]
            dv_ref[...] = dv_in[...]
            grads_ref[:width, :count * TILE] = dq_in[...]
        qa_ref[...] = jnp.zeros_like(qa_ref)
        da_ref[...] = jnp.zeros_like(da_ref)

    source = i ^ me_ref[0]
    for n, g_ref in enumerate((g0_ref, g1_ref, g2_ref, g3_ref)):
        @pl.when(source == n)
        def _(g_ref=g_ref):
            for h in range(heads):
                da_ref[h, :HEAD, :] = g_ref[h * HEAD:(h + 1) * HEAD]

    dq_ref[...] = jnp.zeros_like(dq_ref)
    row = lax.broadcasted_iota(jnp.int32, (16, tile), 0)
    for h in range(heads):
        rows = slice(h * HEAD, (h + 1) * HEAD)
        qa_ref[h, :HEAD, :] = qt_ref[h, :HEAD, :]
        qa_ref[h, HEAD:HEAD + 16, :] = extra_ref[h]
        inner = jnp.sum(da_ref[h, :HEAD, :].astype(F32) * out_ref[0, rows].astype(F32), axis=0, keepdims=True)
        first, second = split(-inner, 2)
        value = jnp.where(row == 0, first, jnp.where(row == 1, second, 0.0))
        da_ref[h, HEAD:HEAD + 16, :] = value.astype(BF16)

    def step(keys, carry):
        every = range(heads)
        rows = [slice(h * HEAD, (h + 1) * HEAD) for h in every]
        scores = [[nn(kn_ref[h, at, :], qa_ref[h]) for at in keys] for h in every]
        slopes = [[nn(vn_ref[h, at, :], da_ref[h]) for at in keys] for h in every]
        probs = [[jnp.exp(score) for score in scores[h]] for h in every]
        ds = [[(p * s).astype(BF16) for p, s in zip(probs[h], slopes[h])] for h in every]
        probs = [[p.astype(BF16) for p in probs[h]] for h in every]
        for h in every:
            total = dq_ref[rows[h]]
            for n, at in enumerate(keys):
                dv_ref[rows[h], at] += nt(da_ref[h, :HEAD, :], probs[h][n])
                dk_ref[rows[h], at] += nt(qa_ref[h, :HEAD, :], ds[h][n])
                total = total + nn(kt_ref[rows[h], at], ds[h][n])
            dq_ref[rows[h]] = total
        return carry

    by_pairs(low, high, step, 0)
    dq = (dq_ref[...] * HEAD ** -0.5).astype(BF16)
    if part == 0:
        dq_out[...] = dq
    else:
        grads_ref[:width, pl.ds(pl.multiple_of(at_here * TILE, TILE), TILE)] = dq

        @pl.when(i == pl.num_programs(0) - 1)
        def _():
            grads_ref[width:2 * width] = dk_ref[...].astype(BF16)
            grads_ref[2 * width:] = dv_ref[...].astype(BF16)


def attend_backward(part, me, seg_row, qt, extra, kn, kt, vn, out, grad, earlier, after):
    heads, _, length = qt.shape
    width = heads * HEAD
    count = length // TILE // PARTS
    offset = part * count

    def body(*refs):
        backward_body(part, *refs)

    in_specs = [
        pl.BlockSpec(memory_space=pltpu.SMEM),
        const((1, length)),
        pl.BlockSpec((heads, WIDE, TILE), lambda i, m: (0, 0, i + offset)),
        pl.BlockSpec((heads, 16, TILE), lambda i, m: (0, 0, i)),
        const(kn.shape), const(kt.shape), const(vn.shape),
        pl.BlockSpec((1, width, TILE), lambda i, m: (i, 0, 0)),
        const(grad[0].shape), const(grad[1].shape), const(grad[2].shape), const(grad[3].shape),
    ] + [const(v.shape) for v in earlier] + [pl.BlockSpec(memory_space=pl.ANY)] * len(after)
    scratch = [
        pltpu.VMEM((heads, WIDE, TILE), BF16),
        pltpu.VMEM((heads, WIDE, TILE), BF16),
        pltpu.VMEM((width, TILE), F32),
    ]
    if part == 0:
        out_specs = [pl.BlockSpec((width, TILE), lambda i, m: (0, i)), const((width, length)), const((width, length))]
        out_shape = [shape_of(width, count * TILE), shape_of(width, length, dtype=F32), shape_of(width, length, dtype=F32)]
    else:
        out_specs = const((3 * width, length))
        out_shape = shape_of(3 * width, length)
        scratch += [pltpu.VMEM((width, length), F32), pltpu.VMEM((width, length), F32)]
    return kernel_call(
        body,
        (me, seg_row, seg_row, qt, extra, kn, kt, vn, out, *grad, *earlier, *after),
        free_in=(10, 11, 12) + tuple(range(13 + len(earlier), 15 + len(earlier))),
        grid_spec=pltpu.PrefetchScalarGridSpec(
            num_scalar_prefetch=1, grid=(count,), in_specs=in_specs, out_specs=out_specs, scratch_shapes=scratch,
        ),
        out_shape=out_shape,
        cost_estimate=cost(16e9, 10e6, 4e6),
        name="attend_backward",
    )


def middle_body(me_ref, x_ref, m0_ref, m1_ref, m2_ref, m3_ref, w0_ref, w1_ref, w2_ref, w3_ref,
                vec_ref, *rest):
    residual_ref, own_ref, mixed_ref = rest[-3:]
    total = x_ref[...].astype(F32) + vec_ref[2:3, :]
    pairs = ((m0_ref, w0_ref), (m1_ref, w1_ref), (m2_ref, w2_ref), (m3_ref, w3_ref))
    for n, (m_ref, w_ref) in enumerate(pairs):
        total = total + tn(m_ref[...], w_ref[...])
        mixed_ref[n] = m_ref[...]
    residual_ref[...] = total
    normed, _, _ = stats(total)
    own_ref[...] = (normed * vec_ref[3:4, :] + vec_ref[4:5, :]).astype(BF16)


def middle(part, me, tokens, mixed, weights, vectors, after):
    features = tokens.shape[1]
    width = weights[0].shape[0]
    return kernel_call(
        middle_body,
        (me, tokens, *mixed, *weights, vectors, *after),
        free_in=(3, 4, 5),
        free_out=(1,),
        grid_spec=pltpu.PrefetchScalarGridSpec(
            num_scalar_prefetch=1,
            grid=(1,),
            in_specs=[pl.BlockSpec((TILE, features), lambda i, m: (4 * part + m[0], 0))]
            + [const(v.shape) for v in mixed] + [const(v.shape) for v in weights] + [const(vectors.shape)]
            + [pl.BlockSpec(memory_space=pl.ANY)] * len(after),
            out_specs=[const((TILE, features)), const((TILE, features)), const((4, width, TILE))],
        ),
        out_shape=[shape_of(TILE, features, dtype=F32), shape_of(TILE, features), shape_of(4, width, TILE)],
        cost_estimate=cost(2e9, 3e6),
        name="middle",
    )


def feed_piece(x, g, inner_ref, vec_ref, outer_ref):
    hidden = nn(x, inner_ref[...]) + vec_ref[7:8, :]
    half = 0.5 + 0.5 * lax.erf(hidden * 0.5 ** 0.5)
    act = (hidden * half).astype(BF16)
    slope = half + hidden * (jnp.exp(-0.5 * hidden * hidden) * 0.3989422804014327)
    dh = (nt(g, outer_ref[...]) * slope).astype(BF16)
    out = nn(act, outer_ref[...]).astype(BF16)
    return act, dh, out, nt(dh, inner_ref[...]).astype(BF16)


def near_body(me_ref, *refs):
    count = 2 * PARTS
    x_refs = refs[:count]
    g_ref, inner_ref, vec_ref, outer_ref = refs[count:count + 4]
    out_refs, back_refs = refs[count + 4:count + 6], refs[count + 6:-6]
    sum_ref, grad_ref, x_all, g_all, act_all, dh_all = refs[-6:]
    i = pl.program_id(0)
    at = pl.ds(pl.multiple_of(i * TILE, TILE), TILE)
    for n, x_ref in enumerate(x_refs):
        @pl.when(i == n)
        def _(n=n, x_ref=x_ref):
            x_all[n * TILE:(n + 1) * TILE] = x_ref[...]

    g_all[at] = g_ref[...]
    act, dh, out, back = feed_piece(x_all[at], g_ref[...], inner_ref, vec_ref, outer_ref)
    act_all[at] = act
    dh_all[at] = dh
    sums = fold(dh.astype(F32))

    @pl.when(i == 0)
    def _():
        sum_ref[...] = jnp.zeros_like(sum_ref)

    sum_ref[...] += sums
    for n in range(count):
        @pl.when(i == n)
        def _(n=n):
            out_refs[n % 2][n // 2 * TILE:(n // 2 + 1) * TILE] = out
            back_refs[n][...] = back

    @pl.when(i == count - 1)
    def _():
        grad_ref[0] = tn(act_all[...], g_all[...]).astype(BF16)
        grad_ref[1] = tn(x_all[...], dh_all[...]).astype(BF16)


def feed_near(me, pieces, cot, inner, vectors, outer):
    features = cot.shape[1]
    units = inner.shape[1]
    count = 2 * PARTS
    piece = const((TILE, features))
    scratch = lambda n: pltpu.VMEM((count * TILE, n), BF16)
    return kernel_call(
        near_body,
        (me, *pieces, cot, inner, vectors, outer),
        free_in=tuple(range(1, count + 1)),
        free_out=(3, 5),
        grid_spec=pltpu.PrefetchScalarGridSpec(
            num_scalar_prefetch=1,
            grid=(count,),
            in_specs=[piece] * count
            + [pl.BlockSpec((TILE, features), lambda i, m: (4 * (i // 2) + (m[0] ^ (i % 2)), 0)),
               const(inner.shape), const(vectors.shape), const(outer.shape)],
            out_specs=[const((PARTS * TILE, features))] * 2 + [piece] * count
            + [const((8, units)), const((2, units, features))],
            scratch_shapes=[scratch(features), scratch(features), scratch(units), scratch(units)],
        ),
        out_shape=[shape_of(PARTS * TILE, features)] * 2 + [shape_of(TILE, features)] * count
        + [shape_of(8, units, dtype=F32), shape_of(2, units, features)],
        cost_estimate=cost(15e9, 12e6, 2e6),
        name="feed_near",
    )


def far_body(me_ref, x0_ref, x1_ref, g_ref, inner_ref, vec_ref, outer_ref, *rest):
    left_ref, right_ref, out0_ref, out1_ref, back0_ref, back1_ref, sum_ref = rest[-7:]
    i = pl.program_id(0)
    for n, x_ref in enumerate((x0_ref, x1_ref)):
        @pl.when(i == n)
        def _(x_ref=x_ref):
            left_ref[1] = x_ref[...]

    right_ref[0] = g_ref[...]
    act, dh, out, back = feed_piece(left_ref[1], g_ref[...], inner_ref, vec_ref, outer_ref)
    left_ref[0] = act
    right_ref[1] = dh
    sums = fold(dh.astype(F32))
    for n, (out_ref, back_ref) in enumerate(((out0_ref, back0_ref), (out1_ref, back1_ref))):
        @pl.when(i == n)
        def _(n=n, out_ref=out_ref, back_ref=back_ref):
            sum_ref[...] = sum_ref[...] + sums if n else sums
            out_ref[...] = out
            back_ref[...] = back


def feed_far(part, me, first, second, cot, inner, vectors, outer, kept):
    features = cot.shape[1]
    units = inner.shape[1]
    rows = pl.BlockSpec((2, TILE, features), lambda i, m: (0, 2 * part + i, 0))
    piece = const((TILE, features))
    half = pl.BlockSpec((TILE, features), lambda i, m: (part, 0))
    return kernel_call(
        far_body,
        (me, first, second, cot, inner, vectors, outer, *kept),
        free_in=(1, 2),
        free_out=(5,),
        grid_spec=pltpu.PrefetchScalarGridSpec(
            num_scalar_prefetch=1,
            grid=(2,),
            in_specs=[
                piece, piece,
                pl.BlockSpec((TILE, features), lambda i, m: (4 * part + (m[0] ^ (2 + i)), 0)),
                const(inner.shape), const(vectors.shape), const(outer.shape),
            ] + [pl.BlockSpec(memory_space=pl.ANY)] * len(kept),
            out_specs=[rows, rows, half, half, piece, piece, const((8, units))],
        ),
        out_shape=[shape_of(2, 2 * PARTS * TILE, features)] * 2 + [shape_of(PARTS * TILE, features)] * 2
        + [shape_of(TILE, features)] * 2 + [shape_of(8, units, dtype=F32)],
        input_output_aliases={7 + n: n for n in range(len(kept))},
        cost_estimate=cost(5e9, 8e6, 1e6),
        name="feed_far",
    )


def feed_grad_body(left_ref, right_ref, before_ref, *rest):
    rest[-1][0] = (tn(left_ref[0], right_ref[0]) + before_ref[0].astype(F32)).astype(BF16)


def feed_grad(left, right, before, after):
    _, rows, features = left.shape
    both = pl.BlockSpec((1, rows, features), lambda i: (i, 0, 0))
    square = pl.BlockSpec((1, features, features), lambda i: (i, 0, 0))
    return kernel_call(
        feed_grad_body,
        (left, right, before, *after),
        free_in=tuple(range(3, 3 + len(after))),
        grid=(2,),
        in_specs=[both, both, square] + [pl.BlockSpec(memory_space=pl.ANY)] * len(after),
        out_specs=[square],
        out_shape=[shape_of(*before.shape)],
        cost_estimate=cost(5e9, 10e6),
        name="feed_grad",
    )[0]


def back_body(me_ref, b0_ref, b1_ref, b2_ref, residual_ref, g_ref, vec_ref, w0_ref, w1_ref, w2_ref, w3_ref,
              grad_ref, low_ref, a0_ref, a1_ref, a2_ref, a3_ref, sum_ref):
    grad_mid = b0_ref[...].astype(F32) + b1_ref[...].astype(F32) + b2_ref[...].astype(F32)
    normed, scale, _ = stats(residual_ref[...])
    upstream = g_ref[...].astype(F32)
    grad = upstream + norm_back(grad_mid, normed, scale, vec_ref[3:4, :])
    grad_ref[...] = grad
    low = grad.astype(BF16)
    low_ref[...] = low
    for w_ref, a_ref in ((w0_ref, a0_ref), (w1_ref, a1_ref), (w2_ref, a2_ref), (w3_ref, a3_ref)):
        a_ref[...] = nt(w_ref[...], low).astype(BF16)
    for n, value in enumerate((grad_mid * normed, grad_mid, grad, upstream)):
        sum_ref[8 * n:8 * n + 8] = fold(value)


def middle_back(part, me, sums, residual, cot, vectors, weights):
    features = cot.shape[1]
    piece = const((TILE, features))
    width = weights[0].shape[0]
    return kernel_call(
        back_body,
        (me, *sums, residual, cot, vectors, *weights),
        free_in=(2, 3),
        free_out=(3, 4, 5),
        grid_spec=pltpu.PrefetchScalarGridSpec(
            num_scalar_prefetch=1,
            grid=(1,),
            in_specs=[piece] * 4
            + [pl.BlockSpec((TILE, features), lambda i, m: (4 * part + m[0], 0)), const(vectors.shape)]
            + [const(v.shape) for v in weights],
            out_specs=[piece, piece] + [const((width, TILE))] * 4 + [const((32, features))],
        ),
        out_shape=[shape_of(TILE, features, dtype=F32), shape_of(TILE, features)]
        + [shape_of(width, TILE)] * 4 + [shape_of(32, features, dtype=F32)],
        cost_estimate=cost(2e9, 4e6),
        name="middle_back",
    )


def output_body(*refs):
    mixed, lows, outs = refs[:PARTS], refs[PARTS:2 * PARTS], refs[2 * PARTS:]
    for n in range(4):
        total = nn(mixed[0][n], lows[0][...])
        for p in range(1, PARTS):
            total = total + nn(mixed[p][n], lows[p][...])
        outs[n][...] = total.astype(BF16)


def output_grad(mixed, lows):
    width, features = mixed[0].shape[1], lows[0].shape[1]
    return kernel_call(
        output_body,
        (*mixed, *lows),
        free_out=(1, 3),
        out_shape=[shape_of(width, features)] * 4,
        cost_estimate=cost(2e9, 4e6),
        name="output_grad",
    )


def tail_body(me_ref, g_ref, wq_ref, wk_ref, wv_ref, x_ref, stat_ref, *rest):
    early, units = rest[:PARTS], rest[PARTS:2 * PARTS + 1]
    o0_ref, o1_ref, o2_ref, o3_ref, apart_ref, vec_ref, sum_ref, row_ref = rest[-8:]
    i, p = pl.program_id(0), pl.program_id(1)
    grads = g_ref[...]
    width = wq_ref.shape[0]
    value = tn(grads[:width], wq_ref[...]) + tn(grads[width:2 * width], wk_ref[...])
    value = value + tn(grads[2 * width:], wv_ref[...])

    @pl.when((i == 0) & (p == 0))
    def _():
        row_ref[...] = jnp.zeros_like(row_ref)
        sum_ref[...] = jnp.zeros_like(sum_ref)

    row_ref[...] += nt(jnp.ones((8, grads.shape[1]), BF16), grads)
    normed = (x_ref[...].astype(F32) - stat_ref[:, 0:1]) * stat_ref[:, 1:2]
    sum_ref[:8] += fold(value * normed)
    sum_ref[8:] += fold(value)
    value = value.astype(BF16)
    for step, o_ref in enumerate((o3_ref, o2_ref, o1_ref, o0_ref)):
        @pl.when(i == step)
        def _(o_ref=o_ref):
            o_ref[pl.ds(pl.multiple_of(p * TILE, TILE), TILE), :] = value

    @pl.when((i == 3) & (p == PARTS - 1))
    def _():
        row = lax.broadcasted_iota(jnp.int32, vec_ref.shape, 0)
        vectors = jnp.zeros(vec_ref.shape, F32)
        before = early[0][...]
        for ref in early[1:]:
            before = before + ref[...]
        parts = [before[8 * n:8 * n + 8] for n in range(4)] + [sum_ref[:8], sum_ref[8:]]
        for n, part in enumerate(parts):
            vectors = jnp.where(row == n, jnp.sum(part, axis=0, keepdims=True), vectors)
        vec_ref[...] = vectors
        inside = units[0][...]
        for ref in units[1:]:
            inside = inside + ref[...]
        apart_ref[...] = jnp.where(row == 6, jnp.sum(inside, axis=0, keepdims=True), 0.0)
        apart_ref[7:8, :row_ref.shape[1]] = row_ref[0:1]
        o3_ref[PARTS * TILE:] = paired(vectors)


def tail(me, grads, wq, wk, wv, tokens, stat, early, units, after):
    deep = grads.shape[0]
    features = wq.shape[1]
    share = const((PARTS * TILE, features))
    more = const((PARTS * TILE + 16, features))
    at = lambda i, p, m: 4 * p + (m[0] ^ (3 - i))
    return kernel_call(
        tail_body,
        (me, grads, wq, wk, wv, tokens, stat, *early, *units, *after),
        free_out=(1, 3),
        grid_spec=pltpu.PrefetchScalarGridSpec(
            num_scalar_prefetch=1,
            grid=(4, PARTS),
            in_specs=[pl.BlockSpec((deep, TILE), lambda i, p, m: (0, at(i, p, m))),
                      const(wq.shape), const(wk.shape), const(wv.shape),
                      pl.BlockSpec((TILE, features), lambda i, p, m: (at(i, p, m), 0)),
                      pl.BlockSpec((TILE, WIDE), lambda i, p, m: (at(i, p, m), 0))]
            + [const(v.shape) for v in (*early, *units)] + [pl.BlockSpec(memory_space=pl.ANY)] * len(after),
            out_specs=[share, share, share, more, const((8, features)), const((8, features))],
            scratch_shapes=[pltpu.VMEM((16, features), F32), pltpu.VMEM((8, deep), F32)],
        ),
        out_shape=[shape_of(PARTS * TILE, features)] * 3 + [shape_of(PARTS * TILE + 16, features)]
        + [shape_of(8, features, dtype=F32)] * 2,
        cost_estimate=cost(4e9, 10e6),
        name="tail",
    )


def chip_body(one_ref, two_ref, vec_ref, *rest):
    out_ref = rest[-1]
    rows = one_ref.shape[0]
    out_ref[:rows] = (one_ref[...].astype(F32) + two_ref[:rows].astype(F32)).astype(BF16)
    out_ref[rows:] = paired(vec_ref[...] + joined(two_ref[rows:]))


def chip_sum(one, two, vectors, after):
    return kernel_call(
        chip_body,
        (one, two, vectors, *after),
        free_in=(1,) + tuple(range(3, 3 + len(after))),
        free_out=(0,),
        grid=(1,),
        in_specs=[const(one.shape), const(two.shape), const(vectors.shape)]
        + [pl.BlockSpec(memory_space=pl.ANY)] * len(after),
        out_specs=[const(two.shape)],
        out_shape=[shape_of(*two.shape)],
        name="chip_sum",
    )[0]


def halves_body(xz_ref, g_ref, go_ref, *rest):
    keep_ref, send_ref = rest[-2:]
    width = go_ref.shape[0]
    for to_ref, half in ((keep_ref, xz_ref[0]), (send_ref, 1 - xz_ref[0])):
        @pl.when(half == 0)
        def _(to_ref=to_ref):
            to_ref[...] = g_ref[:2 * width]

        @pl.when(half == 1)
        def _(to_ref=to_ref):
            to_ref[:width] = g_ref[2 * width:]
            to_ref[width:] = go_ref[...]


def halves(xz, grad_weights, grad_output, after):
    width, features = grad_output.shape
    half = const((2 * width, features))
    return kernel_call(
        halves_body,
        (xz, grad_weights, grad_output, *after),
        free_in=(1, 2, 3),
        grid_spec=pltpu.PrefetchScalarGridSpec(
            num_scalar_prefetch=1,
            grid=(1,),
            in_specs=[const(grad_weights.shape), const(grad_output.shape)]
            + [pl.BlockSpec(memory_space=pl.ANY)] * len(after),
            out_specs=[half, half],
        ),
        out_shape=[shape_of(2 * width, features)] * 2,
        cost_estimate=cost(1e6, 4e6),
        name="halves",
    )


def quarter_body(count, xz_ref, one_ref, two_ref, *rest):
    rows = one_ref.shape[0] // count
    for n, out_ref in enumerate(rest[-count:]):
        at = pl.ds(pl.multiple_of(lax.rem(xz_ref[1] + n, count) * rows, rows), rows)
        out_ref[...] = (one_ref[at, :].astype(F32) + two_ref[at, :].astype(F32)).astype(BF16)


def quarters(xz, one, two, count, after):
    rows, features = one.shape

    def body(*refs):
        quarter_body(count, *refs)

    return kernel_call(
        body,
        (xz, one, two, *after),
        free_in=(2, 3, 4),
        grid_spec=pltpu.PrefetchScalarGridSpec(
            num_scalar_prefetch=1,
            grid=(1,),
            in_specs=[const(one.shape), const(two.shape)] + [pl.BlockSpec(memory_space=pl.ANY)] * len(after),
            out_specs=[const((rows // count, features))] * count,
        ),
        out_shape=[shape_of(rows // count, features)] * count,
        cost_estimate=cost(1e6, 2e6),
        name="quarters",
    )


def paired(value):
    return jnp.concatenate(split(value, 2), axis=0).astype(BF16)


def joined(both):
    both = both.astype(F32)
    half = both.shape[0] // 2
    return both[:half] + both[half:]


def second_body(count, *refs):
    one_ref, two_ref, apart_ref, out_ref = refs[count], refs[count + 1], refs[count + 2], refs[-1]
    rows = refs[0].shape[0]
    total = refs[0][...].astype(F32)
    for ref in refs[1:count]:
        total = total + ref[...].astype(F32)
    out_ref[:rows] = total.astype(BF16)
    out_ref[rows:] = paired(joined(one_ref[...]) + joined(two_ref[...]) + apart_ref[...])


def second(parts, one, two, apart, after):
    count = len(parts)
    rows, features = parts[0].shape
    last = pl.BlockSpec((16, features), lambda i: (one.shape[0] // 16 - 1, 0))

    def body(*refs):
        second_body(count, *refs)

    return kernel_call(
        body,
        (*parts, one, two, apart, *after),
        free_in=tuple(range(1, count + 2)) + tuple(range(count + 3, count + 3 + len(after))),
        grid=(1,),
        in_specs=[const((rows, features))] * count + [last, last, const(apart.shape)]
        + [pl.BlockSpec(memory_space=pl.ANY)] * len(after),
        out_specs=[const((rows + 16, features))],
        out_shape=[shape_of(rows + 16, features)],
        name="second",
    )[0]


def third_body(count, xz_ref, *refs):
    out_ref = refs[-1]
    step = out_ref.shape[0] - (refs[0].shape[0] * count - out_ref.shape[0]) // (count - 1)
    rows = step // count
    sums = None
    for n, ref in enumerate(refs[:count]):
        place_at = lax.rem(xz_ref[1] + count - n, count)
        out_ref[pl.ds(pl.multiple_of(place_at * rows, rows), rows), :] = ref[:rows]
        value = joined(ref[rows:])
        sums = value if sums is None else sums + value
    out_ref[step:] = paired(sums)


def third(xz, pieces, extra, after):
    count = len(pieces)
    rows, features = pieces[0].shape
    total = (rows - extra) * count + extra

    def body(*refs):
        third_body(count, *refs)

    return kernel_call(
        body,
        (xz, *pieces, *after),
        free_in=tuple(range(1, count + 1)),
        grid_spec=pltpu.PrefetchScalarGridSpec(
            num_scalar_prefetch=1,
            grid=(1,),
            in_specs=[const((rows, features))] * count + [pl.BlockSpec(memory_space=pl.ANY)] * len(after),
            out_specs=[const((total, features))],
        ),
        out_shape=[shape_of(total, features)],
        name="third",
    )[0]


def ready_body(xz_ref, mine_ref, other_ref, *rest):
    outs = rest[-14:]
    width = outs[0].shape[0]
    for n, out_ref in enumerate(outs[:4]):
        rows = slice(n % 2 * width, (n % 2 + 1) * width)
        for to_ref, chosen in ((mine_ref, xz_ref[0] == n // 2), (other_ref, xz_ref[0] != n // 2)):
            @pl.when(chosen)
            def _(to_ref=to_ref, out_ref=out_ref, rows=rows):
                out_ref[...] = to_ref[rows].astype(F32)

    small = joined(mine_ref[2 * width:]) + joined(other_ref[2 * width:])
    for n, out_ref in enumerate(outs[4:11]):
        out_ref[...] = small[n]
    for n, out_ref in enumerate(outs[11:]):
        out_ref[...] = small[7, n * width:(n + 1) * width]


def ready(xz, mine, other, width, after):
    rows, features = mine.shape
    sizes = [(features,)] * 7 + [(width,)] * 3
    return kernel_call(
        ready_body,
        (xz, mine, other, *after),
        free_in=(2,),
        grid_spec=pltpu.PrefetchScalarGridSpec(
            num_scalar_prefetch=1,
            grid=(1,),
            in_specs=[const(mine.shape), const(other.shape)] + [pl.BlockSpec(memory_space=pl.ANY)] * len(after),
            out_specs=[const((width, features))] * 4 + [const(size) for size in sizes],
        ),
        out_shape=[shape_of(width, features, dtype=F32)] * 4 + [shape_of(*size, dtype=F32) for size in sizes],
        cost_estimate=cost(1e6, 4e6),
        name="ready",
    )


def final_body(me_ref, b0_ref, b1_ref, b2_ref, x_ref, *rest):
    grad_refs, vec_ref, out_ref = rest[:PARTS], rest[PARTS], rest[-1]
    p = pl.program_id(0)
    grad_attend = b0_ref[...].astype(F32) + b1_ref[...].astype(F32) + b2_ref[...].astype(F32)
    normed, scale, _ = stats(x_ref[...].astype(F32))
    back = norm_back(grad_attend, normed, scale, vec_ref[0:1, :])
    for n, grad_ref in enumerate(grad_refs):
        @pl.when(p == n)
        def _(grad_ref=grad_ref):
            out_ref[...] = (grad_ref[...] + back).astype(BF16)


def final(me, sums, tokens, grads, vectors, after):
    features = tokens.shape[1]
    rows = pl.BlockSpec((TILE, features), lambda p, m: (p, 0))
    return kernel_call(
        final_body,
        (me, *sums, tokens, *grads, vectors, *after),
        free_in=(2, 3) + tuple(range(6 + PARTS, 6 + PARTS + len(after))),
        free_out=(0,),
        grid_spec=pltpu.PrefetchScalarGridSpec(
            num_scalar_prefetch=1,
            grid=(PARTS,),
            in_specs=[rows] * 3 + [pl.BlockSpec((TILE, features), lambda p, m: (4 * p + m[0], 0))]
            + [const((TILE, features))] * PARTS + [const(vectors.shape)]
            + [pl.BlockSpec(memory_space=pl.ANY)] * len(after),
            out_specs=[rows],
        ),
        out_shape=[shape_of(PARTS * TILE, features)],
        cost_estimate=cost(1e8, 5e6),
        name="final",
    )[0]


def place_body(me_ref, p0_ref, p1_ref, p2_ref, p3_ref, *rest):
    out_ref = rest[-1]
    for step, p_ref in enumerate((p0_ref, p1_ref, p2_ref, p3_ref)):
        @pl.when(pl.program_id(0) == step)
        def _(p_ref=p_ref):
            at = pl.ds(pl.multiple_of(pl.program_id(1) * TILE, TILE), TILE)
            out_ref[...] = p_ref[at, :].astype(out_ref.dtype)


def place(me, shares, dtype, after):
    rows, features = shares[0].shape
    return kernel_call(
        place_body,
        (me, *shares, *after),
        free_in=(1, 2, 3, 4),
        grid_spec=pltpu.PrefetchScalarGridSpec(
            num_scalar_prefetch=1,
            grid=(4, PARTS),
            in_specs=[const((rows, features))] * 4 + [pl.BlockSpec(memory_space=pl.ANY)] * len(after),
            out_specs=pl.BlockSpec((TILE, features), lambda i, p, m: (4 * p + (m[0] ^ i), 0)),
        ),
        out_shape=shape_of(4 * rows, features, dtype=dtype),
        cost_estimate=cost(1e6, 9e6),
        name="place",
    )


def fence_body(*refs):
    pass


def fence(value, *after, space=pltpu.HBM):
    anywhere = pl.BlockSpec(memory_space=pl.ANY)
    return pl.pallas_call(
        fence_body,
        in_specs=[anywhere] * (1 + len(after)),
        out_specs=anywhere,
        out_shape=space(value.shape, value.dtype),
        input_output_aliases={0: 0},
        name="fence",
    )(pltpu.with_memory_space_constraint(value, space), *after)


def other_core(value):
    return lax.ppermute(value, "core", SWAP)


def other_chip(value):
    return lax.ppermute(value, "y", SWAP)


def crosswise(value):
    return lax.ppermute(value, MP, [(n, n ^ 3) for n in range(4)])


def exchange(pieces):
    return [pieces[0], other_core(pieces[1]), other_chip(pieces[2]), crosswise(pieces[3])]


def gather_sum(pieces):
    near = other_core(pieces[1])
    far = (pieces[2].astype(F32) + other_core(pieces[3]).astype(F32)).astype(BF16)
    return [pieces[0], near, other_chip(far)], far


def spread(value):
    far = other_chip(value)
    return [value, other_core(value), far, other_core(far)]


def pick(values, at):
    return lax.dynamic_index_in_dim(values, at, 0, keepdims=False)


def turned(values, way):
    size = lax.axis_size("z")
    return lax.ppermute(values, "z", [(n, (n + way) % size) for n in range(size)])


def sum_first(xz, keep, got, after):
    size = lax.axis_size("z")
    if size > 4:
        return [lax.psum(keep + got, "z")]
    return quarters(xz, keep, got, size, after)


def gather_z(value):
    size = lax.axis_size("z")
    if size > 4:
        return [lax.all_gather(value, "z", axis=0, tiled=True)]
    return [turned(value, way) if way else value for way in range(size)]


def local(
    tokens,
    segment_ids,
    gain_one,
    bias_one,
    query_weight,
    query_bias,
    key_weight,
    value_weight,
    value_bias,
    output_weight,
    output_bias,
    gain_two,
    bias_two,
    inner_weight,
    inner_bias,
    outer_weight,
    outer_bias,
    cotangent,
):
    _, length, features = tokens.shape
    width = query_weight.shape[1]
    heads = width // HEAD
    tokens = tokens.reshape(length, features)
    cot = cotangent.reshape(length, features)
    at = lax.axis_index(MP).astype(jnp.int32)
    me = at[None]
    apart = jnp.concatenate([query_bias, value_bias, jnp.zeros((features - 2 * width,), F32)])
    vectors = jnp.concatenate([gain_one, bias_one, output_bias, gain_two, bias_two, outer_bias, apart, inner_bias])
    vectors = vectors.reshape(8, features)
    wq, wk, wv = query_weight.T, key_weight.T, value_weight.T

    output_weights = spread(output_weight)
    attend_in, qt, kt, vt, kn, vn, stat = project(tokens, segment_ids, vectors, wq, wk, wv, heads)

    parts = range(PARTS)
    attended, extras, fours = [], [], []
    for p in parts:
        out, extra, *four = attend_forward(p, me, segment_ids, qt, kn, vt, output_weights[1:3] if p == 0 else ())
        attended.append(out)
        extras.append(extra)
        fours.append(exchange(four))
    mixed, residuals, pieces = [], [], []
    for p in parts:
        residual, own, together = middle(p, me, tokens, fours[p], output_weights, vectors, extras[p + 1:])
        mixed.append(together)
        residuals.append(residual)
        pieces.append([own, other_core(own), other_chip(own)])

    backs = {}
    *outs, b00, b01, b10, b11, near_sum, near_grad = feed_near(
        me, [pieces[p][n] for p in parts for n in (0, 1)], cot, inner_weight, vectors, outer_weight
    )
    backs[0, 0], backs[0, 1], backs[1, 0], backs[1, 1] = b00, b01, b10, b11
    sums, kept, gathered, far_sums = [near_sum], (), [], [b00]
    for p in parts:
        far = fence(pieces[p][2], far_sums[-1], space=pltpu.VMEM)
        *kept, backs[p, 2], backs[p, 3], far_sum = feed_far(
            p, me, far, other_core(far), cot, inner_weight, vectors, outer_weight, kept
        )
        sums.append(far_sum)
        if p:
            backs[p, 3] = fence(backs[p, 3], gathered[-1][2], space=pltpu.VMEM)
        summed, far_sum = gather_sum([backs[p, n] for n in range(4)])
        gathered.append(summed)
        far_sums.append(far_sum)
    far_sums = far_sums[1:]
    left, right, *far_outs = kept
    outs += far_outs
    feed_sum = feed_grad(left, right, near_grad, far_sums).reshape(-1, features)
    feed_sum = lax.psum_scatter(feed_sum, DP, scatter_dimension=0, tiled=True)
    grad_residuals, lows, grads_attended, inner_sums = [], [], [], []
    for p in parts:
        grad, low, a0, a1, a2, a3, vector = middle_back(
            p, me, gathered[p], residuals[p], cot, vectors, output_weights
        )
        grad_residuals.append(grad)
        lows.append(low)
        inner_sums.append(vector)
        grads_attended.append(exchange([a0, a1, a2, a3]))

    near = other_core(fence(outs[1], *far_sums))
    far = (outs[2].astype(F32) + other_core(fence(outs[3], *far_sums)).astype(F32)).astype(BF16)
    far = fence(far, lows[-1], space=pltpu.VMEM)
    part = output_grad(mixed, lows)
    earlier = attend_backward(0, me, segment_ids, qt, extras[0], kn, kt, vn, attended[0], grads_attended[0], (),
                              (far, near, part[0]))
    there = other_chip(far)
    part_far = fence(part[2], earlier[0])
    part_far = (part_far.astype(F32) + other_core(part[3]).astype(F32)).astype(BF16)
    part_near = other_core(part[1])
    grads = attend_backward(1, me, segment_ids, qt, extras[1], kn, kt, vn, attended[1], grads_attended[1], earlier,
                            (part_near, part_far, there))

    xz = jnp.stack([lax.axis_index("x"), lax.axis_index("z")]).astype(jnp.int32)
    part_across = other_chip(part_far)
    grad_output = fence(part[0], grads).astype(F32) + part_near.astype(F32) + part_across.astype(F32)
    keep, send = halves(xz, nn(grads, attend_in).astype(BF16), grad_output.astype(BF16), ())
    result = jnp.concatenate(residuals) + fence(outs[0], send).astype(F32) + near.astype(F32)
    result = (result + there.astype(F32) + outer_bias).astype(BF16)
    near, far = other_core(result), other_chip(result)
    got = lax.ppermute(send, "x", SWAP)
    back_own, back_near, back_far, back_across, apart, summed = tail(
        me, grads, wq, wk, wv, tokens, stat, inner_sums, sums, (send,)
    )
    quarter = sum_first(xz, keep, got, (near, far, apart))
    feed_sum = lax.all_gather(fence(feed_sum, quarter[-1]), DP, axis=0, tiled=True)
    feed_sum = (feed_sum[:features].astype(F32), feed_sum[features:].astype(F32))
    back_across = other_core(fence(back_across, quarter[-1], space=pltpu.VMEM))
    back_far = chip_sum(back_far, back_across, summed, ())
    back_there = other_chip(back_far)
    share = final(me, [back_own, other_core(back_near), back_there], tokens, grad_residuals, vectors, ())
    if len(quarter) > 1:
        turns = [quarter[0]] + [turned(part, n + 1) for n, part in enumerate(quarter[1:])]
        held = second(turns, back_far, back_there, apart, (share,))
        layer_out = place(me, [result, near, far, other_core(far)], BF16, (held,))
        mine = third(xz, gather_z(held), 16, (layer_out,))
    else:
        small = joined(back_far[-16:]) + joined(back_there[-16:]) + apart
        layer_out = place(me, [result, near, far, other_core(far)], BF16, ())
        mine = jnp.concatenate([quarter[0], paired(lax.psum(small, "z"))])
    share = fence(share, held if len(quarter) > 1 else mine, space=pltpu.VMEM)
    near, far = other_core(share), fence(other_chip(share), mine, space=pltpu.VMEM)
    input_grad = place(me, [share, near, far, other_core(far)], F32, (mine,))
    *wide, two_gain, two_bias, output_sum, outer_bias, one_gain, one_bias, inner_bias, query, _, value = ready(
        xz, mine, lax.ppermute(mine, "x", SWAP), width, feed_sum
    )
    return (
        layer_out.reshape(1, length, features),
        input_grad.reshape(1, length, features),
        one_gain,
        one_bias,
        wide[0].T,
        query,
        wide[1].T,
        wide[2].T,
        value,
        wide[3],
        output_sum,
        two_gain,
        two_bias,
        feed_sum[1],
        inner_bias,
        feed_sum[0],
        outer_bias,
    )


def solution(mesh):
    rows = mesh.shape["dp"]
    inner = Mesh(mesh.devices.reshape(rows // 2, 2, 2, 2), DP + MP)
    placed = (
        P(DP, None, None),
        P(DP, None),
        P(),
        P(),
        P(None, MP),
        P(MP),
        P(None, MP),
        P(None, MP),
        P(MP),
        P(MP, None),
        P(),
        P(),
        P(),
        P(None, MP),
        P(MP),
        P(MP, None),
        P(),
        P(DP, None, None),
    )
    return jax.shard_map(
        local,
        mesh=inner,
        in_specs=placed,
        out_specs=(
            P(DP, None, None),
            P(DP, None, None),
            P(),
            P(),
            P(None, MP),
            P(MP),
            P(None, MP),
            P(None, MP),
            P(MP),
            P(MP, None),
            P(),
            P(),
            P(),
            P(None, MP),
            P(MP),
            P(MP, None),
            P(),
        ),
        check_vma=False,
    )
```

```python
import jax
import jax.numpy as jnp
from jax import lax
from jax.experimental import pallas as pl
from jax.experimental.pallas import tpu as pltpu
from jax.sharding import Mesh
from jax.sharding import PartitionSpec as P

HEAD = 64
WIDE = 128
TILE = 256
PARTS = 2
MASKED = 1e30
SCALE = 1
F32 = jnp.float32
BF16 = jnp.bfloat16
DP = ("z", "x")
MP = ("y", "core")
SWAP = [(0, 1), (1, 0)]


def nn(left, right):
    return lax.dot_general(left, right, (((1,), (0,)), ((), ())), preferred_element_type=F32)


def nt(left, right):
    return lax.dot_general(left, right, (((1,), (1,)), ((), ())), preferred_element_type=F32)


def tn(left, right):
    return lax.dot_general(left, right, (((0,), (0,)), ((), ())), preferred_element_type=F32)


def stats(values):
    mean = jnp.mean(values, axis=-1, keepdims=True)
    center = values - mean
    scale = lax.rsqrt(jnp.mean(center * center, axis=-1, keepdims=True) + 1e-05)
    return center * scale, scale, mean


def norm_back(grad_out, normed, scale, gain):
    upstream = grad_out * gain
    return scale * (
        upstream
        - jnp.mean(upstream, axis=-1, keepdims=True)
        - normed * jnp.mean(upstream * normed, axis=-1, keepdims=True)
    )


def fold(values):
    return jnp.sum(values.reshape(-1, 8, values.shape[-1]), axis=0)


def split(value, parts):
    out = []
    for _ in range(parts):
        piece = value.astype(BF16).astype(F32)
        out.append(piece)
        value = value - piece
    return out


def const(shape):
    return pl.BlockSpec(shape, lambda *_: (0,) * len(shape))


def shape_of(*dims, dtype=BF16):
    return jax.ShapeDtypeStruct(dims, dtype)


def params(mib=40):
    return pltpu.CompilerParams(vmem_limit_bytes=mib << 20)


def kernel_call(body, values, free_in=(), free_out=(), **options):
    shapes = options.pop("out_shape")
    many = isinstance(shapes, (list, tuple))
    shapes = [s if n in free_out else pltpu.HBM(s.shape, s.dtype) for n, s in enumerate(shapes if many else [shapes])]
    values = [
        v if n in free_in or v.dtype == jnp.int32 else pltpu.with_memory_space_constraint(v, pltpu.HBM)
        for n, v in enumerate(values)
    ]
    return pl.pallas_call(
        body, out_shape=shapes if many else shapes[0], compiler_params=params(), **options
    )(*values)


def cost(flops, moved, special=0):
    return pl.CostEstimate(flops=int(flops * SCALE), bytes_accessed=int(moved * SCALE), transcendentals=0)


def project_body(x_ref, seg_ref, vec_ref, wq_ref, wk_ref, wv_ref,
                 ai_ref, qt_ref, kt_ref, vt_ref, kn_ref, vn_ref, stat_ref):
    heads = kn_ref.shape[0]
    width = heads * HEAD
    tile = x_ref.shape[0]
    normed, scale, mean = stats(x_ref[...].astype(F32))
    lane = lax.broadcasted_iota(jnp.int32, stat_ref.shape, 1)
    stat_ref[...] = jnp.where(lane == 0, mean, scale)
    ai = (normed * vec_ref[0:1, :] + vec_ref[1:2, :]).astype(BF16)
    ai_ref[...] = ai
    column = vec_ref[...].T[:2 * width, 6:7]
    queries = ((nt(wq_ref[...], ai) + column[:width]).astype(BF16)).astype(F32) * HEAD ** -0.5
    keys = nt(wk_ref[...], ai)
    kt_ref[...] = keys.astype(BF16)
    values = nt(wv_ref[...], ai) + column[width:]
    row = lax.broadcasted_iota(jnp.int32, (HEAD, tile), 0)
    same = jnp.where(row == seg_ref[...], 1.0, 0.0)
    mask = jnp.where(row < 8, (same - 1.0) * MASKED, jnp.where(row < 11, 1.0, 0.0))
    ones = jnp.where(row < 2, 1.0, 0.0)
    first = jnp.where(row[:16] == 0, 1.0, 0.0).astype(BF16)
    for h in range(heads):
        rows = slice(h * HEAD, (h + 1) * HEAD)
        qt_ref[h, :HEAD, :] = queries[rows].astype(BF16)
        qt_ref[h, HEAD:, :] = same.astype(BF16)
        vt_ref[h, :HEAD, :] = values[rows].astype(BF16)
        vt_ref[h, HEAD:, :] = first
        kn_ref[h] = jnp.concatenate([keys[rows], mask], axis=0).T.astype(BF16)
        vn_ref[h] = jnp.concatenate([values[rows], ones], axis=0).T.astype(BF16)


def project(tokens, seg_row, vectors, wq, wk, wv, heads):
    length, features = tokens.shape
    width = heads * HEAD
    return kernel_call(
        project_body,
        (tokens, seg_row, vectors, wq, wk, wv),
        grid=(length // TILE,),
        in_specs=[
            pl.BlockSpec((TILE, features), lambda i: (i, 0)),
            pl.BlockSpec((1, TILE), lambda i: (0, i)),
            const(vectors.shape), const(wq.shape), const(wk.shape), const(wv.shape),
        ],
        out_specs=[
            pl.BlockSpec((TILE, features), lambda i: (i, 0)),
            pl.BlockSpec((heads, WIDE, TILE), lambda i: (0, 0, i)),
            pl.BlockSpec((width, TILE), lambda i: (0, i)),
            pl.BlockSpec((heads, HEAD + 16, TILE), lambda i: (0, 0, i)),
            pl.BlockSpec((heads, TILE, WIDE), lambda i: (0, i, 0)),
            pl.BlockSpec((heads, TILE, WIDE), lambda i: (0, i, 0)),
            pl.BlockSpec((TILE, WIDE), lambda i: (i, 0)),
        ],
        out_shape=[
            shape_of(length, features),
            shape_of(heads, WIDE, length),
            shape_of(width, length),
            shape_of(heads, HEAD + 16, length),
            shape_of(heads, length, WIDE),
            shape_of(heads, length, WIDE),
            shape_of(length, WIDE, dtype=F32),
        ],
        cost_estimate=cost(6e9, 14e6),
        name="project",
    )


def key_range(seg_ref, seg_all, i):
    first = seg_ref[0, i * TILE]
    last = seg_ref[0, i * TILE + TILE - 1]
    before = jnp.sum(jnp.where(seg_all < first, 1.0, 0.0)).astype(jnp.int32)
    until = jnp.sum(jnp.where(seg_all <= last, 1.0, 0.0)).astype(jnp.int32)
    return before // TILE, (until + TILE - 1) // TILE


def by_pairs(low, high, step, carry):
    keys = lambda kb: pl.ds(pl.multiple_of(kb * TILE, TILE), TILE)
    pairs = (high - low) // 2
    carry = lax.fori_loop(0, pairs, lambda n, c: step([keys(low + 2 * n), keys(low + 2 * n + 1)], c), carry)
    return lax.fori_loop(low + 2 * pairs, high, lambda kb, c: step([keys(kb)], c), carry)


def shifted(one_hot, pieces):
    row = lax.broadcasted_iota(jnp.int32, one_hot.shape, 0)
    value = one_hot
    for n, piece in enumerate(pieces):
        value = jnp.where(row == 8 + n, piece, value)
    return value.astype(BF16)


def forward_body(offset, me_ref, segs_ref, seg_ref, qt_ref, kn_ref, vt_ref, *rest):
    out_ref, extra_ref, o0_ref, o1_ref, o2_ref, o3_ref, acc_ref = rest[-7:]
    heads, _, tile = qt_ref.shape
    i = pl.program_id(0)
    low, high = key_range(segs_ref, seg_ref[...], i + offset)
    acc_ref[...] = jnp.zeros_like(acc_ref)

    def step(keys, tops):
        scores = [[nn(kn_ref[h, at, :], qt_ref[h]) for at in keys] for h in range(heads)]
        new_tops = []
        for h in range(heads):
            top = tops[h]
            for score in scores[h]:
                top = jnp.maximum(top, jnp.max(score, axis=0, keepdims=True))
            new_tops.append(top)
        powered = [[jnp.exp(score - new_tops[h]).astype(BF16) for score in scores[h]] for h in range(heads)]
        for h in range(heads):
            total = acc_ref[h] * jnp.exp(tops[h] - new_tops[h])
            for at, power in zip(keys, powered[h]):
                total = total + nn(vt_ref[h, :, at], power)
            acc_ref[h] = total
        return tuple(new_tops)

    tops = by_pairs(low, high, step, (jnp.full((1, tile), -jnp.inf, F32),) * heads)
    for h in range(heads):
        total = acc_ref[h, HEAD:HEAD + 1, :]
        out_ref[0, h * HEAD:(h + 1) * HEAD, :] = (acc_ref[h, :HEAD, :] / total).astype(BF16)
        one_hot = qt_ref[h, HEAD:HEAD + 16, :].astype(F32)
        extra_ref[h] = shifted(one_hot, split(-(tops[h] + jnp.log(total)), 3))
    for n, o_ref in enumerate((o0_ref, o1_ref, o2_ref, o3_ref)):
        @pl.when((i ^ me_ref[0]) == n)
        def _(o_ref=o_ref):
            o_ref[...] = out_ref[0]


def attend_forward(part, me, seg_row, qt, kn, vt, after):
    heads, _, length = qt.shape
    width = heads * HEAD
    count = length // TILE // PARTS
    offset = part * count

    def body(*refs):
        forward_body(offset, *refs)

    return kernel_call(
        body,
        (me, seg_row, seg_row, qt, kn, vt, *after),
        free_in=tuple(range(6, 6 + len(after))),
        free_out=(3, 4, 5),
        grid_spec=pltpu.PrefetchScalarGridSpec(
            num_scalar_prefetch=1,
            grid=(count,),
            in_specs=[
                pl.BlockSpec(memory_space=pltpu.SMEM),
                const((1, length)),
                pl.BlockSpec((heads, WIDE, TILE), lambda i, m: (0, 0, i + offset)),
                const(kn.shape), const(vt.shape),
            ] + [pl.BlockSpec(memory_space=pl.ANY)] * len(after),
            out_specs=[
                pl.BlockSpec((1, width, TILE), lambda i, m: (i, 0, 0)),
                pl.BlockSpec((heads, 16, TILE), lambda i, m: (0, 0, i)),
            ] + [const((width, TILE))] * 4,
            scratch_shapes=[pltpu.VMEM((heads, HEAD + 16, TILE), F32)],
        ),
        out_shape=[shape_of(count, width, TILE), shape_of(heads, 16, count * TILE)] + [shape_of(width, TILE)] * 4,
        cost_estimate=cost(9e9, 5e6, 4e6),
        name="attend_forward",
    )


def backward_body(part, me_ref, segs_ref, seg_ref, qt_ref, extra_ref, kn_ref, kt_ref, vn_ref, out_ref,
                  g0_ref, g1_ref, g2_ref, g3_ref, *rest):
    heads, _, tile = qt_ref.shape
    width = heads * HEAD
    length = kt_ref.shape[1]
    if part == 0:
        dq_out, dk_ref, dv_ref, qa_ref, da_ref, dq_ref = rest[-6:]
    else:
        dq_in, dk_in, dv_in = rest[:3]
        grads_ref, qa_ref, da_ref, dq_ref, dk_ref, dv_ref = rest[-6:]
    i = pl.program_id(0)
    count = length // TILE // PARTS
    at_here = i + part * count
    low, high = key_range(segs_ref, seg_ref[...], at_here)

    @pl.when(i == 0)
    def _():
        if part == 0:
            dk_ref[...] = jnp.zeros_like(dk_ref)
            dv_ref[...] = jnp.zeros_like(dv_ref)
        else:
            dk_ref[...] = dk_in[...]
            dv_ref[...] = dv_in[...]
            grads_ref[:width, :count * TILE] = dq_in[...]
        qa_ref[...] = jnp.zeros_like(qa_ref)
        da_ref[...] = jnp.zeros_like(da_ref)

    source = i ^ me_ref[0]
    for n, g_ref in enumerate((g0_ref, g1_ref, g2_ref, g3_ref)):
        @pl.when(source == n)
        def _(g_ref=g_ref):
            for h in range(heads):
                da_ref[h, :HEAD, :] = g_ref[h * HEAD:(h + 1) * HEAD]

    dq_ref[...] = jnp.zeros_like(dq_ref)
    row = lax.broadcasted_iota(jnp.int32, (16, tile), 0)
    for h in range(heads):
        rows = slice(h * HEAD, (h + 1) * HEAD)
        qa_ref[h, :HEAD, :] = qt_ref[h, :HEAD, :]
        qa_ref[h, HEAD:HEAD + 16, :] = extra_ref[h]
        inner = jnp.sum(da_ref[h, :HEAD, :].astype(F32) * out_ref[0, rows].astype(F32), axis=0, keepdims=True)
        first, second = split(-inner, 2)
        value = jnp.where(row == 0, first, jnp.where(row == 1, second, 0.0))
        da_ref[h, HEAD:HEAD + 16, :] = value.astype(BF16)

    def step(keys, carry):
        every = range(heads)
        rows = [slice(h * HEAD, (h + 1) * HEAD) for h in every]
        scores = [[nn(kn_ref[h, at, :], qa_ref[h]) for at in keys] for h in every]
        slopes = [[nn(vn_ref[h, at, :], da_ref[h]) for at in keys] for h in every]
        probs = [[jnp.exp(score) for score in scores[h]] for h in every]
        ds = [[(p * s).astype(BF16) for p, s in zip(probs[h], slopes[h])] for h in every]
        probs = [[p.astype(BF16) for p in probs[h]] for h in every]
        for h in every:
            total = dq_ref[rows[h]]
            for n, at in enumerate(keys):
                dv_ref[rows[h], at] += nt(da_ref[h, :HEAD, :], probs[h][n])
                dk_ref[rows[h], at] += nt(qa_ref[h, :HEAD, :], ds[h][n])
                total = total + nn(kt_ref[rows[h], at], ds[h][n])
            dq_ref[rows[h]] = total
        return carry

    by_pairs(low, high, step, 0)
    dq = (dq_ref[...] * HEAD ** -0.5).astype(BF16)
    if part == 0:
        dq_out[...] = dq
    else:
        grads_ref[:width, pl.ds(pl.multiple_of(at_here * TILE, TILE), TILE)] = dq

        @pl.when(i == pl.num_programs(0) - 1)
        def _():
            grads_ref[width:2 * width] = dk_ref[...].astype(BF16)
            grads_ref[2 * width:] = dv_ref[...].astype(BF16)


def attend_backward(part, me, seg_row, qt, extra, kn, kt, vn, out, grad, earlier, after):
    heads, _, length = qt.shape
    width = heads * HEAD
    count = length // TILE // PARTS
    offset = part * count

    def body(*refs):
        backward_body(part, *refs)

    in_specs = [
        pl.BlockSpec(memory_space=pltpu.SMEM),
        const((1, length)),
        pl.BlockSpec((heads, WIDE, TILE), lambda i, m: (0, 0, i + offset)),
        pl.BlockSpec((heads, 16, TILE), lambda i, m: (0, 0, i)),
        const(kn.shape), const(kt.shape), const(vn.shape),
        pl.BlockSpec((1, width, TILE), lambda i, m: (i, 0, 0)),
        const(grad[0].shape), const(grad[1].shape), const(grad[2].shape), const(grad[3].shape),
    ] + [const(v.shape) for v in earlier] + [pl.BlockSpec(memory_space=pl.ANY)] * len(after)
    scratch = [
        pltpu.VMEM((heads, WIDE, TILE), BF16),
        pltpu.VMEM((heads, WIDE, TILE), BF16),
        pltpu.VMEM((width, TILE), F32),
    ]
    if part == 0:
        out_specs = [pl.BlockSpec((width, TILE), lambda i, m: (0, i)), const((width, length)), const((width, length))]
        out_shape = [shape_of(width, count * TILE), shape_of(width, length, dtype=F32), shape_of(width, length, dtype=F32)]
    else:
        out_specs = const((3 * width, length))
        out_shape = shape_of(3 * width, length)
        scratch += [pltpu.VMEM((width, length), F32), pltpu.VMEM((width, length), F32)]
    return kernel_call(
        body,
        (me, seg_row, seg_row, qt, extra, kn, kt, vn, out, *grad, *earlier, *after),
        free_in=(10, 11, 12) + tuple(range(13 + len(earlier), 15 + len(earlier))),
        grid_spec=pltpu.PrefetchScalarGridSpec(
            num_scalar_prefetch=1, grid=(count,), in_specs=in_specs, out_specs=out_specs, scratch_shapes=scratch,
        ),
        out_shape=out_shape,
        cost_estimate=cost(16e9, 10e6, 4e6),
        name="attend_backward",
    )


def middle_body(me_ref, x_ref, m0_ref, m1_ref, m2_ref, m3_ref, w0_ref, w1_ref, w2_ref, w3_ref,
                vec_ref, *rest):
    residual_ref, own_ref, mixed_ref = rest[-3:]
    total = x_ref[...].astype(F32) + vec_ref[2:3, :]
    pairs = ((m0_ref, w0_ref), (m1_ref, w1_ref), (m2_ref, w2_ref), (m3_ref, w3_ref))
    for n, (m_ref, w_ref) in enumerate(pairs):
        total = total + tn(m_ref[...], w_ref[...])
        mixed_ref[n] = m_ref[...]
    residual_ref[...] = total
    normed, _, _ = stats(total)
    own_ref[...] = (normed * vec_ref[3:4, :] + vec_ref[4:5, :]).astype(BF16)


def middle(part, me, tokens, mixed, weights, vectors, after):
    features = tokens.shape[1]
    width = weights[0].shape[0]
    return kernel_call(
        middle_body,
        (me, tokens, *mixed, *weights, vectors, *after),
        free_in=(3, 4, 5),
        free_out=(1,),
        grid_spec=pltpu.PrefetchScalarGridSpec(
            num_scalar_prefetch=1,
            grid=(1,),
            in_specs=[pl.BlockSpec((TILE, features), lambda i, m: (4 * part + m[0], 0))]
            + [const(v.shape) for v in mixed] + [const(v.shape) for v in weights] + [const(vectors.shape)]
            + [pl.BlockSpec(memory_space=pl.ANY)] * len(after),
            out_specs=[const((TILE, features)), const((TILE, features)), const((4, width, TILE))],
        ),
        out_shape=[shape_of(TILE, features, dtype=F32), shape_of(TILE, features), shape_of(4, width, TILE)],
        cost_estimate=cost(2e9, 3e6),
        name="middle",
    )


def feed_piece(x, g, inner_ref, vec_ref, outer_ref):
    hidden = nn(x, inner_ref[...]) + vec_ref[7:8, :]
    half = 0.5 + 0.5 * lax.erf(hidden * 0.5 ** 0.5)
    act = (hidden * half).astype(BF16)
    slope = half + hidden * (jnp.exp(-0.5 * hidden * hidden) * 0.3989422804014327)
    dh = (nt(g, outer_ref[...]) * slope).astype(BF16)
    out = nn(act, outer_ref[...]).astype(BF16)
    return act, dh, out, nt(dh, inner_ref[...]).astype(BF16)


def near_body(me_ref, *refs):
    count = 2 * PARTS
    x_refs = refs[:count]
    g_ref, inner_ref, vec_ref, outer_ref = refs[count:count + 4]
    out_refs, back_refs = refs[count + 4:count + 6], refs[count + 6:-6]
    sum_ref, grad_ref, x_all, g_all, act_all, dh_all = refs[-6:]
    i = pl.program_id(0)
    at = pl.ds(pl.multiple_of(i * TILE, TILE), TILE)
    for n, x_ref in enumerate(x_refs):
        @pl.when(i == n)
        def _(n=n, x_ref=x_ref):
            x_all[n * TILE:(n + 1) * TILE] = x_ref[...]

    g_all[at] = g_ref[...]
    act, dh, out, back = feed_piece(x_all[at], g_ref[...], inner_ref, vec_ref, outer_ref)
    act_all[at] = act
    dh_all[at] = dh
    sums = fold(dh.astype(F32))

    @pl.when(i == 0)
    def _():
        sum_ref[...] = jnp.zeros_like(sum_ref)

    sum_ref[...] += sums
    for n in range(count):
        @pl.when(i == n)
        def _(n=n):
            out_refs[n % 2][n // 2 * TILE:(n // 2 + 1) * TILE] = out
            back_refs[n][...] = back

    @pl.when(i == count - 1)
    def _():
        grad_ref[0] = tn(act_all[...], g_all[...]).astype(BF16)
        grad_ref[1] = tn(x_all[...], dh_all[...]).astype(BF16)


def feed_near(me, pieces, cot, inner, vectors, outer):
    features = cot.shape[1]
    units = inner.shape[1]
    count = 2 * PARTS
    piece = const((TILE, features))
    scratch = lambda n: pltpu.VMEM((count * TILE, n), BF16)
    return kernel_call(
        near_body,
        (me, *pieces, cot, inner, vectors, outer),
        free_in=tuple(range(1, count + 1)),
        free_out=(3, 5),
        grid_spec=pltpu.PrefetchScalarGridSpec(
            num_scalar_prefetch=1,
            grid=(count,),
            in_specs=[piece] * count
            + [pl.BlockSpec((TILE, features), lambda i, m: (4 * (i // 2) + (m[0] ^ (i % 2)), 0)),
               const(inner.shape), const(vectors.shape), const(outer.shape)],
            out_specs=[const((PARTS * TILE, features))] * 2 + [piece] * count
            + [const((8, units)), const((2, units, features))],
            scratch_shapes=[scratch(features), scratch(features), scratch(units), scratch(units)],
        ),
        out_shape=[shape_of(PARTS * TILE, features)] * 2 + [shape_of(TILE, features)] * count
        + [shape_of(8, units, dtype=F32), shape_of(2, units, features)],
        cost_estimate=cost(15e9, 12e6, 2e6),
        name="feed_near",
    )


def far_body(me_ref, x0_ref, x1_ref, g_ref, inner_ref, vec_ref, outer_ref, *rest):
    left_ref, right_ref, out0_ref, out1_ref, back0_ref, back1_ref, sum_ref = rest[-7:]
    i = pl.program_id(0)
    for n, x_ref in enumerate((x0_ref, x1_ref)):
        @pl.when(i == n)
        def _(x_ref=x_ref):
            left_ref[1] = x_ref[...]

    right_ref[0] = g_ref[...]
    act, dh, out, back = feed_piece(left_ref[1], g_ref[...], inner_ref, vec_ref, outer_ref)
    left_ref[0] = act
    right_ref[1] = dh
    sums = fold(dh.astype(F32))
    for n, (out_ref, back_ref) in enumerate(((out0_ref, back0_ref), (out1_ref, back1_ref))):
        @pl.when(i == n)
        def _(n=n, out_ref=out_ref, back_ref=back_ref):
            sum_ref[...] = sum_ref[...] + sums if n else sums
            out_ref[...] = out
            back_ref[...] = back


def feed_far(part, me, first, second, cot, inner, vectors, outer, kept):
    features = cot.shape[1]
    units = inner.shape[1]
    rows = pl.BlockSpec((2, TILE, features), lambda i, m: (0, 2 * part + i, 0))
    piece = const((TILE, features))
    half = pl.BlockSpec((TILE, features), lambda i, m: (part, 0))
    return kernel_call(
        far_body,
        (me, first, second, cot, inner, vectors, outer, *kept),
        free_in=(1, 2),
        free_out=(5,),
        grid_spec=pltpu.PrefetchScalarGridSpec(
            num_scalar_prefetch=1,
            grid=(2,),
            in_specs=[
                piece, piece,
                pl.BlockSpec((TILE, features), lambda i, m: (4 * part + (m[0] ^ (2 + i)), 0)),
                const(inner.shape), const(vectors.shape), const(outer.shape),
            ] + [pl.BlockSpec(memory_space=pl.ANY)] * len(kept),
            out_specs=[rows, rows, half, half, piece, piece, const((8, units))],
        ),
        out_shape=[shape_of(2, 2 * PARTS * TILE, features)] * 2 + [shape_of(PARTS * TILE, features)] * 2
        + [shape_of(TILE, features)] * 2 + [shape_of(8, units, dtype=F32)],
        input_output_aliases={7 + n: n for n in range(len(kept))},
        cost_estimate=cost(5e9, 8e6, 1e6),
        name="feed_far",
    )


def feed_grad_body(left_ref, right_ref, before_ref, *rest):
    rest[-1][0] = (tn(left_ref[0], right_ref[0]) + before_ref[0].astype(F32)).astype(BF16)


def feed_grad(left, right, before, after):
    _, rows, features = left.shape
    both = pl.BlockSpec((1, rows, features), lambda i: (i, 0, 0))
    square = pl.BlockSpec((1, features, features), lambda i: (i, 0, 0))
    return kernel_call(
        feed_grad_body,
        (left, right, before, *after),
        free_in=tuple(range(3, 3 + len(after))),
        grid=(2,),
        in_specs=[both, both, square] + [pl.BlockSpec(memory_space=pl.ANY)] * len(after),
        out_specs=[square],
        out_shape=[shape_of(*before.shape)],
        cost_estimate=cost(5e9, 10e6),
        name="feed_grad",
    )[0]


def back_body(me_ref, b0_ref, b1_ref, b2_ref, residual_ref, g_ref, vec_ref, w0_ref, w1_ref, w2_ref, w3_ref,
              *rest):
    grad_ref, low_ref, a0_ref, a1_ref, a2_ref, a3_ref, sum_ref = rest[-7:]
    grad_mid = b0_ref[...].astype(F32) + b1_ref[...].astype(F32) + b2_ref[...].astype(F32)
    normed, scale, _ = stats(residual_ref[...])
    upstream = g_ref[...].astype(F32)
    grad = upstream + norm_back(grad_mid, normed, scale, vec_ref[3:4, :])
    grad_ref[...] = grad
    low = grad.astype(BF16)
    low_ref[...] = low
    for w_ref, a_ref in ((w0_ref, a0_ref), (w1_ref, a1_ref), (w2_ref, a2_ref), (w3_ref, a3_ref)):
        a_ref[...] = nt(w_ref[...], low).astype(BF16)
    for n, value in enumerate((grad_mid * normed, grad_mid, grad, upstream)):
        sum_ref[8 * n:8 * n + 8] = fold(value)


def middle_back(part, me, sums, residual, cot, vectors, weights, after):
    features = cot.shape[1]
    piece = const((TILE, features))
    width = weights[0].shape[0]
    return kernel_call(
        back_body,
        (me, *sums, residual, cot, vectors, *weights, *after),
        free_in=(2, 3) + tuple(range(11, 11 + len(after))),
        free_out=(3, 4, 5),
        grid_spec=pltpu.PrefetchScalarGridSpec(
            num_scalar_prefetch=1,
            grid=(1,),
            in_specs=[piece] * 4
            + [pl.BlockSpec((TILE, features), lambda i, m: (4 * part + m[0], 0)), const(vectors.shape)]
            + [const(v.shape) for v in weights] + [pl.BlockSpec(memory_space=pl.ANY)] * len(after),
            out_specs=[piece, piece] + [const((width, TILE))] * 4 + [const((32, features))],
        ),
        out_shape=[shape_of(TILE, features, dtype=F32), shape_of(TILE, features)]
        + [shape_of(width, TILE)] * 4 + [shape_of(32, features, dtype=F32)],
        cost_estimate=cost(2e9, 4e6),
        name="middle_back",
    )


def output_body(*refs):
    mixed, lows, outs = refs[:PARTS], refs[PARTS:2 * PARTS], refs[2 * PARTS:]
    for n in range(4):
        total = nn(mixed[0][n], lows[0][...])
        for p in range(1, PARTS):
            total = total + nn(mixed[p][n], lows[p][...])
        outs[n][...] = total.astype(BF16)


def output_grad(mixed, lows):
    width, features = mixed[0].shape[1], lows[0].shape[1]
    return kernel_call(
        output_body,
        (*mixed, *lows),
        free_out=(1, 3),
        out_shape=[shape_of(width, features)] * 4,
        cost_estimate=cost(2e9, 4e6),
        name="output_grad",
    )


def tail_body(me_ref, g_ref, wq_ref, wk_ref, wv_ref, x_ref, stat_ref, *rest):
    early, units = rest[:PARTS], rest[PARTS:2 * PARTS + 1]
    o0_ref, o1_ref, o2_ref, o3_ref, apart_ref, vec_ref, sum_ref, row_ref = rest[-8:]
    i, p = pl.program_id(0), pl.program_id(1)
    grads = g_ref[...]
    width = wq_ref.shape[0]
    value = tn(grads[:width], wq_ref[...]) + tn(grads[width:2 * width], wk_ref[...])
    value = value + tn(grads[2 * width:], wv_ref[...])

    @pl.when((i == 0) & (p == 0))
    def _():
        row_ref[...] = jnp.zeros_like(row_ref)
        sum_ref[...] = jnp.zeros_like(sum_ref)

    row_ref[...] += nt(jnp.ones((8, grads.shape[1]), BF16), grads)
    normed = (x_ref[...].astype(F32) - stat_ref[:, 0:1]) * stat_ref[:, 1:2]
    sum_ref[:8] += fold(value * normed)
    sum_ref[8:] += fold(value)
    value = value.astype(BF16)
    for step, o_ref in enumerate((o3_ref, o2_ref, o1_ref, o0_ref)):
        @pl.when(i == step)
        def _(o_ref=o_ref):
            o_ref[pl.ds(pl.multiple_of(p * TILE, TILE), TILE), :] = value

    @pl.when((i == 3) & (p == PARTS - 1))
    def _():
        row = lax.broadcasted_iota(jnp.int32, vec_ref.shape, 0)
        vectors = jnp.zeros(vec_ref.shape, F32)
        before = early[0][...]
        for ref in early[1:]:
            before = before + ref[...]
        parts = [before[8 * n:8 * n + 8] for n in range(4)] + [sum_ref[:8], sum_ref[8:]]
        for n, part in enumerate(parts):
            vectors = jnp.where(row == n, jnp.sum(part, axis=0, keepdims=True), vectors)
        vec_ref[...] = vectors
        inside = units[0][...]
        for ref in units[1:]:
            inside = inside + ref[...]
        apart_ref[...] = jnp.where(row == 6, jnp.sum(inside, axis=0, keepdims=True), 0.0)
        apart_ref[7:8, :row_ref.shape[1]] = row_ref[0:1]
        o3_ref[PARTS * TILE:] = paired(vectors)


def tail(me, grads, wq, wk, wv, tokens, stat, early, units, after):
    deep = grads.shape[0]
    features = wq.shape[1]
    share = const((PARTS * TILE, features))
    more = const((PARTS * TILE + 16, features))
    at = lambda i, p, m: 4 * p + (m[0] ^ (3 - i))
    return kernel_call(
        tail_body,
        (me, grads, wq, wk, wv, tokens, stat, *early, *units, *after),
        free_out=(1, 3),
        grid_spec=pltpu.PrefetchScalarGridSpec(
            num_scalar_prefetch=1,
            grid=(4, PARTS),
            in_specs=[pl.BlockSpec((deep, TILE), lambda i, p, m: (0, at(i, p, m))),
                      const(wq.shape), const(wk.shape), const(wv.shape),
                      pl.BlockSpec((TILE, features), lambda i, p, m: (at(i, p, m), 0)),
                      pl.BlockSpec((TILE, WIDE), lambda i, p, m: (at(i, p, m), 0))]
            + [const(v.shape) for v in (*early, *units)] + [pl.BlockSpec(memory_space=pl.ANY)] * len(after),
            out_specs=[share, share, share, more, const((8, features)), const((8, features))],
            scratch_shapes=[pltpu.VMEM((16, features), F32), pltpu.VMEM((8, deep), F32)],
        ),
        out_shape=[shape_of(PARTS * TILE, features)] * 3 + [shape_of(PARTS * TILE + 16, features)]
        + [shape_of(8, features, dtype=F32)] * 2,
        cost_estimate=cost(4e9, 10e6),
        name="tail",
    )


def chip_body(one_ref, two_ref, vec_ref, *rest):
    out_ref = rest[-1]
    rows = one_ref.shape[0]
    out_ref[:rows] = (one_ref[...].astype(F32) + two_ref[:rows].astype(F32)).astype(BF16)
    out_ref[rows:] = paired(vec_ref[...] + joined(two_ref[rows:]))


def chip_sum(one, two, vectors, after):
    return kernel_call(
        chip_body,
        (one, two, vectors, *after),
        free_in=(1,) + tuple(range(3, 3 + len(after))),
        free_out=(0,),
        grid=(1,),
        in_specs=[const(one.shape), const(two.shape), const(vectors.shape)]
        + [pl.BlockSpec(memory_space=pl.ANY)] * len(after),
        out_specs=[const(two.shape)],
        out_shape=[shape_of(*two.shape)],
        name="chip_sum",
    )[0]


def halves_body(xz_ref, g_ref, go_ref, *rest):
    keep_ref, send_ref = rest[-2:]
    width = go_ref.shape[0]
    for to_ref, half in ((keep_ref, xz_ref[0]), (send_ref, 1 - xz_ref[0])):
        @pl.when(half == 0)
        def _(to_ref=to_ref):
            to_ref[...] = g_ref[:2 * width]

        @pl.when(half == 1)
        def _(to_ref=to_ref):
            to_ref[:width] = g_ref[2 * width:]
            to_ref[width:] = go_ref[...]


def halves(xz, grad_weights, grad_output, after):
    width, features = grad_output.shape
    half = const((2 * width, features))
    return kernel_call(
        halves_body,
        (xz, grad_weights, grad_output, *after),
        free_in=(1, 2, 3),
        grid_spec=pltpu.PrefetchScalarGridSpec(
            num_scalar_prefetch=1,
            grid=(1,),
            in_specs=[const(grad_weights.shape), const(grad_output.shape)]
            + [pl.BlockSpec(memory_space=pl.ANY)] * len(after),
            out_specs=[half, half],
        ),
        out_shape=[shape_of(2 * width, features)] * 2,
        cost_estimate=cost(1e6, 4e6),
        name="halves",
    )


def quarter_body(count, xz_ref, one_ref, two_ref, *rest):
    rows = one_ref.shape[0] // count
    for n, out_ref in enumerate(rest[-count:]):
        at = pl.ds(pl.multiple_of(lax.rem(xz_ref[1] + n, count) * rows, rows), rows)
        out_ref[...] = (one_ref[at, :].astype(F32) + two_ref[at, :].astype(F32)).astype(BF16)


def quarters(xz, one, two, count, after):
    rows, features = one.shape

    def body(*refs):
        quarter_body(count, *refs)

    return kernel_call(
        body,
        (xz, one, two, *after),
        free_in=(2, 3, 4),
        grid_spec=pltpu.PrefetchScalarGridSpec(
            num_scalar_prefetch=1,
            grid=(1,),
            in_specs=[const(one.shape), const(two.shape)] + [pl.BlockSpec(memory_space=pl.ANY)] * len(after),
            out_specs=[const((rows // count, features))] * count,
        ),
        out_shape=[shape_of(rows // count, features)] * count,
        cost_estimate=cost(1e6, 2e6),
        name="quarters",
    )


def paired(value):
    return jnp.concatenate(split(value, 2), axis=0).astype(BF16)


def joined(both):
    both = both.astype(F32)
    half = both.shape[0] // 2
    return both[:half] + both[half:]


def second_body(count, *refs):
    one_ref, two_ref, apart_ref, out_ref = refs[count], refs[count + 1], refs[count + 2], refs[-1]
    rows = refs[0].shape[0]
    total = refs[0][...].astype(F32)
    for ref in refs[1:count]:
        total = total + ref[...].astype(F32)
    out_ref[:rows] = total.astype(BF16)
    out_ref[rows:] = paired(joined(one_ref[...]) + joined(two_ref[...]) + apart_ref[...])


def second(parts, one, two, apart, after):
    count = len(parts)
    rows, features = parts[0].shape
    last = pl.BlockSpec((16, features), lambda i: (one.shape[0] // 16 - 1, 0))

    def body(*refs):
        second_body(count, *refs)

    return kernel_call(
        body,
        (*parts, one, two, apart, *after),
        free_in=tuple(range(1, count + 2)) + tuple(range(count + 3, count + 3 + len(after))),
        grid=(1,),
        in_specs=[const((rows, features))] * count + [last, last, const(apart.shape)]
        + [pl.BlockSpec(memory_space=pl.ANY)] * len(after),
        out_specs=[const((rows + 16, features))],
        out_shape=[shape_of(rows + 16, features)],
        name="second",
    )[0]


def third_body(count, xz_ref, *refs):
    out_ref = refs[-1]
    step = out_ref.shape[0] - (refs[0].shape[0] * count - out_ref.shape[0]) // (count - 1)
    rows = step // count
    sums = None
    for n, ref in enumerate(refs[:count]):
        place_at = lax.rem(xz_ref[1] + count - n, count)
        out_ref[pl.ds(pl.multiple_of(place_at * rows, rows), rows), :] = ref[:rows]
        value = joined(ref[rows:])
        sums = value if sums is None else sums + value
    out_ref[step:] = paired(sums)


def third(xz, pieces, extra, after):
    count = len(pieces)
    rows, features = pieces[0].shape
    total = (rows - extra) * count + extra

    def body(*refs):
        third_body(count, *refs)

    return kernel_call(
        body,
        (xz, *pieces, *after),
        free_in=tuple(range(1, count + 1)),
        grid_spec=pltpu.PrefetchScalarGridSpec(
            num_scalar_prefetch=1,
            grid=(1,),
            in_specs=[const((rows, features))] * count + [pl.BlockSpec(memory_space=pl.ANY)] * len(after),
            out_specs=[const((total, features))],
        ),
        out_shape=[shape_of(total, features)],
        name="third",
    )[0]


def ready_body(xz_ref, mine_ref, other_ref, *rest):
    outs = rest[-14:]
    width = outs[0].shape[0]
    for n, out_ref in enumerate(outs[:4]):
        rows = slice(n % 2 * width, (n % 2 + 1) * width)
        for to_ref, chosen in ((mine_ref, xz_ref[0] == n // 2), (other_ref, xz_ref[0] != n // 2)):
            @pl.when(chosen)
            def _(to_ref=to_ref, out_ref=out_ref, rows=rows):
                out_ref[...] = to_ref[rows].astype(F32)

    small = joined(mine_ref[2 * width:]) + joined(other_ref[2 * width:])
    for n, out_ref in enumerate(outs[4:11]):
        out_ref[...] = small[n]
    for n, out_ref in enumerate(outs[11:]):
        out_ref[...] = small[7, n * width:(n + 1) * width]


def ready(xz, mine, other, width, after):
    rows, features = mine.shape
    sizes = [(features,)] * 7 + [(width,)] * 3
    return kernel_call(
        ready_body,
        (xz, mine, other, *after),
        free_in=(2,),
        grid_spec=pltpu.PrefetchScalarGridSpec(
            num_scalar_prefetch=1,
            grid=(1,),
            in_specs=[const(mine.shape), const(other.shape)] + [pl.BlockSpec(memory_space=pl.ANY)] * len(after),
            out_specs=[const((width, features))] * 4 + [const(size) for size in sizes],
        ),
        out_shape=[shape_of(width, features, dtype=F32)] * 4 + [shape_of(*size, dtype=F32) for size in sizes],
        cost_estimate=cost(1e6, 4e6),
        name="ready",
    )


def final_body(me_ref, b0_ref, b1_ref, b2_ref, x_ref, *rest):
    grad_refs, vec_ref, out_ref = rest[:PARTS], rest[PARTS], rest[-1]
    p = pl.program_id(0)
    grad_attend = b0_ref[...].astype(F32) + b1_ref[...].astype(F32) + b2_ref[...].astype(F32)
    normed, scale, _ = stats(x_ref[...].astype(F32))
    back = norm_back(grad_attend, normed, scale, vec_ref[0:1, :])
    for n, grad_ref in enumerate(grad_refs):
        @pl.when(p == n)
        def _(grad_ref=grad_ref):
            out_ref[...] = (grad_ref[...] + back).astype(BF16)


def final(me, sums, tokens, grads, vectors, after):
    features = tokens.shape[1]
    rows = pl.BlockSpec((TILE, features), lambda p, m: (p, 0))
    return kernel_call(
        final_body,
        (me, *sums, tokens, *grads, vectors, *after),
        free_in=(2, 3) + tuple(range(6 + PARTS, 6 + PARTS + len(after))),
        free_out=(0,),
        grid_spec=pltpu.PrefetchScalarGridSpec(
            num_scalar_prefetch=1,
            grid=(PARTS,),
            in_specs=[rows] * 3 + [pl.BlockSpec((TILE, features), lambda p, m: (4 * p + m[0], 0))]
            + [const((TILE, features))] * PARTS + [const(vectors.shape)]
            + [pl.BlockSpec(memory_space=pl.ANY)] * len(after),
            out_specs=[rows],
        ),
        out_shape=[shape_of(PARTS * TILE, features)],
        cost_estimate=cost(1e8, 5e6),
        name="final",
    )[0]


def place_body(me_ref, p0_ref, p1_ref, p2_ref, p3_ref, *rest):
    out_ref = rest[-1]
    for step, p_ref in enumerate((p0_ref, p1_ref, p2_ref, p3_ref)):
        @pl.when(pl.program_id(0) == step)
        def _(p_ref=p_ref):
            at = pl.ds(pl.multiple_of(pl.program_id(1) * TILE, TILE), TILE)
            out_ref[...] = p_ref[at, :].astype(out_ref.dtype)


def place(me, shares, dtype, after):
    rows, features = shares[0].shape
    return kernel_call(
        place_body,
        (me, *shares, *after),
        free_in=(1, 2, 3, 4),
        grid_spec=pltpu.PrefetchScalarGridSpec(
            num_scalar_prefetch=1,
            grid=(4, PARTS),
            in_specs=[const((rows, features))] * 4 + [pl.BlockSpec(memory_space=pl.ANY)] * len(after),
            out_specs=pl.BlockSpec((TILE, features), lambda i, p, m: (4 * p + (m[0] ^ i), 0)),
        ),
        out_shape=shape_of(4 * rows, features, dtype=dtype),
        cost_estimate=cost(1e6, 9e6),
        name="place",
    )


def fence_body(*refs):
    pass


def fence(value, *after, space=pltpu.HBM):
    anywhere = pl.BlockSpec(memory_space=pl.ANY)
    return pl.pallas_call(
        fence_body,
        in_specs=[anywhere] * (1 + len(after)),
        out_specs=anywhere,
        out_shape=space(value.shape, value.dtype),
        input_output_aliases={0: 0},
        name="fence",
    )(pltpu.with_memory_space_constraint(value, space), *after)


def other_core(value):
    return lax.ppermute(value, "core", SWAP)


def other_chip(value):
    return lax.ppermute(value, "y", SWAP)


def crosswise(value):
    return lax.ppermute(value, MP, [(n, n ^ 3) for n in range(4)])


def exchange(pieces):
    return [pieces[0], other_core(pieces[1]), other_chip(pieces[2]), crosswise(pieces[3])]


def gather_sum(pieces):
    near = other_core(pieces[1])
    far = (pieces[2].astype(F32) + other_core(pieces[3]).astype(F32)).astype(BF16)
    return [pieces[0], near, other_chip(far)], far


def spread(value):
    far = other_chip(value)
    return [value, other_core(value), far, other_core(far)]


def pick(values, at):
    return lax.dynamic_index_in_dim(values, at, 0, keepdims=False)


def turned(values, way):
    size = lax.axis_size("z")
    return lax.ppermute(values, "z", [(n, (n + way) % size) for n in range(size)])


def sum_first(xz, keep, got, after):
    size = lax.axis_size("z")
    if size > 4:
        return [lax.psum(keep + got, "z")]
    return quarters(xz, keep, got, size, after)


def gather_z(value):
    size = lax.axis_size("z")
    if size > 4:
        return [lax.all_gather(value, "z", axis=0, tiled=True)]
    return [turned(value, way) if way else value for way in range(size)]


def local(
    tokens,
    segment_ids,
    gain_one,
    bias_one,
    query_weight,
    query_bias,
    key_weight,
    value_weight,
    value_bias,
    output_weight,
    output_bias,
    gain_two,
    bias_two,
    inner_weight,
    inner_bias,
    outer_weight,
    outer_bias,
    cotangent,
):
    _, length, features = tokens.shape
    width = query_weight.shape[1]
    heads = width // HEAD
    tokens = tokens.reshape(length, features)
    cot = cotangent.reshape(length, features)
    at = lax.axis_index(MP).astype(jnp.int32)
    me = at[None]
    apart = jnp.concatenate([query_bias, value_bias, jnp.zeros((features - 2 * width,), F32)])
    vectors = jnp.concatenate([gain_one, bias_one, output_bias, gain_two, bias_two, outer_bias, apart, inner_bias])
    vectors = vectors.reshape(8, features)
    wq, wk, wv = query_weight.T, key_weight.T, value_weight.T

    output_weights = spread(output_weight)
    attend_in, qt, kt, vt, kn, vn, stat = project(tokens, segment_ids, vectors, wq, wk, wv, heads)

    parts = range(PARTS)
    attended, extras, fours = [], [], []
    for p in parts:
        out, extra, *four = attend_forward(p, me, segment_ids, qt, kn, vt, output_weights[1:3] if p == 0 else ())
        attended.append(out)
        extras.append(extra)
        fours.append(exchange(four))
    mixed, residuals, pieces = [], [], []
    for p in parts:
        residual, own, together = middle(p, me, tokens, fours[p], output_weights, vectors, extras[p + 1:])
        mixed.append(together)
        residuals.append(residual)
        pieces.append([own, other_core(own), other_chip(own)])

    backs = {}
    *outs, b00, b01, b10, b11, near_sum, near_grad = feed_near(
        me, [pieces[p][n] for p in parts for n in (0, 1)], cot, inner_weight, vectors, outer_weight
    )
    backs[0, 0], backs[0, 1], backs[1, 0], backs[1, 1] = b00, b01, b10, b11
    sums, kept, gathered, far_sums, behind = [near_sum], (), [], [], b00
    for p in parts:
        far = fence(pieces[p][2], behind, space=pltpu.VMEM)
        *kept, backs[p, 2], backs[p, 3], far_sum = feed_far(
            p, me, far, other_core(far), cot, inner_weight, vectors, outer_weight, kept
        )
        behind = backs[p, 2]
        sums.append(far_sum)
        if p:
            backs[p, 3] = fence(backs[p, 3], gathered[-1][2], space=pltpu.VMEM)
            feed_sum = feed_grad(kept[0], kept[1], near_grad, ())
            backs[p, 2] = fence(backs[p, 2], feed_sum)
        summed, far_sum = gather_sum([backs[p, n] for n in range(4)])
        gathered.append(summed)
        far_sums.append(far_sum)
    left, right, *far_outs = kept
    outs += far_outs
    feed_sum = lax.psum_scatter(feed_sum.reshape(-1, features), DP, scatter_dimension=0, tiled=True)
    grad_residuals, lows, grads_attended, inner_sums = [], [], [], []
    for p in parts:
        grad, low, a0, a1, a2, a3, vector = middle_back(
            p, me, gathered[p], residuals[p], cot, vectors, output_weights, far_sums[p + 1:]
        )
        grad_residuals.append(grad)
        lows.append(low)
        inner_sums.append(vector)
        grads_attended.append(exchange([a0, a1, a2, a3]))

    near = other_core(fence(outs[1], *far_sums))
    far = (outs[2].astype(F32) + other_core(fence(outs[3], *far_sums)).astype(F32)).astype(BF16)
    far = fence(far, lows[-1], space=pltpu.VMEM)
    part = output_grad(mixed, lows)
    earlier = attend_backward(0, me, segment_ids, qt, extras[0], kn, kt, vn, attended[0], grads_attended[0], (),
                              (far, near, part[0]))
    there = other_chip(far)
    part_far = fence(part[2], earlier[0])
    part_far = (part_far.astype(F32) + other_core(part[3]).astype(F32)).astype(BF16)
    part_near = other_core(part[1])
    grads = attend_backward(1, me, segment_ids, qt, extras[1], kn, kt, vn, attended[1], grads_attended[1], earlier,
                            (part_near, part_far, there))

    xz = jnp.stack([lax.axis_index("x"), lax.axis_index("z")]).astype(jnp.int32)
    part_across = other_chip(part_far)
    grad_output = fence(part[0], grads).astype(F32) + part_near.astype(F32) + part_across.astype(F32)
    keep, send = halves(xz, nn(grads, attend_in).astype(BF16), grad_output.astype(BF16), ())
    result = jnp.concatenate(residuals) + fence(outs[0], send).astype(F32) + near.astype(F32)
    result = (result + there.astype(F32) + outer_bias).astype(BF16)
    near, far = other_core(result), other_chip(result)
    got = lax.ppermute(send, "x", SWAP)
    back_own, back_near, back_far, back_across, apart, summed = tail(
        me, grads, wq, wk, wv, tokens, stat, inner_sums, sums, (send,)
    )
    feed_sum = lax.all_gather(fence(feed_sum, send), DP, axis=0, tiled=True)
    feed_sum = (feed_sum[:features].astype(F32), feed_sum[features:].astype(F32))
    quarter = sum_first(xz, keep, got, (near, far, apart))
    back_across = other_core(fence(back_across, quarter[-1], space=pltpu.VMEM))
    back_far = chip_sum(back_far, back_across, summed, ())
    back_there = other_chip(back_far)
    share = final(me, [back_own, other_core(back_near), back_there], tokens, grad_residuals, vectors, ())
    if len(quarter) > 1:
        turns = [quarter[0]] + [turned(part, n + 1) for n, part in enumerate(quarter[1:])]
        held = second(turns, back_far, back_there, apart, (share,))
        layer_out = place(me, [result, near, far, other_core(far)], BF16, (held,))
        mine = third(xz, gather_z(held), 16, (layer_out,))
    else:
        small = joined(back_far[-16:]) + joined(back_there[-16:]) + apart
        layer_out = place(me, [result, near, far, other_core(far)], BF16, ())
        mine = jnp.concatenate([quarter[0], paired(lax.psum(small, "z"))])
    share = fence(share, held if len(quarter) > 1 else mine, space=pltpu.VMEM)
    near, far = other_core(share), fence(other_chip(share), mine, space=pltpu.VMEM)
    input_grad = place(me, [share, near, far, other_core(far)], F32, (mine,))
    *wide, two_gain, two_bias, output_sum, outer_bias, one_gain, one_bias, inner_bias, query, _, value = ready(
        xz, mine, lax.ppermute(mine, "x", SWAP), width, feed_sum
    )
    return (
        layer_out.reshape(1, length, features),
        input_grad.reshape(1, length, features),
        one_gain,
        one_bias,
        wide[0].T,
        query,
        wide[1].T,
        wide[2].T,
        value,
        wide[3],
        output_sum,
        two_gain,
        two_bias,
        feed_sum[1],
        inner_bias,
        feed_sum[0],
        outer_bias,
    )


def solution(mesh):
    rows = mesh.shape["dp"]
    inner = Mesh(mesh.devices.reshape(rows // 2, 2, 2, 2), DP + MP)
    placed = (
        P(DP, None, None),
        P(DP, None),
        P(),
        P(),
        P(None, MP),
        P(MP),
        P(None, MP),
        P(None, MP),
        P(MP),
        P(MP, None),
        P(),
        P(),
        P(),
        P(None, MP),
        P(MP),
        P(MP, None),
        P(),
        P(DP, None, None),
    )
    return jax.shard_map(
        local,
        mesh=inner,
        in_specs=placed,
        out_specs=(
            P(DP, None, None),
            P(DP, None, None),
            P(),
            P(),
            P(None, MP),
            P(MP),
            P(None, MP),
            P(None, MP),
            P(MP),
            P(MP, None),
            P(),
            P(),
            P(),
            P(None, MP),
            P(MP),
            P(MP, None),
            P(),
        ),
        check_vma=False,
    )
```

```python
import jax
import jax.numpy as jnp
from jax import lax
from jax.experimental import pallas as pl
from jax.experimental.pallas import tpu as pltpu
from jax.sharding import Mesh
from jax.sharding import PartitionSpec as P

HEAD = 64
WIDE = 128
TILE = 256
LONG = 512
PARTS = 2
MASKED = 1e30
SCALE = 1
F32 = jnp.float32
BF16 = jnp.bfloat16
DP = ("z", "x")
MP = ("y", "core")
SWAP = [(0, 1), (1, 0)]


def nn(left, right):
    return lax.dot_general(left, right, (((1,), (0,)), ((), ())), preferred_element_type=F32)


def nt(left, right):
    return lax.dot_general(left, right, (((1,), (1,)), ((), ())), preferred_element_type=F32)


def tn(left, right):
    return lax.dot_general(left, right, (((0,), (0,)), ((), ())), preferred_element_type=F32)


def stats(values):
    mean = jnp.mean(values, axis=-1, keepdims=True)
    center = values - mean
    scale = lax.rsqrt(jnp.mean(center * center, axis=-1, keepdims=True) + 1e-05)
    return center * scale, scale, mean


def norm_back(grad_out, normed, scale, gain):
    upstream = grad_out * gain
    return scale * (
        upstream
        - jnp.mean(upstream, axis=-1, keepdims=True)
        - normed * jnp.mean(upstream * normed, axis=-1, keepdims=True)
    )


def fold(values):
    return jnp.sum(values.reshape(-1, 8, values.shape[-1]), axis=0)


def split(value, parts):
    out = []
    for _ in range(parts):
        piece = value.astype(BF16).astype(F32)
        out.append(piece)
        value = value - piece
    return out


def const(shape):
    return pl.BlockSpec(shape, lambda *_: (0,) * len(shape))


def shape_of(*dims, dtype=BF16):
    return jax.ShapeDtypeStruct(dims, dtype)


def params(mib=40):
    return pltpu.CompilerParams(vmem_limit_bytes=mib << 20)


def kernel_call(body, values, free_in=(), free_out=(), **options):
    shapes = options.pop("out_shape")
    many = isinstance(shapes, (list, tuple))
    shapes = [s if n in free_out else pltpu.HBM(s.shape, s.dtype) for n, s in enumerate(shapes if many else [shapes])]
    values = [
        v if n in free_in or v.dtype == jnp.int32 else pltpu.with_memory_space_constraint(v, pltpu.HBM)
        for n, v in enumerate(values)
    ]
    return pl.pallas_call(
        body, out_shape=shapes if many else shapes[0], compiler_params=params(), **options
    )(*values)


def cost(flops, moved, special=0):
    return pl.CostEstimate(flops=int(flops * SCALE), bytes_accessed=int(moved * SCALE), transcendentals=0)


def project_body(x_ref, seg_ref, vec_ref, wq_ref, wk_ref, wv_ref,
                 ai_ref, qt_ref, kt_ref, vt_ref, kn_ref, vn_ref, stat_ref):
    heads = kn_ref.shape[0]
    width = heads * HEAD
    tile = x_ref.shape[0]
    normed, scale, mean = stats(x_ref[...].astype(F32))
    lane = lax.broadcasted_iota(jnp.int32, stat_ref.shape, 1)
    stat_ref[...] = jnp.where(lane == 0, mean, scale)
    ai = (normed * vec_ref[0:1, :] + vec_ref[1:2, :]).astype(BF16)
    ai_ref[...] = ai
    column = vec_ref[...].T[:2 * width, 6:7]
    queries = ((nt(wq_ref[...], ai) + column[:width]).astype(BF16)).astype(F32) * HEAD ** -0.5
    keys = nt(wk_ref[...], ai)
    kt_ref[...] = keys.astype(BF16)
    values = nt(wv_ref[...], ai) + column[width:]
    row = lax.broadcasted_iota(jnp.int32, (HEAD, tile), 0)
    same = jnp.where(row == seg_ref[...], 1.0, 0.0)
    mask = jnp.where(row < 8, (same - 1.0) * MASKED, jnp.where(row < 11, 1.0, 0.0))
    ones = jnp.where(row < 2, 1.0, 0.0)
    first = jnp.where(row[:16] == 0, 1.0, 0.0).astype(BF16)
    for h in range(heads):
        rows = slice(h * HEAD, (h + 1) * HEAD)
        qt_ref[h, :HEAD, :] = queries[rows].astype(BF16)
        qt_ref[h, HEAD:, :] = same.astype(BF16)
        vt_ref[h, :HEAD, :] = values[rows].astype(BF16)
        vt_ref[h, HEAD:, :] = first
        kn_ref[h] = jnp.concatenate([keys[rows], mask], axis=0).T.astype(BF16)
        vn_ref[h] = jnp.concatenate([values[rows], ones], axis=0).T.astype(BF16)


def project(tokens, seg_row, vectors, wq, wk, wv, heads):
    length, features = tokens.shape
    width = heads * HEAD
    return kernel_call(
        project_body,
        (tokens, seg_row, vectors, wq, wk, wv),
        grid=(length // LONG,),
        in_specs=[
            pl.BlockSpec((LONG, features), lambda i: (i, 0)),
            pl.BlockSpec((1, LONG), lambda i: (0, i)),
            const(vectors.shape), const(wq.shape), const(wk.shape), const(wv.shape),
        ],
        out_specs=[
            pl.BlockSpec((LONG, features), lambda i: (i, 0)),
            pl.BlockSpec((heads, WIDE, LONG), lambda i: (0, 0, i)),
            pl.BlockSpec((width, LONG), lambda i: (0, i)),
            pl.BlockSpec((heads, HEAD + 16, LONG), lambda i: (0, 0, i)),
            pl.BlockSpec((heads, LONG, WIDE), lambda i: (0, i, 0)),
            pl.BlockSpec((heads, LONG, WIDE), lambda i: (0, i, 0)),
            pl.BlockSpec((LONG, WIDE), lambda i: (i, 0)),
        ],
        out_shape=[
            shape_of(length, features),
            shape_of(heads, WIDE, length),
            shape_of(width, length),
            shape_of(heads, HEAD + 16, length),
            shape_of(heads, length, WIDE),
            shape_of(heads, length, WIDE),
            shape_of(length, WIDE, dtype=F32),
        ],
        cost_estimate=cost(6e9, 14e6),
        name="project",
    )


def key_range(seg_ref, seg_all, i):
    first = seg_ref[0, i * TILE]
    last = seg_ref[0, i * TILE + TILE - 1]
    before = jnp.sum(jnp.where(seg_all < first, 1.0, 0.0)).astype(jnp.int32)
    until = jnp.sum(jnp.where(seg_all <= last, 1.0, 0.0)).astype(jnp.int32)
    return before // TILE, (until + TILE - 1) // TILE


def by_blocks(low, high, step, carry):
    keys = lambda kb: pl.ds(pl.multiple_of(kb * TILE, TILE), TILE)
    for many in (3, 2, 1):
        rounds = (high - low) // many
        run = lambda n, c, low=low, many=many: step([keys(low + many * n + k) for k in range(many)], c)
        carry = lax.fori_loop(0, rounds, run, carry)
        low = low + many * rounds
    return carry


def shifted(one_hot, pieces):
    row = lax.broadcasted_iota(jnp.int32, one_hot.shape, 0)
    value = one_hot
    for n, piece in enumerate(pieces):
        value = jnp.where(row == 8 + n, piece, value)
    return value.astype(BF16)


def forward_body(offset, me_ref, segs_ref, seg_ref, qt_ref, kn_ref, vt_ref, *rest):
    out_ref, extra_ref, o0_ref, o1_ref, o2_ref, o3_ref, acc_ref = rest[-7:]
    heads, _, tile = qt_ref.shape
    i = pl.program_id(0)
    low, high = key_range(segs_ref, seg_ref[...], i + offset)
    acc_ref[...] = jnp.zeros_like(acc_ref)

    def step(keys, tops):
        scores = [[nn(kn_ref[h, at, :], qt_ref[h]) for at in keys] for h in range(heads)]
        new_tops = []
        for h in range(heads):
            top = tops[h]
            for score in scores[h]:
                top = jnp.maximum(top, jnp.max(score, axis=0, keepdims=True))
            new_tops.append(top)
        powered = [[jnp.exp(score - new_tops[h]).astype(BF16) for score in scores[h]] for h in range(heads)]
        for h in range(heads):
            total = acc_ref[h] * jnp.exp(tops[h] - new_tops[h])
            for at, power in zip(keys, powered[h]):
                total = total + nn(vt_ref[h, :, at], power)
            acc_ref[h] = total
        return tuple(new_tops)

    tops = by_blocks(low, high, step, (jnp.full((1, tile), -jnp.inf, F32),) * heads)
    for h in range(heads):
        total = acc_ref[h, HEAD:HEAD + 1, :]
        out_ref[0, h * HEAD:(h + 1) * HEAD, :] = (acc_ref[h, :HEAD, :] / total).astype(BF16)
        one_hot = qt_ref[h, HEAD:HEAD + 16, :].astype(F32)
        extra_ref[h] = shifted(one_hot, split(-(tops[h] + jnp.log(total)), 3))
    for n, o_ref in enumerate((o0_ref, o1_ref, o2_ref, o3_ref)):
        @pl.when((i ^ me_ref[0]) == n)
        def _(o_ref=o_ref):
            o_ref[...] = out_ref[0]


def attend_forward(part, me, seg_row, qt, kn, vt, after):
    heads, _, length = qt.shape
    width = heads * HEAD
    count = length // TILE // PARTS
    offset = part * count

    def body(*refs):
        forward_body(offset, *refs)

    return kernel_call(
        body,
        (me, seg_row, seg_row, qt, kn, vt, *after),
        free_in=tuple(range(6, 6 + len(after))),
        free_out=(3, 4, 5),
        grid_spec=pltpu.PrefetchScalarGridSpec(
            num_scalar_prefetch=1,
            grid=(count,),
            in_specs=[
                pl.BlockSpec(memory_space=pltpu.SMEM),
                const((1, length)),
                pl.BlockSpec((heads, WIDE, TILE), lambda i, m: (0, 0, i + offset)),
                const(kn.shape), const(vt.shape),
            ] + [pl.BlockSpec(memory_space=pl.ANY)] * len(after),
            out_specs=[
                pl.BlockSpec((1, width, TILE), lambda i, m: (i, 0, 0)),
                pl.BlockSpec((heads, 16, TILE), lambda i, m: (0, 0, i)),
            ] + [const((width, TILE))] * 4,
            scratch_shapes=[pltpu.VMEM((heads, HEAD + 16, TILE), F32)],
        ),
        out_shape=[shape_of(count, width, TILE), shape_of(heads, 16, count * TILE)] + [shape_of(width, TILE)] * 4,
        cost_estimate=cost(9e9, 5e6, 4e6),
        name="attend_forward",
    )


def backward_body(part, me_ref, segs_ref, seg_ref, qt_ref, extra_ref, kn_ref, kt_ref, vn_ref, out_ref,
                  g0_ref, g1_ref, g2_ref, g3_ref, *rest):
    heads, _, tile = qt_ref.shape
    width = heads * HEAD
    length = kt_ref.shape[1]
    if part == 0:
        dq_out, dk_ref, dv_ref, qa_ref, da_ref, dq_ref = rest[-6:]
    else:
        dq_in, dk_in, dv_in = rest[:3]
        grads_ref, qa_ref, da_ref, dq_ref, dk_ref, dv_ref = rest[-6:]
    i = pl.program_id(0)
    count = length // TILE // PARTS
    at_here = i + part * count
    low, high = key_range(segs_ref, seg_ref[...], at_here)

    @pl.when(i == 0)
    def _():
        if part == 0:
            dk_ref[...] = jnp.zeros_like(dk_ref)
            dv_ref[...] = jnp.zeros_like(dv_ref)
        else:
            dk_ref[...] = dk_in[...]
            dv_ref[...] = dv_in[...]
            grads_ref[:width, :count * TILE] = dq_in[...]
        qa_ref[...] = jnp.zeros_like(qa_ref)
        da_ref[...] = jnp.zeros_like(da_ref)

    source = i ^ me_ref[0]
    for n, g_ref in enumerate((g0_ref, g1_ref, g2_ref, g3_ref)):
        @pl.when(source == n)
        def _(g_ref=g_ref):
            for h in range(heads):
                da_ref[h, :HEAD, :] = g_ref[h * HEAD:(h + 1) * HEAD]

    dq_ref[...] = jnp.zeros_like(dq_ref)
    row = lax.broadcasted_iota(jnp.int32, (16, tile), 0)
    for h in range(heads):
        rows = slice(h * HEAD, (h + 1) * HEAD)
        qa_ref[h, :HEAD, :] = qt_ref[h, :HEAD, :]
        qa_ref[h, HEAD:HEAD + 16, :] = extra_ref[h]
        inner = jnp.sum(da_ref[h, :HEAD, :].astype(F32) * out_ref[0, rows].astype(F32), axis=0, keepdims=True)
        first, second = split(-inner, 2)
        value = jnp.where(row == 0, first, jnp.where(row == 1, second, 0.0))
        da_ref[h, HEAD:HEAD + 16, :] = value.astype(BF16)

    def step(keys, carry):
        every = range(heads)
        rows = [slice(h * HEAD, (h + 1) * HEAD) for h in every]
        scores = [[nn(kn_ref[h, at, :], qa_ref[h]) for at in keys] for h in every]
        slopes = [[nn(vn_ref[h, at, :], da_ref[h]) for at in keys] for h in every]
        probs = [[jnp.exp(score) for score in scores[h]] for h in every]
        ds = [[(p * s).astype(BF16) for p, s in zip(probs[h], slopes[h])] for h in every]
        probs = [[p.astype(BF16) for p in probs[h]] for h in every]
        for h in every:
            total = dq_ref[rows[h]]
            for n, at in enumerate(keys):
                dv_ref[rows[h], at] += nt(da_ref[h, :HEAD, :], probs[h][n])
                dk_ref[rows[h], at] += nt(qa_ref[h, :HEAD, :], ds[h][n])
                total = total + nn(kt_ref[rows[h], at], ds[h][n])
            dq_ref[rows[h]] = total
        return carry

    by_blocks(low, high, step, 0)
    dq = (dq_ref[...] * HEAD ** -0.5).astype(BF16)
    if part == 0:
        dq_out[...] = dq
    else:
        grads_ref[:width, pl.ds(pl.multiple_of(at_here * TILE, TILE), TILE)] = dq

        @pl.when(i == pl.num_programs(0) - 1)
        def _():
            grads_ref[width:2 * width] = dk_ref[...].astype(BF16)
            grads_ref[2 * width:] = dv_ref[...].astype(BF16)


def attend_backward(part, me, seg_row, qt, extra, kn, kt, vn, out, grad, earlier, after):
    heads, _, length = qt.shape
    width = heads * HEAD
    count = length // TILE // PARTS
    offset = part * count

    def body(*refs):
        backward_body(part, *refs)

    in_specs = [
        pl.BlockSpec(memory_space=pltpu.SMEM),
        const((1, length)),
        pl.BlockSpec((heads, WIDE, TILE), lambda i, m: (0, 0, i + offset)),
        pl.BlockSpec((heads, 16, TILE), lambda i, m: (0, 0, i)),
        const(kn.shape), const(kt.shape), const(vn.shape),
        pl.BlockSpec((1, width, TILE), lambda i, m: (i, 0, 0)),
        const(grad[0].shape), const(grad[1].shape), const(grad[2].shape), const(grad[3].shape),
    ] + [const(v.shape) for v in earlier] + [pl.BlockSpec(memory_space=pl.ANY)] * len(after)
    scratch = [
        pltpu.VMEM((heads, WIDE, TILE), BF16),
        pltpu.VMEM((heads, WIDE, TILE), BF16),
        pltpu.VMEM((width, TILE), F32),
    ]
    if part == 0:
        out_specs = [pl.BlockSpec((width, TILE), lambda i, m: (0, i)), const((width, length)), const((width, length))]
        out_shape = [shape_of(width, count * TILE), shape_of(width, length, dtype=F32), shape_of(width, length, dtype=F32)]
    else:
        out_specs = const((3 * width, length))
        out_shape = shape_of(3 * width, length)
        scratch += [pltpu.VMEM((width, length), F32), pltpu.VMEM((width, length), F32)]
    return kernel_call(
        body,
        (me, seg_row, seg_row, qt, extra, kn, kt, vn, out, *grad, *earlier, *after),
        free_in=(10, 11, 12) + tuple(range(13 + len(earlier), 15 + len(earlier))),
        grid_spec=pltpu.PrefetchScalarGridSpec(
            num_scalar_prefetch=1, grid=(count,), in_specs=in_specs, out_specs=out_specs, scratch_shapes=scratch,
        ),
        out_shape=out_shape,
        cost_estimate=cost(16e9, 10e6, 4e6),
        name="attend_backward",
    )


def middle_body(me_ref, x_ref, m0_ref, m1_ref, m2_ref, m3_ref, w0_ref, w1_ref, w2_ref, w3_ref,
                vec_ref, *rest):
    residual_ref, own_ref, mixed_ref = rest[-3:]
    total = x_ref[...].astype(F32) + vec_ref[2:3, :]
    pairs = ((m0_ref, w0_ref), (m1_ref, w1_ref), (m2_ref, w2_ref), (m3_ref, w3_ref))
    for n, (m_ref, w_ref) in enumerate(pairs):
        total = total + tn(m_ref[...], w_ref[...])
        mixed_ref[n] = m_ref[...]
    residual_ref[...] = total
    normed, _, _ = stats(total)
    own_ref[...] = (normed * vec_ref[3:4, :] + vec_ref[4:5, :]).astype(BF16)


def middle(part, me, tokens, mixed, weights, vectors, after):
    features = tokens.shape[1]
    width = weights[0].shape[0]
    return kernel_call(
        middle_body,
        (me, tokens, *mixed, *weights, vectors, *after),
        free_in=(3, 4, 5),
        free_out=(1,),
        grid_spec=pltpu.PrefetchScalarGridSpec(
            num_scalar_prefetch=1,
            grid=(1,),
            in_specs=[pl.BlockSpec((TILE, features), lambda i, m: (4 * part + m[0], 0))]
            + [const(v.shape) for v in mixed] + [const(v.shape) for v in weights] + [const(vectors.shape)]
            + [pl.BlockSpec(memory_space=pl.ANY)] * len(after),
            out_specs=[const((TILE, features)), const((TILE, features)), const((4, width, TILE))],
        ),
        out_shape=[shape_of(TILE, features, dtype=F32), shape_of(TILE, features), shape_of(4, width, TILE)],
        cost_estimate=cost(2e9, 3e6),
        name="middle",
    )


def feed_piece(x, g, inner_ref, vec_ref, outer_ref):
    hidden = nn(x, inner_ref[...]) + vec_ref[7:8, :]
    half = 0.5 + 0.5 * lax.erf(hidden * 0.5 ** 0.5)
    act = (hidden * half).astype(BF16)
    slope = half + hidden * (jnp.exp(-0.5 * hidden * hidden) * 0.3989422804014327)
    dh = (nt(g, outer_ref[...]) * slope).astype(BF16)
    out = nn(act, outer_ref[...]).astype(BF16)
    return act, dh, out, nt(dh, inner_ref[...]).astype(BF16)


def near_body(me_ref, *refs):
    count = 2 * PARTS
    x_refs = refs[:count]
    g_ref, inner_ref, vec_ref, outer_ref = refs[count:count + 4]
    out_refs, back_refs = refs[count + 4:count + 6], refs[count + 6:-6]
    sum_ref, grad_ref, x_all, g_all, act_all, dh_all = refs[-6:]
    i = pl.program_id(0)
    at = pl.ds(pl.multiple_of(i * TILE, TILE), TILE)
    for n, x_ref in enumerate(x_refs):
        @pl.when(i == n)
        def _(n=n, x_ref=x_ref):
            x_all[n * TILE:(n + 1) * TILE] = x_ref[...]

    g_all[at] = g_ref[...]
    act, dh, out, back = feed_piece(x_all[at], g_ref[...], inner_ref, vec_ref, outer_ref)
    act_all[at] = act
    dh_all[at] = dh
    sums = fold(dh.astype(F32))

    @pl.when(i == 0)
    def _():
        sum_ref[...] = jnp.zeros_like(sum_ref)

    sum_ref[...] += sums
    for n in range(count):
        @pl.when(i == n)
        def _(n=n):
            out_refs[n % 2][n // 2 * TILE:(n // 2 + 1) * TILE] = out
            back_refs[n][...] = back

    @pl.when(i == count - 1)
    def _():
        grad_ref[0] = tn(act_all[...], g_all[...]).astype(BF16)
        grad_ref[1] = tn(x_all[...], dh_all[...]).astype(BF16)


def feed_near(me, pieces, cot, inner, vectors, outer):
    features = cot.shape[1]
    units = inner.shape[1]
    count = 2 * PARTS
    piece = const((TILE, features))
    scratch = lambda n: pltpu.VMEM((count * TILE, n), BF16)
    return kernel_call(
        near_body,
        (me, *pieces, cot, inner, vectors, outer),
        free_in=tuple(range(1, count + 1)),
        free_out=(3, 5),
        grid_spec=pltpu.PrefetchScalarGridSpec(
            num_scalar_prefetch=1,
            grid=(count,),
            in_specs=[piece] * count
            + [pl.BlockSpec((TILE, features), lambda i, m: (4 * (i // 2) + (m[0] ^ (i % 2)), 0)),
               const(inner.shape), const(vectors.shape), const(outer.shape)],
            out_specs=[const((PARTS * TILE, features))] * 2 + [piece] * count
            + [const((8, units)), const((2, units, features))],
            scratch_shapes=[scratch(features), scratch(features), scratch(units), scratch(units)],
        ),
        out_shape=[shape_of(PARTS * TILE, features)] * 2 + [shape_of(TILE, features)] * count
        + [shape_of(8, units, dtype=F32), shape_of(2, units, features)],
        cost_estimate=cost(15e9, 12e6, 2e6),
        name="feed_near",
    )


def far_body(me_ref, x0_ref, x1_ref, g_ref, inner_ref, vec_ref, outer_ref, *rest):
    left_ref, right_ref, out0_ref, out1_ref, back0_ref, back1_ref, sum_ref = rest[-7:]
    i = pl.program_id(0)
    for n, x_ref in enumerate((x0_ref, x1_ref)):
        @pl.when(i == n)
        def _(x_ref=x_ref):
            left_ref[1] = x_ref[...]

    right_ref[0] = g_ref[...]
    act, dh, out, back = feed_piece(left_ref[1], g_ref[...], inner_ref, vec_ref, outer_ref)
    left_ref[0] = act
    right_ref[1] = dh
    sums = fold(dh.astype(F32))
    for n, (out_ref, back_ref) in enumerate(((out0_ref, back0_ref), (out1_ref, back1_ref))):
        @pl.when(i == n)
        def _(n=n, out_ref=out_ref, back_ref=back_ref):
            sum_ref[...] = sum_ref[...] + sums if n else sums
            out_ref[...] = out
            back_ref[...] = back


def feed_far(part, me, first, second, cot, inner, vectors, outer, kept):
    features = cot.shape[1]
    units = inner.shape[1]
    rows = pl.BlockSpec((2, TILE, features), lambda i, m: (0, 2 * part + i, 0))
    piece = const((TILE, features))
    half = pl.BlockSpec((TILE, features), lambda i, m: (part, 0))
    return kernel_call(
        far_body,
        (me, first, second, cot, inner, vectors, outer, *kept),
        free_in=(1, 2),
        free_out=(5,),
        grid_spec=pltpu.PrefetchScalarGridSpec(
            num_scalar_prefetch=1,
            grid=(2,),
            in_specs=[
                piece, piece,
                pl.BlockSpec((TILE, features), lambda i, m: (4 * part + (m[0] ^ (2 + i)), 0)),
                const(inner.shape), const(vectors.shape), const(outer.shape),
            ] + [pl.BlockSpec(memory_space=pl.ANY)] * len(kept),
            out_specs=[rows, rows, half, half, piece, piece, const((8, units))],
        ),
        out_shape=[shape_of(2, 2 * PARTS * TILE, features)] * 2 + [shape_of(PARTS * TILE, features)] * 2
        + [shape_of(TILE, features)] * 2 + [shape_of(8, units, dtype=F32)],
        input_output_aliases={7 + n: n for n in range(len(kept))},
        cost_estimate=cost(5e9, 8e6, 1e6),
        name="feed_far",
    )


def feed_grad_body(left_ref, right_ref, before_ref, *rest):
    rest[-1][0] = (tn(left_ref[0], right_ref[0]) + before_ref[0].astype(F32)).astype(BF16)


def feed_grad(left, right, before, after):
    _, rows, features = left.shape
    both = pl.BlockSpec((1, rows, features), lambda i: (i, 0, 0))
    square = pl.BlockSpec((1, features, features), lambda i: (i, 0, 0))
    return kernel_call(
        feed_grad_body,
        (left, right, before, *after),
        free_in=tuple(range(3, 3 + len(after))),
        grid=(2,),
        in_specs=[both, both, square] + [pl.BlockSpec(memory_space=pl.ANY)] * len(after),
        out_specs=[square],
        out_shape=[shape_of(*before.shape)],
        cost_estimate=cost(5e9, 10e6),
        name="feed_grad",
    )[0]


def back_body(me_ref, b0_ref, b1_ref, b2_ref, residual_ref, g_ref, vec_ref, w0_ref, w1_ref, w2_ref, w3_ref,
              *rest):
    grad_ref, low_ref, a0_ref, a1_ref, a2_ref, a3_ref, sum_ref = rest[-7:]
    grad_mid = b0_ref[...].astype(F32) + b1_ref[...].astype(F32) + b2_ref[...].astype(F32)
    normed, scale, _ = stats(residual_ref[...])
    upstream = g_ref[...].astype(F32)
    grad = upstream + norm_back(grad_mid, normed, scale, vec_ref[3:4, :])
    grad_ref[...] = grad
    low = grad.astype(BF16)
    low_ref[...] = low
    for w_ref, a_ref in ((w0_ref, a0_ref), (w1_ref, a1_ref), (w2_ref, a2_ref), (w3_ref, a3_ref)):
        a_ref[...] = nt(w_ref[...], low).astype(BF16)
    for n, value in enumerate((grad_mid * normed, grad_mid, grad, upstream)):
        sum_ref[8 * n:8 * n + 8] = fold(value)


def middle_back(part, me, sums, residual, cot, vectors, weights, after):
    features = cot.shape[1]
    piece = const((TILE, features))
    width = weights[0].shape[0]
    return kernel_call(
        back_body,
        (me, *sums, residual, cot, vectors, *weights, *after),
        free_in=(2, 3) + tuple(range(11, 11 + len(after))),
        free_out=(3, 4, 5),
        grid_spec=pltpu.PrefetchScalarGridSpec(
            num_scalar_prefetch=1,
            grid=(1,),
            in_specs=[piece] * 4
            + [pl.BlockSpec((TILE, features), lambda i, m: (4 * part + m[0], 0)), const(vectors.shape)]
            + [const(v.shape) for v in weights] + [pl.BlockSpec(memory_space=pl.ANY)] * len(after),
            out_specs=[piece, piece] + [const((width, TILE))] * 4 + [const((32, features))],
        ),
        out_shape=[shape_of(TILE, features, dtype=F32), shape_of(TILE, features)]
        + [shape_of(width, TILE)] * 4 + [shape_of(32, features, dtype=F32)],
        cost_estimate=cost(2e9, 4e6),
        name="middle_back",
    )


def output_body(*refs):
    mixed, lows, outs = refs[:PARTS], refs[PARTS:2 * PARTS], refs[2 * PARTS:]
    for n in range(4):
        total = nn(mixed[0][n], lows[0][...])
        for p in range(1, PARTS):
            total = total + nn(mixed[p][n], lows[p][...])
        outs[n][...] = total.astype(BF16)


def output_grad(mixed, lows):
    width, features = mixed[0].shape[1], lows[0].shape[1]
    return kernel_call(
        output_body,
        (*mixed, *lows),
        free_out=(1, 3),
        out_shape=[shape_of(width, features)] * 4,
        cost_estimate=cost(2e9, 4e6),
        name="output_grad",
    )


def tail_body(me_ref, g_ref, wq_ref, wk_ref, wv_ref, x_ref, stat_ref, *rest):
    early, units = rest[:PARTS], rest[PARTS:2 * PARTS + 1]
    o0_ref, o1_ref, o2_ref, o3_ref, apart_ref, vec_ref, sum_ref, row_ref = rest[-8:]
    i, p = pl.program_id(0), pl.program_id(1)
    grads = g_ref[...]
    width = wq_ref.shape[0]
    value = tn(grads[:width], wq_ref[...]) + tn(grads[width:2 * width], wk_ref[...])
    value = value + tn(grads[2 * width:], wv_ref[...])

    @pl.when((i == 0) & (p == 0))
    def _():
        row_ref[...] = jnp.zeros_like(row_ref)
        sum_ref[...] = jnp.zeros_like(sum_ref)

    row_ref[...] += nt(jnp.ones((8, grads.shape[1]), BF16), grads)
    normed = (x_ref[...].astype(F32) - stat_ref[:, 0:1]) * stat_ref[:, 1:2]
    sum_ref[:8] += fold(value * normed)
    sum_ref[8:] += fold(value)
    value = value.astype(BF16)
    for step, o_ref in enumerate((o3_ref, o2_ref, o1_ref, o0_ref)):
        @pl.when(i == step)
        def _(o_ref=o_ref):
            o_ref[pl.ds(pl.multiple_of(p * TILE, TILE), TILE), :] = value

    @pl.when((i == 3) & (p == PARTS - 1))
    def _():
        row = lax.broadcasted_iota(jnp.int32, vec_ref.shape, 0)
        vectors = jnp.zeros(vec_ref.shape, F32)
        before = early[0][...]
        for ref in early[1:]:
            before = before + ref[...]
        parts = [before[8 * n:8 * n + 8] for n in range(4)] + [sum_ref[:8], sum_ref[8:]]
        for n, part in enumerate(parts):
            vectors = jnp.where(row == n, jnp.sum(part, axis=0, keepdims=True), vectors)
        vec_ref[...] = vectors
        inside = units[0][...]
        for ref in units[1:]:
            inside = inside + ref[...]
        apart_ref[...] = jnp.where(row == 6, jnp.sum(inside, axis=0, keepdims=True), 0.0)
        apart_ref[7:8, :row_ref.shape[1]] = row_ref[0:1]
        o3_ref[PARTS * TILE:] = paired(vectors)


def tail(me, grads, wq, wk, wv, tokens, stat, early, units, after):
    deep = grads.shape[0]
    features = wq.shape[1]
    share = const((PARTS * TILE, features))
    more = const((PARTS * TILE + 16, features))
    at = lambda i, p, m: 4 * p + (m[0] ^ (3 - i))
    return kernel_call(
        tail_body,
        (me, grads, wq, wk, wv, tokens, stat, *early, *units, *after),
        free_out=(1, 3),
        grid_spec=pltpu.PrefetchScalarGridSpec(
            num_scalar_prefetch=1,
            grid=(4, PARTS),
            in_specs=[pl.BlockSpec((deep, TILE), lambda i, p, m: (0, at(i, p, m))),
                      const(wq.shape), const(wk.shape), const(wv.shape),
                      pl.BlockSpec((TILE, features), lambda i, p, m: (at(i, p, m), 0)),
                      pl.BlockSpec((TILE, WIDE), lambda i, p, m: (at(i, p, m), 0))]
            + [const(v.shape) for v in (*early, *units)] + [pl.BlockSpec(memory_space=pl.ANY)] * len(after),
            out_specs=[share, share, share, more, const((8, features)), const((8, features))],
            scratch_shapes=[pltpu.VMEM((16, features), F32), pltpu.VMEM((8, deep), F32)],
        ),
        out_shape=[shape_of(PARTS * TILE, features)] * 3 + [shape_of(PARTS * TILE + 16, features)]
        + [shape_of(8, features, dtype=F32)] * 2,
        cost_estimate=cost(4e9, 10e6),
        name="tail",
    )


def chip_body(one_ref, two_ref, vec_ref, *rest):
    out_ref = rest[-1]
    rows = one_ref.shape[0]
    out_ref[:rows] = (one_ref[...].astype(F32) + two_ref[:rows].astype(F32)).astype(BF16)
    out_ref[rows:] = paired(vec_ref[...] + joined(two_ref[rows:]))


def chip_sum(one, two, vectors, after):
    return kernel_call(
        chip_body,
        (one, two, vectors, *after),
        free_in=(1,) + tuple(range(3, 3 + len(after))),
        free_out=(0,),
        grid=(1,),
        in_specs=[const(one.shape), const(two.shape), const(vectors.shape)]
        + [pl.BlockSpec(memory_space=pl.ANY)] * len(after),
        out_specs=[const(two.shape)],
        out_shape=[shape_of(*two.shape)],
        name="chip_sum",
    )[0]


def halves_body(xz_ref, g_ref, go_ref, *rest):
    keep_ref, send_ref = rest[-2:]
    width = go_ref.shape[0]
    for to_ref, half in ((keep_ref, xz_ref[0]), (send_ref, 1 - xz_ref[0])):
        @pl.when(half == 0)
        def _(to_ref=to_ref):
            to_ref[...] = g_ref[:2 * width]

        @pl.when(half == 1)
        def _(to_ref=to_ref):
            to_ref[:width] = g_ref[2 * width:]
            to_ref[width:] = go_ref[...]


def halves(xz, grad_weights, grad_output, after):
    width, features = grad_output.shape
    half = const((2 * width, features))
    return kernel_call(
        halves_body,
        (xz, grad_weights, grad_output, *after),
        free_in=(1, 2, 3),
        grid_spec=pltpu.PrefetchScalarGridSpec(
            num_scalar_prefetch=1,
            grid=(1,),
            in_specs=[const(grad_weights.shape), const(grad_output.shape)]
            + [pl.BlockSpec(memory_space=pl.ANY)] * len(after),
            out_specs=[half, half],
        ),
        out_shape=[shape_of(2 * width, features)] * 2,
        cost_estimate=cost(1e6, 4e6),
        name="halves",
    )


def quarter_body(count, xz_ref, one_ref, two_ref, *rest):
    rows = one_ref.shape[0] // count
    for n, out_ref in enumerate(rest[-count:]):
        at = pl.ds(pl.multiple_of(lax.rem(xz_ref[1] + n, count) * rows, rows), rows)
        out_ref[...] = (one_ref[at, :].astype(F32) + two_ref[at, :].astype(F32)).astype(BF16)


def quarters(xz, one, two, count, after):
    rows, features = one.shape

    def body(*refs):
        quarter_body(count, *refs)

    return kernel_call(
        body,
        (xz, one, two, *after),
        free_in=(2, 3, 4),
        grid_spec=pltpu.PrefetchScalarGridSpec(
            num_scalar_prefetch=1,
            grid=(1,),
            in_specs=[const(one.shape), const(two.shape)] + [pl.BlockSpec(memory_space=pl.ANY)] * len(after),
            out_specs=[const((rows // count, features))] * count,
        ),
        out_shape=[shape_of(rows // count, features)] * count,
        cost_estimate=cost(1e6, 2e6),
        name="quarters",
    )


def paired(value):
    return jnp.concatenate(split(value, 2), axis=0).astype(BF16)


def joined(both):
    both = both.astype(F32)
    half = both.shape[0] // 2
    return both[:half] + both[half:]


def second_body(count, *refs):
    one_ref, two_ref, apart_ref, out_ref = refs[count], refs[count + 1], refs[count + 2], refs[-1]
    rows = refs[0].shape[0]
    total = refs[0][...].astype(F32)
    for ref in refs[1:count]:
        total = total + ref[...].astype(F32)
    out_ref[:rows] = total.astype(BF16)
    out_ref[rows:] = paired(joined(one_ref[...]) + joined(two_ref[...]) + apart_ref[...])


def second(parts, one, two, apart, after):
    count = len(parts)
    rows, features = parts[0].shape
    last = pl.BlockSpec((16, features), lambda i: (one.shape[0] // 16 - 1, 0))

    def body(*refs):
        second_body(count, *refs)

    return kernel_call(
        body,
        (*parts, one, two, apart, *after),
        free_in=tuple(range(1, count + 2)) + tuple(range(count + 3, count + 3 + len(after))),
        grid=(1,),
        in_specs=[const((rows, features))] * count + [last, last, const(apart.shape)]
        + [pl.BlockSpec(memory_space=pl.ANY)] * len(after),
        out_specs=[const((rows + 16, features))],
        out_shape=[shape_of(rows + 16, features)],
        name="second",
    )[0]


def third_body(count, xz_ref, *refs):
    out_ref = refs[-1]
    step = out_ref.shape[0] - (refs[0].shape[0] * count - out_ref.shape[0]) // (count - 1)
    rows = step // count
    sums = None
    for n, ref in enumerate(refs[:count]):
        place_at = lax.rem(xz_ref[1] + count - n, count)
        out_ref[pl.ds(pl.multiple_of(place_at * rows, rows), rows), :] = ref[:rows]
        value = joined(ref[rows:])
        sums = value if sums is None else sums + value
    out_ref[step:] = paired(sums)


def third(xz, pieces, extra, after):
    count = len(pieces)
    rows, features = pieces[0].shape
    total = (rows - extra) * count + extra

    def body(*refs):
        third_body(count, *refs)

    return kernel_call(
        body,
        (xz, *pieces, *after),
        free_in=tuple(range(1, count + 1)),
        grid_spec=pltpu.PrefetchScalarGridSpec(
            num_scalar_prefetch=1,
            grid=(1,),
            in_specs=[const((rows, features))] * count + [pl.BlockSpec(memory_space=pl.ANY)] * len(after),
            out_specs=[const((total, features))],
        ),
        out_shape=[shape_of(total, features)],
        name="third",
    )[0]


def ready_body(xz_ref, mine_ref, other_ref, *rest):
    outs = rest[-14:]
    width = outs[0].shape[0]
    for n, out_ref in enumerate(outs[:4]):
        rows = slice(n % 2 * width, (n % 2 + 1) * width)
        for to_ref, chosen in ((mine_ref, xz_ref[0] == n // 2), (other_ref, xz_ref[0] != n // 2)):
            @pl.when(chosen)
            def _(to_ref=to_ref, out_ref=out_ref, rows=rows):
                out_ref[...] = to_ref[rows].astype(F32)

    small = joined(mine_ref[2 * width:]) + joined(other_ref[2 * width:])
    for n, out_ref in enumerate(outs[4:11]):
        out_ref[...] = small[n]
    for n, out_ref in enumerate(outs[11:]):
        out_ref[...] = small[7, n * width:(n + 1) * width]


def ready(xz, mine, other, width, after):
    rows, features = mine.shape
    sizes = [(features,)] * 7 + [(width,)] * 3
    return kernel_call(
        ready_body,
        (xz, mine, other, *after),
        free_in=(2,),
        grid_spec=pltpu.PrefetchScalarGridSpec(
            num_scalar_prefetch=1,
            grid=(1,),
            in_specs=[const(mine.shape), const(other.shape)] + [pl.BlockSpec(memory_space=pl.ANY)] * len(after),
            out_specs=[const((width, features))] * 4 + [const(size) for size in sizes],
        ),
        out_shape=[shape_of(width, features, dtype=F32)] * 4 + [shape_of(*size, dtype=F32) for size in sizes],
        cost_estimate=cost(1e6, 4e6),
        name="ready",
    )


def final_body(me_ref, b0_ref, b1_ref, b2_ref, x_ref, *rest):
    grad_refs, vec_ref, out_ref = rest[:PARTS], rest[PARTS], rest[-1]
    p = pl.program_id(0)
    grad_attend = b0_ref[...].astype(F32) + b1_ref[...].astype(F32) + b2_ref[...].astype(F32)
    normed, scale, _ = stats(x_ref[...].astype(F32))
    back = norm_back(grad_attend, normed, scale, vec_ref[0:1, :])
    for n, grad_ref in enumerate(grad_refs):
        @pl.when(p == n)
        def _(grad_ref=grad_ref):
            out_ref[...] = (grad_ref[...] + back).astype(BF16)


def final(me, sums, tokens, grads, vectors, after):
    features = tokens.shape[1]
    rows = pl.BlockSpec((TILE, features), lambda p, m: (p, 0))
    return kernel_call(
        final_body,
        (me, *sums, tokens, *grads, vectors, *after),
        free_in=(2, 3) + tuple(range(6 + PARTS, 6 + PARTS + len(after))),
        free_out=(0,),
        grid_spec=pltpu.PrefetchScalarGridSpec(
            num_scalar_prefetch=1,
            grid=(PARTS,),
            in_specs=[rows] * 3 + [pl.BlockSpec((TILE, features), lambda p, m: (4 * p + m[0], 0))]
            + [const((TILE, features))] * PARTS + [const(vectors.shape)]
            + [pl.BlockSpec(memory_space=pl.ANY)] * len(after),
            out_specs=[rows],
        ),
        out_shape=[shape_of(PARTS * TILE, features)],
        cost_estimate=cost(1e8, 5e6),
        name="final",
    )[0]


def place_body(me_ref, p0_ref, p1_ref, p2_ref, p3_ref, *rest):
    out_ref = rest[-1]
    for step, p_ref in enumerate((p0_ref, p1_ref, p2_ref, p3_ref)):
        @pl.when(pl.program_id(0) == step)
        def _(p_ref=p_ref):
            at = pl.ds(pl.multiple_of(pl.program_id(1) * TILE, TILE), TILE)
            out_ref[...] = p_ref[at, :].astype(out_ref.dtype)


def place(me, shares, dtype, after):
    rows, features = shares[0].shape
    return kernel_call(
        place_body,
        (me, *shares, *after),
        free_in=(1, 2, 3, 4),
        grid_spec=pltpu.PrefetchScalarGridSpec(
            num_scalar_prefetch=1,
            grid=(4, PARTS),
            in_specs=[const((rows, features))] * 4 + [pl.BlockSpec(memory_space=pl.ANY)] * len(after),
            out_specs=pl.BlockSpec((TILE, features), lambda i, p, m: (4 * p + (m[0] ^ i), 0)),
        ),
        out_shape=shape_of(4 * rows, features, dtype=dtype),
        cost_estimate=cost(1e6, 9e6),
        name="place",
    )


def fence_body(*refs):
    pass


def fence(value, *after, space=pltpu.HBM):
    anywhere = pl.BlockSpec(memory_space=pl.ANY)
    return pl.pallas_call(
        fence_body,
        in_specs=[anywhere] * (1 + len(after)),
        out_specs=anywhere,
        out_shape=space(value.shape, value.dtype),
        input_output_aliases={0: 0},
        name="fence",
    )(pltpu.with_memory_space_constraint(value, space), *after)


def other_core(value):
    return lax.ppermute(value, "core", SWAP)


def other_chip(value):
    return lax.ppermute(value, "y", SWAP)


def crosswise(value):
    return lax.ppermute(value, MP, [(n, n ^ 3) for n in range(4)])


def exchange(pieces):
    return [pieces[0], other_core(pieces[1]), other_chip(pieces[2]), crosswise(pieces[3])]


def gather_sum(pieces):
    near = other_core(pieces[1])
    far = (pieces[2].astype(F32) + other_core(pieces[3]).astype(F32)).astype(BF16)
    return [pieces[0], near, other_chip(far)], far


def spread(value):
    far = other_chip(value)
    return [value, other_core(value), far, other_core(far)]


def pick(values, at):
    return lax.dynamic_index_in_dim(values, at, 0, keepdims=False)


def turned(values, way):
    size = lax.axis_size("z")
    return lax.ppermute(values, "z", [(n, (n + way) % size) for n in range(size)])


def sum_first(xz, keep, got, after):
    size = lax.axis_size("z")
    if size > 4:
        return [lax.psum(keep + got, "z")]
    return quarters(xz, keep, got, size, after)


def gather_z(value):
    size = lax.axis_size("z")
    if size > 4:
        return [lax.all_gather(value, "z", axis=0, tiled=True)]
    return [turned(value, way) if way else value for way in range(size)]


def local(
    tokens,
    segment_ids,
    gain_one,
    bias_one,
    query_weight,
    query_bias,
    key_weight,
    value_weight,
    value_bias,
    output_weight,
    output_bias,
    gain_two,
    bias_two,
    inner_weight,
    inner_bias,
    outer_weight,
    outer_bias,
    cotangent,
):
    _, length, features = tokens.shape
    width = query_weight.shape[1]
    heads = width // HEAD
    tokens = tokens.reshape(length, features)
    cot = cotangent.reshape(length, features)
    at = lax.axis_index(MP).astype(jnp.int32)
    me = at[None]
    apart = jnp.concatenate([query_bias, value_bias, jnp.zeros((features - 2 * width,), F32)])
    vectors = jnp.concatenate([gain_one, bias_one, output_bias, gain_two, bias_two, outer_bias, apart, inner_bias])
    vectors = vectors.reshape(8, features)
    wq, wk, wv = query_weight.T, key_weight.T, value_weight.T

    output_weights = spread(output_weight)
    attend_in, qt, kt, vt, kn, vn, stat = project(tokens, segment_ids, vectors, wq, wk, wv, heads)

    parts = range(PARTS)
    attended, extras, fours = [], [], []
    for p in parts:
        out, extra, *four = attend_forward(p, me, segment_ids, qt, kn, vt, output_weights[1:3] if p == 0 else ())
        attended.append(out)
        extras.append(extra)
        fours.append(exchange(four))
    mixed, residuals, pieces = [], [], []
    for p in parts:
        residual, own, together = middle(p, me, tokens, fours[p], output_weights, vectors, extras[p + 1:])
        mixed.append(together)
        residuals.append(residual)
        pieces.append([own, other_core(own), other_chip(own)])

    backs = {}
    *outs, b00, b01, b10, b11, near_sum, near_grad = feed_near(
        me, [pieces[p][n] for p in parts for n in (0, 1)], cot, inner_weight, vectors, outer_weight
    )
    backs[0, 0], backs[0, 1], backs[1, 0], backs[1, 1] = b00, b01, b10, b11
    sums, kept, gathered, far_sums, behind = [near_sum], (), [], [], b00
    for p in parts:
        far = fence(pieces[p][2], behind, space=pltpu.VMEM)
        *kept, backs[p, 2], backs[p, 3], far_sum = feed_far(
            p, me, far, other_core(far), cot, inner_weight, vectors, outer_weight, kept
        )
        behind = backs[p, 2]
        sums.append(far_sum)
        if p:
            backs[p, 3] = fence(backs[p, 3], gathered[-1][2], space=pltpu.VMEM)
            feed_sum = feed_grad(kept[0], kept[1], near_grad, ())
            backs[p, 2] = fence(backs[p, 2], feed_sum)
        summed, far_sum = gather_sum([backs[p, n] for n in range(4)])
        gathered.append(summed)
        far_sums.append(far_sum)
    left, right, *far_outs = kept
    outs += far_outs
    feed_sum = lax.psum_scatter(feed_sum.reshape(-1, features), DP, scatter_dimension=0, tiled=True)
    grad_residuals, lows, grads_attended, inner_sums = [], [], [], []
    for p in parts:
        grad, low, a0, a1, a2, a3, vector = middle_back(
            p, me, gathered[p], residuals[p], cot, vectors, output_weights, far_sums[p + 1:]
        )
        grad_residuals.append(grad)
        lows.append(low)
        inner_sums.append(vector)
        grads_attended.append(exchange([a0, a1, a2, a3]))

    near = other_core(fence(outs[1], *far_sums))
    far = (outs[2].astype(F32) + other_core(fence(outs[3], *far_sums)).astype(F32)).astype(BF16)
    far = fence(far, lows[-1], space=pltpu.VMEM)
    part = output_grad(mixed, lows)
    earlier = attend_backward(0, me, segment_ids, qt, extras[0], kn, kt, vn, attended[0], grads_attended[0], (),
                              (far, near, part[0]))
    there = other_chip(far)
    part_far = fence(part[2], earlier[0])
    part_far = (part_far.astype(F32) + other_core(part[3]).astype(F32)).astype(BF16)
    part_near = other_core(part[1])
    grads = attend_backward(1, me, segment_ids, qt, extras[1], kn, kt, vn, attended[1], grads_attended[1], earlier,
                            (part_near, part_far, there))

    xz = jnp.stack([lax.axis_index("x"), lax.axis_index("z")]).astype(jnp.int32)
    part_across = other_chip(part_far)
    grad_output = fence(part[0], grads).astype(F32) + part_near.astype(F32) + part_across.astype(F32)
    keep, send = halves(xz, nn(grads, attend_in).astype(BF16), grad_output.astype(BF16), ())
    result = jnp.concatenate(residuals) + fence(outs[0], send).astype(F32) + near.astype(F32)
    result = (result + there.astype(F32) + outer_bias).astype(BF16)
    near, far = other_core(result), other_chip(result)
    got = lax.ppermute(send, "x", SWAP)
    back_own, back_near, back_far, back_across, apart, summed = tail(
        me, grads, wq, wk, wv, tokens, stat, inner_sums, sums, (send,)
    )
    feed_sum = lax.all_gather(fence(feed_sum, send), DP, axis=0, tiled=True)
    feed_sum = (feed_sum[:features].astype(F32), feed_sum[features:].astype(F32))
    quarter = sum_first(xz, keep, got, (near, far, apart))
    back_across = other_core(fence(back_across, quarter[-1], space=pltpu.VMEM))
    back_far = chip_sum(back_far, back_across, summed, ())
    back_there = other_chip(back_far)
    share = final(me, [back_own, other_core(back_near), back_there], tokens, grad_residuals, vectors, ())
    if len(quarter) > 1:
        turns = [quarter[0]] + [turned(part, n + 1) for n, part in enumerate(quarter[1:])]
        held = second(turns, back_far, back_there, apart, (share,))
        layer_out = place(me, [result, near, far, other_core(far)], BF16, (held,))
        mine = third(xz, gather_z(held), 16, (layer_out,))
    else:
        small = joined(back_far[-16:]) + joined(back_there[-16:]) + apart
        layer_out = place(me, [result, near, far, other_core(far)], BF16, ())
        mine = jnp.concatenate([quarter[0], paired(lax.psum(small, "z"))])
    share = fence(share, held if len(quarter) > 1 else mine, space=pltpu.VMEM)
    near, far = other_core(share), fence(other_chip(share), mine, space=pltpu.VMEM)
    input_grad = place(me, [share, near, far, other_core(far)], F32, (mine,))
    *wide, two_gain, two_bias, output_sum, outer_bias, one_gain, one_bias, inner_bias, query, _, value = ready(
        xz, mine, lax.ppermute(mine, "x", SWAP), width, feed_sum
    )
    return (
        layer_out.reshape(1, length, features),
        input_grad.reshape(1, length, features),
        one_gain,
        one_bias,
        wide[0].T,
        query,
        wide[1].T,
        wide[2].T,
        value,
        wide[3],
        output_sum,
        two_gain,
        two_bias,
        feed_sum[1],
        inner_bias,
        feed_sum[0],
        outer_bias,
    )


def solution(mesh):
    rows = mesh.shape["dp"]
    inner = Mesh(mesh.devices.reshape(rows // 2, 2, 2, 2), DP + MP)
    placed = (
        P(DP, None, None),
        P(DP, None),
        P(),
        P(),
        P(None, MP),
        P(MP),
        P(None, MP),
        P(None, MP),
        P(MP),
        P(MP, None),
        P(),
        P(),
        P(),
        P(None, MP),
        P(MP),
        P(MP, None),
        P(),
        P(DP, None, None),
    )
    return jax.shard_map(
        local,
        mesh=inner,
        in_specs=placed,
        out_specs=(
            P(DP, None, None),
            P(DP, None, None),
            P(),
            P(),
            P(None, MP),
            P(MP),
            P(None, MP),
            P(None, MP),
            P(MP),
            P(MP, None),
            P(),
            P(),
            P(),
            P(None, MP),
            P(MP),
            P(MP, None),
            P(),
        ),
        check_vma=False,
    )
```

```python
import jax
import jax.numpy as jnp
from jax import lax
from jax.experimental import pallas as pl
from jax.experimental.pallas import tpu as pltpu
from jax.sharding import Mesh
from jax.sharding import PartitionSpec as P

HEAD = 64
WIDE = 128
TILE = 256
LONG = 512
PARTS = 2
MASKED = 1e30
SCALE = 1
F32 = jnp.float32
BF16 = jnp.bfloat16
DP = ("z", "x")
MP = ("y", "core")
SWAP = [(0, 1), (1, 0)]


def nn(left, right):
    return lax.dot_general(left, right, (((1,), (0,)), ((), ())), preferred_element_type=F32)


def nt(left, right):
    return lax.dot_general(left, right, (((1,), (1,)), ((), ())), preferred_element_type=F32)


def tn(left, right):
    return lax.dot_general(left, right, (((0,), (0,)), ((), ())), preferred_element_type=F32)


def stats(values):
    mean = jnp.mean(values, axis=-1, keepdims=True)
    center = values - mean
    scale = lax.rsqrt(jnp.mean(center * center, axis=-1, keepdims=True) + 1e-05)
    return center * scale, scale, mean


def norm_back(grad_out, normed, scale, gain):
    upstream = grad_out * gain
    return scale * (
        upstream
        - jnp.mean(upstream, axis=-1, keepdims=True)
        - normed * jnp.mean(upstream * normed, axis=-1, keepdims=True)
    )


def fold(values):
    return jnp.sum(values.reshape(-1, 8, values.shape[-1]), axis=0)


def split(value, parts):
    out = []
    for _ in range(parts):
        piece = value.astype(BF16).astype(F32)
        out.append(piece)
        value = value - piece
    return out


def const(shape):
    return pl.BlockSpec(shape, lambda *_: (0,) * len(shape))


def shape_of(*dims, dtype=BF16):
    return jax.ShapeDtypeStruct(dims, dtype)


def params(mib=40):
    return pltpu.CompilerParams(vmem_limit_bytes=mib << 20)


def kernel_call(body, values, free_in=(), free_out=(), **options):
    shapes = options.pop("out_shape")
    many = isinstance(shapes, (list, tuple))
    shapes = [s if n in free_out else pltpu.HBM(s.shape, s.dtype) for n, s in enumerate(shapes if many else [shapes])]
    values = [
        v if n in free_in or v.dtype == jnp.int32 else pltpu.with_memory_space_constraint(v, pltpu.HBM)
        for n, v in enumerate(values)
    ]
    return pl.pallas_call(
        body, out_shape=shapes if many else shapes[0], compiler_params=params(), **options
    )(*values)


def cost(flops, moved, special=0):
    return pl.CostEstimate(flops=int(flops * SCALE), bytes_accessed=int(moved * SCALE), transcendentals=0)


def project_body(x_ref, seg_ref, vec_ref, wq_ref, wk_ref, wv_ref,
                 ai_ref, qt_ref, kt_ref, vt_ref, kn_ref, vn_ref, stat_ref):
    heads = kn_ref.shape[0]
    width = heads * HEAD
    tile = x_ref.shape[0]
    normed, scale, mean = stats(x_ref[...].astype(F32))
    lane = lax.broadcasted_iota(jnp.int32, stat_ref.shape, 1)
    stat_ref[...] = jnp.where(lane == 0, mean, scale)
    ai = (normed * vec_ref[0:1, :] + vec_ref[1:2, :]).astype(BF16)
    ai_ref[...] = ai
    column = vec_ref[...].T[:2 * width, 6:7]
    queries = ((nt(wq_ref[...], ai) + column[:width]).astype(BF16)).astype(F32) * HEAD ** -0.5
    keys = nt(wk_ref[...], ai)
    kt_ref[...] = keys.astype(BF16)
    values = nt(wv_ref[...], ai) + column[width:]
    row = lax.broadcasted_iota(jnp.int32, (HEAD, tile), 0)
    same = jnp.where(row == seg_ref[...], 1.0, 0.0)
    mask = jnp.where(row < 8, (same - 1.0) * MASKED, jnp.where(row < 11, 1.0, 0.0))
    ones = jnp.where(row < 2, 1.0, 0.0)
    first = jnp.where(row[:16] == 0, 1.0, 0.0).astype(BF16)
    for h in range(heads):
        rows = slice(h * HEAD, (h + 1) * HEAD)
        qt_ref[h, :HEAD, :] = queries[rows].astype(BF16)
        qt_ref[h, HEAD:, :] = same.astype(BF16)
        vt_ref[h, :HEAD, :] = values[rows].astype(BF16)
        vt_ref[h, HEAD:, :] = first
        kn_ref[h] = jnp.concatenate([keys[rows], mask], axis=0).T.astype(BF16)
        vn_ref[h] = jnp.concatenate([values[rows], ones], axis=0).T.astype(BF16)


def project(tokens, seg_row, vectors, wq, wk, wv, heads):
    length, features = tokens.shape
    width = heads * HEAD
    return kernel_call(
        project_body,
        (tokens, seg_row, vectors, wq, wk, wv),
        grid=(length // LONG,),
        in_specs=[
            pl.BlockSpec((LONG, features), lambda i: (i, 0)),
            pl.BlockSpec((1, LONG), lambda i: (0, i)),
            const(vectors.shape), const(wq.shape), const(wk.shape), const(wv.shape),
        ],
        out_specs=[
            pl.BlockSpec((LONG, features), lambda i: (i, 0)),
            pl.BlockSpec((heads, WIDE, LONG), lambda i: (0, 0, i)),
            pl.BlockSpec((width, LONG), lambda i: (0, i)),
            pl.BlockSpec((heads, HEAD + 16, LONG), lambda i: (0, 0, i)),
            pl.BlockSpec((heads, LONG, WIDE), lambda i: (0, i, 0)),
            pl.BlockSpec((heads, LONG, WIDE), lambda i: (0, i, 0)),
            pl.BlockSpec((LONG, WIDE), lambda i: (i, 0)),
        ],
        out_shape=[
            shape_of(length, features),
            shape_of(heads, WIDE, length),
            shape_of(width, length),
            shape_of(heads, HEAD + 16, length),
            shape_of(heads, length, WIDE),
            shape_of(heads, length, WIDE),
            shape_of(length, WIDE, dtype=F32),
        ],
        cost_estimate=cost(6e9, 14e6),
        name="project",
    )


def key_range(seg_ref, seg_all, i):
    first = seg_ref[0, i * TILE]
    last = seg_ref[0, i * TILE + TILE - 1]
    before = jnp.sum(jnp.where(seg_all < first, 1.0, 0.0)).astype(jnp.int32)
    until = jnp.sum(jnp.where(seg_all <= last, 1.0, 0.0)).astype(jnp.int32)
    return before // TILE, (until + TILE - 1) // TILE


def by_blocks(low, high, step, carry):
    keys = lambda kb: pl.ds(pl.multiple_of(kb * TILE, TILE), TILE)
    for many in (3, 2, 1):
        rounds = (high - low) // many
        run = lambda n, c, low=low, many=many: step([keys(low + many * n + k) for k in range(many)], c)
        carry = lax.fori_loop(0, rounds, run, carry)
        low = low + many * rounds
    return carry


def shifted(one_hot, pieces):
    row = lax.broadcasted_iota(jnp.int32, one_hot.shape, 0)
    value = one_hot
    for n, piece in enumerate(pieces):
        value = jnp.where(row == 8 + n, piece, value)
    return value.astype(BF16)


def forward_body(offset, me_ref, segs_ref, seg_ref, qt_ref, kn_ref, vt_ref, *rest):
    out_ref, extra_ref, o0_ref, o1_ref, o2_ref, o3_ref, acc_ref = rest[-7:]
    heads, _, tile = qt_ref.shape
    i = pl.program_id(0)
    low, high = key_range(segs_ref, seg_ref[...], i + offset)
    acc_ref[...] = jnp.zeros_like(acc_ref)

    def step(keys, tops):
        scores = [[nn(kn_ref[h, at, :], qt_ref[h]) for at in keys] for h in range(heads)]
        new_tops = []
        for h in range(heads):
            top = tops[h]
            for score in scores[h]:
                top = jnp.maximum(top, jnp.max(score, axis=0, keepdims=True))
            new_tops.append(top)
        powered = [[jnp.exp(score - new_tops[h]).astype(BF16) for score in scores[h]] for h in range(heads)]
        for h in range(heads):
            total = acc_ref[h] * jnp.exp(tops[h] - new_tops[h])
            for at, power in zip(keys, powered[h]):
                total = total + nn(vt_ref[h, :, at], power)
            acc_ref[h] = total
        return tuple(new_tops)

    tops = by_blocks(low, high, step, (jnp.full((1, tile), -jnp.inf, F32),) * heads)
    for h in range(heads):
        total = acc_ref[h, HEAD:HEAD + 1, :]
        out_ref[0, h * HEAD:(h + 1) * HEAD, :] = (acc_ref[h, :HEAD, :] / total).astype(BF16)
        one_hot = qt_ref[h, HEAD:HEAD + 16, :].astype(F32)
        extra_ref[h] = shifted(one_hot, split(-(tops[h] + jnp.log(total)), 3))
    for n, o_ref in enumerate((o0_ref, o1_ref, o2_ref, o3_ref)):
        @pl.when((i ^ me_ref[0]) == n)
        def _(o_ref=o_ref):
            o_ref[...] = out_ref[0]


def attend_forward(part, me, seg_row, qt, kn, vt, after):
    heads, _, length = qt.shape
    width = heads * HEAD
    count = length // TILE // PARTS
    offset = part * count

    def body(*refs):
        forward_body(offset, *refs)

    return kernel_call(
        body,
        (me, seg_row, seg_row, qt, kn, vt, *after),
        free_in=tuple(range(6, 6 + len(after))),
        free_out=(3, 4, 5),
        grid_spec=pltpu.PrefetchScalarGridSpec(
            num_scalar_prefetch=1,
            grid=(count,),
            in_specs=[
                pl.BlockSpec(memory_space=pltpu.SMEM),
                const((1, length)),
                pl.BlockSpec((heads, WIDE, TILE), lambda i, m: (0, 0, i + offset)),
                const(kn.shape), const(vt.shape),
            ] + [pl.BlockSpec(memory_space=pl.ANY)] * len(after),
            out_specs=[
                pl.BlockSpec((1, width, TILE), lambda i, m: (i, 0, 0)),
                pl.BlockSpec((heads, 16, TILE), lambda i, m: (0, 0, i)),
            ] + [const((width, TILE))] * 4,
            scratch_shapes=[pltpu.VMEM((heads, HEAD + 16, TILE), F32)],
        ),
        out_shape=[shape_of(count, width, TILE), shape_of(heads, 16, count * TILE)] + [shape_of(width, TILE)] * 4,
        cost_estimate=cost(9e9, 5e6, 4e6),
        name="attend_forward",
    )


def backward_body(part, me_ref, segs_ref, seg_ref, qt_ref, extra_ref, kn_ref, kt_ref, vn_ref, out_ref,
                  g0_ref, g1_ref, g2_ref, g3_ref, *rest):
    heads, _, tile = qt_ref.shape
    width = heads * HEAD
    length = kt_ref.shape[1]
    if part == 0:
        dq_out, dk_ref, dv_ref, qa_ref, da_ref, dq_ref = rest[-6:]
    else:
        dq_in, dk_in, dv_in = rest[:3]
        grads_ref, qa_ref, da_ref, dq_ref, dk_ref, dv_ref = rest[-6:]
    i = pl.program_id(0)
    count = length // TILE // PARTS
    at_here = i + part * count
    low, high = key_range(segs_ref, seg_ref[...], at_here)

    @pl.when(i == 0)
    def _():
        if part == 0:
            dk_ref[...] = jnp.zeros_like(dk_ref)
            dv_ref[...] = jnp.zeros_like(dv_ref)
        else:
            dk_ref[...] = dk_in[...]
            dv_ref[...] = dv_in[...]
            grads_ref[:width, :count * TILE] = dq_in[...]
        qa_ref[...] = jnp.zeros_like(qa_ref)
        da_ref[...] = jnp.zeros_like(da_ref)

    source = i ^ me_ref[0]
    for n, g_ref in enumerate((g0_ref, g1_ref, g2_ref, g3_ref)):
        @pl.when(source == n)
        def _(g_ref=g_ref):
            for h in range(heads):
                da_ref[h, :HEAD, :] = g_ref[h * HEAD:(h + 1) * HEAD]

    dq_ref[...] = jnp.zeros_like(dq_ref)
    row = lax.broadcasted_iota(jnp.int32, (16, tile), 0)
    for h in range(heads):
        rows = slice(h * HEAD, (h + 1) * HEAD)
        qa_ref[h, :HEAD, :] = qt_ref[h, :HEAD, :]
        qa_ref[h, HEAD:HEAD + 16, :] = extra_ref[h]
        inner = jnp.sum(da_ref[h, :HEAD, :].astype(F32) * out_ref[0, rows].astype(F32), axis=0, keepdims=True)
        first, second = split(-inner, 2)
        value = jnp.where(row == 0, first, jnp.where(row == 1, second, 0.0))
        da_ref[h, HEAD:HEAD + 16, :] = value.astype(BF16)

    def step(keys, carry):
        every = range(heads)
        rows = [slice(h * HEAD, (h + 1) * HEAD) for h in every]
        scores = [[nn(kn_ref[h, at, :], qa_ref[h]) for at in keys] for h in every]
        slopes = [[nn(vn_ref[h, at, :], da_ref[h]) for at in keys] for h in every]
        probs = [[jnp.exp(score) for score in scores[h]] for h in every]
        ds = [[(p * s).astype(BF16) for p, s in zip(probs[h], slopes[h])] for h in every]
        probs = [[p.astype(BF16) for p in probs[h]] for h in every]
        for h in every:
            total = dq_ref[rows[h]]
            for n, at in enumerate(keys):
                dv_ref[rows[h], at] += nt(da_ref[h, :HEAD, :], probs[h][n])
                dk_ref[rows[h], at] += nt(qa_ref[h, :HEAD, :], ds[h][n])
                total = total + nn(kt_ref[rows[h], at], ds[h][n])
            dq_ref[rows[h]] = total
        return carry

    by_blocks(low, high, step, 0)
    dq = (dq_ref[...] * HEAD ** -0.5).astype(BF16)
    if part == 0:
        dq_out[...] = dq
    else:
        grads_ref[:width, pl.ds(pl.multiple_of(at_here * TILE, TILE), TILE)] = dq

        @pl.when(i == pl.num_programs(0) - 1)
        def _():
            grads_ref[width:2 * width] = dk_ref[...].astype(BF16)
            grads_ref[2 * width:] = dv_ref[...].astype(BF16)


def attend_backward(part, me, seg_row, qt, extra, kn, kt, vn, out, grad, earlier, after):
    heads, _, length = qt.shape
    width = heads * HEAD
    count = length // TILE // PARTS
    offset = part * count

    def body(*refs):
        backward_body(part, *refs)

    in_specs = [
        pl.BlockSpec(memory_space=pltpu.SMEM),
        const((1, length)),
        pl.BlockSpec((heads, WIDE, TILE), lambda i, m: (0, 0, i + offset)),
        pl.BlockSpec((heads, 16, TILE), lambda i, m: (0, 0, i)),
        const(kn.shape), const(kt.shape), const(vn.shape),
        pl.BlockSpec((1, width, TILE), lambda i, m: (i, 0, 0)),
        const(grad[0].shape), const(grad[1].shape), const(grad[2].shape), const(grad[3].shape),
    ] + [const(v.shape) for v in earlier] + [pl.BlockSpec(memory_space=pl.ANY)] * len(after)
    scratch = [
        pltpu.VMEM((heads, WIDE, TILE), BF16),
        pltpu.VMEM((heads, WIDE, TILE), BF16),
        pltpu.VMEM((width, TILE), F32),
    ]
    if part == 0:
        out_specs = [pl.BlockSpec((width, TILE), lambda i, m: (0, i)), const((width, length)), const((width, length))]
        out_shape = [shape_of(width, count * TILE), shape_of(width, length, dtype=F32), shape_of(width, length, dtype=F32)]
    else:
        out_specs = const((3 * width, length))
        out_shape = shape_of(3 * width, length)
        scratch += [pltpu.VMEM((width, length), F32), pltpu.VMEM((width, length), F32)]
    return kernel_call(
        body,
        (me, seg_row, seg_row, qt, extra, kn, kt, vn, out, *grad, *earlier, *after),
        free_in=(10, 11, 12) + tuple(range(13 + len(earlier), 15 + len(earlier))),
        grid_spec=pltpu.PrefetchScalarGridSpec(
            num_scalar_prefetch=1, grid=(count,), in_specs=in_specs, out_specs=out_specs, scratch_shapes=scratch,
        ),
        out_shape=out_shape,
        cost_estimate=cost(16e9, 10e6, 4e6),
        name="attend_backward",
    )


def middle_body(me_ref, x_ref, m0_ref, m1_ref, m2_ref, m3_ref, w0_ref, w1_ref, w2_ref, w3_ref,
                vec_ref, *rest):
    residual_ref, own_ref, mixed_ref = rest[-3:]
    total = x_ref[...].astype(F32) + vec_ref[2:3, :]
    pairs = ((m0_ref, w0_ref), (m1_ref, w1_ref), (m2_ref, w2_ref), (m3_ref, w3_ref))
    for n, (m_ref, w_ref) in enumerate(pairs):
        total = total + tn(m_ref[...], w_ref[...])
        mixed_ref[n] = m_ref[...]
    residual_ref[...] = total
    normed, _, _ = stats(total)
    own_ref[...] = (normed * vec_ref[3:4, :] + vec_ref[4:5, :]).astype(BF16)


def middle(part, me, tokens, mixed, weights, vectors, after):
    features = tokens.shape[1]
    width = weights[0].shape[0]
    return kernel_call(
        middle_body,
        (me, tokens, *mixed, *weights, vectors, *after),
        free_in=(3, 4, 5),
        free_out=(1,),
        grid_spec=pltpu.PrefetchScalarGridSpec(
            num_scalar_prefetch=1,
            grid=(1,),
            in_specs=[pl.BlockSpec((TILE, features), lambda i, m: (4 * part + m[0], 0))]
            + [const(v.shape) for v in mixed] + [const(v.shape) for v in weights] + [const(vectors.shape)]
            + [pl.BlockSpec(memory_space=pl.ANY)] * len(after),
            out_specs=[const((TILE, features)), const((TILE, features)), const((4, width, TILE))],
        ),
        out_shape=[shape_of(TILE, features, dtype=F32), shape_of(TILE, features), shape_of(4, width, TILE)],
        cost_estimate=cost(2e9, 3e6),
        name="middle",
    )


def feed_piece(x, g, inner_ref, vec_ref, outer_ref):
    hidden = nn(x, inner_ref[...]) + vec_ref[7:8, :]
    half = 0.5 + 0.5 * lax.erf(hidden * 0.5 ** 0.5)
    act = (hidden * half).astype(BF16)
    slope = half + hidden * (jnp.exp(-0.5 * hidden * hidden) * 0.3989422804014327)
    dh = (nt(g, outer_ref[...]) * slope).astype(BF16)
    out = nn(act, outer_ref[...]).astype(BF16)
    return act, dh, out, nt(dh, inner_ref[...]).astype(BF16)


def near_body(me_ref, *refs):
    count = 2 * PARTS
    x_refs = refs[:count]
    g_ref, inner_ref, vec_ref, outer_ref = refs[count:count + 4]
    out_refs, back_refs = refs[count + 4:count + 6], refs[count + 6:-6]
    sum_ref, grad_ref, x_all, g_all, act_all, dh_all = refs[-6:]
    i = pl.program_id(0)
    at = pl.ds(pl.multiple_of(i * TILE, TILE), TILE)
    for n, x_ref in enumerate(x_refs):
        @pl.when(i == n)
        def _(n=n, x_ref=x_ref):
            x_all[n * TILE:(n + 1) * TILE] = x_ref[...]

    g_all[at] = g_ref[...]
    act, dh, out, back = feed_piece(x_all[at], g_ref[...], inner_ref, vec_ref, outer_ref)
    act_all[at] = act
    dh_all[at] = dh
    sums = fold(dh.astype(F32))

    @pl.when(i == 0)
    def _():
        sum_ref[...] = jnp.zeros_like(sum_ref)

    sum_ref[...] += sums
    for n in range(count):
        @pl.when(i == n)
        def _(n=n):
            out_refs[n % 2][n // 2 * TILE:(n // 2 + 1) * TILE] = out
            back_refs[n][...] = back

    @pl.when(i == count - 1)
    def _():
        grad_ref[0] = tn(act_all[...], g_all[...]).astype(BF16)
        grad_ref[1] = tn(x_all[...], dh_all[...]).astype(BF16)


def feed_near(me, pieces, cot, inner, vectors, outer):
    features = cot.shape[1]
    units = inner.shape[1]
    count = 2 * PARTS
    piece = const((TILE, features))
    scratch = lambda n: pltpu.VMEM((count * TILE, n), BF16)
    return kernel_call(
        near_body,
        (me, *pieces, cot, inner, vectors, outer),
        free_in=tuple(range(1, count + 1)),
        free_out=(3, 5),
        grid_spec=pltpu.PrefetchScalarGridSpec(
            num_scalar_prefetch=1,
            grid=(count,),
            in_specs=[piece] * count
            + [pl.BlockSpec((TILE, features), lambda i, m: (4 * (i // 2) + (m[0] ^ (i % 2)), 0)),
               const(inner.shape), const(vectors.shape), const(outer.shape)],
            out_specs=[const((PARTS * TILE, features))] * 2 + [piece] * count
            + [const((8, units)), const((2, units, features))],
            scratch_shapes=[scratch(features), scratch(features), scratch(units), scratch(units)],
        ),
        out_shape=[shape_of(PARTS * TILE, features)] * 2 + [shape_of(TILE, features)] * count
        + [shape_of(8, units, dtype=F32), shape_of(2, units, features)],
        cost_estimate=cost(15e9, 12e6, 2e6),
        name="feed_near",
    )


def far_body(me_ref, x0_ref, x1_ref, g_ref, inner_ref, vec_ref, outer_ref, *rest):
    left_ref, right_ref, out0_ref, out1_ref, back0_ref, back1_ref, sum_ref = rest[-7:]
    i = pl.program_id(0)
    for n, x_ref in enumerate((x0_ref, x1_ref)):
        @pl.when(i == n)
        def _(x_ref=x_ref):
            left_ref[1] = x_ref[...]

    right_ref[0] = g_ref[...]
    act, dh, out, back = feed_piece(left_ref[1], g_ref[...], inner_ref, vec_ref, outer_ref)
    left_ref[0] = act
    right_ref[1] = dh
    sums = fold(dh.astype(F32))
    for n, (out_ref, back_ref) in enumerate(((out0_ref, back0_ref), (out1_ref, back1_ref))):
        @pl.when(i == n)
        def _(n=n, out_ref=out_ref, back_ref=back_ref):
            sum_ref[...] = sum_ref[...] + sums if n else sums
            out_ref[...] = out
            back_ref[...] = back


def feed_far(part, me, first, second, cot, inner, vectors, outer, kept):
    features = cot.shape[1]
    units = inner.shape[1]
    rows = pl.BlockSpec((2, TILE, features), lambda i, m: (0, 2 * part + i, 0))
    piece = const((TILE, features))
    half = pl.BlockSpec((TILE, features), lambda i, m: (part, 0))
    return kernel_call(
        far_body,
        (me, first, second, cot, inner, vectors, outer, *kept),
        free_in=(1, 2),
        free_out=(5,),
        grid_spec=pltpu.PrefetchScalarGridSpec(
            num_scalar_prefetch=1,
            grid=(2,),
            in_specs=[
                piece, piece,
                pl.BlockSpec((TILE, features), lambda i, m: (4 * part + (m[0] ^ (2 + i)), 0)),
                const(inner.shape), const(vectors.shape), const(outer.shape),
            ] + [pl.BlockSpec(memory_space=pl.ANY)] * len(kept),
            out_specs=[rows, rows, half, half, piece, piece, const((8, units))],
        ),
        out_shape=[shape_of(2, 2 * PARTS * TILE, features)] * 2 + [shape_of(PARTS * TILE, features)] * 2
        + [shape_of(TILE, features)] * 2 + [shape_of(8, units, dtype=F32)],
        input_output_aliases={7 + n: n for n in range(len(kept))},
        cost_estimate=cost(5e9, 8e6, 1e6),
        name="feed_far",
    )


def feed_grad_body(xz_ref, left_ref, right_ref, before_ref, keep_ref, send_ref):
    value = (tn(left_ref[0], right_ref[0]) + before_ref[0].astype(F32)).astype(BF16)
    mine = pl.program_id(0) == xz_ref[0]

    @pl.when(mine)
    def _():
        keep_ref[...] = value

    @pl.when(jnp.logical_not(mine))
    def _():
        send_ref[...] = value


def feed_grad(xz, left, right, before):
    _, rows, features = left.shape
    both = pl.BlockSpec((1, rows, features), lambda i, m: (i, 0, 0))
    return kernel_call(
        feed_grad_body,
        (xz, left, right, before),
        grid_spec=pltpu.PrefetchScalarGridSpec(
            num_scalar_prefetch=1,
            grid=(2,),
            in_specs=[both, both, pl.BlockSpec((1, features, features), lambda i, m: (i, 0, 0))],
            out_specs=[const(before.shape[1:])] * 2,
        ),
        out_shape=[shape_of(*before.shape[1:])] * 2,
        cost_estimate=cost(5e9, 10e6),
        name="feed_grad",
    )


def feed_ready_body(xz_ref, mine_ref, other_ref, outer_ref, inner_ref):
    for from_ref, here in ((mine_ref, xz_ref[0]), (other_ref, 1 - xz_ref[0])):
        for n, to_ref in enumerate((outer_ref, inner_ref)):
            @pl.when(here == n)
            def _(from_ref=from_ref, to_ref=to_ref):
                to_ref[...] = from_ref[...].astype(F32)


def feed_ready(xz, mine, other):
    rows, features = mine.shape
    block = pl.BlockSpec((TILE, features), lambda i, m: (i, 0))
    return kernel_call(
        feed_ready_body,
        (xz, mine, other),
        free_in=(1, 2),
        grid_spec=pltpu.PrefetchScalarGridSpec(
            num_scalar_prefetch=1,
            grid=(rows // TILE,),
            in_specs=[block, block],
            out_specs=[block, block],
        ),
        out_shape=[shape_of(rows, features, dtype=F32)] * 2,
        cost_estimate=cost(1e6, 7e6),
        name="feed_ready",
    )


def back_body(me_ref, b0_ref, b1_ref, b2_ref, residual_ref, g_ref, vec_ref, w0_ref, w1_ref, w2_ref, w3_ref,
              *rest):
    grad_ref, low_ref, a0_ref, a1_ref, a2_ref, a3_ref, sum_ref = rest[-7:]
    grad_mid = b0_ref[...].astype(F32) + b1_ref[...].astype(F32) + b2_ref[...].astype(F32)
    normed, scale, _ = stats(residual_ref[...])
    upstream = g_ref[...].astype(F32)
    grad = upstream + norm_back(grad_mid, normed, scale, vec_ref[3:4, :])
    grad_ref[...] = grad
    low = grad.astype(BF16)
    low_ref[...] = low
    for w_ref, a_ref in ((w0_ref, a0_ref), (w1_ref, a1_ref), (w2_ref, a2_ref), (w3_ref, a3_ref)):
        a_ref[...] = nt(w_ref[...], low).astype(BF16)
    for n, value in enumerate((grad_mid * normed, grad_mid, grad, upstream)):
        sum_ref[8 * n:8 * n + 8] = fold(value)


def middle_back(part, me, sums, residual, cot, vectors, weights, after):
    features = cot.shape[1]
    piece = const((TILE, features))
    width = weights[0].shape[0]
    return kernel_call(
        back_body,
        (me, *sums, residual, cot, vectors, *weights, *after),
        free_in=(2, 3) + tuple(range(11, 11 + len(after))),
        free_out=(3, 4, 5),
        grid_spec=pltpu.PrefetchScalarGridSpec(
            num_scalar_prefetch=1,
            grid=(1,),
            in_specs=[piece] * 4
            + [pl.BlockSpec((TILE, features), lambda i, m: (4 * part + m[0], 0)), const(vectors.shape)]
            + [const(v.shape) for v in weights] + [pl.BlockSpec(memory_space=pl.ANY)] * len(after),
            out_specs=[piece, piece] + [const((width, TILE))] * 4 + [const((32, features))],
        ),
        out_shape=[shape_of(TILE, features, dtype=F32), shape_of(TILE, features)]
        + [shape_of(width, TILE)] * 4 + [shape_of(32, features, dtype=F32)],
        cost_estimate=cost(2e9, 4e6),
        name="middle_back",
    )


def output_body(*refs):
    mixed, lows, outs = refs[:PARTS], refs[PARTS:2 * PARTS], refs[2 * PARTS:]
    for n in range(4):
        total = nn(mixed[0][n], lows[0][...])
        for p in range(1, PARTS):
            total = total + nn(mixed[p][n], lows[p][...])
        outs[n][...] = total.astype(BF16)


def output_grad(mixed, lows):
    width, features = mixed[0].shape[1], lows[0].shape[1]
    return kernel_call(
        output_body,
        (*mixed, *lows),
        free_out=(1, 3),
        out_shape=[shape_of(width, features)] * 4,
        cost_estimate=cost(2e9, 4e6),
        name="output_grad",
    )


def tail_body(me_ref, g_ref, wq_ref, wk_ref, wv_ref, x_ref, stat_ref, *rest):
    early, units = rest[:PARTS], rest[PARTS:2 * PARTS + 1]
    o0_ref, o1_ref, o2_ref, o3_ref, apart_ref, vec_ref, sum_ref, row_ref = rest[-8:]
    i, p = pl.program_id(0), pl.program_id(1)
    grads = g_ref[...]
    width = wq_ref.shape[0]
    value = tn(grads[:width], wq_ref[...]) + tn(grads[width:2 * width], wk_ref[...])
    value = value + tn(grads[2 * width:], wv_ref[...])

    @pl.when((i == 0) & (p == 0))
    def _():
        row_ref[...] = jnp.zeros_like(row_ref)
        sum_ref[...] = jnp.zeros_like(sum_ref)

    row_ref[...] += nt(jnp.ones((8, grads.shape[1]), BF16), grads)
    normed = (x_ref[...].astype(F32) - stat_ref[:, 0:1]) * stat_ref[:, 1:2]
    sum_ref[:8] += fold(value * normed)
    sum_ref[8:] += fold(value)
    value = value.astype(BF16)
    for step, o_ref in enumerate((o3_ref, o2_ref, o1_ref, o0_ref)):
        @pl.when(i == step)
        def _(o_ref=o_ref):
            o_ref[pl.ds(pl.multiple_of(p * TILE, TILE), TILE), :] = value

    @pl.when((i == 3) & (p == PARTS - 1))
    def _():
        row = lax.broadcasted_iota(jnp.int32, vec_ref.shape, 0)
        vectors = jnp.zeros(vec_ref.shape, F32)
        before = early[0][...]
        for ref in early[1:]:
            before = before + ref[...]
        parts = [before[8 * n:8 * n + 8] for n in range(4)] + [sum_ref[:8], sum_ref[8:]]
        for n, part in enumerate(parts):
            vectors = jnp.where(row == n, jnp.sum(part, axis=0, keepdims=True), vectors)
        vec_ref[...] = vectors
        inside = units[0][...]
        for ref in units[1:]:
            inside = inside + ref[...]
        apart_ref[...] = jnp.where(row == 6, jnp.sum(inside, axis=0, keepdims=True), 0.0)
        apart_ref[7:8, :row_ref.shape[1]] = row_ref[0:1]
        o3_ref[PARTS * TILE:] = paired(vectors)


def tail(me, grads, wq, wk, wv, tokens, stat, early, units, after):
    deep = grads.shape[0]
    features = wq.shape[1]
    share = const((PARTS * TILE, features))
    more = const((PARTS * TILE + 16, features))
    at = lambda i, p, m: 4 * p + (m[0] ^ (3 - i))
    return kernel_call(
        tail_body,
        (me, grads, wq, wk, wv, tokens, stat, *early, *units, *after),
        free_out=(1, 3),
        grid_spec=pltpu.PrefetchScalarGridSpec(
            num_scalar_prefetch=1,
            grid=(4, PARTS),
            in_specs=[pl.BlockSpec((deep, TILE), lambda i, p, m: (0, at(i, p, m))),
                      const(wq.shape), const(wk.shape), const(wv.shape),
                      pl.BlockSpec((TILE, features), lambda i, p, m: (at(i, p, m), 0)),
                      pl.BlockSpec((TILE, WIDE), lambda i, p, m: (at(i, p, m), 0))]
            + [const(v.shape) for v in (*early, *units)] + [pl.BlockSpec(memory_space=pl.ANY)] * len(after),
            out_specs=[share, share, share, more, const((8, features)), const((8, features))],
            scratch_shapes=[pltpu.VMEM((16, features), F32), pltpu.VMEM((8, deep), F32)],
        ),
        out_shape=[shape_of(PARTS * TILE, features)] * 3 + [shape_of(PARTS * TILE + 16, features)]
        + [shape_of(8, features, dtype=F32)] * 2,
        cost_estimate=cost(4e9, 10e6),
        name="tail",
    )


def chip_body(one_ref, two_ref, vec_ref, *rest):
    out_ref = rest[-1]
    rows = one_ref.shape[0]
    out_ref[:rows] = (one_ref[...].astype(F32) + two_ref[:rows].astype(F32)).astype(BF16)
    out_ref[rows:] = paired(vec_ref[...] + joined(two_ref[rows:]))


def chip_sum(one, two, vectors, after):
    return kernel_call(
        chip_body,
        (one, two, vectors, *after),
        free_in=(1,) + tuple(range(3, 3 + len(after))),
        free_out=(0,),
        grid=(1,),
        in_specs=[const(one.shape), const(two.shape), const(vectors.shape)]
        + [pl.BlockSpec(memory_space=pl.ANY)] * len(after),
        out_specs=[const(two.shape)],
        out_shape=[shape_of(*two.shape)],
        name="chip_sum",
    )[0]


def halves_body(xz_ref, g_ref, go_ref, *rest):
    keep_ref, send_ref = rest[-2:]
    width = go_ref.shape[0]
    for to_ref, half in ((keep_ref, xz_ref[0]), (send_ref, 1 - xz_ref[0])):
        @pl.when(half == 0)
        def _(to_ref=to_ref):
            to_ref[...] = g_ref[:2 * width]

        @pl.when(half == 1)
        def _(to_ref=to_ref):
            to_ref[:width] = g_ref[2 * width:]
            to_ref[width:] = go_ref[...]


def halves(xz, grad_weights, grad_output, after):
    width, features = grad_output.shape
    half = const((2 * width, features))
    return kernel_call(
        halves_body,
        (xz, grad_weights, grad_output, *after),
        free_in=(1, 2, 3),
        grid_spec=pltpu.PrefetchScalarGridSpec(
            num_scalar_prefetch=1,
            grid=(1,),
            in_specs=[const(grad_weights.shape), const(grad_output.shape)]
            + [pl.BlockSpec(memory_space=pl.ANY)] * len(after),
            out_specs=[half, half],
        ),
        out_shape=[shape_of(2 * width, features)] * 2,
        cost_estimate=cost(1e6, 4e6),
        name="halves",
    )


def quarter_body(count, xz_ref, one_ref, two_ref, *rest):
    rows = one_ref.shape[0] // count
    for n, out_ref in enumerate(rest[-count:]):
        at = pl.ds(pl.multiple_of(lax.rem(xz_ref[1] + n, count) * rows, rows), rows)
        out_ref[...] = (one_ref[at, :].astype(F32) + two_ref[at, :].astype(F32)).astype(BF16)


def quarters(xz, one, two, count, after):
    rows, features = one.shape

    def body(*refs):
        quarter_body(count, *refs)

    return kernel_call(
        body,
        (xz, one, two, *after),
        free_in=(2, 3, 4),
        grid_spec=pltpu.PrefetchScalarGridSpec(
            num_scalar_prefetch=1,
            grid=(1,),
            in_specs=[const(one.shape), const(two.shape)] + [pl.BlockSpec(memory_space=pl.ANY)] * len(after),
            out_specs=[const((rows // count, features))] * count,
        ),
        out_shape=[shape_of(rows // count, features)] * count,
        cost_estimate=cost(1e6, 2e6),
        name="quarters",
    )


def paired(value):
    return jnp.concatenate(split(value, 2), axis=0).astype(BF16)


def joined(both):
    both = both.astype(F32)
    half = both.shape[0] // 2
    return both[:half] + both[half:]


def second_body(count, *refs):
    one_ref, two_ref, apart_ref, out_ref = refs[count], refs[count + 1], refs[count + 2], refs[-1]
    rows = refs[0].shape[0]
    total = refs[0][...].astype(F32)
    for ref in refs[1:count]:
        total = total + ref[...].astype(F32)
    out_ref[:rows] = total.astype(BF16)
    out_ref[rows:] = paired(joined(one_ref[...]) + joined(two_ref[...]) + apart_ref[...])


def second(parts, one, two, apart, after):
    count = len(parts)
    rows, features = parts[0].shape
    last = pl.BlockSpec((16, features), lambda i: (one.shape[0] // 16 - 1, 0))

    def body(*refs):
        second_body(count, *refs)

    return kernel_call(
        body,
        (*parts, one, two, apart, *after),
        free_in=tuple(range(1, count + 2)) + tuple(range(count + 3, count + 3 + len(after))),
        grid=(1,),
        in_specs=[const((rows, features))] * count + [last, last, const(apart.shape)]
        + [pl.BlockSpec(memory_space=pl.ANY)] * len(after),
        out_specs=[const((rows + 16, features))],
        out_shape=[shape_of(rows + 16, features)],
        name="second",
    )[0]


def third_body(count, xz_ref, *refs):
    out_ref = refs[-1]
    step = out_ref.shape[0] - (refs[0].shape[0] * count - out_ref.shape[0]) // (count - 1)
    rows = step // count
    sums = None
    for n, ref in enumerate(refs[:count]):
        place_at = lax.rem(xz_ref[1] + count - n, count)
        out_ref[pl.ds(pl.multiple_of(place_at * rows, rows), rows), :] = ref[:rows]
        value = joined(ref[rows:])
        sums = value if sums is None else sums + value
    out_ref[step:] = paired(sums)


def third(xz, pieces, extra, after):
    count = len(pieces)
    rows, features = pieces[0].shape
    total = (rows - extra) * count + extra

    def body(*refs):
        third_body(count, *refs)

    return kernel_call(
        body,
        (xz, *pieces, *after),
        free_in=tuple(range(1, count + 1)),
        grid_spec=pltpu.PrefetchScalarGridSpec(
            num_scalar_prefetch=1,
            grid=(1,),
            in_specs=[const((rows, features))] * count + [pl.BlockSpec(memory_space=pl.ANY)] * len(after),
            out_specs=[const((total, features))],
        ),
        out_shape=[shape_of(total, features)],
        name="third",
    )[0]


def ready_body(xz_ref, mine_ref, other_ref, *rest):
    outs = rest[-14:]
    width = outs[0].shape[0]
    for n, out_ref in enumerate(outs[:4]):
        rows = slice(n % 2 * width, (n % 2 + 1) * width)
        for to_ref, chosen in ((mine_ref, xz_ref[0] == n // 2), (other_ref, xz_ref[0] != n // 2)):
            @pl.when(chosen)
            def _(to_ref=to_ref, out_ref=out_ref, rows=rows):
                out_ref[...] = to_ref[rows].astype(F32)

    small = joined(mine_ref[2 * width:]) + joined(other_ref[2 * width:])
    for n, out_ref in enumerate(outs[4:11]):
        out_ref[...] = small[n]
    for n, out_ref in enumerate(outs[11:]):
        out_ref[...] = small[7, n * width:(n + 1) * width]


def ready(xz, mine, other, width, after):
    rows, features = mine.shape
    sizes = [(features,)] * 7 + [(width,)] * 3
    return kernel_call(
        ready_body,
        (xz, mine, other, *after),
        free_in=(2,),
        grid_spec=pltpu.PrefetchScalarGridSpec(
            num_scalar_prefetch=1,
            grid=(1,),
            in_specs=[const(mine.shape), const(other.shape)] + [pl.BlockSpec(memory_space=pl.ANY)] * len(after),
            out_specs=[const((width, features))] * 4 + [const(size) for size in sizes],
        ),
        out_shape=[shape_of(width, features, dtype=F32)] * 4 + [shape_of(*size, dtype=F32) for size in sizes],
        cost_estimate=cost(1e6, 4e6),
        name="ready",
    )


def final_body(me_ref, b0_ref, b1_ref, b2_ref, x_ref, *rest):
    grad_refs, vec_ref, out_ref = rest[:PARTS], rest[PARTS], rest[-1]
    p = pl.program_id(0)
    grad_attend = b0_ref[...].astype(F32) + b1_ref[...].astype(F32) + b2_ref[...].astype(F32)
    normed, scale, _ = stats(x_ref[...].astype(F32))
    back = norm_back(grad_attend, normed, scale, vec_ref[0:1, :])
    for n, grad_ref in enumerate(grad_refs):
        @pl.when(p == n)
        def _(grad_ref=grad_ref):
            out_ref[...] = (grad_ref[...] + back).astype(BF16)


def final(me, sums, tokens, grads, vectors, after):
    features = tokens.shape[1]
    rows = pl.BlockSpec((TILE, features), lambda p, m: (p, 0))
    return kernel_call(
        final_body,
        (me, *sums, tokens, *grads, vectors, *after),
        free_in=(2, 3) + tuple(range(6 + PARTS, 6 + PARTS + len(after))),
        free_out=(0,),
        grid_spec=pltpu.PrefetchScalarGridSpec(
            num_scalar_prefetch=1,
            grid=(PARTS,),
            in_specs=[rows] * 3 + [pl.BlockSpec((TILE, features), lambda p, m: (4 * p + m[0], 0))]
            + [const((TILE, features))] * PARTS + [const(vectors.shape)]
            + [pl.BlockSpec(memory_space=pl.ANY)] * len(after),
            out_specs=[rows],
        ),
        out_shape=[shape_of(PARTS * TILE, features)],
        cost_estimate=cost(1e8, 5e6),
        name="final",
    )[0]


def place_body(me_ref, p0_ref, p1_ref, p2_ref, p3_ref, *rest):
    out_ref = rest[-1]
    for step, p_ref in enumerate((p0_ref, p1_ref, p2_ref, p3_ref)):
        @pl.when(pl.program_id(0) == step)
        def _(p_ref=p_ref):
            at = pl.ds(pl.multiple_of(pl.program_id(1) * TILE, TILE), TILE)
            out_ref[...] = p_ref[at, :].astype(out_ref.dtype)


def place(me, shares, dtype, after):
    rows, features = shares[0].shape
    return kernel_call(
        place_body,
        (me, *shares, *after),
        free_in=(1, 2, 3, 4),
        grid_spec=pltpu.PrefetchScalarGridSpec(
            num_scalar_prefetch=1,
            grid=(4, PARTS),
            in_specs=[const((rows, features))] * 4 + [pl.BlockSpec(memory_space=pl.ANY)] * len(after),
            out_specs=pl.BlockSpec((TILE, features), lambda i, p, m: (4 * p + (m[0] ^ i), 0)),
        ),
        out_shape=shape_of(4 * rows, features, dtype=dtype),
        cost_estimate=cost(1e6, 9e6),
        name="place",
    )


def fence_body(*refs):
    pass


def fence(value, *after, space=pltpu.HBM):
    anywhere = pl.BlockSpec(memory_space=pl.ANY)
    return pl.pallas_call(
        fence_body,
        in_specs=[anywhere] * (1 + len(after)),
        out_specs=anywhere,
        out_shape=space(value.shape, value.dtype),
        input_output_aliases={0: 0},
        name="fence",
    )(pltpu.with_memory_space_constraint(value, space), *after)


def other_core(value):
    return lax.ppermute(value, "core", SWAP)


def other_chip(value):
    return lax.ppermute(value, "y", SWAP)


def crosswise(value):
    return lax.ppermute(value, MP, [(n, n ^ 3) for n in range(4)])


def exchange(pieces):
    return [pieces[0], other_core(pieces[1]), other_chip(pieces[2]), crosswise(pieces[3])]


def gather_sum(pieces):
    near = other_core(pieces[1])
    far = (pieces[2].astype(F32) + other_core(pieces[3]).astype(F32)).astype(BF16)
    return [pieces[0], near, other_chip(far)], far


def spread(value):
    far = other_chip(value)
    return [value, other_core(value), far, other_core(far)]


def pick(values, at):
    return lax.dynamic_index_in_dim(values, at, 0, keepdims=False)


def turned(values, way):
    size = lax.axis_size("z")
    return lax.ppermute(values, "z", [(n, (n + way) % size) for n in range(size)])


def sum_first(xz, keep, got, after):
    size = lax.axis_size("z")
    if size > 4:
        return [lax.psum(keep + got, "z")]
    return quarters(xz, keep, got, size, after)


def gather_z(value):
    size = lax.axis_size("z")
    if size > 4:
        return [lax.all_gather(value, "z", axis=0, tiled=True)]
    return [turned(value, way) if way else value for way in range(size)]


def local(
    tokens,
    segment_ids,
    gain_one,
    bias_one,
    query_weight,
    query_bias,
    key_weight,
    value_weight,
    value_bias,
    output_weight,
    output_bias,
    gain_two,
    bias_two,
    inner_weight,
    inner_bias,
    outer_weight,
    outer_bias,
    cotangent,
):
    _, length, features = tokens.shape
    width = query_weight.shape[1]
    heads = width // HEAD
    tokens = tokens.reshape(length, features)
    cot = cotangent.reshape(length, features)
    at = lax.axis_index(MP).astype(jnp.int32)
    me = at[None]
    xz = jnp.stack([lax.axis_index("x"), lax.axis_index("z")]).astype(jnp.int32)
    apart = jnp.concatenate([query_bias, value_bias, jnp.zeros((features - 2 * width,), F32)])
    vectors = jnp.concatenate([gain_one, bias_one, output_bias, gain_two, bias_two, outer_bias, apart, inner_bias])
    vectors = vectors.reshape(8, features)
    wq, wk, wv = query_weight.T, key_weight.T, value_weight.T

    output_weights = spread(output_weight)
    attend_in, qt, kt, vt, kn, vn, stat = project(tokens, segment_ids, vectors, wq, wk, wv, heads)

    parts = range(PARTS)
    attended, extras, fours = [], [], []
    for p in parts:
        out, extra, *four = attend_forward(p, me, segment_ids, qt, kn, vt, output_weights[1:3] if p == 0 else ())
        attended.append(out)
        extras.append(extra)
        fours.append(exchange(four))
    mixed, residuals, pieces = [], [], []
    for p in parts:
        residual, own, together = middle(p, me, tokens, fours[p], output_weights, vectors, extras[p + 1:])
        mixed.append(together)
        residuals.append(residual)
        pieces.append([own, other_core(own), other_chip(own)])

    backs = {}
    *outs, b00, b01, b10, b11, near_sum, near_grad = feed_near(
        me, [pieces[p][n] for p in parts for n in (0, 1)], cot, inner_weight, vectors, outer_weight
    )
    backs[0, 0], backs[0, 1], backs[1, 0], backs[1, 1] = b00, b01, b10, b11
    sums, kept, gathered, far_sums, behind = [near_sum], (), [], [], b00
    for p in parts:
        far = fence(pieces[p][2], behind, space=pltpu.VMEM)
        *kept, backs[p, 2], backs[p, 3], far_sum = feed_far(
            p, me, far, other_core(far), cot, inner_weight, vectors, outer_weight, kept
        )
        behind = backs[p, 2]
        sums.append(far_sum)
        if p:
            backs[p, 3] = fence(backs[p, 3], gathered[-1][2], space=pltpu.VMEM)
            feed_keep, feed_send = feed_grad(xz, kept[0], kept[1], near_grad)
            backs[p, 2] = fence(backs[p, 2], feed_send)
        summed, far_sum = gather_sum([backs[p, n] for n in range(4)])
        gathered.append(summed)
        far_sums.append(far_sum)
    left, right, *far_outs = kept
    outs += far_outs
    feed_sum = (feed_keep.astype(F32) + lax.ppermute(feed_send, "x", SWAP).astype(F32)).astype(BF16)
    feed_sum = lax.psum_scatter(feed_sum, "z", scatter_dimension=0, tiled=True)
    grad_residuals, lows, grads_attended, inner_sums = [], [], [], []
    for p in parts:
        grad, low, a0, a1, a2, a3, vector = middle_back(
            p, me, gathered[p], residuals[p], cot, vectors, output_weights, far_sums[p + 1:]
        )
        grad_residuals.append(grad)
        lows.append(low)
        inner_sums.append(vector)
        grads_attended.append(exchange([a0, a1, a2, a3]))

    near = other_core(fence(outs[1], *far_sums))
    far = (outs[2].astype(F32) + other_core(fence(outs[3], *far_sums)).astype(F32)).astype(BF16)
    far = fence(far, lows[-1], space=pltpu.VMEM)
    part = output_grad(mixed, lows)
    earlier = attend_backward(0, me, segment_ids, qt, extras[0], kn, kt, vn, attended[0], grads_attended[0], (),
                              (far, near, part[0]))
    there = other_chip(far)
    part_far = fence(part[2], earlier[0])
    part_far = (part_far.astype(F32) + other_core(part[3]).astype(F32)).astype(BF16)
    part_near = other_core(part[1])
    grads = attend_backward(1, me, segment_ids, qt, extras[1], kn, kt, vn, attended[1], grads_attended[1], earlier,
                            (part_near, part_far, there))

    part_across = other_chip(part_far)
    grad_output = fence(part[0], grads).astype(F32) + part_near.astype(F32) + part_across.astype(F32)
    keep, send = halves(xz, nn(grads, attend_in).astype(BF16), grad_output.astype(BF16), ())
    result = jnp.concatenate(residuals) + fence(outs[0], send).astype(F32) + near.astype(F32)
    result = (result + there.astype(F32) + outer_bias).astype(BF16)
    near, far = other_core(result), other_chip(result)
    got = lax.ppermute(send, "x", SWAP)
    back_own, back_near, back_far, back_across, apart, summed = tail(
        me, grads, wq, wk, wv, tokens, stat, inner_sums, sums, (send,)
    )
    feed_sum = lax.all_gather(fence(feed_sum, send), "z", axis=0, tiled=True)
    feed_other = lax.ppermute(feed_sum, "x", SWAP)
    quarter = sum_first(xz, keep, got, (near, far, apart))
    back_across = other_core(fence(back_across, quarter[-1], space=pltpu.VMEM))
    back_far = chip_sum(back_far, back_across, summed, ())
    back_there = other_chip(back_far)
    share = final(me, [back_own, other_core(back_near), back_there], tokens, grad_residuals, vectors, (feed_other,))
    if len(quarter) > 1:
        turns = [quarter[0]] + [turned(part, n + 1) for n, part in enumerate(quarter[1:])]
        held = second(turns, back_far, back_there, apart, (share,))
        layer_out = place(me, [result, near, far, other_core(far)], BF16, (held,))
        mine = third(xz, gather_z(held), 16, (layer_out,))
    else:
        small = joined(back_far[-16:]) + joined(back_there[-16:]) + apart
        layer_out = place(me, [result, near, far, other_core(far)], BF16, ())
        mine = jnp.concatenate([quarter[0], paired(lax.psum(small, "z"))])
    share = fence(share, held if len(quarter) > 1 else mine, space=pltpu.VMEM)
    near, far = other_core(share), fence(other_chip(share), mine, space=pltpu.VMEM)
    input_grad = place(me, [share, near, far, other_core(far)], F32, (mine,))
    feed_sum = feed_ready(xz, feed_sum, feed_other)
    *wide, two_gain, two_bias, output_sum, outer_bias, one_gain, one_bias, inner_bias, query, _, value = ready(
        xz, mine, lax.ppermute(mine, "x", SWAP), width, (*feed_sum, input_grad)
    )
    return (
        layer_out.reshape(1, length, features),
        input_grad.reshape(1, length, features),
        one_gain,
        one_bias,
        wide[0].T,
        query,
        wide[1].T,
        wide[2].T,
        value,
        wide[3],
        output_sum,
        two_gain,
        two_bias,
        feed_sum[1],
        inner_bias,
        feed_sum[0],
        outer_bias,
    )


def solution(mesh):
    rows = mesh.shape["dp"]
    inner = Mesh(mesh.devices.reshape(rows // 2, 2, 2, 2), DP + MP)
    placed = (
        P(DP, None, None),
        P(DP, None),
        P(),
        P(),
        P(None, MP),
        P(MP),
        P(None, MP),
        P(None, MP),
        P(MP),
        P(MP, None),
        P(),
        P(),
        P(),
        P(None, MP),
        P(MP),
        P(MP, None),
        P(),
        P(DP, None, None),
    )
    return jax.shard_map(
        local,
        mesh=inner,
        in_specs=placed,
        out_specs=(
            P(DP, None, None),
            P(DP, None, None),
            P(),
            P(),
            P(None, MP),
            P(MP),
            P(None, MP),
            P(None, MP),
            P(MP),
            P(MP, None),
            P(),
            P(),
            P(),
            P(None, MP),
            P(MP),
            P(MP, None),
            P(),
        ),
        check_vma=False,
    )
```

```python
import jax
import jax.numpy as jnp
from jax import lax
from jax.experimental import pallas as pl
from jax.experimental.pallas import tpu as pltpu
from jax.sharding import Mesh
from jax.sharding import PartitionSpec as P

HEAD = 64
WIDE = 128
TILE = 256
LONG = 512
PARTS = 2
MASKED = 1e30
SCALE = 1
F32 = jnp.float32
BF16 = jnp.bfloat16
DP = ("z", "x")
MP = ("y", "core")
SWAP = [(0, 1), (1, 0)]


def nn(left, right):
    return lax.dot_general(left, right, (((1,), (0,)), ((), ())), preferred_element_type=F32)


def nt(left, right):
    return lax.dot_general(left, right, (((1,), (1,)), ((), ())), preferred_element_type=F32)


def tn(left, right):
    return lax.dot_general(left, right, (((0,), (0,)), ((), ())), preferred_element_type=F32)


def stats(values):
    mean = jnp.mean(values, axis=-1, keepdims=True)
    center = values - mean
    scale = lax.rsqrt(jnp.mean(center * center, axis=-1, keepdims=True) + 1e-05)
    return center * scale, scale, mean


def norm_back(grad_out, normed, scale, gain):
    upstream = grad_out * gain
    return scale * (
        upstream
        - jnp.mean(upstream, axis=-1, keepdims=True)
        - normed * jnp.mean(upstream * normed, axis=-1, keepdims=True)
    )


def fold(values):
    return jnp.sum(values.reshape(-1, 8, values.shape[-1]), axis=0)


def split(value, parts):
    out = []
    for _ in range(parts):
        piece = value.astype(BF16).astype(F32)
        out.append(piece)
        value = value - piece
    return out


def const(shape):
    return pl.BlockSpec(shape, lambda *_: (0,) * len(shape))


def shape_of(*dims, dtype=BF16):
    return jax.ShapeDtypeStruct(dims, dtype)


def params(mib=40):
    return pltpu.CompilerParams(vmem_limit_bytes=mib << 20)


def kernel_call(body, values, free_in=(), free_out=(), **options):
    shapes = options.pop("out_shape")
    many = isinstance(shapes, (list, tuple))
    shapes = [s if n in free_out else pltpu.HBM(s.shape, s.dtype) for n, s in enumerate(shapes if many else [shapes])]
    values = [
        v if n in free_in or v.dtype == jnp.int32 else pltpu.with_memory_space_constraint(v, pltpu.HBM)
        for n, v in enumerate(values)
    ]
    return pl.pallas_call(
        body, out_shape=shapes if many else shapes[0], compiler_params=params(), **options
    )(*values)


def cost(flops, moved, special=0):
    return pl.CostEstimate(flops=int(flops * SCALE), bytes_accessed=int(moved * SCALE), transcendentals=0)


def project_body(x_ref, seg_ref, vec_ref, wq_ref, wk_ref, wv_ref,
                 ai_ref, qt_ref, kt_ref, vt_ref, kn_ref, vn_ref, stat_ref):
    heads = kn_ref.shape[0]
    width = heads * HEAD
    tile = x_ref.shape[0]
    normed, scale, mean = stats(x_ref[...].astype(F32))
    lane = lax.broadcasted_iota(jnp.int32, stat_ref.shape, 1)
    stat_ref[...] = jnp.where(lane == 0, mean, scale)
    ai = (normed * vec_ref[0:1, :] + vec_ref[1:2, :]).astype(BF16)
    ai_ref[...] = ai
    column = vec_ref[...].T[:2 * width, 6:7]
    queries = ((nt(wq_ref[...], ai) + column[:width]).astype(BF16)).astype(F32) * HEAD ** -0.5
    keys = nt(wk_ref[...], ai)
    kt_ref[...] = keys.astype(BF16)
    values = nt(wv_ref[...], ai) + column[width:]
    row = lax.broadcasted_iota(jnp.int32, (HEAD, tile), 0)
    same = jnp.where(row == seg_ref[...], 1.0, 0.0)
    mask = jnp.where(row < 8, (same - 1.0) * MASKED, jnp.where(row < 11, 1.0, 0.0))
    ones = jnp.where(row < 2, 1.0, 0.0)
    first = jnp.where(row[:16] == 0, 1.0, 0.0).astype(BF16)
    for h in range(heads):
        rows = slice(h * HEAD, (h + 1) * HEAD)
        qt_ref[h, :HEAD, :] = queries[rows].astype(BF16)
        qt_ref[h, HEAD:, :] = same.astype(BF16)
        vt_ref[h, :HEAD, :] = values[rows].astype(BF16)
        vt_ref[h, HEAD:, :] = first
        kn_ref[h] = jnp.concatenate([keys[rows], mask], axis=0).T.astype(BF16)
        vn_ref[h] = jnp.concatenate([values[rows], ones], axis=0).T.astype(BF16)


def project(tokens, seg_row, vectors, wq, wk, wv, heads):
    length, features = tokens.shape
    width = heads * HEAD
    return kernel_call(
        project_body,
        (tokens, seg_row, vectors, wq, wk, wv),
        grid=(length // LONG,),
        in_specs=[
            pl.BlockSpec((LONG, features), lambda i: (i, 0)),
            pl.BlockSpec((1, LONG), lambda i: (0, i)),
            const(vectors.shape), const(wq.shape), const(wk.shape), const(wv.shape),
        ],
        out_specs=[
            pl.BlockSpec((LONG, features), lambda i: (i, 0)),
            pl.BlockSpec((heads, WIDE, LONG), lambda i: (0, 0, i)),
            pl.BlockSpec((width, LONG), lambda i: (0, i)),
            pl.BlockSpec((heads, HEAD + 16, LONG), lambda i: (0, 0, i)),
            pl.BlockSpec((heads, LONG, WIDE), lambda i: (0, i, 0)),
            pl.BlockSpec((heads, LONG, WIDE), lambda i: (0, i, 0)),
            pl.BlockSpec((LONG, WIDE), lambda i: (i, 0)),
        ],
        out_shape=[
            shape_of(length, features),
            shape_of(heads, WIDE, length),
            shape_of(width, length),
            shape_of(heads, HEAD + 16, length),
            shape_of(heads, length, WIDE),
            shape_of(heads, length, WIDE),
            shape_of(length, WIDE, dtype=F32),
        ],
        cost_estimate=cost(6e9, 14e6),
        name="project",
    )


def key_range(seg_ref, seg_all, i):
    first = seg_ref[0, i * TILE]
    last = seg_ref[0, i * TILE + TILE - 1]
    before = jnp.sum(jnp.where(seg_all < first, 1.0, 0.0)).astype(jnp.int32)
    until = jnp.sum(jnp.where(seg_all <= last, 1.0, 0.0)).astype(jnp.int32)
    return before // TILE, (until + TILE - 1) // TILE


def by_blocks(low, high, step, carry):
    keys = lambda kb: pl.ds(pl.multiple_of(kb * TILE, TILE), TILE)
    for many in (3, 2, 1):
        rounds = (high - low) // many
        run = lambda n, c, low=low, many=many: step([keys(low + many * n + k) for k in range(many)], c)
        carry = lax.fori_loop(0, rounds, run, carry)
        low = low + many * rounds
    return carry


def shifted(one_hot, pieces):
    row = lax.broadcasted_iota(jnp.int32, one_hot.shape, 0)
    value = one_hot
    for n, piece in enumerate(pieces):
        value = jnp.where(row == 8 + n, piece, value)
    return value.astype(BF16)


def forward_body(offset, me_ref, segs_ref, seg_ref, qt_ref, kn_ref, vt_ref, *rest):
    out_ref, extra_ref, o0_ref, o1_ref, o2_ref, o3_ref, acc_ref = rest[-7:]
    heads, _, tile = qt_ref.shape
    i = pl.program_id(0)
    low, high = key_range(segs_ref, seg_ref[...], i + offset)
    acc_ref[...] = jnp.zeros_like(acc_ref)

    def step(keys, tops):
        scores = [[nn(kn_ref[h, at, :], qt_ref[h]) for at in keys] for h in range(heads)]
        new_tops = []
        for h in range(heads):
            top = tops[h]
            for score in scores[h]:
                top = jnp.maximum(top, jnp.max(score, axis=0, keepdims=True))
            new_tops.append(top)
        powered = [[jnp.exp(score - new_tops[h]).astype(BF16) for score in scores[h]] for h in range(heads)]
        for h in range(heads):
            total = acc_ref[h] * jnp.exp(tops[h] - new_tops[h])
            for at, power in zip(keys, powered[h]):
                total = total + nn(vt_ref[h, :, at], power)
            acc_ref[h] = total
        return tuple(new_tops)

    tops = by_blocks(low, high, step, (jnp.full((1, tile), -jnp.inf, F32),) * heads)
    for h in range(heads):
        total = acc_ref[h, HEAD:HEAD + 1, :]
        out_ref[0, h * HEAD:(h + 1) * HEAD, :] = (acc_ref[h, :HEAD, :] / total).astype(BF16)
        one_hot = qt_ref[h, HEAD:HEAD + 16, :].astype(F32)
        extra_ref[h] = shifted(one_hot, split(-(tops[h] + jnp.log(total)), 3))
    for n, o_ref in enumerate((o0_ref, o1_ref, o2_ref, o3_ref)):
        @pl.when((i ^ me_ref[0]) == n)
        def _(o_ref=o_ref):
            o_ref[...] = out_ref[0]


def attend_forward(part, me, seg_row, qt, kn, vt, after):
    heads, _, length = qt.shape
    width = heads * HEAD
    count = length // TILE // PARTS
    offset = part * count

    def body(*refs):
        forward_body(offset, *refs)

    return kernel_call(
        body,
        (me, seg_row, seg_row, qt, kn, vt, *after),
        free_in=tuple(range(6, 6 + len(after))),
        free_out=(3, 4, 5),
        grid_spec=pltpu.PrefetchScalarGridSpec(
            num_scalar_prefetch=1,
            grid=(count,),
            in_specs=[
                pl.BlockSpec(memory_space=pltpu.SMEM),
                const((1, length)),
                pl.BlockSpec((heads, WIDE, TILE), lambda i, m: (0, 0, i + offset)),
                const(kn.shape), const(vt.shape),
            ] + [pl.BlockSpec(memory_space=pl.ANY)] * len(after),
            out_specs=[
                pl.BlockSpec((1, width, TILE), lambda i, m: (i, 0, 0)),
                pl.BlockSpec((heads, 16, TILE), lambda i, m: (0, 0, i)),
            ] + [const((width, TILE))] * 4,
            scratch_shapes=[pltpu.VMEM((heads, HEAD + 16, TILE), F32)],
        ),
        out_shape=[shape_of(count, width, TILE), shape_of(heads, 16, count * TILE)] + [shape_of(width, TILE)] * 4,
        cost_estimate=cost(9e9, 5e6, 4e6),
        name="attend_forward",
    )


def backward_body(part, me_ref, segs_ref, seg_ref, qt_ref, extra_ref, kn_ref, kt_ref, vn_ref, out_ref,
                  g0_ref, g1_ref, g2_ref, g3_ref, *rest):
    heads, _, tile = qt_ref.shape
    width = heads * HEAD
    length = kt_ref.shape[1]
    if part == 0:
        dq_out, dk_ref, dv_ref, qa_ref, da_ref, dq_ref = rest[-6:]
    else:
        dq_in, dk_in, dv_in = rest[:3]
        grads_ref, qa_ref, da_ref, dq_ref, dk_ref, dv_ref = rest[-6:]
    i = pl.program_id(0)
    count = length // TILE // PARTS
    at_here = i + part * count
    low, high = key_range(segs_ref, seg_ref[...], at_here)

    @pl.when(i == 0)
    def _():
        if part == 0:
            dk_ref[...] = jnp.zeros_like(dk_ref)
            dv_ref[...] = jnp.zeros_like(dv_ref)
        else:
            dk_ref[...] = dk_in[...]
            dv_ref[...] = dv_in[...]
            grads_ref[:width, :count * TILE] = dq_in[...]
        qa_ref[...] = jnp.zeros_like(qa_ref)
        da_ref[...] = jnp.zeros_like(da_ref)

    source = i ^ me_ref[0]
    for n, g_ref in enumerate((g0_ref, g1_ref, g2_ref, g3_ref)):
        @pl.when(source == n)
        def _(g_ref=g_ref):
            for h in range(heads):
                da_ref[h, :HEAD, :] = g_ref[h * HEAD:(h + 1) * HEAD]

    dq_ref[...] = jnp.zeros_like(dq_ref)
    row = lax.broadcasted_iota(jnp.int32, (16, tile), 0)
    for h in range(heads):
        rows = slice(h * HEAD, (h + 1) * HEAD)
        qa_ref[h, :HEAD, :] = qt_ref[h, :HEAD, :]
        qa_ref[h, HEAD:HEAD + 16, :] = extra_ref[h]
        inner = jnp.sum(da_ref[h, :HEAD, :].astype(F32) * out_ref[0, rows].astype(F32), axis=0, keepdims=True)
        first, second = split(-inner, 2)
        value = jnp.where(row == 0, first, jnp.where(row == 1, second, 0.0))
        da_ref[h, HEAD:HEAD + 16, :] = value.astype(BF16)

    def step(keys, carry):
        every = range(heads)
        rows = [slice(h * HEAD, (h + 1) * HEAD) for h in every]
        scores = [[nn(kn_ref[h, at, :], qa_ref[h]) for at in keys] for h in every]
        slopes = [[nn(vn_ref[h, at, :], da_ref[h]) for at in keys] for h in every]
        probs = [[jnp.exp(score) for score in scores[h]] for h in every]
        ds = [[(p * s).astype(BF16) for p, s in zip(probs[h], slopes[h])] for h in every]
        probs = [[p.astype(BF16) for p in probs[h]] for h in every]
        for h in every:
            total = dq_ref[rows[h]]
            for n, at in enumerate(keys):
                dv_ref[rows[h], at] += nt(da_ref[h, :HEAD, :], probs[h][n])
                dk_ref[rows[h], at] += nt(qa_ref[h, :HEAD, :], ds[h][n])
                total = total + nn(kt_ref[rows[h], at], ds[h][n])
            dq_ref[rows[h]] = total
        return carry

    by_blocks(low, high, step, 0)
    dq = (dq_ref[...] * HEAD ** -0.5).astype(BF16)
    if part == 0:
        dq_out[...] = dq
    else:
        grads_ref[:width, pl.ds(pl.multiple_of(at_here * TILE, TILE), TILE)] = dq

        @pl.when(i == pl.num_programs(0) - 1)
        def _():
            grads_ref[width:2 * width] = dk_ref[...].astype(BF16)
            grads_ref[2 * width:] = dv_ref[...].astype(BF16)


def attend_backward(part, me, seg_row, qt, extra, kn, kt, vn, out, grad, earlier, after):
    heads, _, length = qt.shape
    width = heads * HEAD
    count = length // TILE // PARTS
    offset = part * count

    def body(*refs):
        backward_body(part, *refs)

    in_specs = [
        pl.BlockSpec(memory_space=pltpu.SMEM),
        const((1, length)),
        pl.BlockSpec((heads, WIDE, TILE), lambda i, m: (0, 0, i + offset)),
        pl.BlockSpec((heads, 16, TILE), lambda i, m: (0, 0, i)),
        const(kn.shape), const(kt.shape), const(vn.shape),
        pl.BlockSpec((1, width, TILE), lambda i, m: (i, 0, 0)),
        const(grad[0].shape), const(grad[1].shape), const(grad[2].shape), const(grad[3].shape),
    ] + [const(v.shape) for v in earlier] + [pl.BlockSpec(memory_space=pl.ANY)] * len(after)
    scratch = [
        pltpu.VMEM((heads, WIDE, TILE), BF16),
        pltpu.VMEM((heads, WIDE, TILE), BF16),
        pltpu.VMEM((width, TILE), F32),
    ]
    if part == 0:
        out_specs = [pl.BlockSpec((width, TILE), lambda i, m: (0, i)), const((width, length)), const((width, length))]
        out_shape = [shape_of(width, count * TILE), shape_of(width, length, dtype=F32), shape_of(width, length, dtype=F32)]
    else:
        out_specs = const((3 * width, length))
        out_shape = shape_of(3 * width, length)
        scratch += [pltpu.VMEM((width, length), F32), pltpu.VMEM((width, length), F32)]
    return kernel_call(
        body,
        (me, seg_row, seg_row, qt, extra, kn, kt, vn, out, *grad, *earlier, *after),
        free_in=(10, 11, 12) + tuple(range(13 + len(earlier), 15 + len(earlier))),
        grid_spec=pltpu.PrefetchScalarGridSpec(
            num_scalar_prefetch=1, grid=(count,), in_specs=in_specs, out_specs=out_specs, scratch_shapes=scratch,
        ),
        out_shape=out_shape,
        cost_estimate=cost(16e9, 10e6, 4e6),
        name="attend_backward",
    )


def middle_body(me_ref, x_ref, m0_ref, m1_ref, m2_ref, m3_ref, w0_ref, w1_ref, w2_ref, w3_ref,
                vec_ref, *rest):
    residual_ref, own_ref, mixed_ref = rest[-3:]
    total = x_ref[...].astype(F32) + vec_ref[2:3, :]
    pairs = ((m0_ref, w0_ref), (m1_ref, w1_ref), (m2_ref, w2_ref), (m3_ref, w3_ref))
    for n, (m_ref, w_ref) in enumerate(pairs):
        total = total + tn(m_ref[...], w_ref[...])
        mixed_ref[n] = m_ref[...]
    residual_ref[...] = total
    normed, _, _ = stats(total)
    own_ref[...] = (normed * vec_ref[3:4, :] + vec_ref[4:5, :]).astype(BF16)


def middle(part, me, tokens, mixed, weights, vectors, after):
    features = tokens.shape[1]
    width = weights[0].shape[0]
    return kernel_call(
        middle_body,
        (me, tokens, *mixed, *weights, vectors, *after),
        free_in=(3, 4, 5),
        free_out=(1,),
        grid_spec=pltpu.PrefetchScalarGridSpec(
            num_scalar_prefetch=1,
            grid=(1,),
            in_specs=[pl.BlockSpec((TILE, features), lambda i, m: (4 * part + m[0], 0))]
            + [const(v.shape) for v in mixed] + [const(v.shape) for v in weights] + [const(vectors.shape)]
            + [pl.BlockSpec(memory_space=pl.ANY)] * len(after),
            out_specs=[const((TILE, features)), const((TILE, features)), const((4, width, TILE))],
        ),
        out_shape=[shape_of(TILE, features, dtype=F32), shape_of(TILE, features), shape_of(4, width, TILE)],
        cost_estimate=cost(2e9, 3e6),
        name="middle",
    )


def feed_piece(x, g, inner_ref, vec_ref, outer_ref):
    hidden = nn(x, inner_ref[...]) + vec_ref[7:8, :]
    half = 0.5 + 0.5 * lax.erf(hidden * 0.5 ** 0.5)
    act = (hidden * half).astype(BF16)
    slope = half + hidden * (jnp.exp(-0.5 * hidden * hidden) * 0.3989422804014327)
    dh = (nt(g, outer_ref[...]) * slope).astype(BF16)
    out = nn(act, outer_ref[...]).astype(BF16)
    return act, dh, out, nt(dh, inner_ref[...]).astype(BF16)


def near_body(me_ref, *refs):
    count = 2 * PARTS
    x_refs = refs[:count]
    g_ref, inner_ref, vec_ref, outer_ref = refs[count:count + 4]
    out_refs, back_refs = refs[count + 4:count + 6], refs[count + 6:-6]
    sum_ref, grad_ref, x_all, g_all, act_all, dh_all = refs[-6:]
    i = pl.program_id(0)
    at = pl.ds(pl.multiple_of(i * TILE, TILE), TILE)
    for n, x_ref in enumerate(x_refs):
        @pl.when(i == n)
        def _(n=n, x_ref=x_ref):
            x_all[n * TILE:(n + 1) * TILE] = x_ref[...]

    g_all[at] = g_ref[...]
    act, dh, out, back = feed_piece(x_all[at], g_ref[...], inner_ref, vec_ref, outer_ref)
    act_all[at] = act
    dh_all[at] = dh
    sums = fold(dh.astype(F32))

    @pl.when(i == 0)
    def _():
        sum_ref[...] = jnp.zeros_like(sum_ref)

    sum_ref[...] += sums
    for n in range(count):
        @pl.when(i == n)
        def _(n=n):
            out_refs[n % 2][n // 2 * TILE:(n // 2 + 1) * TILE] = out
            back_refs[n][...] = back

    @pl.when(i == count - 1)
    def _():
        grad_ref[0] = tn(act_all[...], g_all[...]).astype(BF16)
        grad_ref[1] = tn(x_all[...], dh_all[...]).astype(BF16)


def feed_near(me, pieces, cot, inner, vectors, outer):
    features = cot.shape[1]
    units = inner.shape[1]
    count = 2 * PARTS
    piece = const((TILE, features))
    scratch = lambda n: pltpu.VMEM((count * TILE, n), BF16)
    return kernel_call(
        near_body,
        (me, *pieces, cot, inner, vectors, outer),
        free_in=tuple(range(1, count + 1)),
        free_out=(3, 5),
        grid_spec=pltpu.PrefetchScalarGridSpec(
            num_scalar_prefetch=1,
            grid=(count,),
            in_specs=[piece] * count
            + [pl.BlockSpec((TILE, features), lambda i, m: (4 * (i // 2) + (m[0] ^ (i % 2)), 0)),
               const(inner.shape), const(vectors.shape), const(outer.shape)],
            out_specs=[const((PARTS * TILE, features))] * 2 + [piece] * count
            + [const((8, units)), const((2, units, features))],
            scratch_shapes=[scratch(features), scratch(features), scratch(units), scratch(units)],
        ),
        out_shape=[shape_of(PARTS * TILE, features)] * 2 + [shape_of(TILE, features)] * count
        + [shape_of(8, units, dtype=F32), shape_of(2, units, features)],
        cost_estimate=cost(15e9, 12e6, 2e6),
        name="feed_near",
    )


def far_body(me_ref, x0_ref, x1_ref, g_ref, inner_ref, vec_ref, outer_ref, *rest):
    left_ref, right_ref, out0_ref, out1_ref, back0_ref, back1_ref, sum_ref = rest[-7:]
    i = pl.program_id(0)
    for n, x_ref in enumerate((x0_ref, x1_ref)):
        @pl.when(i == n)
        def _(x_ref=x_ref):
            left_ref[1] = x_ref[...]

    right_ref[0] = g_ref[...]
    act, dh, out, back = feed_piece(left_ref[1], g_ref[...], inner_ref, vec_ref, outer_ref)
    left_ref[0] = act
    right_ref[1] = dh
    sums = fold(dh.astype(F32))
    for n, (out_ref, back_ref) in enumerate(((out0_ref, back0_ref), (out1_ref, back1_ref))):
        @pl.when(i == n)
        def _(n=n, out_ref=out_ref, back_ref=back_ref):
            sum_ref[...] = sum_ref[...] + sums if n else sums
            out_ref[...] = out
            back_ref[...] = back


def feed_far(part, me, first, second, cot, inner, vectors, outer, kept):
    features = cot.shape[1]
    units = inner.shape[1]
    rows = pl.BlockSpec((2, TILE, features), lambda i, m: (0, 2 * part + i, 0))
    piece = const((TILE, features))
    half = pl.BlockSpec((TILE, features), lambda i, m: (part, 0))
    return kernel_call(
        far_body,
        (me, first, second, cot, inner, vectors, outer, *kept),
        free_in=(1, 2),
        free_out=(5,),
        grid_spec=pltpu.PrefetchScalarGridSpec(
            num_scalar_prefetch=1,
            grid=(2,),
            in_specs=[
                piece, piece,
                pl.BlockSpec((TILE, features), lambda i, m: (4 * part + (m[0] ^ (2 + i)), 0)),
                const(inner.shape), const(vectors.shape), const(outer.shape),
            ] + [pl.BlockSpec(memory_space=pl.ANY)] * len(kept),
            out_specs=[rows, rows, half, half, piece, piece, const((8, units))],
        ),
        out_shape=[shape_of(2, 2 * PARTS * TILE, features)] * 2 + [shape_of(PARTS * TILE, features)] * 2
        + [shape_of(TILE, features)] * 2 + [shape_of(8, units, dtype=F32)],
        input_output_aliases={7 + n: n for n in range(len(kept))},
        cost_estimate=cost(5e9, 8e6, 1e6),
        name="feed_far",
    )


def feed_grad_body(xz_ref, left_ref, right_ref, before_ref, keep_ref, send_ref):
    value = (tn(left_ref[0], right_ref[0]) + before_ref[0].astype(F32)).astype(BF16)
    mine = pl.program_id(0) == xz_ref[0]

    @pl.when(mine)
    def _():
        keep_ref[...] = value

    @pl.when(jnp.logical_not(mine))
    def _():
        send_ref[...] = value


def feed_grad(xz, left, right, before):
    _, rows, features = left.shape
    both = pl.BlockSpec((1, rows, features), lambda i, m: (i, 0, 0))
    return kernel_call(
        feed_grad_body,
        (xz, left, right, before),
        grid_spec=pltpu.PrefetchScalarGridSpec(
            num_scalar_prefetch=1,
            grid=(2,),
            in_specs=[both, both, pl.BlockSpec((1, features, features), lambda i, m: (i, 0, 0))],
            out_specs=[const(before.shape[1:])] * 2,
        ),
        out_shape=[shape_of(*before.shape[1:])] * 2,
        cost_estimate=cost(5e9, 10e6),
        name="feed_grad",
    )


def feed_ready_body(xz_ref, mine_ref, other_ref, outer_ref, inner_ref):
    for from_ref, here in ((mine_ref, xz_ref[0]), (other_ref, 1 - xz_ref[0])):
        for n, to_ref in enumerate((outer_ref, inner_ref)):
            @pl.when(here == n)
            def _(from_ref=from_ref, to_ref=to_ref):
                to_ref[...] = from_ref[...].astype(F32)


def feed_ready(xz, mine, other):
    rows, features = mine.shape
    block = pl.BlockSpec((TILE, features), lambda i, m: (i, 0))
    return kernel_call(
        feed_ready_body,
        (xz, mine, other),
        free_in=(1, 2),
        grid_spec=pltpu.PrefetchScalarGridSpec(
            num_scalar_prefetch=1,
            grid=(rows // TILE,),
            in_specs=[block, block],
            out_specs=[block, block],
        ),
        out_shape=[shape_of(rows, features, dtype=F32)] * 2,
        cost_estimate=cost(1e6, 7e6),
        name="feed_ready",
    )


def back_body(me_ref, b0_ref, b1_ref, b2_ref, residual_ref, g_ref, vec_ref, w0_ref, w1_ref, w2_ref, w3_ref,
              *rest):
    grad_ref, low_ref, a0_ref, a1_ref, a2_ref, a3_ref, sum_ref = rest[-7:]
    grad_mid = b0_ref[...].astype(F32) + b1_ref[...].astype(F32) + b2_ref[...].astype(F32)
    normed, scale, _ = stats(residual_ref[...])
    upstream = g_ref[...].astype(F32)
    grad = upstream + norm_back(grad_mid, normed, scale, vec_ref[3:4, :])
    grad_ref[...] = grad
    low = grad.astype(BF16)
    low_ref[...] = low
    for w_ref, a_ref in ((w0_ref, a0_ref), (w1_ref, a1_ref), (w2_ref, a2_ref), (w3_ref, a3_ref)):
        a_ref[...] = nt(w_ref[...], low).astype(BF16)
    for n, value in enumerate((grad_mid * normed, grad_mid, grad, upstream)):
        sum_ref[8 * n:8 * n + 8] = fold(value)


def middle_back(part, me, sums, residual, cot, vectors, weights, after):
    features = cot.shape[1]
    piece = const((TILE, features))
    width = weights[0].shape[0]
    return kernel_call(
        back_body,
        (me, *sums, residual, cot, vectors, *weights, *after),
        free_in=(2, 3) + tuple(range(11, 11 + len(after))),
        free_out=(3, 4, 5),
        grid_spec=pltpu.PrefetchScalarGridSpec(
            num_scalar_prefetch=1,
            grid=(1,),
            in_specs=[piece] * 4
            + [pl.BlockSpec((TILE, features), lambda i, m: (4 * part + m[0], 0)), const(vectors.shape)]
            + [const(v.shape) for v in weights] + [pl.BlockSpec(memory_space=pl.ANY)] * len(after),
            out_specs=[piece, piece] + [const((width, TILE))] * 4 + [const((32, features))],
        ),
        out_shape=[shape_of(TILE, features, dtype=F32), shape_of(TILE, features)]
        + [shape_of(width, TILE)] * 4 + [shape_of(32, features, dtype=F32)],
        cost_estimate=cost(2e9, 4e6),
        name="middle_back",
    )


def output_body(*refs):
    mixed, lows, outs = refs[:PARTS], refs[PARTS:2 * PARTS], refs[2 * PARTS:]
    for n in range(4):
        total = nn(mixed[0][n], lows[0][...])
        for p in range(1, PARTS):
            total = total + nn(mixed[p][n], lows[p][...])
        outs[n][...] = total.astype(BF16)


def output_grad(mixed, lows):
    width, features = mixed[0].shape[1], lows[0].shape[1]
    return kernel_call(
        output_body,
        (*mixed, *lows),
        free_out=(1, 3),
        out_shape=[shape_of(width, features)] * 4,
        cost_estimate=cost(2e9, 4e6),
        name="output_grad",
    )


def tail_body(me_ref, g_ref, wq_ref, wk_ref, wv_ref, x_ref, stat_ref, *rest):
    early, units = rest[:PARTS], rest[PARTS:2 * PARTS + 1]
    o0_ref, o1_ref, o2_ref, o3_ref, apart_ref, vec_ref, sum_ref, row_ref = rest[-8:]
    i, p = pl.program_id(0), pl.program_id(1)
    grads = g_ref[...]
    width = wq_ref.shape[0]
    value = tn(grads[:width], wq_ref[...]) + tn(grads[width:2 * width], wk_ref[...])
    value = value + tn(grads[2 * width:], wv_ref[...])

    @pl.when((i == 0) & (p == 0))
    def _():
        row_ref[...] = jnp.zeros_like(row_ref)
        sum_ref[...] = jnp.zeros_like(sum_ref)

    row_ref[...] += nt(jnp.ones((8, grads.shape[1]), BF16), grads)
    normed = (x_ref[...].astype(F32) - stat_ref[:, 0:1]) * stat_ref[:, 1:2]
    sum_ref[:8] += fold(value * normed)
    sum_ref[8:] += fold(value)
    value = value.astype(BF16)
    for step, o_ref in enumerate((o3_ref, o2_ref, o1_ref, o0_ref)):
        @pl.when(i == step)
        def _(o_ref=o_ref):
            o_ref[pl.ds(pl.multiple_of(p * TILE, TILE), TILE), :] = value

    @pl.when((i == 3) & (p == PARTS - 1))
    def _():
        row = lax.broadcasted_iota(jnp.int32, vec_ref.shape, 0)
        vectors = jnp.zeros(vec_ref.shape, F32)
        before = early[0][...]
        for ref in early[1:]:
            before = before + ref[...]
        parts = [before[8 * n:8 * n + 8] for n in range(4)] + [sum_ref[:8], sum_ref[8:]]
        for n, part in enumerate(parts):
            vectors = jnp.where(row == n, jnp.sum(part, axis=0, keepdims=True), vectors)
        vec_ref[...] = vectors
        inside = units[0][...]
        for ref in units[1:]:
            inside = inside + ref[...]
        apart_ref[...] = jnp.where(row == 6, jnp.sum(inside, axis=0, keepdims=True), 0.0)
        apart_ref[7:8, :row_ref.shape[1]] = row_ref[0:1]
        o3_ref[PARTS * TILE:] = paired(vectors)


def tail(me, grads, wq, wk, wv, tokens, stat, early, units, after):
    deep = grads.shape[0]
    features = wq.shape[1]
    share = const((PARTS * TILE, features))
    more = const((PARTS * TILE + 16, features))
    at = lambda i, p, m: 4 * p + (m[0] ^ (3 - i))
    return kernel_call(
        tail_body,
        (me, grads, wq, wk, wv, tokens, stat, *early, *units, *after),
        free_out=(1, 3),
        grid_spec=pltpu.PrefetchScalarGridSpec(
            num_scalar_prefetch=1,
            grid=(4, PARTS),
            in_specs=[pl.BlockSpec((deep, TILE), lambda i, p, m: (0, at(i, p, m))),
                      const(wq.shape), const(wk.shape), const(wv.shape),
                      pl.BlockSpec((TILE, features), lambda i, p, m: (at(i, p, m), 0)),
                      pl.BlockSpec((TILE, WIDE), lambda i, p, m: (at(i, p, m), 0))]
            + [const(v.shape) for v in (*early, *units)] + [pl.BlockSpec(memory_space=pl.ANY)] * len(after),
            out_specs=[share, share, share, more, const((8, features)), const((8, features))],
            scratch_shapes=[pltpu.VMEM((16, features), F32), pltpu.VMEM((8, deep), F32)],
        ),
        out_shape=[shape_of(PARTS * TILE, features)] * 3 + [shape_of(PARTS * TILE + 16, features)]
        + [shape_of(8, features, dtype=F32)] * 2,
        cost_estimate=cost(4e9, 10e6),
        name="tail",
    )


def chip_body(one_ref, two_ref, vec_ref, *rest):
    out_ref = rest[-1]
    rows = one_ref.shape[0]
    out_ref[:rows] = (one_ref[...].astype(F32) + two_ref[:rows].astype(F32)).astype(BF16)
    out_ref[rows:] = paired(vec_ref[...] + joined(two_ref[rows:]))


def chip_sum(one, two, vectors, after):
    return kernel_call(
        chip_body,
        (one, two, vectors, *after),
        free_in=(1,) + tuple(range(3, 3 + len(after))),
        free_out=(0,),
        grid=(1,),
        in_specs=[const(one.shape), const(two.shape), const(vectors.shape)]
        + [pl.BlockSpec(memory_space=pl.ANY)] * len(after),
        out_specs=[const(two.shape)],
        out_shape=[shape_of(*two.shape)],
        name="chip_sum",
    )[0]


def halves_body(xz_ref, g_ref, go_ref, *rest):
    keep_ref, send_ref = rest[-2:]
    width = go_ref.shape[0]
    for to_ref, half in ((keep_ref, xz_ref[0]), (send_ref, 1 - xz_ref[0])):
        @pl.when(half == 0)
        def _(to_ref=to_ref):
            to_ref[...] = g_ref[:2 * width]

        @pl.when(half == 1)
        def _(to_ref=to_ref):
            to_ref[:width] = g_ref[2 * width:]
            to_ref[width:] = go_ref[...]


def halves(xz, grad_weights, grad_output, after):
    width, features = grad_output.shape
    half = const((2 * width, features))
    return kernel_call(
        halves_body,
        (xz, grad_weights, grad_output, *after),
        free_in=(1, 2, 3),
        grid_spec=pltpu.PrefetchScalarGridSpec(
            num_scalar_prefetch=1,
            grid=(1,),
            in_specs=[const(grad_weights.shape), const(grad_output.shape)]
            + [pl.BlockSpec(memory_space=pl.ANY)] * len(after),
            out_specs=[half, half],
        ),
        out_shape=[shape_of(2 * width, features)] * 2,
        cost_estimate=cost(1e6, 4e6),
        name="halves",
    )


def quarter_body(count, xz_ref, one_ref, two_ref, *rest):
    rows = one_ref.shape[0] // count
    for n, out_ref in enumerate(rest[-count:]):
        at = pl.ds(pl.multiple_of(lax.rem(xz_ref[1] + n, count) * rows, rows), rows)
        out_ref[...] = (one_ref[at, :].astype(F32) + two_ref[at, :].astype(F32)).astype(BF16)


def quarters(xz, one, two, count, after):
    rows, features = one.shape

    def body(*refs):
        quarter_body(count, *refs)

    return kernel_call(
        body,
        (xz, one, two, *after),
        free_in=(2, 3, 4),
        grid_spec=pltpu.PrefetchScalarGridSpec(
            num_scalar_prefetch=1,
            grid=(1,),
            in_specs=[const(one.shape), const(two.shape)] + [pl.BlockSpec(memory_space=pl.ANY)] * len(after),
            out_specs=[const((rows // count, features))] * count,
        ),
        out_shape=[shape_of(rows // count, features)] * count,
        cost_estimate=cost(1e6, 2e6),
        name="quarters",
    )


def paired(value):
    return jnp.concatenate(split(value, 2), axis=0).astype(BF16)


def joined(both):
    both = both.astype(F32)
    half = both.shape[0] // 2
    return both[:half] + both[half:]


def second_body(count, *refs):
    one_ref, two_ref, apart_ref, out_ref = refs[count], refs[count + 1], refs[count + 2], refs[-1]
    rows = refs[0].shape[0]
    total = refs[0][...].astype(F32)
    for ref in refs[1:count]:
        total = total + ref[...].astype(F32)
    out_ref[:rows] = total.astype(BF16)
    out_ref[rows:] = paired(joined(one_ref[...]) + joined(two_ref[...]) + apart_ref[...])


def second(parts, one, two, apart, after):
    count = len(parts)
    rows, features = parts[0].shape
    last = pl.BlockSpec((16, features), lambda i: (one.shape[0] // 16 - 1, 0))

    def body(*refs):
        second_body(count, *refs)

    return kernel_call(
        body,
        (*parts, one, two, apart, *after),
        free_in=tuple(range(1, count + 2)) + tuple(range(count + 3, count + 3 + len(after))),
        grid=(1,),
        in_specs=[const((rows, features))] * count + [last, last, const(apart.shape)]
        + [pl.BlockSpec(memory_space=pl.ANY)] * len(after),
        out_specs=[const((rows + 16, features))],
        out_shape=[shape_of(rows + 16, features)],
        name="second",
    )[0]


def third_body(count, xz_ref, *refs):
    out_ref = refs[-1]
    step = out_ref.shape[0] - (refs[0].shape[0] * count - out_ref.shape[0]) // (count - 1)
    rows = step // count
    sums = None
    for n, ref in enumerate(refs[:count]):
        place_at = lax.rem(xz_ref[1] + count - n, count)
        out_ref[pl.ds(pl.multiple_of(place_at * rows, rows), rows), :] = ref[:rows]
        value = joined(ref[rows:])
        sums = value if sums is None else sums + value
    out_ref[step:] = paired(sums)


def third(xz, pieces, extra, after):
    count = len(pieces)
    rows, features = pieces[0].shape
    total = (rows - extra) * count + extra

    def body(*refs):
        third_body(count, *refs)

    return kernel_call(
        body,
        (xz, *pieces, *after),
        free_in=tuple(range(1, count + 1)),
        grid_spec=pltpu.PrefetchScalarGridSpec(
            num_scalar_prefetch=1,
            grid=(1,),
            in_specs=[const((rows, features))] * count + [pl.BlockSpec(memory_space=pl.ANY)] * len(after),
            out_specs=[const((total, features))],
        ),
        out_shape=[shape_of(total, features)],
        name="third",
    )[0]


def ready_body(xz_ref, mine_ref, other_ref, *rest):
    outs = rest[-14:]
    width = outs[0].shape[0]
    for n, out_ref in enumerate(outs[:4]):
        rows = slice(n % 2 * width, (n % 2 + 1) * width)
        for to_ref, chosen in ((mine_ref, xz_ref[0] == n // 2), (other_ref, xz_ref[0] != n // 2)):
            @pl.when(chosen)
            def _(to_ref=to_ref, out_ref=out_ref, rows=rows):
                out_ref[...] = to_ref[rows].astype(F32)

    small = joined(mine_ref[2 * width:]) + joined(other_ref[2 * width:])
    for n, out_ref in enumerate(outs[4:11]):
        out_ref[...] = small[n]
    for n, out_ref in enumerate(outs[11:]):
        out_ref[...] = small[7, n * width:(n + 1) * width]


def ready(xz, mine, other, width, after):
    rows, features = mine.shape
    sizes = [(features,)] * 7 + [(width,)] * 3
    return kernel_call(
        ready_body,
        (xz, mine, other, *after),
        free_in=(2,),
        grid_spec=pltpu.PrefetchScalarGridSpec(
            num_scalar_prefetch=1,
            grid=(1,),
            in_specs=[const(mine.shape), const(other.shape)] + [pl.BlockSpec(memory_space=pl.ANY)] * len(after),
            out_specs=[const((width, features))] * 4 + [const(size) for size in sizes],
        ),
        out_shape=[shape_of(width, features, dtype=F32)] * 4 + [shape_of(*size, dtype=F32) for size in sizes],
        cost_estimate=cost(1e6, 4e6),
        name="ready",
    )


def final_body(me_ref, b0_ref, b1_ref, b2_ref, x_ref, *rest):
    grad_refs, vec_ref, out_ref = rest[:PARTS], rest[PARTS], rest[-1]
    p = pl.program_id(0)
    grad_attend = b0_ref[...].astype(F32) + b1_ref[...].astype(F32) + b2_ref[...].astype(F32)
    normed, scale, _ = stats(x_ref[...].astype(F32))
    back = norm_back(grad_attend, normed, scale, vec_ref[0:1, :])
    for n, grad_ref in enumerate(grad_refs):
        @pl.when(p == n)
        def _(grad_ref=grad_ref):
            out_ref[...] = (grad_ref[...] + back).astype(BF16)


def final(me, sums, tokens, grads, vectors, after):
    features = tokens.shape[1]
    rows = pl.BlockSpec((TILE, features), lambda p, m: (p, 0))
    return kernel_call(
        final_body,
        (me, *sums, tokens, *grads, vectors, *after),
        free_in=(2, 3) + tuple(range(6 + PARTS, 6 + PARTS + len(after))),
        free_out=(0,),
        grid_spec=pltpu.PrefetchScalarGridSpec(
            num_scalar_prefetch=1,
            grid=(PARTS,),
            in_specs=[rows] * 3 + [pl.BlockSpec((TILE, features), lambda p, m: (4 * p + m[0], 0))]
            + [const((TILE, features))] * PARTS + [const(vectors.shape)]
            + [pl.BlockSpec(memory_space=pl.ANY)] * len(after),
            out_specs=[rows],
        ),
        out_shape=[shape_of(PARTS * TILE, features)],
        cost_estimate=cost(1e8, 5e6),
        name="final",
    )[0]


def place_body(me_ref, p0_ref, p1_ref, p2_ref, p3_ref, *rest):
    out_ref = rest[-1]
    for step, p_ref in enumerate((p0_ref, p1_ref, p2_ref, p3_ref)):
        @pl.when(pl.program_id(0) == step)
        def _(p_ref=p_ref):
            at = pl.ds(pl.multiple_of(pl.program_id(1) * TILE, TILE), TILE)
            out_ref[...] = p_ref[at, :].astype(out_ref.dtype)


def place(me, shares, dtype, after):
    rows, features = shares[0].shape
    return kernel_call(
        place_body,
        (me, *shares, *after),
        free_in=(1, 2, 3, 4),
        grid_spec=pltpu.PrefetchScalarGridSpec(
            num_scalar_prefetch=1,
            grid=(4, PARTS),
            in_specs=[const((rows, features))] * 4 + [pl.BlockSpec(memory_space=pl.ANY)] * len(after),
            out_specs=pl.BlockSpec((TILE, features), lambda i, p, m: (4 * p + (m[0] ^ i), 0)),
        ),
        out_shape=shape_of(4 * rows, features, dtype=dtype),
        cost_estimate=cost(1e6, 9e6),
        name="place",
    )


def fence_body(*refs):
    pass


def fence(value, *after, space=pltpu.HBM):
    anywhere = pl.BlockSpec(memory_space=pl.ANY)
    return pl.pallas_call(
        fence_body,
        in_specs=[anywhere] * (1 + len(after)),
        out_specs=anywhere,
        out_shape=space(value.shape, value.dtype),
        input_output_aliases={0: 0},
        name="fence",
    )(pltpu.with_memory_space_constraint(value, space), *after)


def other_core(value):
    return lax.ppermute(value, "core", SWAP)


def other_chip(value):
    return lax.ppermute(value, "y", SWAP)


def crosswise(value):
    return lax.ppermute(value, MP, [(n, n ^ 3) for n in range(4)])


def exchange(pieces):
    return [pieces[0], other_core(pieces[1]), other_chip(pieces[2]), crosswise(pieces[3])]


def gather_sum(pieces):
    near = other_core(pieces[1])
    far = (pieces[2].astype(F32) + other_core(pieces[3]).astype(F32)).astype(BF16)
    return [pieces[0], near, other_chip(far)], far


def spread(value):
    far = other_chip(value)
    return [value, other_core(value), far, other_core(far)]


def pick(values, at):
    return lax.dynamic_index_in_dim(values, at, 0, keepdims=False)


def turned(values, way):
    size = lax.axis_size("z")
    return lax.ppermute(values, "z", [(n, (n + way) % size) for n in range(size)])


def sum_first(xz, keep, got, after):
    size = lax.axis_size("z")
    if size > 4:
        return [lax.psum(keep + got, "z")]
    return quarters(xz, keep, got, size, after)


def gather_z(value):
    size = lax.axis_size("z")
    if size > 4:
        return [lax.all_gather(value, "z", axis=0, tiled=True)]
    return [turned(value, way) if way else value for way in range(size)]


def local(
    tokens,
    segment_ids,
    gain_one,
    bias_one,
    query_weight,
    query_bias,
    key_weight,
    value_weight,
    value_bias,
    output_weight,
    output_bias,
    gain_two,
    bias_two,
    inner_weight,
    inner_bias,
    outer_weight,
    outer_bias,
    cotangent,
):
    _, length, features = tokens.shape
    width = query_weight.shape[1]
    heads = width // HEAD
    tokens = tokens.reshape(length, features)
    cot = cotangent.reshape(length, features)
    at = lax.axis_index(MP).astype(jnp.int32)
    me = at[None]
    xz = jnp.stack([lax.axis_index("x"), lax.axis_index("z")]).astype(jnp.int32)
    apart = jnp.concatenate([query_bias, value_bias, jnp.zeros((features - 2 * width,), F32)])
    vectors = jnp.concatenate([gain_one, bias_one, output_bias, gain_two, bias_two, outer_bias, apart, inner_bias])
    vectors = vectors.reshape(8, features)
    wq, wk, wv = query_weight.T, key_weight.T, value_weight.T

    output_weights = spread(output_weight)
    attend_in, qt, kt, vt, kn, vn, stat = project(tokens, segment_ids, vectors, wq, wk, wv, heads)

    parts = range(PARTS)
    attended, extras, fours = [], [], []
    for p in parts:
        out, extra, *four = attend_forward(p, me, segment_ids, qt, kn, vt, output_weights[1:3] if p == 0 else ())
        attended.append(out)
        extras.append(extra)
        fours.append(exchange(four))
    mixed, residuals, pieces = [], [], []
    for p in parts:
        residual, own, together = middle(p, me, tokens, fours[p], output_weights, vectors, extras[p + 1:])
        mixed.append(together)
        residuals.append(residual)
        pieces.append([own, other_core(own), other_chip(own)])

    backs = {}
    *outs, b00, b01, b10, b11, near_sum, near_grad = feed_near(
        me, [pieces[p][n] for p in parts for n in (0, 1)], cot, inner_weight, vectors, outer_weight
    )
    backs[0, 0], backs[0, 1], backs[1, 0], backs[1, 1] = b00, b01, b10, b11
    sums, kept, gathered, far_sums, behind = [near_sum], (), [], [], b00
    for p in parts:
        far = fence(pieces[p][2], behind, space=pltpu.VMEM)
        *kept, backs[p, 2], backs[p, 3], far_sum = feed_far(
            p, me, far, other_core(far), cot, inner_weight, vectors, outer_weight, kept
        )
        behind = backs[p, 2]
        sums.append(far_sum)
        if p:
            backs[p, 3] = fence(backs[p, 3], gathered[-1][2], space=pltpu.VMEM)
            feed_keep, feed_send = feed_grad(xz, kept[0], kept[1], near_grad)
            backs[p, 2] = fence(backs[p, 2], feed_send)
        summed, far_sum = gather_sum([backs[p, n] for n in range(4)])
        gathered.append(summed)
        far_sums.append(far_sum)
    left, right, *far_outs = kept
    outs += far_outs
    grad_residuals, lows, grads_attended, inner_sums = [], [], [], []
    for p in parts:
        grad, low, a0, a1, a2, a3, vector = middle_back(
            p, me, gathered[p], residuals[p], cot, vectors, output_weights, far_sums[p + 1:]
        )
        grad_residuals.append(grad)
        lows.append(low)
        inner_sums.append(vector)
        grads_attended.append(exchange([a0, a1, a2, a3]))

    near = other_core(fence(outs[1], *far_sums))
    far = (outs[2].astype(F32) + other_core(fence(outs[3], *far_sums)).astype(F32)).astype(BF16)
    far = fence(far, lows[-1], space=pltpu.VMEM)
    part = output_grad(mixed, lows)
    earlier = attend_backward(0, me, segment_ids, qt, extras[0], kn, kt, vn, attended[0], grads_attended[0], (),
                              (far, near, part[0]))
    there = other_chip(far)
    feed_sum = fence(feed_keep, earlier[0]).astype(F32) + lax.ppermute(feed_send, "x", SWAP).astype(F32)
    feed_sum = lax.psum_scatter(feed_sum.astype(BF16), "z", scatter_dimension=0, tiled=True)
    part_far = fence(part[2], earlier[0])
    part_far = (part_far.astype(F32) + other_core(part[3]).astype(F32)).astype(BF16)
    part_near = other_core(part[1])
    grads = attend_backward(1, me, segment_ids, qt, extras[1], kn, kt, vn, attended[1], grads_attended[1], earlier,
                            (part_near, part_far, there))

    part_across = other_chip(part_far)
    grad_output = fence(part[0], grads).astype(F32) + part_near.astype(F32) + part_across.astype(F32)
    keep, send = halves(xz, nn(grads, attend_in).astype(BF16), grad_output.astype(BF16), ())
    result = jnp.concatenate(residuals) + fence(outs[0], send).astype(F32) + near.astype(F32)
    result = (result + there.astype(F32) + outer_bias).astype(BF16)
    near, far = other_core(result), other_chip(result)
    got = lax.ppermute(send, "x", SWAP)
    back_own, back_near, back_far, back_across, apart, summed = tail(
        me, grads, wq, wk, wv, tokens, stat, inner_sums, sums, (send,)
    )
    feed_sum = lax.all_gather(fence(feed_sum, send), "z", axis=0, tiled=True)
    feed_other = lax.ppermute(feed_sum, "x", SWAP)
    quarter = sum_first(xz, keep, got, (near, far, apart))
    back_across = other_core(fence(back_across, quarter[-1], space=pltpu.VMEM))
    back_far = chip_sum(back_far, back_across, summed, ())
    back_there = other_chip(back_far)
    share = final(me, [back_own, other_core(back_near), back_there], tokens, grad_residuals, vectors, ())
    if len(quarter) > 1:
        turns = [quarter[0]] + [turned(part, n + 1) for n, part in enumerate(quarter[1:])]
        held = second(turns, back_far, back_there, apart, (share,))
        layer_out = place(me, [result, near, far, other_core(far)], BF16, (held, feed_other))
        mine = third(xz, gather_z(held), 16, (layer_out,))
    else:
        small = joined(back_far[-16:]) + joined(back_there[-16:]) + apart
        layer_out = place(me, [result, near, far, other_core(far)], BF16, ())
        mine = jnp.concatenate([quarter[0], paired(lax.psum(small, "z"))])
    share = fence(share, held if len(quarter) > 1 else mine, space=pltpu.VMEM)
    near, far = other_core(share), fence(other_chip(share), mine, space=pltpu.VMEM)
    input_grad = place(me, [share, near, far, other_core(far)], F32, (mine,))
    feed_sum = feed_ready(xz, feed_sum, feed_other)
    *wide, two_gain, two_bias, output_sum, outer_bias, one_gain, one_bias, inner_bias, query, _, value = ready(
        xz, mine, lax.ppermute(mine, "x", SWAP), width, (*feed_sum, input_grad)
    )
    return (
        layer_out.reshape(1, length, features),
        input_grad.reshape(1, length, features),
        one_gain,
        one_bias,
        wide[0].T,
        query,
        wide[1].T,
        wide[2].T,
        value,
        wide[3],
        output_sum,
        two_gain,
        two_bias,
        feed_sum[1],
        inner_bias,
        feed_sum[0],
        outer_bias,
    )


def solution(mesh):
    rows = mesh.shape["dp"]
    inner = Mesh(mesh.devices.reshape(rows // 2, 2, 2, 2), DP + MP)
    placed = (
        P(DP, None, None),
        P(DP, None),
        P(),
        P(),
        P(None, MP),
        P(MP),
        P(None, MP),
        P(None, MP),
        P(MP),
        P(MP, None),
        P(),
        P(),
        P(),
        P(None, MP),
        P(MP),
        P(MP, None),
        P(),
        P(DP, None, None),
    )
    return jax.shard_map(
        local,
        mesh=inner,
        in_specs=placed,
        out_specs=(
            P(DP, None, None),
            P(DP, None, None),
            P(),
            P(),
            P(None, MP),
            P(MP),
            P(None, MP),
            P(None, MP),
            P(MP),
            P(MP, None),
            P(),
            P(),
            P(),
            P(None, MP),
            P(MP),
            P(MP, None),
            P(),
        ),
        check_vma=False,
    )
```

```python
import jax
import jax.numpy as jnp
from jax import lax
from jax.experimental import pallas as pl
from jax.experimental.pallas import tpu as pltpu
from jax.sharding import Mesh
from jax.sharding import PartitionSpec as P

HEAD = 64
WIDE = 128
TILE = 256
LONG = 512
PARTS = 2
MASKED = 1e30
SCALE = 1
F32 = jnp.float32
BF16 = jnp.bfloat16
DP = ("z", "x")
MP = ("y", "core")
SWAP = [(0, 1), (1, 0)]


def nn(left, right):
    return lax.dot_general(left, right, (((1,), (0,)), ((), ())), preferred_element_type=F32)


def nt(left, right):
    return lax.dot_general(left, right, (((1,), (1,)), ((), ())), preferred_element_type=F32)


def tn(left, right):
    return lax.dot_general(left, right, (((0,), (0,)), ((), ())), preferred_element_type=F32)


def stats(values):
    mean = jnp.mean(values, axis=-1, keepdims=True)
    center = values - mean
    scale = lax.rsqrt(jnp.mean(center * center, axis=-1, keepdims=True) + 1e-05)
    return center * scale, scale, mean


def norm_back(grad_out, normed, scale, gain):
    upstream = grad_out * gain
    return scale * (
        upstream
        - jnp.mean(upstream, axis=-1, keepdims=True)
        - normed * jnp.mean(upstream * normed, axis=-1, keepdims=True)
    )


def fold(values):
    return jnp.sum(values.reshape(-1, 8, values.shape[-1]), axis=0)


def split(value, parts):
    out = []
    for _ in range(parts):
        piece = value.astype(BF16).astype(F32)
        out.append(piece)
        value = value - piece
    return out


def const(shape):
    return pl.BlockSpec(shape, lambda *_: (0,) * len(shape))


def shape_of(*dims, dtype=BF16):
    return jax.ShapeDtypeStruct(dims, dtype)


def params(mib=40):
    return pltpu.CompilerParams(vmem_limit_bytes=mib << 20)


def kernel_call(body, values, free_in=(), free_out=(), **options):
    shapes = options.pop("out_shape")
    many = isinstance(shapes, (list, tuple))
    shapes = [s if n in free_out else pltpu.HBM(s.shape, s.dtype) for n, s in enumerate(shapes if many else [shapes])]
    values = [
        v if n in free_in or v.dtype == jnp.int32 else pltpu.with_memory_space_constraint(v, pltpu.HBM)
        for n, v in enumerate(values)
    ]
    return pl.pallas_call(
        body, out_shape=shapes if many else shapes[0], compiler_params=params(), **options
    )(*values)


def cost(flops, moved, special=0):
    return pl.CostEstimate(flops=int(flops * SCALE), bytes_accessed=int(moved * SCALE), transcendentals=0)


def project_body(x_ref, seg_ref, vec_ref, wq_ref, wk_ref, wv_ref,
                 ai_ref, qt_ref, kt_ref, vt_ref, kn_ref, vn_ref, stat_ref):
    heads = kn_ref.shape[0]
    width = heads * HEAD
    tile = x_ref.shape[0]
    normed, scale, mean = stats(x_ref[...].astype(F32))
    lane = lax.broadcasted_iota(jnp.int32, stat_ref.shape, 1)
    stat_ref[...] = jnp.where(lane == 0, mean, scale)
    ai = (normed * vec_ref[0:1, :] + vec_ref[1:2, :]).astype(BF16)
    ai_ref[...] = ai
    column = vec_ref[...].T[:2 * width, 6:7]
    queries = ((nt(wq_ref[...], ai) + column[:width]).astype(BF16)).astype(F32) * HEAD ** -0.5
    keys = nt(wk_ref[...], ai)
    kt_ref[...] = keys.astype(BF16)
    values = nt(wv_ref[...], ai) + column[width:]
    row = lax.broadcasted_iota(jnp.int32, (HEAD, tile), 0)
    same = jnp.where(row == seg_ref[...], 1.0, 0.0)
    mask = jnp.where(row < 8, (same - 1.0) * MASKED, jnp.where(row < 11, 1.0, 0.0))
    ones = jnp.where(row < 2, 1.0, 0.0)
    first = jnp.where(row[:16] == 0, 1.0, 0.0).astype(BF16)
    for h in range(heads):
        rows = slice(h * HEAD, (h + 1) * HEAD)
        qt_ref[h, :HEAD, :] = queries[rows].astype(BF16)
        qt_ref[h, HEAD:, :] = same.astype(BF16)
        vt_ref[h, :HEAD, :] = values[rows].astype(BF16)
        vt_ref[h, HEAD:, :] = first
        kn_ref[h] = jnp.concatenate([keys[rows], mask], axis=0).T.astype(BF16)
        vn_ref[h] = jnp.concatenate([values[rows], ones], axis=0).T.astype(BF16)


def project(tokens, seg_row, vectors, wq, wk, wv, heads):
    length, features = tokens.shape
    width = heads * HEAD
    return kernel_call(
        project_body,
        (tokens, seg_row, vectors, wq, wk, wv),
        grid=(length // LONG,),
        in_specs=[
            pl.BlockSpec((LONG, features), lambda i: (i, 0)),
            pl.BlockSpec((1, LONG), lambda i: (0, i)),
            const(vectors.shape), const(wq.shape), const(wk.shape), const(wv.shape),
        ],
        out_specs=[
            pl.BlockSpec((LONG, features), lambda i: (i, 0)),
            pl.BlockSpec((heads, WIDE, LONG), lambda i: (0, 0, i)),
            pl.BlockSpec((width, LONG), lambda i: (0, i)),
            pl.BlockSpec((heads, HEAD + 16, LONG), lambda i: (0, 0, i)),
            pl.BlockSpec((heads, LONG, WIDE), lambda i: (0, i, 0)),
            pl.BlockSpec((heads, LONG, WIDE), lambda i: (0, i, 0)),
            pl.BlockSpec((LONG, WIDE), lambda i: (i, 0)),
        ],
        out_shape=[
            shape_of(length, features),
            shape_of(heads, WIDE, length),
            shape_of(width, length),
            shape_of(heads, HEAD + 16, length),
            shape_of(heads, length, WIDE),
            shape_of(heads, length, WIDE),
            shape_of(length, WIDE, dtype=F32),
        ],
        cost_estimate=cost(6e9, 14e6),
        name="project",
    )


def key_range(seg_ref, seg_all, i):
    first = seg_ref[0, i * TILE]
    last = seg_ref[0, i * TILE + TILE - 1]
    before = jnp.sum(jnp.where(seg_all < first, 1.0, 0.0)).astype(jnp.int32)
    until = jnp.sum(jnp.where(seg_all <= last, 1.0, 0.0)).astype(jnp.int32)
    return before // TILE, (until + TILE - 1) // TILE


def by_blocks(low, high, step, carry):
    keys = lambda kb: pl.ds(pl.multiple_of(kb * TILE, TILE), TILE)
    for many in (3, 2, 1):
        rounds = (high - low) // many
        run = lambda n, c, low=low, many=many: step([keys(low + many * n + k) for k in range(many)], c)
        carry = lax.fori_loop(0, rounds, run, carry)
        low = low + many * rounds
    return carry


def shifted(one_hot, pieces):
    row = lax.broadcasted_iota(jnp.int32, one_hot.shape, 0)
    value = one_hot
    for n, piece in enumerate(pieces):
        value = jnp.where(row == 8 + n, piece, value)
    return value.astype(BF16)


def forward_body(offset, me_ref, segs_ref, seg_ref, qt_ref, kn_ref, vt_ref, *rest):
    out_ref, extra_ref, o0_ref, o1_ref, o2_ref, o3_ref, acc_ref = rest[-7:]
    heads, _, tile = qt_ref.shape
    i = pl.program_id(0)
    low, high = key_range(segs_ref, seg_ref[...], i + offset)
    acc_ref[...] = jnp.zeros_like(acc_ref)

    def step(keys, tops):
        scores = [[nn(kn_ref[h, at, :], qt_ref[h]) for at in keys] for h in range(heads)]
        new_tops = []
        for h in range(heads):
            top = tops[h]
            for score in scores[h]:
                top = jnp.maximum(top, jnp.max(score, axis=0, keepdims=True))
            new_tops.append(top)
        powered = [[jnp.exp(score - new_tops[h]).astype(BF16) for score in scores[h]] for h in range(heads)]
        for h in range(heads):
            total = acc_ref[h] * jnp.exp(tops[h] - new_tops[h])
            for at, power in zip(keys, powered[h]):
                total = total + nn(vt_ref[h, :, at], power)
            acc_ref[h] = total
        return tuple(new_tops)

    tops = by_blocks(low, high, step, (jnp.full((1, tile), -jnp.inf, F32),) * heads)
    for h in range(heads):
        total = acc_ref[h, HEAD:HEAD + 1, :]
        out_ref[0, h * HEAD:(h + 1) * HEAD, :] = (acc_ref[h, :HEAD, :] / total).astype(BF16)
        one_hot = qt_ref[h, HEAD:HEAD + 16, :].astype(F32)
        extra_ref[h] = shifted(one_hot, split(-(tops[h] + jnp.log(total)), 3))
    for n, o_ref in enumerate((o0_ref, o1_ref, o2_ref, o3_ref)):
        @pl.when((i ^ me_ref[0]) == n)
        def _(o_ref=o_ref):
            o_ref[...] = out_ref[0]


def attend_forward(part, me, seg_row, qt, kn, vt, after):
    heads, _, length = qt.shape
    width = heads * HEAD
    count = length // TILE // PARTS
    offset = part * count

    def body(*refs):
        forward_body(offset, *refs)

    return kernel_call(
        body,
        (me, seg_row, seg_row, qt, kn, vt, *after),
        free_in=tuple(range(6, 6 + len(after))),
        free_out=(3, 4, 5),
        grid_spec=pltpu.PrefetchScalarGridSpec(
            num_scalar_prefetch=1,
            grid=(count,),
            in_specs=[
                pl.BlockSpec(memory_space=pltpu.SMEM),
                const((1, length)),
                pl.BlockSpec((heads, WIDE, TILE), lambda i, m: (0, 0, i + offset)),
                const(kn.shape), const(vt.shape),
            ] + [pl.BlockSpec(memory_space=pl.ANY)] * len(after),
            out_specs=[
                pl.BlockSpec((1, width, TILE), lambda i, m: (i, 0, 0)),
                pl.BlockSpec((heads, 16, TILE), lambda i, m: (0, 0, i)),
            ] + [const((width, TILE))] * 4,
            scratch_shapes=[pltpu.VMEM((heads, HEAD + 16, TILE), F32)],
        ),
        out_shape=[shape_of(count, width, TILE), shape_of(heads, 16, count * TILE)] + [shape_of(width, TILE)] * 4,
        cost_estimate=cost(9e9, 5e6, 4e6),
        name="attend_forward",
    )


def backward_body(part, me_ref, segs_ref, seg_ref, qt_ref, extra_ref, kn_ref, kt_ref, vn_ref, out_ref,
                  g0_ref, g1_ref, g2_ref, g3_ref, *rest):
    heads, _, tile = qt_ref.shape
    width = heads * HEAD
    length = kt_ref.shape[1]
    if part == 0:
        dq_out, dk_ref, dv_ref, qa_ref, da_ref, dq_ref = rest[-6:]
    else:
        dq_in, dk_in, dv_in = rest[:3]
        grads_ref, qa_ref, da_ref, dq_ref, dk_ref, dv_ref = rest[-6:]
    i = pl.program_id(0)
    count = length // TILE // PARTS
    at_here = i + part * count
    low, high = key_range(segs_ref, seg_ref[...], at_here)

    @pl.when(i == 0)
    def _():
        if part == 0:
            dk_ref[...] = jnp.zeros_like(dk_ref)
            dv_ref[...] = jnp.zeros_like(dv_ref)
        else:
            dk_ref[...] = dk_in[...]
            dv_ref[...] = dv_in[...]
            grads_ref[:width, :count * TILE] = dq_in[...]
        qa_ref[...] = jnp.zeros_like(qa_ref)
        da_ref[...] = jnp.zeros_like(da_ref)

    source = i ^ me_ref[0]
    for n, g_ref in enumerate((g0_ref, g1_ref, g2_ref, g3_ref)):
        @pl.when(source == n)
        def _(g_ref=g_ref):
            for h in range(heads):
                da_ref[h, :HEAD, :] = g_ref[h * HEAD:(h + 1) * HEAD]

    dq_ref[...] = jnp.zeros_like(dq_ref)
    row = lax.broadcasted_iota(jnp.int32, (16, tile), 0)
    for h in range(heads):
        rows = slice(h * HEAD, (h + 1) * HEAD)
        qa_ref[h, :HEAD, :] = qt_ref[h, :HEAD, :]
        qa_ref[h, HEAD:HEAD + 16, :] = extra_ref[h]
        inner = jnp.sum(da_ref[h, :HEAD, :].astype(F32) * out_ref[0, rows].astype(F32), axis=0, keepdims=True)
        first, second = split(-inner, 2)
        value = jnp.where(row == 0, first, jnp.where(row == 1, second, 0.0))
        da_ref[h, HEAD:HEAD + 16, :] = value.astype(BF16)

    def step(keys, carry):
        every = range(heads)
        rows = [slice(h * HEAD, (h + 1) * HEAD) for h in every]
        scores = [[nn(kn_ref[h, at, :], qa_ref[h]) for at in keys] for h in every]
        slopes = [[nn(vn_ref[h, at, :], da_ref[h]) for at in keys] for h in every]
        probs = [[jnp.exp(score) for score in scores[h]] for h in every]
        ds = [[(p * s).astype(BF16) for p, s in zip(probs[h], slopes[h])] for h in every]
        probs = [[p.astype(BF16) for p in probs[h]] for h in every]
        for h in every:
            total = dq_ref[rows[h]]
            for n, at in enumerate(keys):
                dv_ref[rows[h], at] += nt(da_ref[h, :HEAD, :], probs[h][n])
                dk_ref[rows[h], at] += nt(qa_ref[h, :HEAD, :], ds[h][n])
                total = total + nn(kt_ref[rows[h], at], ds[h][n])
            dq_ref[rows[h]] = total
        return carry

    by_blocks(low, high, step, 0)
    dq = (dq_ref[...] * HEAD ** -0.5).astype(BF16)
    if part == 0:
        dq_out[...] = dq
    else:
        grads_ref[:width, pl.ds(pl.multiple_of(at_here * TILE, TILE), TILE)] = dq

        @pl.when(i == pl.num_programs(0) - 1)
        def _():
            grads_ref[width:2 * width] = dk_ref[...].astype(BF16)
            grads_ref[2 * width:] = dv_ref[...].astype(BF16)


def attend_backward(part, me, seg_row, qt, extra, kn, kt, vn, out, grad, earlier, after):
    heads, _, length = qt.shape
    width = heads * HEAD
    count = length // TILE // PARTS
    offset = part * count

    def body(*refs):
        backward_body(part, *refs)

    in_specs = [
        pl.BlockSpec(memory_space=pltpu.SMEM),
        const((1, length)),
        pl.BlockSpec((heads, WIDE, TILE), lambda i, m: (0, 0, i + offset)),
        pl.BlockSpec((heads, 16, TILE), lambda i, m: (0, 0, i)),
        const(kn.shape), const(kt.shape), const(vn.shape),
        pl.BlockSpec((1, width, TILE), lambda i, m: (i, 0, 0)),
        const(grad[0].shape), const(grad[1].shape), const(grad[2].shape), const(grad[3].shape),
    ] + [const(v.shape) for v in earlier] + [pl.BlockSpec(memory_space=pl.ANY)] * len(after)
    scratch = [
        pltpu.VMEM((heads, WIDE, TILE), BF16),
        pltpu.VMEM((heads, WIDE, TILE), BF16),
        pltpu.VMEM((width, TILE), F32),
    ]
    if part == 0:
        out_specs = [pl.BlockSpec((width, TILE), lambda i, m: (0, i)), const((width, length)), const((width, length))]
        out_shape = [shape_of(width, count * TILE), shape_of(width, length, dtype=F32), shape_of(width, length, dtype=F32)]
    else:
        out_specs = const((3 * width, length))
        out_shape = shape_of(3 * width, length)
        scratch += [pltpu.VMEM((width, length), F32), pltpu.VMEM((width, length), F32)]
    return kernel_call(
        body,
        (me, seg_row, seg_row, qt, extra, kn, kt, vn, out, *grad, *earlier, *after),
        free_in=(10, 11, 12) + tuple(range(13 + len(earlier), 15 + len(earlier))),
        grid_spec=pltpu.PrefetchScalarGridSpec(
            num_scalar_prefetch=1, grid=(count,), in_specs=in_specs, out_specs=out_specs, scratch_shapes=scratch,
        ),
        out_shape=out_shape,
        cost_estimate=cost(16e9, 10e6, 4e6),
        name="attend_backward",
    )


def middle_body(me_ref, x_ref, m0_ref, m1_ref, m2_ref, m3_ref, w0_ref, w1_ref, w2_ref, w3_ref,
                vec_ref, *rest):
    residual_ref, own_ref, mixed_ref = rest[-3:]
    total = x_ref[...].astype(F32) + vec_ref[2:3, :]
    pairs = ((m0_ref, w0_ref), (m1_ref, w1_ref), (m2_ref, w2_ref), (m3_ref, w3_ref))
    for n, (m_ref, w_ref) in enumerate(pairs):
        total = total + tn(m_ref[...], w_ref[...])
        mixed_ref[n] = m_ref[...]
    residual_ref[...] = total
    normed, _, _ = stats(total)
    own_ref[...] = (normed * vec_ref[3:4, :] + vec_ref[4:5, :]).astype(BF16)


def middle(part, me, tokens, mixed, weights, vectors, after):
    features = tokens.shape[1]
    width = weights[0].shape[0]
    return kernel_call(
        middle_body,
        (me, tokens, *mixed, *weights, vectors, *after),
        free_in=(3, 4, 5),
        free_out=(1,),
        grid_spec=pltpu.PrefetchScalarGridSpec(
            num_scalar_prefetch=1,
            grid=(1,),
            in_specs=[pl.BlockSpec((TILE, features), lambda i, m: (4 * part + m[0], 0))]
            + [const(v.shape) for v in mixed] + [const(v.shape) for v in weights] + [const(vectors.shape)]
            + [pl.BlockSpec(memory_space=pl.ANY)] * len(after),
            out_specs=[const((TILE, features)), const((TILE, features)), const((4, width, TILE))],
        ),
        out_shape=[shape_of(TILE, features, dtype=F32), shape_of(TILE, features), shape_of(4, width, TILE)],
        cost_estimate=cost(2e9, 3e6),
        name="middle",
    )


def feed_piece(x, g, inner_ref, vec_ref, outer_ref):
    hidden = nn(x, inner_ref[...]) + vec_ref[7:8, :]
    half = 0.5 + 0.5 * lax.erf(hidden * 0.5 ** 0.5)
    act = (hidden * half).astype(BF16)
    slope = half + hidden * (jnp.exp(-0.5 * hidden * hidden) * 0.3989422804014327)
    dh = (nt(g, outer_ref[...]) * slope).astype(BF16)
    out = nn(act, outer_ref[...]).astype(BF16)
    return act, dh, out, nt(dh, inner_ref[...]).astype(BF16)


def near_body(me_ref, *refs):
    count = 2 * PARTS
    x_refs = refs[:count]
    g_ref, inner_ref, vec_ref, outer_ref = refs[count:count + 4]
    out_refs, back_refs = refs[count + 4:count + 6], refs[count + 6:-6]
    sum_ref, grad_ref, x_all, g_all, act_all, dh_all = refs[-6:]
    i = pl.program_id(0)
    at = pl.ds(pl.multiple_of(i * TILE, TILE), TILE)
    for n, x_ref in enumerate(x_refs):
        @pl.when(i == n)
        def _(n=n, x_ref=x_ref):
            x_all[n * TILE:(n + 1) * TILE] = x_ref[...]

    g_all[at] = g_ref[...]
    act, dh, out, back = feed_piece(x_all[at], g_ref[...], inner_ref, vec_ref, outer_ref)
    act_all[at] = act
    dh_all[at] = dh
    sums = fold(dh.astype(F32))

    @pl.when(i == 0)
    def _():
        sum_ref[...] = jnp.zeros_like(sum_ref)

    sum_ref[...] += sums
    for n in range(count):
        @pl.when(i == n)
        def _(n=n):
            out_refs[n % 2][n // 2 * TILE:(n // 2 + 1) * TILE] = out
            back_refs[n][...] = back

    @pl.when(i == count - 1)
    def _():
        grad_ref[0] = tn(act_all[...], g_all[...]).astype(BF16)
        grad_ref[1] = tn(x_all[...], dh_all[...]).astype(BF16)


def feed_near(me, pieces, cot, inner, vectors, outer):
    features = cot.shape[1]
    units = inner.shape[1]
    count = 2 * PARTS
    piece = const((TILE, features))
    scratch = lambda n: pltpu.VMEM((count * TILE, n), BF16)
    return kernel_call(
        near_body,
        (me, *pieces, cot, inner, vectors, outer),
        free_in=tuple(range(1, count + 1)),
        free_out=(3, 5),
        grid_spec=pltpu.PrefetchScalarGridSpec(
            num_scalar_prefetch=1,
            grid=(count,),
            in_specs=[piece] * count
            + [pl.BlockSpec((TILE, features), lambda i, m: (4 * (i // 2) + (m[0] ^ (i % 2)), 0)),
               const(inner.shape), const(vectors.shape), const(outer.shape)],
            out_specs=[const((PARTS * TILE, features))] * 2 + [piece] * count
            + [const((8, units)), const((2, units, features))],
            scratch_shapes=[scratch(features), scratch(features), scratch(units), scratch(units)],
        ),
        out_shape=[shape_of(PARTS * TILE, features)] * 2 + [shape_of(TILE, features)] * count
        + [shape_of(8, units, dtype=F32), shape_of(2, units, features)],
        cost_estimate=cost(15e9, 12e6, 2e6),
        name="feed_near",
    )


def far_body(me_ref, x0_ref, x1_ref, g_ref, inner_ref, vec_ref, outer_ref, *rest):
    left_ref, right_ref, out0_ref, out1_ref, back0_ref, back1_ref, sum_ref = rest[-7:]
    i = pl.program_id(0)
    for n, x_ref in enumerate((x0_ref, x1_ref)):
        @pl.when(i == n)
        def _(x_ref=x_ref):
            left_ref[1] = x_ref[...]

    right_ref[0] = g_ref[...]
    act, dh, out, back = feed_piece(left_ref[1], g_ref[...], inner_ref, vec_ref, outer_ref)
    left_ref[0] = act
    right_ref[1] = dh
    sums = fold(dh.astype(F32))
    for n, (out_ref, back_ref) in enumerate(((out0_ref, back0_ref), (out1_ref, back1_ref))):
        @pl.when(i == n)
        def _(n=n, out_ref=out_ref, back_ref=back_ref):
            sum_ref[...] = sum_ref[...] + sums if n else sums
            out_ref[...] = out
            back_ref[...] = back


def feed_far(part, me, first, second, cot, inner, vectors, outer, kept):
    features = cot.shape[1]
    units = inner.shape[1]
    rows = pl.BlockSpec((2, TILE, features), lambda i, m: (0, 2 * part + i, 0))
    piece = const((TILE, features))
    half = pl.BlockSpec((TILE, features), lambda i, m: (part, 0))
    return kernel_call(
        far_body,
        (me, first, second, cot, inner, vectors, outer, *kept),
        free_in=(1, 2),
        free_out=(5,),
        grid_spec=pltpu.PrefetchScalarGridSpec(
            num_scalar_prefetch=1,
            grid=(2,),
            in_specs=[
                piece, piece,
                pl.BlockSpec((TILE, features), lambda i, m: (4 * part + (m[0] ^ (2 + i)), 0)),
                const(inner.shape), const(vectors.shape), const(outer.shape),
            ] + [pl.BlockSpec(memory_space=pl.ANY)] * len(kept),
            out_specs=[rows, rows, half, half, piece, piece, const((8, units))],
        ),
        out_shape=[shape_of(2, 2 * PARTS * TILE, features)] * 2 + [shape_of(PARTS * TILE, features)] * 2
        + [shape_of(TILE, features)] * 2 + [shape_of(8, units, dtype=F32)],
        input_output_aliases={7 + n: n for n in range(len(kept))},
        cost_estimate=cost(5e9, 8e6, 1e6),
        name="feed_far",
    )


def feed_grad_body(xz_ref, left_ref, right_ref, before_ref, keep_ref, send_ref):
    value = (tn(left_ref[0], right_ref[0]) + before_ref[0].astype(F32)).astype(BF16)
    mine = pl.program_id(0) == xz_ref[0]

    @pl.when(mine)
    def _():
        keep_ref[...] = value

    @pl.when(jnp.logical_not(mine))
    def _():
        send_ref[...] = value


def feed_grad(xz, left, right, before):
    _, rows, features = left.shape
    both = pl.BlockSpec((1, rows, features), lambda i, m: (i, 0, 0))
    return kernel_call(
        feed_grad_body,
        (xz, left, right, before),
        grid_spec=pltpu.PrefetchScalarGridSpec(
            num_scalar_prefetch=1,
            grid=(2,),
            in_specs=[both, both, pl.BlockSpec((1, features, features), lambda i, m: (i, 0, 0))],
            out_specs=[const(before.shape[1:])] * 2,
        ),
        out_shape=[shape_of(*before.shape[1:])] * 2,
        cost_estimate=cost(5e9, 10e6),
        name="feed_grad",
    )


def feed_ready_body(xz_ref, mine_ref, other_ref, outer_ref, inner_ref):
    for from_ref, here in ((mine_ref, xz_ref[0]), (other_ref, 1 - xz_ref[0])):
        for n, to_ref in enumerate((outer_ref, inner_ref)):
            @pl.when(here == n)
            def _(from_ref=from_ref, to_ref=to_ref):
                to_ref[...] = from_ref[...].astype(F32)


def feed_ready(xz, mine, other):
    rows, features = mine.shape
    block = pl.BlockSpec((TILE, features), lambda i, m: (i, 0))
    return kernel_call(
        feed_ready_body,
        (xz, mine, other),
        free_in=(1, 2),
        grid_spec=pltpu.PrefetchScalarGridSpec(
            num_scalar_prefetch=1,
            grid=(rows // TILE,),
            in_specs=[block, block],
            out_specs=[block, block],
        ),
        out_shape=[shape_of(rows, features, dtype=F32)] * 2,
        cost_estimate=cost(1e6, 7e6),
        name="feed_ready",
    )


def back_body(me_ref, b0_ref, b1_ref, b2_ref, residual_ref, g_ref, vec_ref, w0_ref, w1_ref, w2_ref, w3_ref,
              *rest):
    grad_ref, low_ref, a0_ref, a1_ref, a2_ref, a3_ref, sum_ref = rest[-7:]
    grad_mid = b0_ref[...].astype(F32) + b1_ref[...].astype(F32) + b2_ref[...].astype(F32)
    normed, scale, _ = stats(residual_ref[...])
    upstream = g_ref[...].astype(F32)
    grad = upstream + norm_back(grad_mid, normed, scale, vec_ref[3:4, :])
    grad_ref[...] = grad
    low = grad.astype(BF16)
    low_ref[...] = low
    for w_ref, a_ref in ((w0_ref, a0_ref), (w1_ref, a1_ref), (w2_ref, a2_ref), (w3_ref, a3_ref)):
        a_ref[...] = nt(w_ref[...], low).astype(BF16)
    for n, value in enumerate((grad_mid * normed, grad_mid, grad, upstream)):
        sum_ref[8 * n:8 * n + 8] = fold(value)


def middle_back(part, me, sums, residual, cot, vectors, weights, after):
    features = cot.shape[1]
    piece = const((TILE, features))
    width = weights[0].shape[0]
    return kernel_call(
        back_body,
        (me, *sums, residual, cot, vectors, *weights, *after),
        free_in=(2, 3) + tuple(range(11, 11 + len(after))),
        free_out=(3, 4, 5),
        grid_spec=pltpu.PrefetchScalarGridSpec(
            num_scalar_prefetch=1,
            grid=(1,),
            in_specs=[piece] * 4
            + [pl.BlockSpec((TILE, features), lambda i, m: (4 * part + m[0], 0)), const(vectors.shape)]
            + [const(v.shape) for v in weights] + [pl.BlockSpec(memory_space=pl.ANY)] * len(after),
            out_specs=[piece, piece] + [const((width, TILE))] * 4 + [const((32, features))],
        ),
        out_shape=[shape_of(TILE, features, dtype=F32), shape_of(TILE, features)]
        + [shape_of(width, TILE)] * 4 + [shape_of(32, features, dtype=F32)],
        cost_estimate=cost(2e9, 4e6),
        name="middle_back",
    )


def output_body(*refs):
    mixed, lows, outs = refs[:PARTS], refs[PARTS:2 * PARTS], refs[2 * PARTS:]
    for n in range(4):
        total = nn(mixed[0][n], lows[0][...])
        for p in range(1, PARTS):
            total = total + nn(mixed[p][n], lows[p][...])
        outs[n][...] = total.astype(BF16)


def output_grad(mixed, lows):
    width, features = mixed[0].shape[1], lows[0].shape[1]
    return kernel_call(
        output_body,
        (*mixed, *lows),
        free_out=(1, 3),
        out_shape=[shape_of(width, features)] * 4,
        cost_estimate=cost(2e9, 4e6),
        name="output_grad",
    )


def tail_body(me_ref, g_ref, wq_ref, wk_ref, wv_ref, x_ref, stat_ref, *rest):
    early, units = rest[:PARTS], rest[PARTS:2 * PARTS + 1]
    o0_ref, o1_ref, o2_ref, o3_ref, apart_ref, vec_ref, sum_ref, row_ref = rest[-8:]
    i, p = pl.program_id(0), pl.program_id(1)
    grads = g_ref[...]
    width = wq_ref.shape[0]
    value = tn(grads[:width], wq_ref[...]) + tn(grads[width:2 * width], wk_ref[...])
    value = value + tn(grads[2 * width:], wv_ref[...])

    @pl.when((i == 0) & (p == 0))
    def _():
        row_ref[...] = jnp.zeros_like(row_ref)
        sum_ref[...] = jnp.zeros_like(sum_ref)

    row_ref[...] += nt(jnp.ones((8, grads.shape[1]), BF16), grads)
    normed = (x_ref[...].astype(F32) - stat_ref[:, 0:1]) * stat_ref[:, 1:2]
    sum_ref[:8] += fold(value * normed)
    sum_ref[8:] += fold(value)
    value = value.astype(BF16)
    for step, o_ref in enumerate((o3_ref, o2_ref, o1_ref, o0_ref)):
        @pl.when(i == step)
        def _(o_ref=o_ref):
            o_ref[pl.ds(pl.multiple_of(p * TILE, TILE), TILE), :] = value

    @pl.when((i == 3) & (p == PARTS - 1))
    def _():
        row = lax.broadcasted_iota(jnp.int32, vec_ref.shape, 0)
        vectors = jnp.zeros(vec_ref.shape, F32)
        before = early[0][...]
        for ref in early[1:]:
            before = before + ref[...]
        parts = [before[8 * n:8 * n + 8] for n in range(4)] + [sum_ref[:8], sum_ref[8:]]
        for n, part in enumerate(parts):
            vectors = jnp.where(row == n, jnp.sum(part, axis=0, keepdims=True), vectors)
        vec_ref[...] = vectors
        inside = units[0][...]
        for ref in units[1:]:
            inside = inside + ref[...]
        apart_ref[...] = jnp.where(row == 6, jnp.sum(inside, axis=0, keepdims=True), 0.0)
        apart_ref[7:8, :row_ref.shape[1]] = row_ref[0:1]
        o3_ref[PARTS * TILE:] = paired(vectors)


def tail(me, grads, wq, wk, wv, tokens, stat, early, units, after):
    deep = grads.shape[0]
    features = wq.shape[1]
    share = const((PARTS * TILE, features))
    more = const((PARTS * TILE + 16, features))
    at = lambda i, p, m: 4 * p + (m[0] ^ (3 - i))
    return kernel_call(
        tail_body,
        (me, grads, wq, wk, wv, tokens, stat, *early, *units, *after),
        free_out=(1, 3),
        grid_spec=pltpu.PrefetchScalarGridSpec(
            num_scalar_prefetch=1,
            grid=(4, PARTS),
            in_specs=[pl.BlockSpec((deep, TILE), lambda i, p, m: (0, at(i, p, m))),
                      const(wq.shape), const(wk.shape), const(wv.shape),
                      pl.BlockSpec((TILE, features), lambda i, p, m: (at(i, p, m), 0)),
                      pl.BlockSpec((TILE, WIDE), lambda i, p, m: (at(i, p, m), 0))]
            + [const(v.shape) for v in (*early, *units)] + [pl.BlockSpec(memory_space=pl.ANY)] * len(after),
            out_specs=[share, share, share, more, const((8, features)), const((8, features))],
            scratch_shapes=[pltpu.VMEM((16, features), F32), pltpu.VMEM((8, deep), F32)],
        ),
        out_shape=[shape_of(PARTS * TILE, features)] * 3 + [shape_of(PARTS * TILE + 16, features)]
        + [shape_of(8, features, dtype=F32)] * 2,
        cost_estimate=cost(4e9, 10e6),
        name="tail",
    )


def chip_body(one_ref, two_ref, vec_ref, *rest):
    out_ref = rest[-1]
    rows = one_ref.shape[0]
    out_ref[:rows] = (one_ref[...].astype(F32) + two_ref[:rows].astype(F32)).astype(BF16)
    out_ref[rows:] = paired(vec_ref[...] + joined(two_ref[rows:]))


def chip_sum(one, two, vectors, after):
    return kernel_call(
        chip_body,
        (one, two, vectors, *after),
        free_in=(1,) + tuple(range(3, 3 + len(after))),
        free_out=(0,),
        grid=(1,),
        in_specs=[const(one.shape), const(two.shape), const(vectors.shape)]
        + [pl.BlockSpec(memory_space=pl.ANY)] * len(after),
        out_specs=[const(two.shape)],
        out_shape=[shape_of(*two.shape)],
        name="chip_sum",
    )[0]


def halves_body(xz_ref, g_ref, go_ref, *rest):
    keep_ref, send_ref = rest[-2:]
    width = go_ref.shape[0]
    for to_ref, half in ((keep_ref, xz_ref[0]), (send_ref, 1 - xz_ref[0])):
        @pl.when(half == 0)
        def _(to_ref=to_ref):
            to_ref[...] = g_ref[:2 * width]

        @pl.when(half == 1)
        def _(to_ref=to_ref):
            to_ref[:width] = g_ref[2 * width:]
            to_ref[width:] = go_ref[...]


def halves(xz, grad_weights, grad_output, after):
    width, features = grad_output.shape
    half = const((2 * width, features))
    return kernel_call(
        halves_body,
        (xz, grad_weights, grad_output, *after),
        free_in=(1, 2, 3),
        grid_spec=pltpu.PrefetchScalarGridSpec(
            num_scalar_prefetch=1,
            grid=(1,),
            in_specs=[const(grad_weights.shape), const(grad_output.shape)]
            + [pl.BlockSpec(memory_space=pl.ANY)] * len(after),
            out_specs=[half, half],
        ),
        out_shape=[shape_of(2 * width, features)] * 2,
        cost_estimate=cost(1e6, 4e6),
        name="halves",
    )


def quarter_body(count, xz_ref, one_ref, two_ref, *rest):
    rows = one_ref.shape[0] // count
    for n, out_ref in enumerate(rest[-count:]):
        at = pl.ds(pl.multiple_of(lax.rem(xz_ref[1] + n, count) * rows, rows), rows)
        out_ref[...] = (one_ref[at, :].astype(F32) + two_ref[at, :].astype(F32)).astype(BF16)


def quarters(xz, one, two, count, after):
    rows, features = one.shape

    def body(*refs):
        quarter_body(count, *refs)

    return kernel_call(
        body,
        (xz, one, two, *after),
        free_in=(2, 3, 4),
        grid_spec=pltpu.PrefetchScalarGridSpec(
            num_scalar_prefetch=1,
            grid=(1,),
            in_specs=[const(one.shape), const(two.shape)] + [pl.BlockSpec(memory_space=pl.ANY)] * len(after),
            out_specs=[const((rows // count, features))] * count,
        ),
        out_shape=[shape_of(rows // count, features)] * count,
        cost_estimate=cost(1e6, 2e6),
        name="quarters",
    )


def paired(value):
    return jnp.concatenate(split(value, 2), axis=0).astype(BF16)


def joined(both):
    both = both.astype(F32)
    half = both.shape[0] // 2
    return both[:half] + both[half:]


def second_body(count, *refs):
    one_ref, two_ref, apart_ref, out_ref = refs[count], refs[count + 1], refs[count + 2], refs[-1]
    rows = refs[0].shape[0]
    total = refs[0][...].astype(F32)
    for ref in refs[1:count]:
        total = total + ref[...].astype(F32)
    out_ref[:rows] = total.astype(BF16)
    out_ref[rows:] = paired(joined(one_ref[...]) + joined(two_ref[...]) + apart_ref[...])


def second(parts, one, two, apart, after):
    count = len(parts)
    rows, features = parts[0].shape
    last = pl.BlockSpec((16, features), lambda i: (one.shape[0] // 16 - 1, 0))

    def body(*refs):
        second_body(count, *refs)

    return kernel_call(
        body,
        (*parts, one, two, apart, *after),
        free_in=tuple(range(1, count)) + tuple(range(count + 3, count + 3 + len(after))),
        grid=(1,),
        in_specs=[const((rows, features))] * count + [last, last, const(apart.shape)]
        + [pl.BlockSpec(memory_space=pl.ANY)] * len(after),
        out_specs=[const((rows + 16, features))],
        out_shape=[shape_of(rows + 16, features)],
        name="second",
    )[0]


def third_body(count, xz_ref, *refs):
    out_ref = refs[-1]
    step = out_ref.shape[0] - (refs[0].shape[0] * count - out_ref.shape[0]) // (count - 1)
    rows = step // count
    sums = None
    for n, ref in enumerate(refs[:count]):
        place_at = lax.rem(xz_ref[1] + count - n, count)
        out_ref[pl.ds(pl.multiple_of(place_at * rows, rows), rows), :] = ref[:rows]
        value = joined(ref[rows:])
        sums = value if sums is None else sums + value
    out_ref[step:] = paired(sums)


def third(xz, pieces, extra, after):
    count = len(pieces)
    rows, features = pieces[0].shape
    total = (rows - extra) * count + extra

    def body(*refs):
        third_body(count, *refs)

    return kernel_call(
        body,
        (xz, *pieces, *after),
        free_in=tuple(range(1, count + 1)),
        grid_spec=pltpu.PrefetchScalarGridSpec(
            num_scalar_prefetch=1,
            grid=(1,),
            in_specs=[const((rows, features))] * count + [pl.BlockSpec(memory_space=pl.ANY)] * len(after),
            out_specs=[const((total, features))],
        ),
        out_shape=[shape_of(total, features)],
        name="third",
    )[0]


def ready_body(xz_ref, mine_ref, other_ref, *rest):
    outs = rest[-14:]
    width = outs[0].shape[0]
    for n, out_ref in enumerate(outs[:4]):
        rows = slice(n % 2 * width, (n % 2 + 1) * width)
        for to_ref, chosen in ((mine_ref, xz_ref[0] == n // 2), (other_ref, xz_ref[0] != n // 2)):
            @pl.when(chosen)
            def _(to_ref=to_ref, out_ref=out_ref, rows=rows):
                out_ref[...] = to_ref[rows].astype(F32)

    small = joined(mine_ref[2 * width:]) + joined(other_ref[2 * width:])
    for n, out_ref in enumerate(outs[4:11]):
        out_ref[...] = small[n]
    for n, out_ref in enumerate(outs[11:]):
        out_ref[...] = small[7, n * width:(n + 1) * width]


def ready(xz, mine, other, width, after):
    rows, features = mine.shape
    sizes = [(features,)] * 7 + [(width,)] * 3
    return kernel_call(
        ready_body,
        (xz, mine, other, *after),
        free_in=(2,),
        grid_spec=pltpu.PrefetchScalarGridSpec(
            num_scalar_prefetch=1,
            grid=(1,),
            in_specs=[const(mine.shape), const(other.shape)] + [pl.BlockSpec(memory_space=pl.ANY)] * len(after),
            out_specs=[const((width, features))] * 4 + [const(size) for size in sizes],
        ),
        out_shape=[shape_of(width, features, dtype=F32)] * 4 + [shape_of(*size, dtype=F32) for size in sizes],
        cost_estimate=cost(1e6, 4e6),
        name="ready",
    )


def final_body(me_ref, b0_ref, b1_ref, b2_ref, x_ref, *rest):
    grad_refs, vec_ref, out_ref = rest[:PARTS], rest[PARTS], rest[-1]
    p = pl.program_id(0)
    grad_attend = b0_ref[...].astype(F32) + b1_ref[...].astype(F32) + b2_ref[...].astype(F32)
    normed, scale, _ = stats(x_ref[...].astype(F32))
    back = norm_back(grad_attend, normed, scale, vec_ref[0:1, :])
    for n, grad_ref in enumerate(grad_refs):
        @pl.when(p == n)
        def _(grad_ref=grad_ref):
            out_ref[...] = (grad_ref[...] + back).astype(BF16)


def final(me, sums, tokens, grads, vectors, after):
    features = tokens.shape[1]
    rows = pl.BlockSpec((TILE, features), lambda p, m: (p, 0))
    return kernel_call(
        final_body,
        (me, *sums, tokens, *grads, vectors, *after),
        free_out=(0,),
        grid_spec=pltpu.PrefetchScalarGridSpec(
            num_scalar_prefetch=1,
            grid=(PARTS,),
            in_specs=[rows] * 3 + [pl.BlockSpec((TILE, features), lambda p, m: (4 * p + m[0], 0))]
            + [const((TILE, features))] * PARTS + [const(vectors.shape)]
            + [pl.BlockSpec(memory_space=pl.ANY)] * len(after),
            out_specs=[rows],
        ),
        out_shape=[shape_of(PARTS * TILE, features)],
        cost_estimate=cost(1e8, 5e6),
        name="final",
    )[0]


def place_body(me_ref, p0_ref, p1_ref, p2_ref, p3_ref, *rest):
    out_ref = rest[-1]
    for step, p_ref in enumerate((p0_ref, p1_ref, p2_ref, p3_ref)):
        @pl.when(pl.program_id(0) == step)
        def _(p_ref=p_ref):
            at = pl.ds(pl.multiple_of(pl.program_id(1) * TILE, TILE), TILE)
            out_ref[...] = p_ref[at, :].astype(out_ref.dtype)


def place(me, shares, dtype, after):
    rows, features = shares[0].shape
    return kernel_call(
        place_body,
        (me, *shares, *after),
        free_in=(1, 2, 3, 4),
        grid_spec=pltpu.PrefetchScalarGridSpec(
            num_scalar_prefetch=1,
            grid=(4, PARTS),
            in_specs=[const((rows, features))] * 4 + [pl.BlockSpec(memory_space=pl.ANY)] * len(after),
            out_specs=pl.BlockSpec((TILE, features), lambda i, p, m: (4 * p + (m[0] ^ i), 0)),
        ),
        out_shape=shape_of(4 * rows, features, dtype=dtype),
        cost_estimate=cost(1e6, 9e6),
        name="place",
    )


def fence_body(*refs):
    pass


def fence(value, *after, space=pltpu.HBM):
    anywhere = pl.BlockSpec(memory_space=pl.ANY)
    return pl.pallas_call(
        fence_body,
        in_specs=[anywhere] * (1 + len(after)),
        out_specs=anywhere,
        out_shape=space(value.shape, value.dtype),
        input_output_aliases={0: 0},
        name="fence",
    )(pltpu.with_memory_space_constraint(value, space), *after)


def other_core(value):
    return lax.ppermute(value, "core", SWAP)


def other_chip(value):
    return lax.ppermute(value, "y", SWAP)


def crosswise(value):
    return lax.ppermute(value, MP, [(n, n ^ 3) for n in range(4)])


def exchange(pieces):
    return [pieces[0], other_core(pieces[1]), other_chip(pieces[2]), crosswise(pieces[3])]


def gather_sum(pieces):
    near = other_core(pieces[1])
    far = (pieces[2].astype(F32) + other_core(pieces[3]).astype(F32)).astype(BF16)
    return [pieces[0], near, other_chip(far)], far


def spread(value):
    far = other_chip(value)
    return [value, other_core(value), far, other_core(far)]


def pick(values, at):
    return lax.dynamic_index_in_dim(values, at, 0, keepdims=False)


def turned(values, way):
    size = lax.axis_size("z")
    return lax.ppermute(values, "z", [(n, (n + way) % size) for n in range(size)])


def sum_first(xz, keep, got, after):
    size = lax.axis_size("z")
    if size > 4:
        return [lax.psum(keep + got, "z")]
    return quarters(xz, keep, got, size, after)


def gather_z(value):
    size = lax.axis_size("z")
    if size > 4:
        return [lax.all_gather(value, "z", axis=0, tiled=True)]
    return [turned(value, way) if way else value for way in range(size)]


def local(
    tokens,
    segment_ids,
    gain_one,
    bias_one,
    query_weight,
    query_bias,
    key_weight,
    value_weight,
    value_bias,
    output_weight,
    output_bias,
    gain_two,
    bias_two,
    inner_weight,
    inner_bias,
    outer_weight,
    outer_bias,
    cotangent,
):
    _, length, features = tokens.shape
    width = query_weight.shape[1]
    heads = width // HEAD
    tokens = tokens.reshape(length, features)
    cot = cotangent.reshape(length, features)
    at = lax.axis_index(MP).astype(jnp.int32)
    me = at[None]
    xz = jnp.stack([lax.axis_index("x"), lax.axis_index("z")]).astype(jnp.int32)
    apart = jnp.concatenate([query_bias, value_bias, jnp.zeros((features - 2 * width,), F32)])
    vectors = jnp.concatenate([gain_one, bias_one, output_bias, gain_two, bias_two, outer_bias, apart, inner_bias])
    vectors = vectors.reshape(8, features)
    wq, wk, wv = query_weight.T, key_weight.T, value_weight.T

    output_weights = spread(output_weight)
    attend_in, qt, kt, vt, kn, vn, stat = project(tokens, segment_ids, vectors, wq, wk, wv, heads)

    parts = range(PARTS)
    attended, extras, fours = [], [], []
    for p in parts:
        out, extra, *four = attend_forward(p, me, segment_ids, qt, kn, vt, output_weights[1:3] if p == 0 else ())
        attended.append(out)
        extras.append(extra)
        fours.append(exchange(four))
    mixed, residuals, pieces = [], [], []
    for p in parts:
        residual, own, together = middle(p, me, tokens, fours[p], output_weights, vectors, extras[p + 1:])
        mixed.append(together)
        residuals.append(residual)
        pieces.append([own, other_core(own), other_chip(own)])

    backs = {}
    *outs, b00, b01, b10, b11, near_sum, near_grad = feed_near(
        me, [pieces[p][n] for p in parts for n in (0, 1)], cot, inner_weight, vectors, outer_weight
    )
    backs[0, 0], backs[0, 1], backs[1, 0], backs[1, 1] = b00, b01, b10, b11
    sums, kept, gathered, far_sums, behind = [near_sum], (), [], [], b00
    for p in parts:
        far = fence(pieces[p][2], behind, space=pltpu.VMEM)
        *kept, backs[p, 2], backs[p, 3], far_sum = feed_far(
            p, me, far, other_core(far), cot, inner_weight, vectors, outer_weight, kept
        )
        behind = backs[p, 2]
        sums.append(far_sum)
        if p:
            backs[p, 3] = fence(backs[p, 3], gathered[-1][2], space=pltpu.VMEM)
            feed_keep, feed_send = feed_grad(xz, kept[0], kept[1], near_grad)
            backs[p, 2] = fence(backs[p, 2], feed_send)
        summed, far_sum = gather_sum([backs[p, n] for n in range(4)])
        gathered.append(summed)
        far_sums.append(far_sum)
    left, right, *far_outs = kept
    outs += far_outs
    grad_residuals, lows, grads_attended, inner_sums = [], [], [], []
    for p in parts:
        grad, low, a0, a1, a2, a3, vector = middle_back(
            p, me, gathered[p], residuals[p], cot, vectors, output_weights, far_sums[p + 1:]
        )
        grad_residuals.append(grad)
        lows.append(low)
        inner_sums.append(vector)
        grads_attended.append(exchange([a0, a1, a2, a3]))

    near = other_core(fence(outs[1], *far_sums))
    far = (outs[2].astype(F32) + other_core(fence(outs[3], *far_sums)).astype(F32)).astype(BF16)
    far = fence(far, lows[-1], space=pltpu.VMEM)
    part = output_grad(mixed, lows)
    earlier = attend_backward(0, me, segment_ids, qt, extras[0], kn, kt, vn, attended[0], grads_attended[0], (),
                              (far, near, part[0]))
    there = other_chip(far)
    feed_sum = fence(feed_keep, earlier[0]).astype(F32) + lax.ppermute(feed_send, "x", SWAP).astype(F32)
    feed_sum = lax.psum_scatter(feed_sum.astype(BF16), "z", scatter_dimension=0, tiled=True)
    part_far = fence(part[2], earlier[0])
    part_far = (part_far.astype(F32) + other_core(part[3]).astype(F32)).astype(BF16)
    part_near = other_core(part[1])
    grads = attend_backward(1, me, segment_ids, qt, extras[1], kn, kt, vn, attended[1], grads_attended[1], earlier,
                            (part_near, part_far, there))

    part_across = other_chip(part_far)
    grad_output = fence(part[0], grads).astype(F32) + part_near.astype(F32) + part_across.astype(F32)
    keep, send = halves(xz, nn(grads, attend_in).astype(BF16), grad_output.astype(BF16), ())
    result = jnp.concatenate(residuals) + fence(outs[0], send).astype(F32) + near.astype(F32)
    result = (result + there.astype(F32) + outer_bias).astype(BF16)
    near, far = other_core(result), other_chip(result)
    got = lax.ppermute(send, "x", SWAP)
    back_own, back_near, back_far, back_across, apart, summed = tail(
        me, grads, wq, wk, wv, tokens, stat, inner_sums, sums, (send,)
    )
    feed_sum = lax.all_gather(fence(feed_sum, send), "z", axis=0, tiled=True)
    feed_other = lax.ppermute(feed_sum, "x", SWAP)
    quarter = sum_first(xz, keep, got, (near, far, apart))
    back_across = other_core(fence(back_across, quarter[-1], space=pltpu.VMEM))
    back_far = chip_sum(back_far, back_across, summed, ())
    back_there = other_chip(back_far)
    share = final(me, [back_own, other_core(back_near), back_there], tokens, grad_residuals, vectors, ())
    if len(quarter) > 1:
        turns = [quarter[0]] + [turned(part, n + 1) for n, part in enumerate(quarter[1:])]
        held = second(turns, back_far, back_there, apart, (share,))
        layer_out = place(me, [result, near, far, other_core(far)], BF16, (held, feed_other))
        mine = third(xz, gather_z(held), 16, (layer_out,))
    else:
        small = joined(back_far[-16:]) + joined(back_there[-16:]) + apart
        layer_out = place(me, [result, near, far, other_core(far)], BF16, ())
        mine = jnp.concatenate([quarter[0], paired(lax.psum(small, "z"))])
    share = fence(share, held if len(quarter) > 1 else mine, space=pltpu.VMEM)
    near, far = other_core(share), fence(other_chip(share), mine, space=pltpu.VMEM)
    input_grad = place(me, [share, near, far, other_core(far)], F32, (mine,))
    feed_sum = feed_ready(xz, feed_sum, feed_other)
    *wide, two_gain, two_bias, output_sum, outer_bias, one_gain, one_bias, inner_bias, query, _, value = ready(
        xz, mine, lax.ppermute(mine, "x", SWAP), width, (*feed_sum, input_grad)
    )
    return (
        layer_out.reshape(1, length, features),
        input_grad.reshape(1, length, features),
        one_gain,
        one_bias,
        wide[0].T,
        query,
        wide[1].T,
        wide[2].T,
        value,
        wide[3],
        output_sum,
        two_gain,
        two_bias,
        feed_sum[1],
        inner_bias,
        feed_sum[0],
        outer_bias,
    )


def solution(mesh):
    rows = mesh.shape["dp"]
    inner = Mesh(mesh.devices.reshape(rows // 2, 2, 2, 2), DP + MP)
    placed = (
        P(DP, None, None),
        P(DP, None),
        P(),
        P(),
        P(None, MP),
        P(MP),
        P(None, MP),
        P(None, MP),
        P(MP),
        P(MP, None),
        P(),
        P(),
        P(),
        P(None, MP),
        P(MP),
        P(MP, None),
        P(),
        P(DP, None, None),
    )
    return jax.shard_map(
        local,
        mesh=inner,
        in_specs=placed,
        out_specs=(
            P(DP, None, None),
            P(DP, None, None),
            P(),
            P(),
            P(None, MP),
            P(MP),
            P(None, MP),
            P(None, MP),
            P(MP),
            P(MP, None),
            P(),
            P(),
            P(),
            P(None, MP),
            P(MP),
            P(MP, None),
            P(),
        ),
        check_vma=False,
    )
```
